32 devices in a mesh: dp: 8 (over y, x, core), mp: 4 (over z).
Axes of the slice: x: 2, y: 2, z: 4, core: 2. Of those that a mesh axis runs over, the one named last changes fastest.
Arguments:
- inputs: bfloat16 [1024, 2048], P('dp'), may hold values from -6 to 6
- segment_ids: int32 [8, 128], P('dp'), may hold values from 0 to 5, never falling along the last dimension, each value on 1 to 64 neighbouring positions
- cotangent: bfloat16 [1024, 2048], P('dp'), may hold values from -6 to 6
- query_key_value: float32 [3, 2048, 2048], P(None, 'dp', 'mp'), may hold values from -1 to 1
- attention_out: float32 [2048, 2048], P(('mp', 'dp')), may hold values from -1 to 1
- expand_weight: float32 [2048, 8192], P('dp', 'mp'), may hold values from -0.125 to 0.125
- contract_weight: float32 [8192, 2048], P(('mp', 'dp')), may hold values from -0.25 to 0.25
- norm_params: float32 [4, 2048], P(None, 'dp'), may hold values from -2 to 2
- first_query_key_value: float32 [3, 2048, 2048], P(None, 'dp', 'mp'), may hold values from -2 to 2
- first_attention_out: float32 [2048, 2048], P(('mp', 'dp')), may hold values from -0.375 to 0.375
- first_expand_weight: float32 [2048, 8192], P('dp', 'mp'), may hold values from -1.5 to 1.5
- first_contract_weight: float32 [8192, 2048], P(('mp', 'dp')), may hold values from -2 to 2
- first_norm_params: float32 [4, 2048], P(None, 'dp'), may hold values from -2 to 2
- second_query_key_value: float32 [3, 2048, 2048], P(None, 'dp', 'mp'), may hold values from 0.03 to 0.3
- second_attention_out: float32 [2048, 2048], P(('mp', 'dp')), may hold values from 0.0008 to 0.008
- second_expand_weight: float32 [2048, 8192], P('dp', 'mp'), may hold values from 0.015 to 0.15
- second_contract_weight: float32 [8192, 2048], P(('mp', 'dp')), may hold values from 0.03 to 0.3
- second_norm_params: float32 [4, 2048], P(None, 'dp'), may hold values from 0.03 to 0.3
Outputs:
- layer_output: bfloat16 [1024, 2048], P('dp')
- input_grad: float32 [1024, 2048], P('dp')
- grad_query_key_value: float32 [3, 2048, 2048], P(None, 'dp', 'mp')
- grad_attention_out: float32 [2048, 2048], P(('mp', 'dp'))
- grad_expand_weight: float32 [2048, 8192], P('dp', 'mp')
- grad_contract_weight: float32 [8192, 2048], P(('mp', 'dp'))
- grad_norm_params: float32 [4, 2048], P(None, 'dp')
- new_first_query_key_value: float32 [3, 2048, 2048], P(None, 'dp', 'mp')
- new_first_attention_out: float32 [2048, 2048], P(('mp', 'dp'))
- new_first_expand_weight: float32 [2048, 8192], P('dp', 'mp')
- new_first_contract_weight: float32 [8192, 2048], P(('mp', 'dp'))
- new_first_norm_params: float32 [4, 2048], P(None, 'dp')
- new_second_query_key_value: float32 [3, 2048, 2048], P(None, 'dp', 'mp')
- new_second_attention_out: float32 [2048, 2048], P(('mp', 'dp'))
- new_second_expand_weight: float32 [2048, 8192], P('dp', 'mp')
- new_second_contract_weight: float32 [8192, 2048], P(('mp', 'dp'))
- new_second_norm_params: float32 [4, 2048], P(None, 'dp')
- new_query_key_value: float32 [3, 2048, 2048], P(None, 'dp', 'mp')
- new_attention_out: float32 [2048, 2048], P(('mp', 'dp'))
- new_expand_weight: float32 [2048, 8192], P('dp', 'mp')
- new_contract_weight: float32 [8192, 2048], P(('mp', 'dp'))
- new_norm_params: float32 [4, 2048], P(None, 'dp')
- copy_query_key_value: bfloat16 [3, 2048, 2048], P(None, 'dp', 'mp')
- copy_attention_out: bfloat16 [2048, 2048], P(('mp', 'dp'))
- copy_expand_weight: bfloat16 [2048, 8192], P('dp', 'mp')
- copy_contract_weight: bfloat16 [8192, 2048], P(('mp', 'dp'))
- copy_norm_params: bfloat16 [4, 2048], P(None, 'dp')
- gradient_norm: float32 [], replicated
The draws below stay inside these ranges and needn't reach their ends.
Inputs may be any that keep to these rules, and one draw needn't show every extreme that they name: `segment_ids`: along each row the ids never fall; a segment holds 1 to 64 positions.
All inputs are finite; a program needn't handle non-finite values.
Results may differ from the reference program's by a relative error of at most 0.015.
Values may be sent and summed in bfloat16 or wider, within the bound.
A program may use at most 256 MiB of HBM per device.

```python
import math
import jax
import jax.numpy as jnp
import numpy as np
from jax import lax

D = 2048
HEADS = 16
HEAD_DIM = 128
FF = 8192
TOK_DEV = 128
ADAM_STEP = 5
ROWS = 8
TOKENS = 1024
MAX_NORM = 8192


def draw_query_key_value(key, part):
    base_key, column_key = jax.random.split(jax.random.fold_in(key, 11))
    base = jnp.clip(jax.random.normal(base_key, (3, D, D), jnp.float32), -6.0, 6.0)
    column_shift = 0.3 * jnp.clip(jax.random.normal(column_key, (3, 1, D), jnp.float32), -4.0, 4.0)
    return (base + column_shift) * (1.0 / math.sqrt(D))


def draw_norm_params(key, part):
    gain_key, shift_key = jax.random.split(jax.random.fold_in(key, 23))
    gains = 1.0 + 0.15 * jnp.clip(jax.random.normal(gain_key, (2, D), jnp.float32), -4.0, 4.0)
    shifts = 0.3 * jnp.clip(jax.random.normal(shift_key, (2, D), jnp.float32), -4.0, 4.0)
    return jnp.stack([gains[0], shifts[0], gains[1], shifts[1]])


def steps_of(stream_key, dims, cuts, smallest, high):
    loudness = 1.0
    for position, blocks in cuts:
        heights = jax.random.uniform(jax.random.fold_in(jax.random.fold_in(stream_key, 6), position), (blocks,), jnp.float32, smallest / len(cuts), high / len(cuts))
        loudness = loudness * jnp.repeat(jnp.exp(heights), dims[position] // blocks).reshape((-1,) + (1,) * (len(dims) - 1 - position))
    return loudness


def length_profile(count, total, most, lean):
    weights = [(1 << 20) // math.isqrt(standing ** lean) + 1 for standing in range(2, count + 1)]
    rest, given = total - most - (count - 1), [1] * (count - 1)
    while rest > 0:
        movable = [i for i in range(count - 1) if given[i] < most]
        mass, budget = sum([weights[i] for i in movable]), rest
        for i in movable:
            addition = min(most - given[i], max(1, budget * weights[i] // mass), rest)
            given[i] = given[i] + addition
            rest = rest - addition
    return np.array([most] + given)


def ragged_sizes(own_key, number_of, total, limit, skew):
    if number_of == 2:
        one = jax.random.randint(own_key, (), max(1, total - limit), min(limit, total - 1) + 1)
        return jnp.stack([one, total - one])
    sizes = jnp.asarray(length_profile(number_of, total, limit, skew), jnp.int32)
    couples = (number_of - 1) // 2
    source_of, taker = sizes[1:1 + 2 * couples:2], sizes[2:2 + 2 * couples:2]
    room = jnp.minimum(source_of - 1, limit - taker)
    passed = jax.random.randint(jax.random.fold_in(own_key, 1), (couples,), 0, 1 << 20) % (room + 1)
    sizes = sizes.at[1:1 + 2 * couples:2].set(source_of - passed).at[2:2 + 2 * couples:2].set(taker + passed)
    return sizes[jax.random.permutation(jax.random.fold_in(own_key, 2), number_of)]


def scatter_about(own_key, extent, scale, most, cuts=(), kind=jnp.bfloat16):
    values = scale * jax.random.normal(own_key, extent, jnp.float32)
    if cuts:
        values = values * steps_of(own_key, extent, cuts, -0.22, 0.18)
    return jnp.clip(values, -most, most).astype(kind)


def setup_inputs(seed: int = 0) -> dict:
    seeds = jax.random.split(jax.random.key(seed), 19)
    return {
        "inputs": scatter_about(seeds[0], (TOKENS, D), 1.0, 6.0, ((0, 8),)),
        "segment_ids": jax.vmap(lambda own: jnp.searchsorted(jnp.cumsum(ragged_sizes(own, 6, TOK_DEV, TOK_DEV // 2, 2)), jnp.arange(TOK_DEV), side="right"))(jax.random.split(seeds[1], ROWS)).reshape((ROWS, TOK_DEV)).astype(jnp.int32),
        "cotangent": scatter_about(seeds[2], (TOKENS, D), 1.0, 6.0, ((0, 8),)),
        "query_key_value": draw_query_key_value(jax.random.fold_in(seeds[18], 71), 0),
        "attention_out": scatter_about(seeds[4], (D, D), (D // 64) ** -0.5, 1.0, ((0, 32),), jnp.float32),
        "expand_weight": scatter_about(seeds[5], (D, FF), D ** -0.5, 0.125, ((0, 8), (1, 4)), jnp.float32),
        "contract_weight": scatter_about(seeds[6], (FF, D), (FF // 16) ** -0.5, 0.25, ((0, 32),), jnp.float32),
        "norm_params": draw_norm_params(jax.random.fold_in(seeds[18], 71), 0),
        "first_query_key_value": scatter_about(seeds[8], (3, D, D), 0.15, 2.0, ((1, 8), (2, 4)), jnp.float32),
        "first_attention_out": scatter_about(seeds[9], (D, D), 0.025, 0.375, ((0, 32),), jnp.float32),
        "first_expand_weight": scatter_about(seeds[10], (D, FF), 0.1, 1.5, ((0, 8), (1, 4)), jnp.float32),
        "first_contract_weight": scatter_about(seeds[11], (FF, D), 0.15, 2.0, ((0, 32),), jnp.float32),
        "first_norm_params": scatter_about(seeds[12], (4, D), 0.15, 2.0, ((1, 8),), jnp.float32),
        "second_query_key_value": jnp.clip(jnp.exp(math.log(0.3) - 2.3025852 * jax.random.uniform(seeds[13], (3, D, D), jnp.float32) ** steps_of(seeds[13], (3, D, D), ((1, 8), (2, 4)), -0.2, 0.2)), 0.03, 0.3),
        "second_attention_out": jnp.clip(jnp.exp(math.log(0.008) - 2.3025852 * jax.random.uniform(seeds[14], (D, D), jnp.float32) ** steps_of(seeds[14], (D, D), ((0, 32),), -0.2, 0.2)), 0.0008, 0.008),
        "second_expand_weight": jnp.clip(jnp.exp(math.log(0.15) - 2.3025852 * jax.random.uniform(seeds[15], (D, FF), jnp.float32) ** steps_of(seeds[15], (D, FF), ((0, 8), (1, 4)), -0.2, 0.2)), 0.015, 0.15),
        "second_contract_weight": jnp.clip(jnp.exp(math.log(0.3) - 2.3025852 * jax.random.uniform(seeds[16], (FF, D), jnp.float32) ** steps_of(seeds[16], (FF, D), ((0, 32),), -0.2, 0.2)), 0.03, 0.3),
        "second_norm_params": jnp.clip(jnp.exp(math.log(0.3) - 2.3025852 * jax.random.uniform(seeds[17], (4, D), jnp.float32) ** steps_of(seeds[17], (4, D), ((1, 8),), -0.2, 0.2)), 0.03, 0.3),
    }


@jax.custom_vjp
def low(v):
    return lax.optimization_barrier(v.astype(jnp.bfloat16)).astype(jnp.float32)

@jax.custom_vjp
def low_back(v):
    return v

def low_keep(v):
    return (low(v), None)

def low_pass(kept, grad):
    return (grad,)

def back_keep(v):
    return (v, None)

def back_low(kept, grad):
    return (low(grad),)
low.defvjp(low_keep, low_pass)
low_back.defvjp(back_keep, back_low)
BETA_ONE = 0.9
BETA_TWO = 0.95
ADAM_EPSILON = 1e-08
WEIGHT_DECAY = 0.1
NORM_EPSILON = 1e-05
CLIP_EPSILON = 1e-06
LEARN_RATES = (0.01, 0.08, 0.012, 0.02, 0.3)
MASKED_SCORE = -1e+30

def layer_norm(values, gain_row, shift_row):
    row_mean = lax.optimization_barrier(jnp.mean(values, axis=-1, keepdims=True))
    centered = values - row_mean
    spread = lax.optimization_barrier(jnp.mean(centered * centered, axis=-1, keepdims=True))
    return centered * lax.rsqrt(spread + NORM_EPSILON) * gain_row + shift_row

def attend_rows(query_rows, key_rows, value_rows, row_segments):
    row_length = query_rows.shape[1]
    block_rows = min(512, row_length)
    score_scale = 1.0 / math.sqrt(query_rows.shape[-1])
    key_places = jnp.arange(row_length, dtype=jnp.int32)

    def one_block(first_row):
        query_block = lax.dynamic_slice_in_dim(query_rows, first_row, block_rows, 1)
        segment_block = lax.dynamic_slice_in_dim(row_segments, first_row, block_rows, 1)
        raw_scores = low_back(jnp.einsum('gqhd,gkhd->ghqk', query_block, key_rows, precision=lax.Precision.HIGHEST))
        query_places = first_row + jnp.arange(block_rows, dtype=jnp.int32)
        allowed = (segment_block[:, :, None] == row_segments[:, None, :]) & (key_places[None, None, :] <= query_places[None, :, None])
        scores = jnp.where(allowed[:, None], raw_scores * score_scale, MASKED_SCORE)
        weights = low(jax.nn.softmax(scores, axis=-1))
        return jnp.einsum('ghqk,gkhd->gqhd', weights, value_rows, precision=lax.Precision.HIGHEST)
    firsts = jnp.arange(row_length // block_rows, dtype=jnp.int32) * block_rows
    blocks = lax.map(jax.checkpoint(one_block), firsts)
    return jnp.moveaxis(blocks, 0, 1).reshape(query_rows.shape)

def forward(params, tokens, row_segments):
    joint_weight, output_weight, expand_full, contract_full, norm_weights = [low(entry) for entry in params]
    group_rows, row_length = row_segments.shape
    width = tokens.shape[-1]
    normed = low(layer_norm(tokens, norm_weights[0], norm_weights[1]))
    joint = low(low_back(jnp.einsum('td,cde->cte', normed, joint_weight, precision=lax.Precision.HIGHEST)))
    shaped = joint.reshape(3, group_rows, row_length, HEADS, HEAD_DIM)
    attended = attend_rows(shaped[0], shaped[1], shaped[2], row_segments).reshape(group_rows * row_length, width)
    attended = low(low_back(attended))
    branch_one = low_back(jnp.dot(attended, output_weight, precision=lax.Precision.HIGHEST))
    hidden = tokens + branch_one
    second_normed = low(layer_norm(hidden, norm_weights[2], norm_weights[3]))
    pre_gelu = low_back(jnp.dot(second_normed, expand_full, precision=lax.Precision.HIGHEST))
    activated = low(jax.nn.gelu(pre_gelu, approximate=True))
    branch_two = low_back(jnp.dot(activated, contract_full, precision=lax.Precision.HIGHEST))
    return hidden + branch_two

def adam_update(weight, grad, first, second, rate, clip_factor):
    clipped = grad * clip_factor
    new_first = BETA_ONE * first + (1.0 - BETA_ONE) * clipped
    new_second = BETA_TWO * second + (1.0 - BETA_TWO) * clipped * clipped
    first_hat = new_first / (1.0 - BETA_ONE ** ADAM_STEP)
    second_hat = new_second / (1.0 - BETA_TWO ** ADAM_STEP)
    new_weight = weight - rate * (first_hat / (jnp.sqrt(second_hat) + ADAM_EPSILON) + WEIGHT_DECAY * weight)
    return (new_first, new_second, new_weight)

def reference(inputs, segment_ids, cotangent, query_key_value, attention_out, expand_weight, contract_weight, norm_params, first_query_key_value, first_attention_out, first_expand_weight, first_contract_weight, first_norm_params, second_query_key_value, second_attention_out, second_expand_weight, second_contract_weight, second_norm_params):
    params = (query_key_value, attention_out, expand_weight, contract_weight, norm_params)
    firsts = (first_query_key_value, first_attention_out, first_expand_weight, first_contract_weight, first_norm_params)
    seconds = (second_query_key_value, second_attention_out, second_expand_weight, second_contract_weight, second_norm_params)
    row_count = segment_ids.shape[0]
    group_rows = 4 if row_count % 4 == 0 else 1
    group_count = row_count // group_rows
    width = inputs.shape[1]
    token_groups = inputs.astype(jnp.float32).reshape(group_count, group_rows * TOK_DEV, width)
    cotangent_groups = cotangent.astype(jnp.float32).reshape(group_count, group_rows * TOK_DEV, width)
    segment_groups = segment_ids.reshape(group_count, group_rows, TOK_DEV)

    def group_step(accumulated, pieces):
        token_block, cotangent_block, segment_block = pieces

        def apply_layer(weights, values):
            return forward(weights, values, segment_block)
        result, pullback = jax.vjp(apply_layer, params, token_block)
        weight_grads, token_grad = pullback(cotangent_block)
        accumulated = jax.tree.map(jnp.add, accumulated, tuple(weight_grads))
        return (accumulated, (result.astype(jnp.bfloat16), token_grad))
    initial = tuple((jnp.zeros_like(entry) for entry in params))
    grads, (results, token_grads) = lax.scan(group_step, initial, (token_groups, cotangent_groups, segment_groups))
    layer_output = results.reshape(row_count * TOK_DEV, width)
    input_grad = token_grads.reshape(row_count * TOK_DEV, width)
    squares = sum((jnp.sum(entry * entry) for entry in grads))
    gradient_norm = jnp.sqrt(squares)
    clip_factor = jnp.minimum(1.0, MAX_NORM / (gradient_norm + CLIP_EPSILON))
    updates = [adam_update(params[k], grads[k], firsts[k], seconds[k], LEARN_RATES[k], clip_factor) for k in range(5)]
    copies = [entry[2].astype(jnp.bfloat16) for entry in updates]
    return (layer_output, input_grad, grads[0], grads[1], grads[2], grads[3], grads[4], updates[0][0], updates[1][0], updates[2][0], updates[3][0], updates[4][0], updates[0][1], updates[1][1], updates[2][1], updates[3][1], updates[4][1], updates[0][2], updates[1][2], updates[2][2], updates[3][2], updates[4][2], copies[0], copies[1], copies[2], copies[3], copies[4], gradient_norm)
```

```python
import functools
import math

import jax
import jax.numpy as jnp
from jax import lax
from jax.experimental import pallas as pl
from jax.experimental.pallas import tpu as pltpu
from jax.sharding import PartitionSpec as P

HEAD_DIM = 128
ADAM_STEP = 5
MAX_NORM = 8192


BETA_ONE = 0.9
BETA_TWO = 0.95
ADAM_EPSILON = 1e-08
WEIGHT_DECAY = 0.1
NORM_EPSILON = 1e-05
CLIP_EPSILON = 1e-06
LEARN_RATES = (0.01, 0.08, 0.012, 0.02, 0.3)
MASKED_SCORE = -1e30
SCALE = 1.0 / math.sqrt(HEAD_DIM)
F32 = jnp.float32
BF16 = jnp.bfloat16
ROWS_COLS = (((1,), (0,)), ((), ()))
COLS_COLS = (((1,), (1,)), ((), ()))
ROWS_ROWS = (((0,), (0,)), ((), ()))


def mul(left, right, dims=ROWS_COLS):
    return lax.dot_general(left, right, dims, preferred_element_type=F32)


def layer_norm(values, gain_row, shift_row):
    row_mean = jnp.mean(values, axis=-1, keepdims=True)
    centered = values - row_mean
    spread = jnp.mean(centered * centered, axis=-1, keepdims=True)
    return centered * lax.rsqrt(spread + NORM_EPSILON) * gain_row + shift_row


def gelu_tanh(values):
    return jax.nn.gelu(values, approximate=True)


def adam_update(weight, grad, first, second, rate, clip_factor):
    clipped = grad * clip_factor
    new_first = BETA_ONE * first + (1.0 - BETA_ONE) * clipped
    new_second = BETA_TWO * second + (1.0 - BETA_TWO) * clipped * clipped
    first_hat = new_first / (1.0 - BETA_ONE**ADAM_STEP)
    second_hat = new_second / (1.0 - BETA_TWO**ADAM_STEP)
    new_weight = weight - rate * (
        first_hat / (jnp.sqrt(second_hat) + ADAM_EPSILON) + WEIGHT_DECAY * weight
    )
    return (new_first, new_second, new_weight)


class Group:
    def __init__(self, kind, dp_size, mp_size):
        self.kind = kind
        self.mp_size = mp_size
        chips = dp_size // 2
        self.size = {
            "pair": 2,
            "plane": chips,
            "column": mp_size,
            "cross": chips * mp_size,
            "row": dp_size,
            "all": dp_size * mp_size,
        }[kind]

    def me(self):
        dp, mp = lax.axis_index("dp"), lax.axis_index("mp")
        if self.kind == "pair":
            return lax.rem(dp, 2)
        if self.kind == "plane":
            return lax.div(dp, 2)
        if self.kind == "column":
            return mp
        if self.kind == "cross":
            return lax.div(dp, 2) * self.mp_size + mp
        if self.kind == "row":
            return dp
        return dp * self.mp_size + mp

    def device(self, member):
        dp, mp = lax.axis_index("dp"), lax.axis_index("mp")
        core = lax.rem(dp, 2)
        if self.kind == "pair":
            return (dp - core + member, mp)
        if self.kind == "plane":
            return (member * 2 + core, mp)
        if self.kind == "column":
            return (dp, member)
        if self.kind == "cross":
            return (lax.div(member, self.mp_size) * 2 + core, lax.rem(member, self.mp_size))
        if self.kind == "row":
            return (member, mp)
        return (lax.div(member, self.mp_size), lax.rem(member, self.mp_size))


def repeat(low, high, body):
    if high - low <= 8:
        for step in range(low, high):
            body(step)
    else:
        lax.fori_loop(low, high, lambda step, none: (body(step), none)[1], None)


def exchange(group, operands, results, moves, collective_id):
    count = len(operands)
    size = group.size
    lanes = len(moves)

    def kernel(*refs):
        ins, outs = refs[:count], refs[count : count + len(results)]
        send_sems, recv_sems, own_sems = refs[count + len(results) :]
        me = group.me()
        barrier = pltpu.get_barrier_semaphore()

        def greet(step):
            other = lax.rem(me + step, size)
            pl.semaphore_signal(
                barrier, inc=1, device_id=group.device(other), device_id_type=pl.DeviceIdType.MESH
            )

        repeat(1, size, greet)
        pl.semaphore_wait(barrier, size - 1)

        def remote(move, lane, step, sender, target, device):
            return pltpu.make_async_remote_copy(
                src_ref=move(ins, outs, me, target)[0],
                dst_ref=move(ins, outs, sender, me)[1],
                send_sem=send_sems.at[lane, step],
                recv_sem=recv_sems.at[lane, step],
                device_id=group.device(device),
                device_id_type=pl.DeviceIdType.MESH,
            )

        def launch(step):
            other = lax.rem(me + step, size)
            for lane, move in enumerate(moves):
                remote(move, lane, step, me, other, other).start()

        repeat(1, size, launch)
        own = []
        for lane, move in enumerate(moves):
            source, target = move(ins, outs, me, me)
            own.append(pltpu.make_async_copy(source, target, own_sems.at[lane]))
            own[-1].start()

        def finish(step):
            other = lax.rem(me + step, size)
            sender = lax.rem(me + size - step, size)
            for lane, move in enumerate(moves):
                remote(move, lane, step, sender, other, other).wait()

        repeat(1, size, finish)
        for copy in own:
            copy.wait()

    any_space = pl.BlockSpec(memory_space=pl.ANY)
    return pl.pallas_call(
        kernel,
        out_shape=results,
        in_specs=[any_space] * count,
        out_specs=[any_space] * len(results),
        scratch_shapes=[
            pltpu.SemaphoreType.DMA((lanes, size)),
            pltpu.SemaphoreType.DMA((lanes, size)),
            pltpu.SemaphoreType.DMA((lanes,)),
        ],
        compiler_params=pltpu.CompilerParams(collective_id=collective_id, has_side_effects=True),
    )(*operands)


def shape(dims, dtype=BF16):
    return jax.ShapeDtypeStruct(dims, dtype)


def part(index, width):
    return pl.ds(pl.multiple_of(index * width, width), width)


def allowed_pairs(seg_row, seg_col, length):
    places = lax.broadcasted_iota(jnp.int32, (length, length), 0)
    keys = lax.broadcasted_iota(jnp.int32, (length, length), 1)
    return (seg_col[...] == seg_row[...]) & (keys <= places)


def probabilities(query, key, allowed):
    scores = jnp.where(allowed, mul(query, key, COLS_COLS) * SCALE, MASKED_SCORE)
    exponent = jnp.exp(scores - jnp.max(scores, axis=-1, keepdims=True))
    return exponent / jnp.sum(exponent, axis=-1, keepdims=True)


def attend_kernel(width, joint, seg_row, seg_col, out_weight, attended, partial):
    allowed = allowed_pairs(seg_row, seg_col, joint.shape[0])
    for start in range(0, width, HEAD_DIM):
        head = pl.ds(start, HEAD_DIM)
        query, key, value = (joint[:, pl.ds(c * width + start, HEAD_DIM)] for c in range(3))
        prob = probabilities(query, key, allowed)
        attended[:, head] = mul(prob.astype(BF16), value).astype(BF16)
    partial[...] = mul(attended[...], out_weight[...]).astype(BF16)


def attend_back_kernel(
    width, joint, seg_row, seg_col, out_weight, attended, branch, d_joint, grad_out, d_attended
):
    allowed = allowed_pairs(seg_row, seg_col, joint.shape[0])
    d_attended[...] = mul(branch[...], out_weight[...], COLS_COLS).astype(BF16)
    for start in range(0, width, HEAD_DIM):
        query, key, value = (joint[:, pl.ds(c * width + start, HEAD_DIM)] for c in range(3))
        d_out = d_attended[:, pl.ds(start, HEAD_DIM)]
        prob = probabilities(query, key, allowed)
        d_joint[:, pl.ds(2 * width + start, HEAD_DIM)] = mul(
            prob.astype(BF16), d_out, ROWS_ROWS
        ).astype(BF16)
        d_prob = mul(d_out, value, COLS_COLS)
        row_delta = jnp.sum(d_prob * prob, axis=-1, keepdims=True)
        d_raw = (prob * (d_prob - row_delta) * SCALE).astype(BF16)
        d_joint[:, pl.ds(start, HEAD_DIM)] = mul(d_raw, key).astype(BF16)
        d_joint[:, pl.ds(width + start, HEAD_DIM)] = mul(d_raw, query, ROWS_ROWS).astype(BF16)
    grad_out[...] = mul(attended[...], branch[...], ROWS_ROWS).astype(BF16)


def local(
    dp_size,
    mp_size,
    inputs,
    segment_ids,
    cotangent,
    query_key_value,
    attention_out,
    expand_weight,
    contract_weight,
    norm_params,
    first_query_key_value,
    first_attention_out,
    first_expand_weight,
    first_contract_weight,
    first_norm_params,
    second_query_key_value,
    second_attention_out,
    second_expand_weight,
    second_contract_weight,
    second_norm_params,
):
    params = (query_key_value, attention_out, expand_weight, contract_weight, norm_params)
    firsts = (
        first_query_key_value,
        first_attention_out,
        first_expand_weight,
        first_contract_weight,
        first_norm_params,
    )
    seconds = (
        second_query_key_value,
        second_attention_out,
        second_expand_weight,
        second_contract_weight,
        second_norm_params,
    )
    chips = dp_size // 2
    pair, plane, column, cross, row, everyone = (
        Group(kind, dp_size, mp_size)
        for kind in ("pair", "plane", "column", "cross", "row", "all")
    )
    dp, mp = lax.axis_index("dp"), lax.axis_index("mp")
    core = dp % 2
    length, model = inputs.shape
    width = query_key_value.shape[2]
    shard = query_key_value.shape[1]
    slab = 2 * shard
    hidden_units = expand_weight.shape[1]
    own_units = contract_weight.shape[0]
    units = 2 * own_units
    out_rows = attention_out.shape[0]
    strip = length // mp_size
    tokens = chips * length

    (norm_all,) = exchange(
        row,
        [norm_params],
        [shape((dp_size, 4, shard), F32)],
        [lambda ins, outs, me, other: (ins[0], outs[0].at[me])],
        0,
    )
    norm_weights = jnp.swapaxes(norm_all.astype(BF16).astype(F32), 0, 1).reshape(4, model)

    def shared(column_block):
        def move(ins, outs, me, other):
            return (ins[0].at[column_block], outs[0].at[part(me, shard), pl.ds(column_block * width, width)])

        return move

    joint_weight, expand_pair, contract_pair = exchange(
        pair,
        [query_key_value.astype(BF16), expand_weight.astype(BF16), contract_weight.astype(BF16)],
        [shape((slab, 3 * width)), shape((slab, hidden_units)), shape((units, model))],
        [
            shared(0),
            shared(1),
            shared(2),
            lambda ins, outs, me, other: (ins[1], outs[1].at[part(me, shard), :]),
            lambda ins, outs, me, other: (ins[2], outs[2].at[part(me, own_units), :]),
        ],
        1,
    )
    (output_all,) = exchange(
        row,
        [attention_out.astype(BF16)],
        [shape((dp_size * out_rows, model))],
        [lambda ins, outs, me, other: (ins[0], outs[0].at[part(me, out_rows), :])],
        2,
    )
    (grad_rows,) = exchange(
        plane,
        [cotangent],
        [shape((chips, length, model))],
        [lambda ins, outs, me, other: (ins[0], outs[0].at[me])],
        3,
    )
    grad_rows = grad_rows.reshape(tokens, model)

    values = inputs.astype(F32)
    normed = layer_norm(values, norm_weights[0], norm_weights[1]).astype(BF16)
    (normed_low,) = exchange(
        plane,
        [normed],
        [shape((chips, length, slab))],
        [lambda ins, outs, me, other: (ins[0].at[:, part(other, slab)], outs[0].at[me])],
        4,
    )
    normed_low = normed_low.reshape(tokens, slab)
    joint_part = mul(normed_low, joint_weight).astype(BF16).reshape(chips, length, 3 * width)
    (joint_parts,) = exchange(
        plane,
        [joint_part],
        [shape((chips, length, 3 * width))],
        [lambda ins, outs, me, other: (ins[0].at[other], outs[0].at[me])],
        5,
    )
    joint = jnp.sum(joint_parts.astype(F32), axis=0).astype(BF16)

    seg_row = segment_ids
    seg_col = segment_ids.reshape(length, 1)
    attended, branch_part = pl.pallas_call(
        functools.partial(attend_kernel, width),
        out_shape=[shape((length, width)), shape((length, model))],
        compiler_params=pltpu.CompilerParams(vmem_limit_bytes=48 * 2**20),
    )(joint, seg_row, seg_col, output_all)

    (branch_parts,) = exchange(
        column,
        [branch_part.reshape(mp_size, strip, model)],
        [shape((mp_size, strip, model))],
        [lambda ins, outs, me, other: (ins[0].at[other], outs[0].at[me])],
        6,
    )
    own_values = lax.dynamic_slice_in_dim(values, mp * strip, strip, 0)
    hidden = own_values + jnp.sum(branch_parts.astype(F32), axis=0)
    normed_two, pull_two = jax.vjp(layer_norm, hidden, norm_weights[2], norm_weights[3])
    (second_low,) = exchange(
        cross,
        [normed_two.astype(BF16)],
        [shape((chips * mp_size, strip, slab))],
        [
            lambda ins, outs, me, other: (
                ins[0].at[:, part(lax.div(other, mp_size), slab)],
                outs[0].at[me],
            )
        ],
        7,
    )
    second_low = second_low.reshape(tokens, slab)
    pre_part = mul(second_low, expand_pair).astype(BF16)
    (pre_parts,) = exchange(
        plane,
        [pre_part],
        [shape((chips, tokens, units))],
        [lambda ins, outs, me, other: (ins[0].at[:, part(other, units)], outs[0].at[me])],
        8,
    )
    pre_gelu = jnp.sum(pre_parts.astype(F32), axis=0)
    activated, pull_gelu = jax.vjp(gelu_tanh, pre_gelu)
    activated_low = activated.astype(BF16)
    d_activated = mul(grad_rows, contract_pair, COLS_COLS)
    (d_pre,) = pull_gelu(d_activated)
    (d_pre_all,) = exchange(
        plane,
        [d_pre.astype(BF16)],
        [shape((tokens, hidden_units))],
        [lambda ins, outs, me, other: (ins[0], outs[0].at[:, part(me, units)])],
        9,
    )

    def scatter_rows(partial, collective_id):
        (blocks,) = exchange(
            cross,
            [partial.reshape(chips * mp_size, strip, slab)],
            [shape((chips * mp_size, strip, slab))],
            [lambda ins, outs, me, other: (ins[0].at[other], outs[0].at[me])],
            collective_id,
        )
        total = jnp.sum(blocks.reshape(chips, mp_size, strip, slab).astype(F32), axis=1)
        return jnp.swapaxes(total, 0, 1).reshape(strip, model)

    d_normed_two = scatter_rows(mul(d_pre_all, expand_pair, COLS_COLS).astype(BF16), 10)
    d_hidden_norm, gain_two, shift_two = pull_two(d_normed_two)
    own_grad = lax.dynamic_slice_in_dim(cotangent, mp * strip, strip, 0).astype(F32)
    d_hidden = own_grad + d_hidden_norm

    def gather_rows(block, collective_id):
        (rows,) = exchange(
            column,
            [block],
            [shape((mp_size, strip, model))],
            [lambda ins, outs, me, other: (ins[0], outs[0].at[me])],
            collective_id,
        )
        return rows.reshape(length, model)

    branch_grad = gather_rows(d_hidden.astype(BF16), 11)
    d_joint, grad_output_part, _ = pl.pallas_call(
        functools.partial(attend_back_kernel, width),
        out_shape=[shape((length, 3 * width)), shape((width, model)), shape((length, width))],
        compiler_params=pltpu.CompilerParams(vmem_limit_bytes=48 * 2**20),
    )(joint, seg_row, seg_col, output_all, attended, branch_grad)
    (d_joint_all,) = exchange(
        plane,
        [d_joint],
        [shape((chips, length, 3 * width))],
        [lambda ins, outs, me, other: (ins[0], outs[0].at[me])],
        12,
    )
    d_joint_all = d_joint_all.reshape(tokens, 3 * width)
    d_normed_one = scatter_rows(mul(d_joint_all, joint_weight, COLS_COLS).astype(BF16), 13)
    _, pull_one = jax.vjp(layer_norm, own_values, norm_weights[0], norm_weights[1])
    d_values_norm, gain_one, shift_one = pull_one(d_normed_one)
    input_grad = gather_rows((d_hidden + d_values_norm).astype(BF16), 14).astype(F32)

    out_part = mul(activated_low, contract_pair).astype(BF16).reshape(chips, length, model)
    (out_parts,) = exchange(
        plane,
        [out_part],
        [shape((chips, length, model))],
        [lambda ins, outs, me, other: (ins[0].at[other], outs[0].at[me])],
        15,
    )
    out_rows_sum = jnp.sum(out_parts.astype(F32), axis=0).astype(BF16)
    (out_strips,) = exchange(
        column,
        [out_rows_sum.reshape(mp_size, strip, model)],
        [shape((mp_size, strip, model))],
        [lambda ins, outs, me, other: (ins[0].at[other], outs[0].at[me])],
        16,
    )
    layer_output = gather_rows(
        (hidden + jnp.sum(out_strips.astype(F32), axis=0)).astype(BF16), 17
    )

    (grad_output_parts,) = exchange(
        row,
        [grad_output_part.reshape(dp_size, out_rows, model)],
        [shape((dp_size, out_rows, model))],
        [lambda ins, outs, me, other: (ins[0].at[other], outs[0].at[me])],
        18,
    )
    reduced_output = jnp.sum(grad_output_parts.astype(F32), axis=0)
    own_joint, other_joint = [], []
    grad_joint = mul(normed_low, d_joint_all, ROWS_ROWS)
    grad_expand = mul(second_low, d_pre_all, ROWS_ROWS)
    grad_contract = mul(activated_low, grad_rows, ROWS_ROWS)

    def halves(array, index):
        return lax.dynamic_slice_in_dim(array, index * (array.shape[0] // 2), array.shape[0] // 2, 0)

    pieces = (grad_joint, grad_expand, grad_contract)
    sent = [halves(entry, 1 - core).astype(BF16) for entry in pieces]
    got = exchange_pair(pair, sent, 19)
    reduced_joint, reduced_expand, reduced_contract = (
        halves(entry, core) + other.astype(F32) for entry, other in zip(pieces, got)
    )
    reduced_joint = jnp.swapaxes(reduced_joint.reshape(shard, 3, width), 0, 1)

    zero_row = jnp.zeros((model,), F32)
    norm_rows = jnp.stack([gain_one, shift_one, gain_two, shift_two] + [zero_row] * 4)
    norm_rows = jnp.swapaxes(norm_rows.reshape(8, dp_size, shard), 0, 1)
    (norm_parts,) = exchange(
        everyone,
        [norm_rows],
        [shape((dp_size * mp_size, 8, shard), F32)],
        [
            lambda ins, outs, me, other: (
                ins[0].at[lax.div(other, mp_size)],
                outs[0].at[me],
            )
        ],
        20,
    )
    reduced_norms = jnp.sum(norm_parts, axis=0)[:4]

    grads = (reduced_joint, reduced_output, reduced_expand, reduced_contract, reduced_norms)
    squares = sum((jnp.sum(entry * entry) for entry in grads[:4])) + jnp.sum(
        reduced_norms * reduced_norms
    ) / mp_size
    (square_parts,) = exchange(
        everyone,
        [jnp.full((8, 128), squares, F32)],
        [shape((dp_size * mp_size, 8, 128), F32)],
        [lambda ins, outs, me, other: (ins[0], outs[0].at[me])],
        21,
    )
    gradient_norm = jnp.sqrt(jnp.sum(square_parts[:, 0, 0]))
    clip_factor = jnp.minimum(1.0, MAX_NORM / (gradient_norm + CLIP_EPSILON))
    updates = [
        adam_update(params[k], grads[k], firsts[k], seconds[k], LEARN_RATES[k], clip_factor)
        for k in range(5)
    ]
    copies = [entry[2].astype(BF16) for entry in updates]
    return (
        layer_output,
        input_grad,
        *grads,
        *[entry[0] for entry in updates],
        *[entry[1] for entry in updates],
        *[entry[2] for entry in updates],
        *copies,
        gradient_norm,
    )


def exchange_pair(pair, sent, collective_id):
    moves = [
        lambda ins, outs, me, other, lane=lane: (ins[lane], outs[lane]) for lane in range(len(sent))
    ]
    return swap(pair, sent, moves, collective_id)


def swap(pair, sent, moves, collective_id):
    count = len(sent)

    def kernel(*refs):
        ins, outs = refs[:count], refs[count : 2 * count]
        send_sems, recv_sems = refs[2 * count :]
        other = pair.device(1 - pair.me())
        barrier = pltpu.get_barrier_semaphore()
        pl.semaphore_signal(barrier, inc=1, device_id=other, device_id_type=pl.DeviceIdType.MESH)
        pl.semaphore_wait(barrier, 1)
        copies = [
            pltpu.make_async_remote_copy(
                src_ref=ins[lane],
                dst_ref=outs[lane],
                send_sem=send_sems.at[lane],
                recv_sem=recv_sems.at[lane],
                device_id=other,
                device_id_type=pl.DeviceIdType.MESH,
            )
            for lane in range(count)
        ]
        for copy in copies:
            copy.start()
        for copy in copies:
            copy.wait()

    any_space = pl.BlockSpec(memory_space=pl.ANY)
    return pl.pallas_call(
        kernel,
        out_shape=[shape(entry.shape, entry.dtype) for entry in sent],
        in_specs=[any_space] * count,
        out_specs=[any_space] * count,
        scratch_shapes=[pltpu.SemaphoreType.DMA((count,)), pltpu.SemaphoreType.DMA((count,))],
        compiler_params=pltpu.CompilerParams(collective_id=collective_id, has_side_effects=True),
    )(*sent)


def solution(mesh):
    rows = P("dp", None)
    sets = (
        P(None, "dp", "mp"),
        P(("mp", "dp"), None),
        P("dp", "mp"),
        P(("mp", "dp"), None),
        P(None, "dp"),
    )
    return jax.shard_map(
        functools.partial(local, mesh.shape["dp"], mesh.shape["mp"]),
        mesh=mesh,
        in_specs=(rows, rows, rows) + sets * 3,
        out_specs=(rows, rows) + sets * 5 + (P(),),
        check_vma=False,
    )
```

```python
import functools
import math
from types import SimpleNamespace

import jax
import jax.numpy as jnp
from jax import lax
from jax.experimental import pallas as pl
from jax.experimental.pallas import tpu as pltpu
from jax.sharding import PartitionSpec as P

HEAD_DIM = 128
ADAM_STEP = 5
MAX_NORM = 8192


BETA_ONE = 0.9
BETA_TWO = 0.95
ADAM_EPSILON = 1e-08
WEIGHT_DECAY = 0.1
NORM_EPSILON = 1e-05
CLIP_EPSILON = 1e-06
LEARN_RATES = (0.01, 0.08, 0.012, 0.02, 0.3)
MASKED_SCORE = -1e30
SCALE = 1.0 / math.sqrt(HEAD_DIM)
F32 = jnp.float32
BF16 = jnp.bfloat16
ROWS_COLS = (((1,), (0,)), ((), ()))
COLS_COLS = (((1,), (1,)), ((), ()))
ROWS_ROWS = (((0,), (0,)), ((), ()))


def mul(left, right, dims=ROWS_COLS):
    return lax.dot_general(left, right, dims, preferred_element_type=F32)


def layer_norm(values, gain_row, shift_row):
    row_mean = jnp.mean(values, axis=-1, keepdims=True)
    centered = values - row_mean
    spread = jnp.mean(centered * centered, axis=-1, keepdims=True)
    return centered * lax.rsqrt(spread + NORM_EPSILON) * gain_row + shift_row


def gelu_tanh(values):
    return jax.nn.gelu(values, approximate=True)


def adam_update(weight, grad, first, second, rate, clip_factor):
    clipped = grad * clip_factor
    new_first = BETA_ONE * first + (1.0 - BETA_ONE) * clipped
    new_second = BETA_TWO * second + (1.0 - BETA_TWO) * clipped * clipped
    first_hat = new_first / (1.0 - BETA_ONE**ADAM_STEP)
    second_hat = new_second / (1.0 - BETA_TWO**ADAM_STEP)
    new_weight = weight - rate * (
        first_hat / (jnp.sqrt(second_hat) + ADAM_EPSILON) + WEIGHT_DECAY * weight
    )
    return (new_first, new_second, new_weight)


PAIR, PLANE, COLUMN, CROSS, ROW, ALL = (
    "pair",
    "plane",
    "column",
    "cross",
    "row",
    "all",
)


class Group:
    def __init__(self, kind, dp_size, mp_size):
        self.kind = kind
        self.mp_size = mp_size
        chips = dp_size // 2
        self.size = {
            PAIR: 2,
            PLANE: chips,
            COLUMN: mp_size,
            CROSS: chips * mp_size,
            ROW: dp_size,
            ALL: dp_size * mp_size,
        }[kind]

    def me(self):
        dp, mp = lax.axis_index("dp"), lax.axis_index("mp")
        if self.kind == PAIR:
            return lax.rem(dp, 2)
        if self.kind == PLANE:
            return lax.div(dp, 2)
        if self.kind == COLUMN:
            return mp
        if self.kind == CROSS:
            return lax.div(dp, 2) * self.mp_size + mp
        if self.kind == ROW:
            return dp
        return dp * self.mp_size + mp

    def device(self, member):
        dp, mp = lax.axis_index("dp"), lax.axis_index("mp")
        core = lax.rem(dp, 2)
        if self.kind == PAIR:
            return (dp - core + member, mp)
        if self.kind == PLANE:
            return (member * 2 + core, mp)
        if self.kind == COLUMN:
            return (dp, member)
        if self.kind == CROSS:
            return (lax.div(member, self.mp_size) * 2 + core, lax.rem(member, self.mp_size))
        if self.kind == ROW:
            return (member, mp)
        return (lax.div(member, self.mp_size), lax.rem(member, self.mp_size))


def repeat(low, high, body):
    if high - low <= 8:
        for step in range(low, high):
            body(step)
    else:
        lax.fori_loop(low, high, lambda step, none: (body(step), none)[1], None)


def exchange(group, operands, results, moves, collective_id):
    count = len(operands)
    size = group.size
    lanes = len(moves)

    def kernel(*refs):
        ins, outs = refs[:count], refs[count : count + len(results)]
        send_sems, recv_sems, own_sems = refs[count + len(results) :]
        me = group.me()
        barrier = pltpu.get_barrier_semaphore()

        def greet(step):
            other = lax.rem(me + step, size)
            pl.semaphore_signal(
                barrier, inc=1, device_id=group.device(other), device_id_type=pl.DeviceIdType.MESH
            )

        repeat(1, size, greet)
        pl.semaphore_wait(barrier, size - 1)

        def remote(move, lane, step, sender, target, device):
            return pltpu.make_async_remote_copy(
                src_ref=move(ins, outs, me, target)[0],
                dst_ref=move(ins, outs, sender, me)[1],
                send_sem=send_sems.at[lane, step],
                recv_sem=recv_sems.at[lane, step],
                device_id=group.device(device),
                device_id_type=pl.DeviceIdType.MESH,
            )

        def launch(step):
            other = lax.rem(me + step, size)
            for lane, move in enumerate(moves):
                remote(move, lane, step, me, other, other).start()

        repeat(1, size, launch)
        own = []
        for lane, move in enumerate(moves):
            source, target = move(ins, outs, me, me)
            own.append(pltpu.make_async_copy(source, target, own_sems.at[lane]))
            own[-1].start()

        def finish(step):
            other = lax.rem(me + step, size)
            sender = lax.rem(me + size - step, size)
            for lane, move in enumerate(moves):
                remote(move, lane, step, sender, other, other).wait()

        repeat(1, size, finish)
        for copy in own:
            copy.wait()

    any_space = pl.BlockSpec(memory_space=pl.ANY)
    return pl.pallas_call(
        kernel,
        out_shape=results,
        in_specs=[any_space] * count,
        out_specs=[any_space] * len(results),
        scratch_shapes=[
            pltpu.SemaphoreType.DMA((lanes, size)),
            pltpu.SemaphoreType.DMA((lanes, size)),
            pltpu.SemaphoreType.DMA((lanes,)),
        ],
        compiler_params=pltpu.CompilerParams(collective_id=collective_id, has_side_effects=True),
    )(*operands)


def shape(dims, dtype=BF16):
    return jax.ShapeDtypeStruct(dims, dtype)


def part(index, width):
    return pl.ds(pl.multiple_of(index * width, width), width)


def allowed_pairs(seg_row, seg_col, length):
    places = lax.broadcasted_iota(jnp.int32, (length, length), 0)
    keys = lax.broadcasted_iota(jnp.int32, (length, length), 1)
    return (seg_col[...] == seg_row[...]) & (keys <= places)


def probabilities(query, key, allowed):
    scores = jnp.where(allowed, mul(query, key, COLS_COLS) * SCALE, MASKED_SCORE)
    exponent = jnp.exp(scores - jnp.max(scores, axis=-1, keepdims=True))
    return exponent / jnp.sum(exponent, axis=-1, keepdims=True)


def attend_kernel(width, joint, seg_row, seg_col, out_weight, attended, partial):
    allowed = allowed_pairs(seg_row, seg_col, joint.shape[0])
    for start in range(0, width, HEAD_DIM):
        head = pl.ds(start, HEAD_DIM)
        query, key, value = (joint[:, pl.ds(c * width + start, HEAD_DIM)] for c in range(3))
        prob = probabilities(query, key, allowed)
        attended[:, head] = mul(prob.astype(BF16), value).astype(BF16)
    partial[...] = mul(attended[...], out_weight[...]).astype(BF16)


def attend_back_kernel(
    width, joint, seg_row, seg_col, out_weight, attended, branch, d_joint, grad_out, d_attended
):
    allowed = allowed_pairs(seg_row, seg_col, joint.shape[0])
    d_attended[...] = mul(branch[...], out_weight[...], COLS_COLS).astype(BF16)
    for start in range(0, width, HEAD_DIM):
        query, key, value = (joint[:, pl.ds(c * width + start, HEAD_DIM)] for c in range(3))
        d_out = d_attended[:, pl.ds(start, HEAD_DIM)]
        prob = probabilities(query, key, allowed)
        d_joint[:, pl.ds(2 * width + start, HEAD_DIM)] = mul(
            prob.astype(BF16), d_out, ROWS_ROWS
        ).astype(BF16)
        d_prob = mul(d_out, value, COLS_COLS)
        row_delta = jnp.sum(d_prob * prob, axis=-1, keepdims=True)
        d_raw = (prob * (d_prob - row_delta) * SCALE).astype(BF16)
        d_joint[:, pl.ds(start, HEAD_DIM)] = mul(d_raw, key).astype(BF16)
        d_joint[:, pl.ds(width + start, HEAD_DIM)] = mul(d_raw, query, ROWS_ROWS).astype(BF16)
    grad_out[...] = mul(attended[...], branch[...], ROWS_ROWS).astype(BF16)


def local_steps(
    dp_size,
    mp_size,
    inputs,
    segment_ids,
    cotangent,
    query_key_value,
    attention_out,
    expand_weight,
    contract_weight,
    norm_params,
    first_query_key_value,
    first_attention_out,
    first_expand_weight,
    first_contract_weight,
    first_norm_params,
    second_query_key_value,
    second_attention_out,
    second_expand_weight,
    second_contract_weight,
    second_norm_params,
):
    params = (query_key_value, attention_out, expand_weight, contract_weight, norm_params)
    firsts = (
        first_query_key_value,
        first_attention_out,
        first_expand_weight,
        first_contract_weight,
        first_norm_params,
    )
    seconds = (
        second_query_key_value,
        second_attention_out,
        second_expand_weight,
        second_contract_weight,
        second_norm_params,
    )
    chips = dp_size // 2
    pair, plane, column, cross, row, everyone = (
        Group(kind, dp_size, mp_size)
        for kind in (PAIR, PLANE, COLUMN, CROSS, ROW, ALL)
    )
    dp, mp = lax.axis_index("dp"), lax.axis_index("mp")
    core = dp % 2
    length, model = inputs.shape
    width = query_key_value.shape[2]
    shard = query_key_value.shape[1]
    slab = 2 * shard
    hidden_units = expand_weight.shape[1]
    own_units = contract_weight.shape[0]
    units = 2 * own_units
    out_rows = attention_out.shape[0]
    strip = length // mp_size
    tokens = chips * length

    (norm_all,) = exchange(
        row,
        [norm_params],
        [shape((dp_size, 4, shard), F32)],
        [lambda ins, outs, me, other: (ins[0], outs[0].at[me])],
        0,
    )
    norm_weights = jnp.swapaxes(norm_all.astype(BF16).astype(F32), 0, 1).reshape(4, model)

    def shared(column_block):
        def move(ins, outs, me, other):
            return (ins[0].at[column_block], outs[0].at[part(me, shard), pl.ds(column_block * width, width)])

        return move

    joint_weight, expand_pair, contract_pair = exchange(
        pair,
        [query_key_value.astype(BF16), expand_weight.astype(BF16), contract_weight.astype(BF16)],
        [shape((slab, 3 * width)), shape((slab, hidden_units)), shape((units, model))],
        [
            shared(0),
            shared(1),
            shared(2),
            lambda ins, outs, me, other: (ins[1], outs[1].at[part(me, shard), :]),
            lambda ins, outs, me, other: (ins[2], outs[2].at[part(me, own_units), :]),
        ],
        1,
    )
    (output_all,) = exchange(
        row,
        [attention_out.astype(BF16)],
        [shape((dp_size * out_rows, model))],
        [lambda ins, outs, me, other: (ins[0], outs[0].at[part(me, out_rows), :])],
        2,
    )
    (grad_rows,) = exchange(
        plane,
        [cotangent],
        [shape((chips, length, model))],
        [lambda ins, outs, me, other: (ins[0], outs[0].at[me])],
        3,
    )
    grad_rows = grad_rows.reshape(tokens, model)

    values = inputs.astype(F32)
    normed = layer_norm(values, norm_weights[0], norm_weights[1]).astype(BF16)
    (normed_low,) = exchange(
        plane,
        [normed],
        [shape((chips, length, slab))],
        [lambda ins, outs, me, other: (ins[0].at[:, part(other, slab)], outs[0].at[me])],
        4,
    )
    normed_low = normed_low.reshape(tokens, slab)
    joint_part = mul(normed_low, joint_weight).astype(BF16).reshape(chips, length, 3 * width)
    (joint_parts,) = exchange(
        plane,
        [joint_part],
        [shape((chips, length, 3 * width))],
        [lambda ins, outs, me, other: (ins[0].at[other], outs[0].at[me])],
        5,
    )
    joint = jnp.sum(joint_parts.astype(F32), axis=0).astype(BF16)

    seg_row = segment_ids
    seg_col = segment_ids.reshape(length, 1)
    attended, branch_part = pl.pallas_call(
        functools.partial(attend_kernel, width),
        out_shape=[shape((length, width)), shape((length, model))],
        compiler_params=pltpu.CompilerParams(vmem_limit_bytes=48 * 2**20),
    )(joint, seg_row, seg_col, output_all)

    (branch_parts,) = exchange(
        column,
        [branch_part.reshape(mp_size, strip, model)],
        [shape((mp_size, strip, model))],
        [lambda ins, outs, me, other: (ins[0].at[other], outs[0].at[me])],
        6,
    )
    own_values = lax.dynamic_slice_in_dim(values, mp * strip, strip, 0)
    hidden = own_values + jnp.sum(branch_parts.astype(F32), axis=0)
    normed_two, pull_two = jax.vjp(layer_norm, hidden, norm_weights[2], norm_weights[3])
    (second_low,) = exchange(
        cross,
        [normed_two.astype(BF16)],
        [shape((chips * mp_size, strip, slab))],
        [
            lambda ins, outs, me, other: (
                ins[0].at[:, part(lax.div(other, mp_size), slab)],
                outs[0].at[me],
            )
        ],
        7,
    )
    second_low = second_low.reshape(tokens, slab)
    pre_part = mul(second_low, expand_pair).astype(BF16)
    (pre_parts,) = exchange(
        plane,
        [pre_part],
        [shape((chips, tokens, units))],
        [lambda ins, outs, me, other: (ins[0].at[:, part(other, units)], outs[0].at[me])],
        8,
    )
    pre_gelu = jnp.sum(pre_parts.astype(F32), axis=0)
    activated, pull_gelu = jax.vjp(gelu_tanh, pre_gelu)
    activated_low = activated.astype(BF16)
    d_activated = mul(grad_rows, contract_pair, COLS_COLS)
    (d_pre,) = pull_gelu(d_activated)
    (d_pre_all,) = exchange(
        plane,
        [d_pre.astype(BF16)],
        [shape((tokens, hidden_units))],
        [lambda ins, outs, me, other: (ins[0], outs[0].at[:, part(me, units)])],
        9,
    )

    def scatter_rows(partial, collective_id):
        (blocks,) = exchange(
            cross,
            [partial.reshape(chips * mp_size, strip, slab)],
            [shape((chips * mp_size, strip, slab))],
            [lambda ins, outs, me, other: (ins[0].at[other], outs[0].at[me])],
            collective_id,
        )
        total = jnp.sum(blocks.reshape(chips, mp_size, strip, slab).astype(F32), axis=1)
        return jnp.swapaxes(total, 0, 1).reshape(strip, model)

    d_normed_two = scatter_rows(mul(d_pre_all, expand_pair, COLS_COLS).astype(BF16), 10)
    d_hidden_norm, gain_two, shift_two = pull_two(d_normed_two)
    own_grad = lax.dynamic_slice_in_dim(cotangent, mp * strip, strip, 0).astype(F32)
    d_hidden = own_grad + d_hidden_norm

    def gather_rows(block, collective_id):
        (rows,) = exchange(
            column,
            [block],
            [shape((mp_size, strip, model))],
            [lambda ins, outs, me, other: (ins[0], outs[0].at[me])],
            collective_id,
        )
        return rows.reshape(length, model)

    branch_grad = gather_rows(d_hidden.astype(BF16), 11)
    d_joint, grad_output_part, _ = pl.pallas_call(
        functools.partial(attend_back_kernel, width),
        out_shape=[shape((length, 3 * width)), shape((width, model)), shape((length, width))],
        compiler_params=pltpu.CompilerParams(vmem_limit_bytes=48 * 2**20),
    )(joint, seg_row, seg_col, output_all, attended, branch_grad)
    (d_joint_all,) = exchange(
        plane,
        [d_joint],
        [shape((chips, length, 3 * width))],
        [lambda ins, outs, me, other: (ins[0], outs[0].at[me])],
        12,
    )
    d_joint_all = d_joint_all.reshape(tokens, 3 * width)
    d_normed_one = scatter_rows(mul(d_joint_all, joint_weight, COLS_COLS).astype(BF16), 13)
    _, pull_one = jax.vjp(layer_norm, own_values, norm_weights[0], norm_weights[1])
    d_values_norm, gain_one, shift_one = pull_one(d_normed_one)
    input_grad = gather_rows((d_hidden + d_values_norm).astype(BF16), 14).astype(F32)

    out_part = mul(activated_low, contract_pair).astype(BF16).reshape(chips, length, model)
    (out_parts,) = exchange(
        plane,
        [out_part],
        [shape((chips, length, model))],
        [lambda ins, outs, me, other: (ins[0].at[other], outs[0].at[me])],
        15,
    )
    out_rows_sum = jnp.sum(out_parts.astype(F32), axis=0).astype(BF16)
    (out_strips,) = exchange(
        column,
        [out_rows_sum.reshape(mp_size, strip, model)],
        [shape((mp_size, strip, model))],
        [lambda ins, outs, me, other: (ins[0].at[other], outs[0].at[me])],
        16,
    )
    layer_output = gather_rows(
        (hidden + jnp.sum(out_strips.astype(F32), axis=0)).astype(BF16), 17
    )

    (grad_output_parts,) = exchange(
        row,
        [grad_output_part.reshape(dp_size, out_rows, model)],
        [shape((dp_size, out_rows, model))],
        [lambda ins, outs, me, other: (ins[0].at[other], outs[0].at[me])],
        18,
    )
    reduced_output = jnp.sum(grad_output_parts.astype(F32), axis=0)
    own_joint, other_joint = [], []
    grad_joint = mul(normed_low, d_joint_all, ROWS_ROWS)
    grad_expand = mul(second_low, d_pre_all, ROWS_ROWS)
    grad_contract = mul(activated_low, grad_rows, ROWS_ROWS)

    def halves(array, index):
        return lax.dynamic_slice_in_dim(array, index * (array.shape[0] // 2), array.shape[0] // 2, 0)

    pieces = (grad_joint, grad_expand, grad_contract)
    sent = [halves(entry, 1 - core).astype(BF16) for entry in pieces]
    got = exchange_pair(pair, sent, 19)
    reduced_joint, reduced_expand, reduced_contract = (
        halves(entry, core) + other.astype(F32) for entry, other in zip(pieces, got)
    )
    reduced_joint = jnp.swapaxes(reduced_joint.reshape(shard, 3, width), 0, 1)

    zero_row = jnp.zeros((model,), F32)
    norm_rows = jnp.stack([gain_one, shift_one, gain_two, shift_two] + [zero_row] * 4)
    norm_rows = jnp.swapaxes(norm_rows.reshape(8, dp_size, shard), 0, 1)
    (norm_parts,) = exchange(
        everyone,
        [norm_rows],
        [shape((dp_size * mp_size, 8, shard), F32)],
        [
            lambda ins, outs, me, other: (
                ins[0].at[lax.div(other, mp_size)],
                outs[0].at[me],
            )
        ],
        20,
    )
    reduced_norms = jnp.sum(norm_parts, axis=0)[:4]

    grads = (reduced_joint, reduced_output, reduced_expand, reduced_contract, reduced_norms)
    squares = sum((jnp.sum(entry * entry) for entry in grads[:4])) + jnp.sum(
        reduced_norms * reduced_norms
    ) / mp_size
    (square_parts,) = exchange(
        everyone,
        [jnp.full((8, 128), squares, F32)],
        [shape((dp_size * mp_size, 8, 128), F32)],
        [lambda ins, outs, me, other: (ins[0], outs[0].at[me])],
        21,
    )
    gradient_norm = jnp.sqrt(jnp.sum(square_parts[:, 0, 0]))
    clip_factor = jnp.minimum(1.0, MAX_NORM / (gradient_norm + CLIP_EPSILON))
    updates = [
        adam_update(params[k], grads[k], firsts[k], seconds[k], LEARN_RATES[k], clip_factor)
        for k in range(5)
    ]
    copies = [entry[2].astype(BF16) for entry in updates]
    return (
        layer_output,
        input_grad,
        *grads,
        *[entry[0] for entry in updates],
        *[entry[1] for entry in updates],
        *[entry[2] for entry in updates],
        *copies,
        gradient_norm,
    )


def exchange_pair(pair, sent, collective_id):
    moves = [
        lambda ins, outs, me, other, lane=lane: (ins[lane], outs[lane]) for lane in range(len(sent))
    ]
    return swap(pair, sent, moves, collective_id)


def swap(pair, sent, moves, collective_id):
    count = len(sent)

    def kernel(*refs):
        ins, outs = refs[:count], refs[count : 2 * count]
        send_sems, recv_sems = refs[2 * count :]
        other = pair.device(1 - pair.me())
        barrier = pltpu.get_barrier_semaphore()
        pl.semaphore_signal(barrier, inc=1, device_id=other, device_id_type=pl.DeviceIdType.MESH)
        pl.semaphore_wait(barrier, 1)
        copies = [
            pltpu.make_async_remote_copy(
                src_ref=ins[lane],
                dst_ref=outs[lane],
                send_sem=send_sems.at[lane],
                recv_sem=recv_sems.at[lane],
                device_id=other,
                device_id_type=pl.DeviceIdType.MESH,
            )
            for lane in range(count)
        ]
        for copy in copies:
            copy.start()
        for copy in copies:
            copy.wait()

    any_space = pl.BlockSpec(memory_space=pl.ANY)
    return pl.pallas_call(
        kernel,
        out_shape=[shape(entry.shape, entry.dtype) for entry in sent],
        in_specs=[any_space] * count,
        out_specs=[any_space] * count,
        scratch_shapes=[pltpu.SemaphoreType.DMA((count,)), pltpu.SemaphoreType.DMA((count,))],
        compiler_params=pltpu.CompilerParams(collective_id=collective_id, has_side_effects=True),
    )(*sent)


class Lane:
    def __init__(self, group, me, sems, view):
        self.group, self.me, self.view = group, me, view
        self.send_sems, self.recv_sems = sems
        self.size = group.size

    def copy(self, step):
        to = lax.rem(self.me + step, self.size)
        return pltpu.make_async_remote_copy(
            src_ref=self.view(self.me, to)[0],
            dst_ref=self.view(self.me, to)[1],
            send_sem=self.send_sems.at[step],
            recv_sem=self.recv_sems.at[step],
            device_id=self.group.device(to),
            device_id_type=pl.DeviceIdType.MESH,
        )

    def start(self, step):
        self.copy(step).start()

    def start_all(self):
        repeat(1, self.size, self.start)

    def source(self, step):
        return lax.rem(self.me + self.size - step, self.size)

    def take(self, step):
        to = lax.rem(self.me + step, self.size)
        pltpu.make_async_remote_copy(
            src_ref=self.view(self.me, to)[0],
            dst_ref=self.view(self.source(step), self.me)[1],
            send_sem=self.send_sems.at[step],
            recv_sem=self.recv_sems.at[step],
            device_id=self.group.device(to),
            device_id_type=pl.DeviceIdType.MESH,
        ).wait_recv()

    def take_all(self):
        repeat(1, self.size, self.take)

    def sent(self, step):
        self.copy(step).wait_send()

    def sent_all(self):
        repeat(1, self.size, self.sent)


def standardise(values):
    row_mean = jnp.mean(values, axis=-1, keepdims=True)
    centered = values - row_mean
    spread = jnp.mean(centered * centered, axis=-1, keepdims=True)
    return centered, lax.rsqrt(spread + NORM_EPSILON)


def norm_back(grad, values, gain_row):
    centered, inverse = standardise(values)
    unit = centered * inverse
    scaled = grad * gain_row
    inner = jnp.mean(scaled * unit, axis=-1, keepdims=True)
    back = inverse * (scaled - jnp.mean(scaled, axis=-1, keepdims=True) - unit * inner)
    gain_grad = jnp.sum(grad * unit, axis=0, keepdims=True)
    shift_grad = jnp.sum(grad, axis=0, keepdims=True)
    return back, gain_grad, shift_grad


ROOT = math.sqrt(2.0 / math.pi)
CUBE = 0.044715

LANES = dict(
    norms=ROW,
    normed=PLANE,
    joint_weight=PAIR,
    out_own=PAIR,
    out_plane=PLANE,
    out_pass=PLANE,
    joint=PLANE,
    expand=PAIR,
    contract=PAIR,
    cotangent=PLANE,
    branch=COLUMN,
    second=CROSS,
    pre=PLANE,
    d_pre=PLANE,
    g_contract=PAIR,
    d_second=CROSS,
    out=PLANE,
    g_expand=PAIR,
    d_hidden=COLUMN,
    d_joint=PLANE,
    g_out=PLANE,
    g_out_pair=PAIR,
    out_strip=COLUMN,
    d_first=CROSS,
    g_joint=PAIR,
    out_rows=COLUMN,
    in_rows=COLUMN,
    g_norms=CROSS,
    g_norms_pair=PAIR,
)


def layer(dp_size, mp_size, operands):
    x, segments, cotangent, joint_w, out_w, expand_w, contract_w, norms = operands
    chips = dp_size // 2
    groups = SimpleNamespace(
        **{kind: Group(kind, dp_size, mp_size) for kind in (PAIR, PLANE, COLUMN, CROSS, ROW)}
    )
    length, model = x.shape
    width, shard = joint_w.shape[2], joint_w.shape[1]
    slab = 2 * shard
    hidden = expand_w.shape[1]
    own_units = contract_w.shape[0]
    units = 2 * own_units
    out_rows = out_w.shape[0]
    strip = length // mp_size
    tokens = chips * length
    wide = 3 * width

    outs = dict(
        layer_output=shape((length, model)),
        input_grad=shape((length, model), F32),
        own_joint=shape((3, shard, width), F32),
        own_out=shape((out_rows, model), F32),
        own_expand=shape((shard, hidden), F32),
        own_contract=shape((own_units, model), F32),
        own_norms=shape((8, shard), F32),
    )
    far = dict(
        far_joint=shape((3, shard, width)),
        far_out=shape((out_rows, model)),
        far_expand=shape((chips, shard, units)),
        far_contract=shape((own_units, model)),
    )
    scratch = dict(
        norm_all=((dp_size, 4, shard), F32),
        a_mine=((chips, length, slab), BF16),
        a_all=((chips, length, slab), BF16),
        wq=((3, slab, width), BF16),
        wo=((dp_size, out_rows, model), BF16),
        wu=((chips, slab, units), BF16),
        wd=((units, model), BF16),
        j_send=((chips, length, wide), BF16),
        j_recv=((chips, length, wide), BF16),
        joint=((length, wide), BF16),
        dy_all=((chips, length, model), BF16),
        attended=((length, width), BF16),
        b_send=((mp_size, strip, model), BF16),
        b_recv=((mp_size, strip, model), BF16),
        hid=((strip, model), F32),
        c_mine=((chips, strip, slab), BF16),
        c_all=((chips, mp_size, strip, slab), BF16),
        u_send=((chips, tokens, units), BF16),
        u_recv=((chips, tokens, units), BF16),
        u_acc=((tokens, units), F32),
        dz=((tokens, units), F32),
        z=((tokens, units), BF16),
        du_all=((chips, tokens, units), BF16),
        y_send=((chips, length, model), BF16),
        y_recv=((chips, length, model), BF16),
        gc_send=((own_units, model), BF16),
        dc_send=((chips, mp_size, strip, slab), BF16),
        dc_recv=((chips, mp_size, strip, slab), BF16),
        ge_send=((chips, shard, units), BF16),
        dh=((strip, model), F32),
        da_mine=((strip, model), BF16),
        da_rows=((mp_size, strip, model), BF16),
        dq_mine=((length, wide), BF16),
        dq_all=((chips, length, wide), BF16),
        go_send=((chips, 2, out_rows, model), BF16),
        go_recv=((chips, 2, out_rows, model), BF16),
        go_pair=((2, out_rows, model), BF16),
        y2_send=((mp_size, strip, model), BF16),
        y2_recv=((mp_size, strip, model), BF16),
        y_mine=((strip, model), BF16),
        y_rows=((mp_size, strip, model), BF16),
        df_send=((chips, mp_size, strip, slab), BF16),
        df_recv=((chips, mp_size, strip, slab), BF16),
        gj_send=((3, shard, width), BF16),
        ig_mine=((strip, model), BF16),
        ig_rows=((mp_size, strip, model), BF16),
        gn_send=((chips, 8, slab), F32),
        gn_recv=((chips * mp_size, 8, slab), F32),
        gn_pair=((8, shard), F32),
        gn_far=((8, shard), F32),
    )
    in_names = dict(
        x=0, seg_row=1, seg_col=2, cot=3, f_joint=4, f_out=5, f_expand=6, f_contract=7, norm_own=8
    )
    names = list(in_names) + list(outs) + list(far) + list(scratch)

    def kernel(*refs):
        r = SimpleNamespace(**dict(zip(names, refs)))
        sems = refs[len(names) :]
        load_sems = sems[0]
        dp, mp = lax.axis_index("dp"), lax.axis_index("mp")
        core, chip = lax.rem(dp, 2), lax.div(dp, 2)
        mine, other = part(core, shard), part(1 - core, shard)
        cross_me = groups.cross.me()

        def flat(ref, columns=slice(None)):
            values = ref[(slice(None),) * (len(ref.shape) - 1) + (columns,)]
            return values.reshape(-1, values.shape[-1])

        views = dict(
            norms=lambda s, t: (r.norm_own, r.norm_all.at[s]),
            normed=lambda s, t: (r.a_mine.at[t], r.a_all.at[s]),
            joint_weight=lambda s, t: (
                r.wq.at[:, part(s, shard), :],
                r.wq.at[:, part(s, shard), :],
            ),
            out_own=lambda s, t: (r.wo.at[dp - core + s], r.wo.at[dp - core + s]),
            out_plane=lambda s, t: (r.wo.at[2 * s + core], r.wo.at[2 * s + core]),
            joint=lambda s, t: (r.j_send.at[t], r.j_recv.at[s]),
            expand=lambda s, t: (
                r.wu.at[:, part(s, shard), :],
                r.wu.at[:, part(s, shard), :],
            ),
            contract=lambda s, t: (
                r.wd.at[part(s, own_units), :],
                r.wd.at[part(s, own_units), :],
            ),
            cotangent=lambda s, t: (r.cot, r.dy_all.at[s]),
            branch=lambda s, t: (r.b_send.at[t], r.b_recv.at[s]),
            second=lambda s, t: (
                r.c_mine.at[lax.div(t, mp_size)],
                r.c_all.at[lax.div(s, mp_size), lax.rem(s, mp_size)],
            ),
            pre=lambda s, t: (r.u_send.at[t], r.u_recv.at[s]),
            d_pre=lambda s, t: (r.du_all.at[s], r.du_all.at[s]),
            g_contract=lambda s, t: (r.gc_send, r.far_contract),
            d_second=lambda s, t: (
                r.dc_send.at[lax.div(t, mp_size), lax.rem(t, mp_size)],
                r.dc_recv.at[lax.div(s, mp_size), lax.rem(s, mp_size)],
            ),
            out=lambda s, t: (r.y_send.at[t], r.y_recv.at[s]),
            g_expand=lambda s, t: (r.ge_send, r.far_expand),
            d_hidden=lambda s, t: (r.da_mine, r.da_rows.at[s]),
            d_joint=lambda s, t: (r.dq_mine, r.dq_all.at[s]),
            g_out=lambda s, t: (r.go_send.at[t], r.go_recv.at[s]),
            g_out_pair=lambda s, t: (r.go_pair.at[t], r.far_out),
            out_strip=lambda s, t: (r.y2_send.at[t], r.y2_recv.at[s]),
            d_first=lambda s, t: (
                r.df_send.at[lax.div(t, mp_size), lax.rem(t, mp_size)],
                r.df_recv.at[lax.div(s, mp_size), lax.rem(s, mp_size)],
            ),
            g_joint=lambda s, t: (r.gj_send, r.far_joint),
            out_rows=lambda s, t: (r.y_mine, r.y_rows.at[s]),
            in_rows=lambda s, t: (r.ig_mine, r.ig_rows.at[s]),
            g_norms=lambda s, t: (r.gn_send.at[lax.div(t, mp_size)], r.gn_recv.at[s]),
            g_norms_pair=lambda s, t: (r.gn_pair, r.gn_far),
        )
        lane = SimpleNamespace()
        pass_sems = None
        for index, (name, kind) in enumerate(LANES.items()):
            pair_sems = (sems[1 + 2 * index], sems[2 + 2 * index])
            if name in views:
                group = vars(groups)[kind]
                setattr(lane, name, Lane(group, group.me(), pair_sems, views[name]))
            else:
                pass_sems = pair_sems

        def passing(step, to_me):
            block = r.wo.at[2 * lane.out_plane.source(step) + (1 - core if to_me else core)]
            return pltpu.make_async_remote_copy(
                src_ref=block,
                dst_ref=block,
                send_sem=pass_sems[0].at[step],
                recv_sem=pass_sems[1].at[step],
                device_id=(dp + 1 - 2 * core, mp),
                device_id_type=pl.DeviceIdType.MESH,
            )

        loads = [
            pltpu.make_async_copy(source, target, load_sems.at[i])
            for i, (source, target) in enumerate(
                (
                    (r.f_joint, r.own_joint),
                    (r.f_out, r.own_out),
                    (r.f_expand, r.own_expand),
                    (r.f_contract, r.own_contract),
                )
            )
        ]
        for load in loads:
            load.start()

        barrier = pltpu.get_barrier_semaphore()

        def greet(device):
            pl.semaphore_signal(
                barrier, inc=1, device_id=device, device_id_type=pl.DeviceIdType.MESH
            )

        cross = groups.cross
        repeat(1, cross.size, lambda s: greet(cross.device(lax.rem(cross_me + s, cross.size))))
        repeat(0, chips, lambda s: greet((s * 2 + 1 - core, mp)))
        pl.semaphore_wait(barrier, cross.size - 1 + chips)

        lane.norms.start_all()
        r.norm_all[dp] = r.norm_own[...]
        values = r.x[...].astype(F32)
        centered, inverse = standardise(values)
        lane.norms.take_all()

        def norm_row(index, block=None):
            blocks = range(dp_size) if block is None else (block,)
            rows = [r.norm_all[b, pl.ds(index, 1), :] for b in blocks]
            whole = rows[0] if len(rows) == 1 else jnp.concatenate(rows, axis=1)
            return whole.astype(BF16).astype(F32)

        for b in range(dp_size):
            columns = slice(b * shard, (b + 1) * shard)
            r.a_mine[b // 2, :, (b % 2) * shard : (b % 2 + 1) * shard] = (
                centered[:, columns] * inverse * norm_row(0, b) + norm_row(1, b)
            ).astype(BF16)
        lane.normed.start_all()
        r.a_all[chip] = r.a_mine[chip]

        loads[0].wait()
        for c in range(3):
            r.wq[c, mine, :] = r.own_joint[c].astype(BF16)
        lane.joint_weight.start_all()
        loads[1].wait()
        r.wo[dp] = r.own_out[...].astype(BF16)
        lane.out_plane.start_all()
        lane.out_own.start_all()
        lane.joint_weight.take_all()

        def joint_part(block):
            rows = r.a_all[block]
            for c in range(3):
                r.j_send[block, :, c * width : (c + 1) * width] = mul(rows, r.wq[c]).astype(BF16)

        def joint_step(step):
            lane.normed.take(step)
            joint_part(lane.normed.source(step))
            lane.joint.start(chips - step)

        repeat(1, chips, joint_step)
        joint_part(chip)

        loads[2].wait()
        for c in range(chips):
            r.wu[c, mine, :] = r.own_expand[:, c * units : (c + 1) * units].astype(BF16)
        lane.expand.start_all()
        loads[3].wait()
        r.wd[part(core, own_units), :] = r.own_contract[...].astype(BF16)
        lane.contract.start_all()
        for step in range(1, chips):
            lane.out_plane.take(step)
            passing(step, False).start()

        lane.joint.take_all()
        lane.cotangent.start_all()
        total = r.j_send[chip].astype(F32)
        for step in range(1, chips):
            total = total + r.j_recv[lane.joint.source(step)].astype(F32)
        r.joint[...] = total.astype(BF16)

        allowed = allowed_pairs(r.seg_row, r.seg_col, length)
        probs = []
        for start in range(0, width, HEAD_DIM):
            query, key, value = (
                r.joint[:, c * width + start : c * width + start + HEAD_DIM] for c in range(3)
            )
            prob = probabilities(query, key, allowed)
            r.attended[:, start : start + HEAD_DIM] = mul(prob.astype(BF16), value).astype(BF16)

        lane.out_own.take_all()
        for step in range(1, chips):
            passing(step, True).wait_recv()
        branch = mul(r.attended[...], flat(r.wo)).astype(BF16)
        for m in range(mp_size):
            r.b_send[m] = branch[m * strip : (m + 1) * strip]
        lane.branch.start_all()
        r.dy_all[chip] = r.cot[...]
        lane.branch.take_all()
        here = part(mp, strip)
        total = r.x[here, :].astype(F32) + r.b_send[mp].astype(F32)
        for step in range(1, mp_size):
            total = total + r.b_recv[lane.branch.source(step)].astype(F32)
        r.hid[...] = total
        centered, inverse = standardise(total)
        for b in range(dp_size):
            columns = slice(b * shard, (b + 1) * shard)
            r.c_mine[b // 2, :, (b % 2) * shard : (b % 2 + 1) * shard] = (
                centered[:, columns] * inverse * norm_row(2, b) + norm_row(3, b)
            ).astype(BF16)
        lane.second.start_all()
        r.c_all[chip, mp] = r.c_mine[chip]
        lane.expand.take_all()
        lane.contract.take_all()
        lane.cotangent.take_all()
        r.dz[...] = mul(flat(r.dy_all), r.wd[...], COLS_COLS)
        lane.second.take_all()

        def pre_step(step):
            to = lax.rem(chip + step, chips)
            r.u_send[to] = mul(flat(r.c_all), r.wu[to]).astype(BF16)
            lane.pre.start(step)

        repeat(1, chips, pre_step)
        r.u_acc[...] = mul(flat(r.c_all), r.wu[chip])
        lane.pre.take_all()

        tile = 64

        def gelu_tile(i, none):
            rows = part(i, tile)
            pre = r.u_acc[rows, :]
            for step in range(1, chips):
                pre = pre + r.u_recv[lane.pre.source(step), rows, :].astype(F32)
            square = pre * pre
            curve = jnp.tanh(ROOT * pre * (1.0 + CUBE * square))
            half = 0.5 * (1.0 + curve)
            r.z[rows, :] = (pre * half).astype(BF16)
            slope = half + 0.5 * pre * (1.0 - curve * curve) * (ROOT * (1.0 + 3.0 * CUBE * square))
            r.du_all[chip, rows, :] = (r.dz[rows, :] * slope).astype(BF16)
            return none

        lax.fori_loop(0, tokens // tile, gelu_tile, None)
        lane.d_pre.start_all()

        for c in range(chips):
            rows = slice(c * length, (c + 1) * length)
            r.y_send[c] = mul(r.z[rows, :], r.wd[...]).astype(BF16)
        r.gc_send[...] = mul(r.z[:, part(1 - core, own_units)], flat(r.dy_all), ROWS_ROWS).astype(BF16)
        lane.g_contract.start_all()

        total = mul(r.du_all[chip], r.wu[chip], COLS_COLS)
        for step in range(1, chips):
            lane.d_pre.take(step)
            source = lane.d_pre.source(step)
            total = total + mul(r.du_all[source], r.wu[source], COLS_COLS)
        total = total.astype(BF16)
        for c in range(chips):
            for m in range(mp_size):
                first = c * length + m * strip
                r.dc_send[c, m] = total[first : first + strip]
        lane.d_second.start_all()
        lane.out.start_all()
        r.own_contract[...] = mul(r.z[:, part(core, own_units)], flat(r.dy_all), ROWS_ROWS)
        for c in range(chips):
            r.ge_send[c] = mul(flat(r.c_all, other), r.du_all[c], ROWS_ROWS).astype(BF16)
        lane.g_expand.start_all()
        for c in range(chips):
            r.own_expand[:, c * units : (c + 1) * units] = mul(
                flat(r.c_all, mine), r.du_all[c], ROWS_ROWS
            )
        lane.d_second.take_all()

        def gathered(send, recv):
            blocks = []
            for c in range(chips):
                block = jnp.zeros((strip, slab), F32)
                for m in range(mp_size):
                    block = block + recv[c, m].astype(F32)
                blocks.append(block)
            return jnp.concatenate(blocks, axis=1)

        r.dc_recv[chip, mp] = r.dc_send[chip, mp]
        d_normed = gathered(r.dc_send, r.dc_recv)
        back, gain_two, shift_two = norm_back(d_normed, r.hid[...], norm_row(2))
        d_hidden = r.cot[here, :].astype(F32) + back
        r.dh[...] = d_hidden
        r.da_mine[...] = d_hidden.astype(BF16)
        lane.d_hidden.start_all()
        r.da_rows[mp] = r.da_mine[...]
        lane.d_hidden.take_all()
        d_attended = mul(flat(r.da_rows), flat(r.wo), COLS_COLS).astype(BF16)
        for start in range(0, width, HEAD_DIM):
            query, key, value = (
                r.joint[:, c * width + start : c * width + start + HEAD_DIM] for c in range(3)
            )
            d_out = d_attended[:, start : start + HEAD_DIM]
            prob = probabilities(query, key, allowed)
            d_prob = mul(d_out, value, COLS_COLS)
            row_delta = jnp.sum(d_prob * prob, axis=-1, keepdims=True)
            d_raw = (prob * (d_prob - row_delta) * SCALE).astype(BF16)
            r.dq_mine[:, start : start + HEAD_DIM] = mul(d_raw, key).astype(BF16)
            r.dq_mine[:, width + start : width + start + HEAD_DIM] = mul(
                d_raw, query, ROWS_ROWS
            ).astype(BF16)
            r.dq_mine[:, 2 * width + start : 2 * width + start + HEAD_DIM] = mul(
                prob.astype(BF16), d_out, ROWS_ROWS
            ).astype(BF16)
        lane.d_joint.start_all()
        r.dq_all[chip] = r.dq_mine[...]

        lane.out.take_all()
        total = r.y_send[chip].astype(F32)
        for step in range(1, chips):
            total = total + r.y_recv[lane.out.source(step)].astype(F32)
        total = total.astype(BF16)
        for m in range(mp_size):
            r.y2_send[m] = total[m * strip : (m + 1) * strip]
        lane.out_strip.start_all()
        grad_out = mul(r.attended[...], flat(r.da_rows), ROWS_ROWS).astype(BF16)
        for c in range(chips):
            for k in range(2):
                first = (2 * c + k) * out_rows
                r.go_send[c, k] = grad_out[first : first + out_rows]

        def first_block(block):
            rows = r.dq_all[block]
            total = mul(rows[:, :width], r.wq[0], COLS_COLS)
            for c in range(1, 3):
                total = total + mul(rows[:, c * width : (c + 1) * width], r.wq[c], COLS_COLS)
            total = total.astype(BF16)
            for m in range(mp_size):
                r.df_send[block, m] = total[m * strip : (m + 1) * strip]

        first_block(chip)
        for step in range(1, chips):
            lane.d_joint.take(step)
            first_block(lane.d_joint.source(step))
        lane.d_first.start_all()
        lane.g_out.start_all()
        for c in range(3):
            r.gj_send[c] = mul(
                flat(r.a_all, other), flat(r.dq_all, slice(c * width, (c + 1) * width)), ROWS_ROWS
            ).astype(BF16)
        lane.g_joint.start_all()
        for c in range(3):
            r.own_joint[c] = mul(
                flat(r.a_all, mine), flat(r.dq_all, slice(c * width, (c + 1) * width)), ROWS_ROWS
            )
        lane.out_strip.take_all()
        total = r.hid[...] + r.y2_send[mp].astype(F32)
        for step in range(1, mp_size):
            total = total + r.y2_recv[lane.out_strip.source(step)].astype(F32)
        r.y_mine[...] = total.astype(BF16)
        lane.out_rows.start_all()
        r.layer_output[here, :] = r.y_mine[...]

        lane.d_first.take_all()
        r.df_recv[chip, mp] = r.df_send[chip, mp]
        d_normed = gathered(r.df_send, r.df_recv)
        back, gain_one, shift_one = norm_back(d_normed, r.x[here, :].astype(F32), norm_row(0))
        grad = r.dh[...] + back
        r.ig_mine[...] = grad.astype(BF16)
        lane.in_rows.start_all()
        r.input_grad[here, :] = grad
        for c in range(chips):
            columns = slice(c * slab, (c + 1) * slab)
            for index, row in enumerate((gain_one, shift_one, gain_two, shift_two)):
                r.gn_send[c, index : index + 1, :] = row[:, columns]
            r.gn_send[c, 4:8, :] = jnp.zeros((4, slab), F32)
        lane.g_norms.start_all()
        r.gn_recv[cross_me] = r.gn_send[chip]
        lane.g_norms.take_all()
        summed = r.gn_recv[0]
        for index in range(1, chips * mp_size):
            summed = summed + r.gn_recv[index]
        low, high = summed[:, :shard], summed[:, shard:]
        first = core == 0
        r.gn_pair[...] = jnp.where(first, high, low)
        lane.g_norms_pair.start_all()

        lane.g_out.take_all()
        for k in range(2):
            total = r.go_send[chip, k].astype(F32)
            for step in range(1, chips):
                total = total + r.go_recv[lane.g_out.source(step), k].astype(F32)

            @pl.when(core == k)
            def _():
                r.own_out[...] = total

            r.go_pair[k] = total.astype(BF16)
        lane.g_out_pair.start_all()

        lane.g_norms_pair.take_all()
        r.own_norms[...] = jnp.where(first, low, high) + r.gn_far[...]

        def place(rows_lane, rows, output):
            rows_lane.take_all()
            for step in range(1, mp_size):
                source = rows_lane.source(step)
                output[part(source, strip), :] = rows[source].astype(output.dtype)

        place(lane.out_rows, r.y_rows, r.layer_output)
        place(lane.in_rows, r.ig_rows, r.input_grad)
        for entry in (lane.g_contract, lane.g_expand, lane.g_joint, lane.g_out_pair):
            entry.take_all()
        for entry in vars(lane).values():
            entry.sent_all()
        for step in range(1, chips):
            passing(step, False).wait_send()

    vmem = pl.BlockSpec(memory_space=pltpu.VMEM)
    any_space = pl.BlockSpec(memory_space=pl.ANY)
    sem_shapes = [pltpu.SemaphoreType.DMA((4,))]
    for kind in LANES.values():
        sem_shapes += [pltpu.SemaphoreType.DMA((vars(groups)[kind].size,))] * 2
    results = pl.pallas_call(
        kernel,
        out_shape=list(outs.values()) + list(far.values()),
        in_specs=[vmem] * 4 + [any_space] * 4 + [vmem],
        out_specs=[vmem] * len(outs) + [any_space] * len(far),
        scratch_shapes=[pltpu.VMEM(*entry) for entry in scratch.values()] + sem_shapes,
        compiler_params=pltpu.CompilerParams(
            collective_id=30, has_side_effects=True, vmem_limit_bytes=VMEM_LIMIT
        ),
    )(x, segments, segments.reshape(length, 1), cotangent, joint_w, out_w, expand_w, contract_w, norms)
    return SimpleNamespace(**dict(zip(list(outs) + list(far), results)))


VMEM_LIMIT = 60 * 2**20


def local(dp_size, mp_size, *arrays):
    params, firsts, seconds = arrays[3:8], arrays[8:13], arrays[13:18]
    everyone = Group(ALL, dp_size, mp_size)
    r = layer(dp_size, mp_size, arrays[:8])
    shard, hidden = params[2].shape
    far_expand = jnp.swapaxes(r.far_expand, 0, 1).reshape(shard, hidden)
    grads = (
        r.own_joint + r.far_joint.astype(F32),
        r.own_out + r.far_out.astype(F32),
        r.own_expand + far_expand.astype(F32),
        r.own_contract + r.far_contract.astype(F32),
        r.own_norms[:4],
    )
    squares = sum((jnp.sum(entry * entry) for entry in grads[:4])) + jnp.sum(
        grads[4] * grads[4]
    ) / mp_size
    (square_parts,) = exchange(
        everyone,
        [jnp.full((8, 128), squares, F32)],
        [shape((dp_size * mp_size, 8, 128), F32)],
        [lambda ins, outs, me, other: (ins[0], outs[0].at[me])],
        21,
    )
    gradient_norm = jnp.sqrt(jnp.sum(square_parts[:, 0, 0]))
    clip_factor = jnp.minimum(1.0, MAX_NORM / (gradient_norm + CLIP_EPSILON))
    updates = [
        adam_update(params[k], grads[k], firsts[k], seconds[k], LEARN_RATES[k], clip_factor)
        for k in range(5)
    ]
    copies = [entry[2].astype(BF16) for entry in updates]
    return (
        r.layer_output,
        r.input_grad,
        *grads,
        *[entry[0] for entry in updates],
        *[entry[1] for entry in updates],
        *[entry[2] for entry in updates],
        *copies,
        gradient_norm,
    )


def solution(mesh):
    rows = P("dp", None)
    sets = (
        P(None, "dp", "mp"),
        P(("mp", "dp"), None),
        P("dp", "mp"),
        P(("mp", "dp"), None),
        P(None, "dp"),
    )
    form = local if mesh.shape["dp"] <= 8 else local_steps
    return jax.shard_map(
        functools.partial(form, mesh.shape["dp"], mesh.shape["mp"]),
        mesh=mesh,
        in_specs=(rows, rows, rows) + sets * 3,
        out_specs=(rows, rows) + sets * 5 + (P(),),
        check_vma=False,
    )
```

```python
import functools
import math
from types import SimpleNamespace

import jax
import jax.numpy as jnp
from jax import lax
from jax.experimental import pallas as pl
from jax.experimental.pallas import tpu as pltpu
from jax.sharding import PartitionSpec as P

HEAD_DIM = 128
ADAM_STEP = 5
MAX_NORM = 8192


BETA_ONE = 0.9
BETA_TWO = 0.95
ADAM_EPSILON = 1e-08
WEIGHT_DECAY = 0.1
NORM_EPSILON = 1e-05
CLIP_EPSILON = 1e-06
LEARN_RATES = (0.01, 0.08, 0.012, 0.02, 0.3)
MASKED_SCORE = -1e30
SCALE = 1.0 / math.sqrt(HEAD_DIM)
F32 = jnp.float32
BF16 = jnp.bfloat16
ROWS_COLS = (((1,), (0,)), ((), ()))
COLS_COLS = (((1,), (1,)), ((), ()))
ROWS_ROWS = (((0,), (0,)), ((), ()))


def mul(left, right, dims=ROWS_COLS):
    return lax.dot_general(left, right, dims, preferred_element_type=F32)


def layer_norm(values, gain_row, shift_row):
    row_mean = jnp.mean(values, axis=-1, keepdims=True)
    centered = values - row_mean
    spread = jnp.mean(centered * centered, axis=-1, keepdims=True)
    return centered * lax.rsqrt(spread + NORM_EPSILON) * gain_row + shift_row


def gelu_tanh(values):
    return jax.nn.gelu(values, approximate=True)


def adam_update(weight, grad, first, second, rate, clip_factor):
    clipped = grad * clip_factor
    new_first = BETA_ONE * first + (1.0 - BETA_ONE) * clipped
    new_second = BETA_TWO * second + (1.0 - BETA_TWO) * clipped * clipped
    first_hat = new_first / (1.0 - BETA_ONE**ADAM_STEP)
    second_hat = new_second / (1.0 - BETA_TWO**ADAM_STEP)
    new_weight = weight - rate * (
        first_hat / (jnp.sqrt(second_hat) + ADAM_EPSILON) + WEIGHT_DECAY * weight
    )
    return (new_first, new_second, new_weight)


PAIR, PLANE, COLUMN, CROSS, ROW, ALL = ("pair", "plane", "column", "cross", "row", "all")


class Group:
    def __init__(self, kind, dp_size, mp_size):
        self.kind = kind
        self.mp_size = mp_size
        chips = dp_size // 2
        self.size = {
            PAIR: 2,
            PLANE: chips,
            COLUMN: mp_size,
            CROSS: chips * mp_size,
            ROW: dp_size,
            ALL: dp_size * mp_size,
        }[kind]

    def me(self):
        dp, mp = lax.axis_index("dp"), lax.axis_index("mp")
        if self.kind == PAIR:
            return lax.rem(dp, 2)
        if self.kind == PLANE:
            return lax.div(dp, 2)
        if self.kind == COLUMN:
            return mp
        if self.kind == CROSS:
            return lax.div(dp, 2) * self.mp_size + mp
        if self.kind == ROW:
            return dp
        return dp * self.mp_size + mp

    def device(self, member):
        dp, mp = lax.axis_index("dp"), lax.axis_index("mp")
        core = lax.rem(dp, 2)
        if self.kind == PAIR:
            return (dp - core + member, mp)
        if self.kind == PLANE:
            return (member * 2 + core, mp)
        if self.kind == COLUMN:
            return (dp, member)
        if self.kind == CROSS:
            return (lax.div(member, self.mp_size) * 2 + core, lax.rem(member, self.mp_size))
        if self.kind == ROW:
            return (member, mp)
        return (lax.div(member, self.mp_size), lax.rem(member, self.mp_size))


def repeat(low, high, body):
    if high - low <= 8:
        for step in range(low, high):
            body(step)
    else:
        lax.fori_loop(low, high, lambda step, none: (body(step), none)[1], None)


def exchange(group, operands, results, moves, collective_id):
    count = len(operands)
    size = group.size
    lanes = len(moves)

    def kernel(*refs):
        ins, outs = refs[:count], refs[count : count + len(results)]
        send_sems, recv_sems, own_sems = refs[count + len(results) :]
        me = group.me()
        barrier = pltpu.get_barrier_semaphore()

        def greet(step):
            other = lax.rem(me + step, size)
            pl.semaphore_signal(
                barrier, inc=1, device_id=group.device(other), device_id_type=pl.DeviceIdType.MESH
            )

        repeat(1, size, greet)
        pl.semaphore_wait(barrier, size - 1)

        def remote(move, lane, step, sender, target, device):
            return pltpu.make_async_remote_copy(
                src_ref=move(ins, outs, me, target)[0],
                dst_ref=move(ins, outs, sender, me)[1],
                send_sem=send_sems.at[lane, step],
                recv_sem=recv_sems.at[lane, step],
                device_id=group.device(device),
                device_id_type=pl.DeviceIdType.MESH,
            )

        def launch(step):
            other = lax.rem(me + step, size)
            for lane, move in enumerate(moves):
                remote(move, lane, step, me, other, other).start()

        repeat(1, size, launch)
        own = []
        for lane, move in enumerate(moves):
            source, target = move(ins, outs, me, me)
            own.append(pltpu.make_async_copy(source, target, own_sems.at[lane]))
            own[-1].start()

        def finish(step):
            other = lax.rem(me + step, size)
            sender = lax.rem(me + size - step, size)
            for lane, move in enumerate(moves):
                remote(move, lane, step, sender, other, other).wait()

        repeat(1, size, finish)
        for copy in own:
            copy.wait()

    any_space = pl.BlockSpec(memory_space=pl.ANY)
    return pl.pallas_call(
        kernel,
        out_shape=results,
        in_specs=[any_space] * count,
        out_specs=[any_space] * len(results),
        scratch_shapes=[
            pltpu.SemaphoreType.DMA((lanes, size)),
            pltpu.SemaphoreType.DMA((lanes, size)),
            pltpu.SemaphoreType.DMA((lanes,)),
        ],
        compiler_params=pltpu.CompilerParams(collective_id=collective_id, has_side_effects=True),
    )(*operands)


def shape(dims, dtype=BF16):
    return jax.ShapeDtypeStruct(dims, dtype)


def part(index, width):
    return pl.ds(pl.multiple_of(index * width, width), width)


def allowed_pairs(seg_row, seg_col, length):
    places = lax.broadcasted_iota(jnp.int32, (length, length), 0)
    keys = lax.broadcasted_iota(jnp.int32, (length, length), 1)
    return (seg_col[...] == seg_row[...]) & (keys <= places)


def probabilities(query, key, allowed):
    scores = jnp.where(allowed, mul(query, key, COLS_COLS) * SCALE, MASKED_SCORE)
    exponent = jnp.exp(scores - jnp.max(scores, axis=-1, keepdims=True))
    return exponent / jnp.sum(exponent, axis=-1, keepdims=True)


def attend_kernel(width, joint, seg_row, seg_col, out_weight, attended, partial):
    allowed = allowed_pairs(seg_row, seg_col, joint.shape[0])
    for start in range(0, width, HEAD_DIM):
        head = pl.ds(start, HEAD_DIM)
        query, key, value = (joint[:, pl.ds(c * width + start, HEAD_DIM)] for c in range(3))
        prob = probabilities(query, key, allowed)
        attended[:, head] = mul(prob.astype(BF16), value).astype(BF16)
    partial[...] = mul(attended[...], out_weight[...]).astype(BF16)


def attend_back_kernel(
    width, joint, seg_row, seg_col, out_weight, attended, branch, d_joint, grad_out, d_attended
):
    allowed = allowed_pairs(seg_row, seg_col, joint.shape[0])
    d_attended[...] = mul(branch[...], out_weight[...], COLS_COLS).astype(BF16)
    for start in range(0, width, HEAD_DIM):
        query, key, value = (joint[:, pl.ds(c * width + start, HEAD_DIM)] for c in range(3))
        d_out = d_attended[:, pl.ds(start, HEAD_DIM)]
        prob = probabilities(query, key, allowed)
        d_joint[:, pl.ds(2 * width + start, HEAD_DIM)] = mul(
            prob.astype(BF16), d_out, ROWS_ROWS
        ).astype(BF16)
        d_prob = mul(d_out, value, COLS_COLS)
        row_delta = jnp.sum(d_prob * prob, axis=-1, keepdims=True)
        d_raw = (prob * (d_prob - row_delta) * SCALE).astype(BF16)
        d_joint[:, pl.ds(start, HEAD_DIM)] = mul(d_raw, key).astype(BF16)
        d_joint[:, pl.ds(width + start, HEAD_DIM)] = mul(d_raw, query, ROWS_ROWS).astype(BF16)
    grad_out[...] = mul(attended[...], branch[...], ROWS_ROWS).astype(BF16)


def local_steps(
    dp_size,
    mp_size,
    inputs,
    segment_ids,
    cotangent,
    query_key_value,
    attention_out,
    expand_weight,
    contract_weight,
    norm_params,
    first_query_key_value,
    first_attention_out,
    first_expand_weight,
    first_contract_weight,
    first_norm_params,
    second_query_key_value,
    second_attention_out,
    second_expand_weight,
    second_contract_weight,
    second_norm_params,
):
    params = (query_key_value, attention_out, expand_weight, contract_weight, norm_params)
    firsts = (
        first_query_key_value,
        first_attention_out,
        first_expand_weight,
        first_contract_weight,
        first_norm_params,
    )
    seconds = (
        second_query_key_value,
        second_attention_out,
        second_expand_weight,
        second_contract_weight,
        second_norm_params,
    )
    chips = dp_size // 2
    pair, plane, column, cross, row, everyone = (
        Group(kind, dp_size, mp_size)
        for kind in (PAIR, PLANE, COLUMN, CROSS, ROW, ALL)
    )
    dp, mp = lax.axis_index("dp"), lax.axis_index("mp")
    core = dp % 2
    length, model = inputs.shape
    width = query_key_value.shape[2]
    shard = query_key_value.shape[1]
    slab = 2 * shard
    hidden_units = expand_weight.shape[1]
    own_units = contract_weight.shape[0]
    units = 2 * own_units
    out_rows = attention_out.shape[0]
    strip = length // mp_size
    tokens = chips * length

    (norm_all,) = exchange(
        row,
        [norm_params],
        [shape((dp_size, 4, shard), F32)],
        [lambda ins, outs, me, other: (ins[0], outs[0].at[me])],
        0,
    )
    norm_weights = jnp.swapaxes(norm_all.astype(BF16).astype(F32), 0, 1).reshape(4, model)

    def shared(column_block):
        def move(ins, outs, me, other):
            return (ins[0].at[column_block], outs[0].at[part(me, shard), pl.ds(column_block * width, width)])

        return move

    joint_weight, expand_pair, contract_pair = exchange(
        pair,
        [query_key_value.astype(BF16), expand_weight.astype(BF16), contract_weight.astype(BF16)],
        [shape((slab, 3 * width)), shape((slab, hidden_units)), shape((units, model))],
        [
            shared(0),
            shared(1),
            shared(2),
            lambda ins, outs, me, other: (ins[1], outs[1].at[part(me, shard), :]),
            lambda ins, outs, me, other: (ins[2], outs[2].at[part(me, own_units), :]),
        ],
        1,
    )
    (output_all,) = exchange(
        row,
        [attention_out.astype(BF16)],
        [shape((dp_size * out_rows, model))],
        [lambda ins, outs, me, other: (ins[0], outs[0].at[part(me, out_rows), :])],
        2,
    )
    (grad_rows,) = exchange(
        plane,
        [cotangent],
        [shape((chips, length, model))],
        [lambda ins, outs, me, other: (ins[0], outs[0].at[me])],
        3,
    )
    grad_rows = grad_rows.reshape(tokens, model)

    values = inputs.astype(F32)
    normed = layer_norm(values, norm_weights[0], norm_weights[1]).astype(BF16)
    (normed_low,) = exchange(
        plane,
        [normed],
        [shape((chips, length, slab))],
        [lambda ins, outs, me, other: (ins[0].at[:, part(other, slab)], outs[0].at[me])],
        4,
    )
    normed_low = normed_low.reshape(tokens, slab)
    joint_part = mul(normed_low, joint_weight).astype(BF16).reshape(chips, length, 3 * width)
    (joint_parts,) = exchange(
        plane,
        [joint_part],
        [shape((chips, length, 3 * width))],
        [lambda ins, outs, me, other: (ins[0].at[other], outs[0].at[me])],
        5,
    )
    joint = jnp.sum(joint_parts.astype(F32), axis=0).astype(BF16)

    seg_row = segment_ids
    seg_col = segment_ids.reshape(length, 1)
    attended, branch_part = pl.pallas_call(
        functools.partial(attend_kernel, width),
        out_shape=[shape((length, width)), shape((length, model))],
        compiler_params=pltpu.CompilerParams(vmem_limit_bytes=48 * 2**20),
    )(joint, seg_row, seg_col, output_all)

    (branch_parts,) = exchange(
        column,
        [branch_part.reshape(mp_size, strip, model)],
        [shape((mp_size, strip, model))],
        [lambda ins, outs, me, other: (ins[0].at[other], outs[0].at[me])],
        6,
    )
    own_values = lax.dynamic_slice_in_dim(values, mp * strip, strip, 0)
    hidden = own_values + jnp.sum(branch_parts.astype(F32), axis=0)
    normed_two, pull_two = jax.vjp(layer_norm, hidden, norm_weights[2], norm_weights[3])
    (second_low,) = exchange(
        cross,
        [normed_two.astype(BF16)],
        [shape((chips * mp_size, strip, slab))],
        [
            lambda ins, outs, me, other: (
                ins[0].at[:, part(lax.div(other, mp_size), slab)],
                outs[0].at[me],
            )
        ],
        7,
    )
    second_low = second_low.reshape(tokens, slab)
    pre_part = mul(second_low, expand_pair).astype(BF16)
    (pre_parts,) = exchange(
        plane,
        [pre_part],
        [shape((chips, tokens, units))],
        [lambda ins, outs, me, other: (ins[0].at[:, part(other, units)], outs[0].at[me])],
        8,
    )
    pre_gelu = jnp.sum(pre_parts.astype(F32), axis=0)
    activated, pull_gelu = jax.vjp(gelu_tanh, pre_gelu)
    activated_low = activated.astype(BF16)
    d_activated = mul(grad_rows, contract_pair, COLS_COLS)
    (d_pre,) = pull_gelu(d_activated)
    (d_pre_all,) = exchange(
        plane,
        [d_pre.astype(BF16)],
        [shape((tokens, hidden_units))],
        [lambda ins, outs, me, other: (ins[0], outs[0].at[:, part(me, units)])],
        9,
    )

    def scatter_rows(partial, collective_id):
        (blocks,) = exchange(
            cross,
            [partial.reshape(chips * mp_size, strip, slab)],
            [shape((chips * mp_size, strip, slab))],
            [lambda ins, outs, me, other: (ins[0].at[other], outs[0].at[me])],
            collective_id,
        )
        total = jnp.sum(blocks.reshape(chips, mp_size, strip, slab).astype(F32), axis=1)
        return jnp.swapaxes(total, 0, 1).reshape(strip, model)

    d_normed_two = scatter_rows(mul(d_pre_all, expand_pair, COLS_COLS).astype(BF16), 10)
    d_hidden_norm, gain_two, shift_two = pull_two(d_normed_two)
    own_grad = lax.dynamic_slice_in_dim(cotangent, mp * strip, strip, 0).astype(F32)
    d_hidden = own_grad + d_hidden_norm

    def gather_rows(block, collective_id):
        (rows,) = exchange(
            column,
            [block],
            [shape((mp_size, strip, model))],
            [lambda ins, outs, me, other: (ins[0], outs[0].at[me])],
            collective_id,
        )
        return rows.reshape(length, model)

    branch_grad = gather_rows(d_hidden.astype(BF16), 11)
    d_joint, grad_output_part, _ = pl.pallas_call(
        functools.partial(attend_back_kernel, width),
        out_shape=[shape((length, 3 * width)), shape((width, model)), shape((length, width))],
        compiler_params=pltpu.CompilerParams(vmem_limit_bytes=48 * 2**20),
    )(joint, seg_row, seg_col, output_all, attended, branch_grad)
    (d_joint_all,) = exchange(
        plane,
        [d_joint],
        [shape((chips, length, 3 * width))],
        [lambda ins, outs, me, other: (ins[0], outs[0].at[me])],
        12,
    )
    d_joint_all = d_joint_all.reshape(tokens, 3 * width)
    d_normed_one = scatter_rows(mul(d_joint_all, joint_weight, COLS_COLS).astype(BF16), 13)
    _, pull_one = jax.vjp(layer_norm, own_values, norm_weights[0], norm_weights[1])
    d_values_norm, gain_one, shift_one = pull_one(d_normed_one)
    input_grad = gather_rows((d_hidden + d_values_norm).astype(BF16), 14).astype(F32)

    out_part = mul(activated_low, contract_pair).astype(BF16).reshape(chips, length, model)
    (out_parts,) = exchange(
        plane,
        [out_part],
        [shape((chips, length, model))],
        [lambda ins, outs, me, other: (ins[0].at[other], outs[0].at[me])],
        15,
    )
    out_rows_sum = jnp.sum(out_parts.astype(F32), axis=0).astype(BF16)
    (out_strips,) = exchange(
        column,
        [out_rows_sum.reshape(mp_size, strip, model)],
        [shape((mp_size, strip, model))],
        [lambda ins, outs, me, other: (ins[0].at[other], outs[0].at[me])],
        16,
    )
    layer_output = gather_rows(
        (hidden + jnp.sum(out_strips.astype(F32), axis=0)).astype(BF16), 17
    )

    (grad_output_parts,) = exchange(
        row,
        [grad_output_part.reshape(dp_size, out_rows, model)],
        [shape((dp_size, out_rows, model))],
        [lambda ins, outs, me, other: (ins[0].at[other], outs[0].at[me])],
        18,
    )
    reduced_output = jnp.sum(grad_output_parts.astype(F32), axis=0)
    own_joint, other_joint = [], []
    grad_joint = mul(normed_low, d_joint_all, ROWS_ROWS)
    grad_expand = mul(second_low, d_pre_all, ROWS_ROWS)
    grad_contract = mul(activated_low, grad_rows, ROWS_ROWS)

    def halves(array, index):
        return lax.dynamic_slice_in_dim(array, index * (array.shape[0] // 2), array.shape[0] // 2, 0)

    pieces = (grad_joint, grad_expand, grad_contract)
    sent = [halves(entry, 1 - core).astype(BF16) for entry in pieces]
    got = exchange_pair(pair, sent, 19)
    reduced_joint, reduced_expand, reduced_contract = (
        halves(entry, core) + other.astype(F32) for entry, other in zip(pieces, got)
    )
    reduced_joint = jnp.swapaxes(reduced_joint.reshape(shard, 3, width), 0, 1)

    zero_row = jnp.zeros((model,), F32)
    norm_rows = jnp.stack([gain_one, shift_one, gain_two, shift_two] + [zero_row] * 4)
    norm_rows = jnp.swapaxes(norm_rows.reshape(8, dp_size, shard), 0, 1)
    (norm_parts,) = exchange(
        everyone,
        [norm_rows],
        [shape((dp_size * mp_size, 8, shard), F32)],
        [
            lambda ins, outs, me, other: (
                ins[0].at[lax.div(other, mp_size)],
                outs[0].at[me],
            )
        ],
        20,
    )
    reduced_norms = jnp.sum(norm_parts, axis=0)[:4]

    grads = (reduced_joint, reduced_output, reduced_expand, reduced_contract, reduced_norms)
    squares = sum((jnp.sum(entry * entry) for entry in grads[:4])) + jnp.sum(
        reduced_norms * reduced_norms
    ) / mp_size
    (square_parts,) = exchange(
        everyone,
        [jnp.full((8, 128), squares, F32)],
        [shape((dp_size * mp_size, 8, 128), F32)],
        [lambda ins, outs, me, other: (ins[0], outs[0].at[me])],
        21,
    )
    gradient_norm = jnp.sqrt(jnp.sum(square_parts[:, 0, 0]))
    clip_factor = jnp.minimum(1.0, MAX_NORM / (gradient_norm + CLIP_EPSILON))
    updates = [
        adam_update(params[k], grads[k], firsts[k], seconds[k], LEARN_RATES[k], clip_factor)
        for k in range(5)
    ]
    copies = [entry[2].astype(BF16) for entry in updates]
    return (
        layer_output,
        input_grad,
        *grads,
        *[entry[0] for entry in updates],
        *[entry[1] for entry in updates],
        *[entry[2] for entry in updates],
        *copies,
        gradient_norm,
    )


def exchange_pair(pair, sent, collective_id):
    moves = [
        lambda ins, outs, me, other, lane=lane: (ins[lane], outs[lane]) for lane in range(len(sent))
    ]
    return swap(pair, sent, moves, collective_id)


def swap(pair, sent, moves, collective_id):
    count = len(sent)

    def kernel(*refs):
        ins, outs = refs[:count], refs[count : 2 * count]
        send_sems, recv_sems = refs[2 * count :]
        other = pair.device(1 - pair.me())
        barrier = pltpu.get_barrier_semaphore()
        pl.semaphore_signal(barrier, inc=1, device_id=other, device_id_type=pl.DeviceIdType.MESH)
        pl.semaphore_wait(barrier, 1)
        copies = [
            pltpu.make_async_remote_copy(
                src_ref=ins[lane],
                dst_ref=outs[lane],
                send_sem=send_sems.at[lane],
                recv_sem=recv_sems.at[lane],
                device_id=other,
                device_id_type=pl.DeviceIdType.MESH,
            )
            for lane in range(count)
        ]
        for copy in copies:
            copy.start()
        for copy in copies:
            copy.wait()

    any_space = pl.BlockSpec(memory_space=pl.ANY)
    return pl.pallas_call(
        kernel,
        out_shape=[shape(entry.shape, entry.dtype) for entry in sent],
        in_specs=[any_space] * count,
        out_specs=[any_space] * count,
        scratch_shapes=[pltpu.SemaphoreType.DMA((count,)), pltpu.SemaphoreType.DMA((count,))],
        compiler_params=pltpu.CompilerParams(collective_id=collective_id, has_side_effects=True),
    )(*sent)


class Lane:
    def __init__(self, group, me, sems, view):
        self.group, self.me, self.view = group, me, view
        self.send_sems, self.recv_sems = sems
        self.size = group.size

    def copy(self, step):
        to = lax.rem(self.me + step, self.size)
        return pltpu.make_async_remote_copy(
            src_ref=self.view(self.me, to)[0],
            dst_ref=self.view(self.me, to)[1],
            send_sem=self.send_sems.at[step],
            recv_sem=self.recv_sems.at[step],
            device_id=self.group.device(to),
            device_id_type=pl.DeviceIdType.MESH,
        )

    def start(self, step):
        self.copy(step).start()

    def start_all(self):
        repeat(1, self.size, self.start)

    def source(self, step):
        return lax.rem(self.me + self.size - step, self.size)

    def take(self, step):
        to = lax.rem(self.me + step, self.size)
        pltpu.make_async_remote_copy(
            src_ref=self.view(self.me, to)[0],
            dst_ref=self.view(self.source(step), self.me)[1],
            send_sem=self.send_sems.at[step],
            recv_sem=self.recv_sems.at[step],
            device_id=self.group.device(to),
            device_id_type=pl.DeviceIdType.MESH,
        ).wait_recv()

    def take_all(self):
        repeat(1, self.size, self.take)

    def sent(self, step):
        self.copy(step).wait_send()

    def sent_all(self):
        repeat(1, self.size, self.sent)


def standardise(values):
    row_mean = jnp.mean(values, axis=-1, keepdims=True)
    centered = values - row_mean
    spread = jnp.mean(centered * centered, axis=-1, keepdims=True)
    return centered, lax.rsqrt(spread + NORM_EPSILON)


def norm_back(grad, values, gain_row):
    centered, inverse = standardise(values)
    unit = centered * inverse
    scaled = grad * gain_row
    inner = jnp.mean(scaled * unit, axis=-1, keepdims=True)
    back = inverse * (scaled - jnp.mean(scaled, axis=-1, keepdims=True) - unit * inner)
    gain_grad = jnp.sum(grad * unit, axis=0, keepdims=True)
    shift_grad = jnp.sum(grad, axis=0, keepdims=True)
    return back, gain_grad, shift_grad


ROOT = math.sqrt(2.0 / math.pi)
CUBE = 0.044715

LANES = dict(
    norms=ROW,
    normed=PLANE,
    joint_weight=PAIR,
    out_own=PAIR,
    out_plane=PLANE,
    joint=PLANE,
    expand=PAIR,
    contract=PAIR,
    cotangent=PLANE,
    branch=COLUMN,
    second=CROSS,
    pre=PLANE,
    d_pre=PLANE,
    g_contract=PAIR,
    d_second=CROSS,
    out=PLANE,
    g_expand=PAIR,
    d_hidden=COLUMN,
    d_joint=PLANE,
    g_out=PLANE,
    g_out_pair=PAIR,
    out_strip=COLUMN,
    d_first=CROSS,
    g_joint=PAIR,
    out_rows=COLUMN,
    in_rows=COLUMN,
    g_norms=CROSS,
    g_norms_pair=PAIR,
    squares=CROSS,
    squares_pair=PAIR,
)
PIECED = ("joint", "d_joint")


def layer(dp_size, mp_size, operands):
    x, segments, cotangent, joint_w, out_w, expand_w, contract_w, norms = operands
    chips = dp_size // 2
    groups = SimpleNamespace(
        **{kind: Group(kind, dp_size, mp_size) for kind in (PAIR, PLANE, COLUMN, CROSS, ROW)}
    )
    length, model = x.shape
    width, shard = joint_w.shape[2], joint_w.shape[1]
    slab = 2 * shard
    hidden = expand_w.shape[1]
    own_units = contract_w.shape[0]
    units = 2 * own_units
    out_rows = out_w.shape[0]
    strip = length // mp_size
    tokens = chips * length
    wide = 3 * width
    pieces = max(1, width // (2 * HEAD_DIM))
    piece = width // pieces

    outs = dict(
        layer_output=shape((length, model)),
        input_grad=shape((length, model), F32),
        own_joint=shape((3, shard, width), F32),
        own_out=shape((out_rows, model), F32),
        own_expand=shape((shard, hidden), F32),
        own_contract=shape((own_units, model), F32),
        own_norms=shape((8, shard), F32),
        square_sum=shape((8, 128), F32),
        far_joint=shape((3, shard, width)),
        far_out=shape((out_rows, model)),
        far_expand=shape((chips, shard, units)),
        far_contract=shape((own_units, model)),
    )
    scratch = dict(
        norm_all=((dp_size, 4, shard), F32),
        a_mine=((chips, length, slab), BF16),
        a_all=((chips, length, slab), BF16),
        wq=((3, slab, width), BF16),
        wo=((dp_size, out_rows, model), BF16),
        wu=((chips, slab, units), BF16),
        wd=((units, model), BF16),
        j_send=((pieces, chips, length, 3 * piece), BF16),
        j_recv=((pieces, chips, length, 3 * piece), BF16),
        joint=((pieces, length, 3 * piece), BF16),
        dy_all=((chips, length, model), BF16),
        attended=((length, width), BF16),
        b_send=((mp_size, strip, model), BF16),
        b_recv=((mp_size, strip, model), BF16),
        hid=((strip, model), F32),
        c_mine=((chips, strip, slab), BF16),
        c_all=((chips, mp_size, strip, slab), BF16),
        u_send=((chips, tokens, units), BF16),
        u_recv=((chips, tokens, units), BF16),
        u_acc=((tokens, units), F32),
        dz=((tokens, units), F32),
        z=((tokens, units), BF16),
        du_all=((chips, tokens, units), BF16),
        y_send=((chips, length, model), BF16),
        y_recv=((chips, length, model), BF16),
        gc_send=((own_units, model), BF16),
        dc_send=((chips, mp_size, strip, slab), BF16),
        dc_recv=((chips, mp_size, strip, slab), BF16),
        ge_send=((chips, shard, units), BF16),
        dh=((strip, model), F32),
        da_mine=((strip, model), BF16),
        da_rows=((mp_size, strip, model), BF16),
        dq_mine=((pieces, length, 3 * piece), BF16),
        dq_all=((pieces, chips, length, 3 * piece), BF16),
        go_send=((chips, 2, out_rows, model), BF16),
        go_recv=((chips, 2, out_rows, model), BF16),
        go_pair=((2, out_rows, model), BF16),
        y2_send=((mp_size, strip, model), BF16),
        y2_recv=((mp_size, strip, model), BF16),
        y_mine=((strip, model), BF16),
        y_rows=((mp_size, strip, model), BF16),
        df_send=((chips, mp_size, strip, slab), BF16),
        df_recv=((chips, mp_size, strip, slab), BF16),
        gj_send=((3, shard, width), BF16),
        ig_mine=((strip, model), BF16),
        ig_rows=((mp_size, strip, model), BF16),
        gn_send=((chips, 8, slab), F32),
        gn_recv=((chips * mp_size, 8, slab), F32),
        gn_pair=((8, shard), F32),
        gn_far=((8, shard), F32),
        sq_mine=((8, 128), F32),
        sq_recv=((chips * mp_size, 8, 128), F32),
        sq_pair=((8, 128), F32),
        sq_far=((8, 128), F32),
    )
    in_names = dict(
        x=0, seg_row=1, cot=2, f_joint=3, f_out=4, f_expand=5, f_contract=6, norm_own=7
    )
    names = list(in_names) + list(outs) + list(scratch)

    def kernel(*refs):
        r = SimpleNamespace(**dict(zip(names, refs)))
        sems = refs[len(names) :]
        load_sems = sems[0]
        dp, mp = lax.axis_index("dp"), lax.axis_index("mp")
        core, chip = lax.rem(dp, 2), lax.div(dp, 2)
        mine, other = part(core, shard), part(1 - core, shard)
        cross_me = groups.cross.me()

        def flat(ref, columns=slice(None)):
            values = ref[(slice(None),) * (len(ref.shape) - 1) + (columns,)]
            return values.reshape(-1, values.shape[-1])

        views = dict(
            norms=lambda s, t: (r.norm_own, r.norm_all.at[s]),
            normed=lambda s, t: (r.a_mine.at[t], r.a_all.at[s]),
            joint_weight=lambda s, t: (
                r.wq.at[:, part(s, shard), :],
                r.wq.at[:, part(s, shard), :],
            ),
            out_own=lambda s, t: (r.wo.at[dp - core + s], r.wo.at[dp - core + s]),
            out_plane=lambda s, t: (r.wo.at[2 * s + core], r.wo.at[2 * s + core]),
            joint=[
                lambda s, t, p=p: (r.j_send.at[p, t], r.j_recv.at[p, s]) for p in range(pieces)
            ],
            expand=lambda s, t: (
                r.wu.at[:, part(s, shard), :],
                r.wu.at[:, part(s, shard), :],
            ),
            contract=lambda s, t: (
                r.wd.at[part(s, own_units), :],
                r.wd.at[part(s, own_units), :],
            ),
            cotangent=lambda s, t: (r.cot, r.dy_all.at[s]),
            branch=lambda s, t: (r.b_send.at[t], r.b_recv.at[s]),
            second=lambda s, t: (
                r.c_mine.at[lax.div(t, mp_size)],
                r.c_all.at[lax.div(s, mp_size), lax.rem(s, mp_size)],
            ),
            pre=lambda s, t: (r.u_send.at[t], r.u_recv.at[s]),
            d_pre=lambda s, t: (r.du_all.at[s], r.du_all.at[s]),
            g_contract=lambda s, t: (r.gc_send, r.far_contract),
            d_second=lambda s, t: (
                r.dc_send.at[lax.div(t, mp_size), lax.rem(t, mp_size)],
                r.dc_recv.at[lax.div(s, mp_size), lax.rem(s, mp_size)],
            ),
            out=lambda s, t: (r.y_send.at[t], r.y_recv.at[s]),
            g_expand=lambda s, t: (r.ge_send, r.far_expand),
            d_hidden=lambda s, t: (r.da_mine, r.da_rows.at[s]),
            d_joint=[
                lambda s, t, p=p: (r.dq_mine.at[p], r.dq_all.at[p, s]) for p in range(pieces)
            ],
            g_out=lambda s, t: (r.go_send.at[t], r.go_recv.at[s]),
            g_out_pair=lambda s, t: (r.go_pair.at[t], r.far_out),
            out_strip=lambda s, t: (r.y2_send.at[t], r.y2_recv.at[s]),
            d_first=lambda s, t: (
                r.df_send.at[lax.div(t, mp_size), lax.rem(t, mp_size)],
                r.df_recv.at[lax.div(s, mp_size), lax.rem(s, mp_size)],
            ),
            g_joint=lambda s, t: (r.gj_send, r.far_joint),
            out_rows=lambda s, t: (r.y_mine, r.y_rows.at[s]),
            in_rows=lambda s, t: (r.ig_mine, r.ig_rows.at[s]),
            g_norms=lambda s, t: (r.gn_send.at[lax.div(t, mp_size)], r.gn_recv.at[s]),
            g_norms_pair=lambda s, t: (r.gn_pair, r.gn_far),
            squares=lambda s, t: (r.sq_mine, r.sq_recv.at[s]),
            squares_pair=lambda s, t: (r.sq_pair, r.sq_far),
        )
        lane = SimpleNamespace()
        every_lane = []
        used = iter(sems[1:])
        for name, kind in LANES.items():
            group = vars(groups)[kind]
            lanes = [
                Lane(group, group.me(), (next(used), next(used)), view)
                for view in (views[name] if name in PIECED else [views[name]])
            ]
            every_lane += lanes
            setattr(lane, name, lanes if name in PIECED else lanes[0])
        pass_sems = (next(used), next(used))

        def passing(step, to_me):
            block = r.wo.at[2 * lane.out_plane.source(step) + (1 - core if to_me else core)]
            return pltpu.make_async_remote_copy(
                src_ref=block,
                dst_ref=block,
                send_sem=pass_sems[0].at[step],
                recv_sem=pass_sems[1].at[step],
                device_id=(dp + 1 - 2 * core, mp),
                device_id_type=pl.DeviceIdType.MESH,
            )

        loads = [
            pltpu.make_async_copy(source, target, load_sems.at[i])
            for i, (source, target) in enumerate(
                (
                    (r.f_joint, r.own_joint),
                    (r.f_out, r.own_out),
                    (r.f_expand, r.own_expand),
                    (r.f_contract, r.own_contract),
                )
            )
        ]
        for load in (loads[1], loads[0], loads[2], loads[3]):
            load.start()

        barrier = pltpu.get_barrier_semaphore()

        def greet(device):
            pl.semaphore_signal(
                barrier, inc=1, device_id=device, device_id_type=pl.DeviceIdType.MESH
            )

        cross = groups.cross
        repeat(1, cross.size, lambda s: greet(cross.device(lax.rem(cross_me + s, cross.size))))
        repeat(0, chips, lambda s: greet((s * 2 + 1 - core, mp)))

        r.norm_all[dp] = r.norm_own[...]
        loads[1].wait()
        r.wo[dp] = r.own_out[...].astype(BF16)
        values = r.x[...].astype(F32)
        centered, inverse = standardise(values)
        unit = centered * inverse
        loads[0].wait()
        for c in range(3):
            r.wq[c, mine, :] = r.own_joint[c].astype(BF16)
        ids = jnp.broadcast_to(r.seg_row[...].astype(F32), (length, length))
        places = lax.broadcasted_iota(jnp.int32, (length, length), 0)
        keys = lax.broadcasted_iota(jnp.int32, (length, length), 1)
        allowed = (ids == ids.T) & (keys <= places)
        pl.semaphore_wait(barrier, cross.size - 1 + chips)

        lane.norms.start_all()
        lane.joint_weight.start_all()
        lane.out_plane.start_all()
        lane.out_own.start_all()
        lane.norms.take_all()

        def norm_row(index, block=None):
            blocks = range(dp_size) if block is None else (block,)
            rows = [r.norm_all[b, pl.ds(index, 1), :] for b in blocks]
            whole = rows[0] if len(rows) == 1 else jnp.concatenate(rows, axis=1)
            return whole.astype(BF16).astype(F32)

        for b in range(dp_size):
            columns = slice(b * shard, (b + 1) * shard)
            r.a_mine[b // 2, :, (b % 2) * shard : (b % 2 + 1) * shard] = (
                unit[:, columns] * norm_row(0, b) + norm_row(1, b)
            ).astype(BF16)
        lane.normed.start_all()
        r.a_all[chip] = r.a_mine[chip]

        lane.joint_weight.take_all()

        def joint_part(p, block):
            rows = r.a_all[block]
            for c in range(3):
                r.j_send[p, block, :, c * piece : (c + 1) * piece] = mul(
                    rows, r.wq[c, :, p * piece : (p + 1) * piece]
                ).astype(BF16)

        for p in range(pieces):
            for step in range(1, chips):
                if p == 0:
                    lane.normed.take(step)
                joint_part(p, lane.normed.source(step))
                lane.joint[p].start(chips - step)
            joint_part(p, chip)

        loads[2].wait()
        for c in range(chips):
            r.wu[c, mine, :] = r.own_expand[:, c * units : (c + 1) * units].astype(BF16)
        lane.expand.start_all()
        loads[3].wait()
        r.wd[part(core, own_units), :] = r.own_contract[...].astype(BF16)
        lane.contract.start_all()
        for step in range(1, chips):
            lane.out_plane.take(step)
            passing(step, False).start()

        def query_key_value(start):
            p, first = start // piece, start % piece
            return (
                r.joint[p, :, c * piece + first : c * piece + first + HEAD_DIM] for c in range(3)
            )

        for p in range(pieces):
            lane.joint[p].take_all()
            total = r.j_send[p, chip].astype(F32)
            for step in range(1, chips):
                total = total + r.j_recv[p, lane.joint[p].source(step)].astype(F32)
            r.joint[p] = total.astype(BF16)
            if p == pieces - 1:
                lane.cotangent.start_all()
            for start in range(p * piece, (p + 1) * piece, HEAD_DIM):
                query, key, value = query_key_value(start)
                prob = probabilities(query, key, allowed)
                r.attended[:, start : start + HEAD_DIM] = mul(prob.astype(BF16), value).astype(BF16)

        lane.out_own.take_all()
        for step in range(1, chips):
            passing(step, True).wait_recv()
        branch = mul(r.attended[...], flat(r.wo)).astype(BF16)
        for m in range(mp_size):
            r.b_send[m] = branch[m * strip : (m + 1) * strip]
        lane.branch.start_all()
        r.dy_all[chip] = r.cot[...]
        lane.branch.take_all()
        here = part(mp, strip)
        total = r.x[here, :].astype(F32) + r.b_send[mp].astype(F32)
        for step in range(1, mp_size):
            total = total + r.b_recv[lane.branch.source(step)].astype(F32)
        r.hid[...] = total
        centered, inverse = standardise(total)
        for b in range(dp_size):
            columns = slice(b * shard, (b + 1) * shard)
            r.c_mine[b // 2, :, (b % 2) * shard : (b % 2 + 1) * shard] = (
                centered[:, columns] * inverse * norm_row(2, b) + norm_row(3, b)
            ).astype(BF16)
        lane.second.start_all()
        r.c_all[chip, mp] = r.c_mine[chip]
        lane.expand.take_all()
        lane.second.take_all()

        def pre_step(step):
            to = lax.rem(chip + step, chips)
            r.u_send[to] = mul(flat(r.c_all), r.wu[to]).astype(BF16)
            lane.pre.start(step)

        repeat(1, chips, pre_step)
        r.u_acc[...] = mul(flat(r.c_all), r.wu[chip])
        lane.contract.take_all()
        lane.cotangent.take_all()
        r.dz[...] = mul(flat(r.dy_all), r.wd[...], COLS_COLS)
        lane.pre.take_all()

        tile = 64

        def gelu_tile(i, none):
            rows = part(i, tile)
            pre = r.u_acc[rows, :]
            for step in range(1, chips):
                pre = pre + r.u_recv[lane.pre.source(step), rows, :].astype(F32)
            square = pre * pre
            curve = jnp.tanh(ROOT * pre * (1.0 + CUBE * square))
            half = 0.5 * (1.0 + curve)
            r.z[rows, :] = (pre * half).astype(BF16)
            slope = half + 0.5 * pre * (1.0 - curve * curve) * (ROOT * (1.0 + 3.0 * CUBE * square))
            r.du_all[chip, rows, :] = (r.dz[rows, :] * slope).astype(BF16)
            return none

        lax.fori_loop(0, tokens // tile, gelu_tile, None)
        lane.d_pre.start_all()

        for c in range(chips):
            rows = slice(c * length, (c + 1) * length)
            r.y_send[c] = mul(r.z[rows, :], r.wd[...]).astype(BF16)
        r.gc_send[...] = mul(r.z[:, part(1 - core, own_units)], flat(r.dy_all), ROWS_ROWS).astype(BF16)
        lane.g_contract.start_all()

        total = mul(r.du_all[chip], r.wu[chip], COLS_COLS)
        for step in range(1, chips):
            lane.d_pre.take(step)
            source = lane.d_pre.source(step)
            total = total + mul(r.du_all[source], r.wu[source], COLS_COLS)
        total = total.astype(BF16)
        for c in range(chips):
            for m in range(mp_size):
                first = c * length + m * strip
                r.dc_send[c, m] = total[first : first + strip]
        lane.d_second.start_all()
        lane.out.start_all()
        r.own_contract[...] = mul(r.z[:, part(core, own_units)], flat(r.dy_all), ROWS_ROWS)
        for c in range(chips):
            r.ge_send[c] = mul(flat(r.c_all, other), r.du_all[c], ROWS_ROWS).astype(BF16)
        lane.g_expand.start_all()
        for c in range(chips):
            r.own_expand[:, c * units : (c + 1) * units] = mul(
                flat(r.c_all, mine), r.du_all[c], ROWS_ROWS
            )
        lane.d_second.take_all()

        def gathered(send, recv):
            blocks = []
            for c in range(chips):
                block = jnp.zeros((strip, slab), F32)
                for m in range(mp_size):
                    block = block + recv[c, m].astype(F32)
                blocks.append(block)
            return jnp.concatenate(blocks, axis=1)

        r.dc_recv[chip, mp] = r.dc_send[chip, mp]
        d_normed = gathered(r.dc_send, r.dc_recv)
        back, gain_two, shift_two = norm_back(d_normed, r.hid[...], norm_row(2))
        d_hidden = r.cot[here, :].astype(F32) + back
        r.dh[...] = d_hidden
        r.da_mine[...] = d_hidden.astype(BF16)
        lane.d_hidden.start_all()
        r.da_rows[mp] = r.da_mine[...]
        lane.d_hidden.take_all()
        d_attended = mul(flat(r.da_rows), flat(r.wo), COLS_COLS).astype(BF16)
        for p in range(pieces):
            for start in range(p * piece, (p + 1) * piece, HEAD_DIM):
                query, key, value = query_key_value(start)
                d_out = d_attended[:, start : start + HEAD_DIM]
                prob = probabilities(query, key, allowed)
                d_prob = mul(d_out, value, COLS_COLS)
                row_delta = jnp.sum(d_prob * prob, axis=-1, keepdims=True)
                d_raw = (prob * (d_prob - row_delta) * SCALE).astype(BF16)
                thirds = (
                    mul(d_raw, key),
                    mul(d_raw, query, ROWS_ROWS),
                    mul(prob.astype(BF16), d_out, ROWS_ROWS),
                )
                for c in range(3):
                    first = c * piece + start % piece
                    r.dq_mine[p, :, first : first + HEAD_DIM] = thirds[c].astype(BF16)
            lane.d_joint[p].start_all()
            r.dq_all[p, chip] = r.dq_mine[p]

        lane.out.take_all()
        total = r.y_send[chip].astype(F32)
        for step in range(1, chips):
            total = total + r.y_recv[lane.out.source(step)].astype(F32)
        total = total.astype(BF16)
        for m in range(mp_size):
            r.y2_send[m] = total[m * strip : (m + 1) * strip]
        lane.out_strip.start_all()
        grad_out = mul(r.attended[...], flat(r.da_rows), ROWS_ROWS).astype(BF16)
        for c in range(chips):
            for k in range(2):
                first = (2 * c + k) * out_rows
                r.go_send[c, k] = grad_out[first : first + out_rows]

        def first_block(block):
            total = jnp.zeros((length, slab), F32)
            for p in range(pieces):
                for c in range(3):
                    total = total + mul(
                        r.dq_all[p, block, :, c * piece : (c + 1) * piece],
                        r.wq[c, :, p * piece : (p + 1) * piece],
                        COLS_COLS,
                    )
            total = total.astype(BF16)
            for m in range(mp_size):
                r.df_send[block, m] = total[m * strip : (m + 1) * strip]

        def first_send(block, others):
            for j in others:
                to = block * mp_size + lax.rem(mp + j, mp_size)
                lane.d_first.start(lax.rem(to + cross.size - cross_me, cross.size))

        first_block(chip)
        first_send(chip, range(1, mp_size))
        for step in range(1, chips):
            for p in range(pieces):
                lane.d_joint[p].take(step)
            first_block(lane.d_joint[0].source(step))
            first_send(lane.d_joint[0].source(step), range(mp_size))
        lane.g_out.start_all()

        def joint_grad(c, columns, target):
            for p in range(pieces):
                target[c, :, p * piece : (p + 1) * piece] = mul(
                    flat(r.a_all, columns),
                    r.dq_all[p, :, :, c * piece : (c + 1) * piece].reshape(tokens, piece),
                    ROWS_ROWS,
                ).astype(target.dtype)

        for c in range(3):
            joint_grad(c, other, r.gj_send)
        lane.g_joint.start_all()
        for c in range(3):
            joint_grad(c, mine, r.own_joint)
        lane.out_strip.take_all()
        total = r.hid[...] + r.y2_send[mp].astype(F32)
        for step in range(1, mp_size):
            total = total + r.y2_recv[lane.out_strip.source(step)].astype(F32)
        r.y_mine[...] = total.astype(BF16)
        lane.out_rows.start_all()
        r.layer_output[here, :] = r.y_mine[...]

        lane.d_first.take_all()
        r.df_recv[chip, mp] = r.df_send[chip, mp]
        d_normed = gathered(r.df_send, r.df_recv)
        back, gain_one, shift_one = norm_back(d_normed, r.x[here, :].astype(F32), norm_row(0))
        grad = r.dh[...] + back
        r.ig_mine[...] = grad.astype(BF16)
        lane.in_rows.start_all()
        r.input_grad[here, :] = grad
        for c in range(chips):
            columns = slice(c * slab, (c + 1) * slab)
            for index, row in enumerate((gain_one, shift_one, gain_two, shift_two)):
                r.gn_send[c, index : index + 1, :] = row[:, columns]
            r.gn_send[c, 4:8, :] = jnp.zeros((4, slab), F32)
        lane.g_norms.start_all()
        r.gn_recv[cross_me] = r.gn_send[chip]

        def square(own, distant):
            whole = own + distant.astype(F32)
            return jnp.sum(whole * whole, axis=0, keepdims=True)

        def folded(row):
            return sum(row[:, i : i + 128] for i in range(0, row.shape[1], 128))

        lane.g_contract.take_all()
        squares = folded(square(r.own_contract[...], r.far_contract[...]))
        lane.g_expand.take_all()
        for c in range(chips):
            squares = squares + folded(
                square(r.own_expand[:, c * units : (c + 1) * units], r.far_expand[c])
            )
        lane.g_joint.take_all()
        for c in range(3):
            squares = squares + folded(square(r.own_joint[c], r.far_joint[c]))

        lane.g_out.take_all()
        for k in range(2):
            total = r.go_send[chip, k].astype(F32)
            for step in range(1, chips):
                total = total + r.go_recv[lane.g_out.source(step), k].astype(F32)

            @pl.when(core == k)
            def _():
                r.own_out[...] = total

            r.go_pair[k] = total.astype(BF16)
        lane.g_out_pair.start_all()

        lane.g_norms.take_all()
        summed = r.gn_recv[0]
        for index in range(1, chips * mp_size):
            summed = summed + r.gn_recv[index]
        low, high = summed[:, :shard], summed[:, shard:]
        first = core == 0
        r.gn_pair[...] = jnp.where(first, high, low)
        lane.g_norms_pair.start_all()
        lane.g_out_pair.take_all()
        squares = squares + folded(square(r.own_out[...], r.far_out[...]))
        lane.g_norms_pair.take_all()
        own_norms = jnp.where(first, low, high) + r.gn_far[...]
        r.own_norms[...] = own_norms
        own_norms = jnp.sum(own_norms * own_norms, axis=0, keepdims=True) * (1.0 / mp_size)
        squares = squares + folded(own_norms)
        r.sq_mine[...] = jnp.broadcast_to(jnp.sum(squares), (8, 128))
        lane.squares.start_all()
        r.sq_recv[cross_me] = r.sq_mine[...]

        def place(rows_lane, rows, output):
            rows_lane.take_all()
            for step in range(1, mp_size):
                source = rows_lane.source(step)
                output[part(source, strip), :] = rows[source].astype(output.dtype)

        place(lane.out_rows, r.y_rows, r.layer_output)
        place(lane.in_rows, r.ig_rows, r.input_grad)
        lane.squares.take_all()
        total = r.sq_recv[0]
        for index in range(1, chips * mp_size):
            total = total + r.sq_recv[index]
        r.sq_pair[...] = total
        lane.squares_pair.start_all()
        lane.squares_pair.take_all()
        r.square_sum[...] = total + r.sq_far[...]
        for entry in every_lane:
            entry.sent_all()
        for step in range(1, chips):
            passing(step, False).wait_send()

    vmem = pl.BlockSpec(memory_space=pltpu.VMEM)
    any_space = pl.BlockSpec(memory_space=pl.ANY)
    sem_shapes = [pltpu.SemaphoreType.DMA((4,))]
    for name, kind in LANES.items():
        count = 2 * pieces if name in PIECED else 2
        sem_shapes += [pltpu.SemaphoreType.DMA((vars(groups)[kind].size,))] * count
    sem_shapes += [pltpu.SemaphoreType.DMA((chips,))] * 2
    results = pl.pallas_call(
        kernel,
        out_shape=list(outs.values()),
        in_specs=[vmem] * 3 + [any_space] * 4 + [vmem],
        out_specs=[vmem] * len(outs),
        scratch_shapes=[pltpu.VMEM(*entry) for entry in scratch.values()] + sem_shapes,
        compiler_params=pltpu.CompilerParams(
            collective_id=30, has_side_effects=True, vmem_limit_bytes=VMEM_LIMIT
        ),
    )(x, segments, cotangent, joint_w, out_w, expand_w, contract_w, norms)
    return SimpleNamespace(**dict(zip(outs, results)))


VMEM_LIMIT = 60 * 2**20


def local(dp_size, mp_size, *arrays):
    params, firsts, seconds = arrays[3:8], arrays[8:13], arrays[13:18]
    r = layer(dp_size, mp_size, arrays[:8])
    shard, hidden = params[2].shape
    far_expand = jnp.swapaxes(r.far_expand, 0, 1).reshape(shard, hidden)
    grads = (
        r.own_joint + r.far_joint.astype(F32),
        r.own_out + r.far_out.astype(F32),
        r.own_expand + far_expand.astype(F32),
        r.own_contract + r.far_contract.astype(F32),
        r.own_norms[:4],
    )
    gradient_norm = jnp.sqrt(r.square_sum[0, 0])
    clip_factor = jnp.minimum(1.0, MAX_NORM / (gradient_norm + CLIP_EPSILON))
    updates = [
        adam_update(params[k], grads[k], firsts[k], seconds[k], LEARN_RATES[k], clip_factor)
        for k in range(5)
    ]
    copies = [entry[2].astype(BF16) for entry in updates]
    return (
        r.layer_output,
        r.input_grad,
        *grads,
        *[entry[0] for entry in updates],
        *[entry[1] for entry in updates],
        *[entry[2] for entry in updates],
        *copies,
        gradient_norm,
    )


def solution(mesh):
    rows = P("dp", None)
    sets = (
        P(None, "dp", "mp"),
        P(("mp", "dp"), None),
        P("dp", "mp"),
        P(("mp", "dp"), None),
        P(None, "dp"),
    )
    form = local if mesh.shape["dp"] <= 8 else local_steps
    return jax.shard_map(
        functools.partial(form, mesh.shape["dp"], mesh.shape["mp"]),
        mesh=mesh,
        in_specs=(rows, rows, rows) + sets * 3,
        out_specs=(rows, rows) + sets * 5 + (P(),),
        check_vma=False,
    )
```

```python
import functools
import math
from types import SimpleNamespace

import jax
import jax.numpy as jnp
from jax import lax
from jax.experimental import pallas as pl
from jax.experimental.pallas import tpu as pltpu
from jax.sharding import PartitionSpec as P

HEAD_DIM = 128
ADAM_STEP = 5
MAX_NORM = 8192


BETA_ONE = 0.9
BETA_TWO = 0.95
ADAM_EPSILON = 1e-08
WEIGHT_DECAY = 0.1
NORM_EPSILON = 1e-05
CLIP_EPSILON = 1e-06
LEARN_RATES = (0.01, 0.08, 0.012, 0.02, 0.3)
MASKED_SCORE = -1e30
SCALE = 1.0 / math.sqrt(HEAD_DIM)
F32 = jnp.float32
BF16 = jnp.bfloat16
ROWS_COLS = (((1,), (0,)), ((), ()))
COLS_COLS = (((1,), (1,)), ((), ()))
ROWS_ROWS = (((0,), (0,)), ((), ()))


def mul(left, right, dims=ROWS_COLS):
    return lax.dot_general(left, right, dims, preferred_element_type=F32)


def layer_norm(values, gain_row, shift_row):
    row_mean = jnp.mean(values, axis=-1, keepdims=True)
    centered = values - row_mean
    spread = jnp.mean(centered * centered, axis=-1, keepdims=True)
    return centered * lax.rsqrt(spread + NORM_EPSILON) * gain_row + shift_row


def gelu_tanh(values):
    return jax.nn.gelu(values, approximate=True)


def adam_update(weight, grad, first, second, rate, clip_factor):
    clipped = grad * clip_factor
    new_first = BETA_ONE * first + (1.0 - BETA_ONE) * clipped
    new_second = BETA_TWO * second + (1.0 - BETA_TWO) * clipped * clipped
    first_hat = new_first / (1.0 - BETA_ONE**ADAM_STEP)
    second_hat = new_second / (1.0 - BETA_TWO**ADAM_STEP)
    new_weight = weight - rate * (
        first_hat / (jnp.sqrt(second_hat) + ADAM_EPSILON) + WEIGHT_DECAY * weight
    )
    return (new_first, new_second, new_weight)


PAIR, PLANE, COLUMN, CROSS, ROW, ALL = ("pair", "plane", "column", "cross", "row", "all")


class Group:
    def __init__(self, kind, dp_size, mp_size):
        self.kind = kind
        self.mp_size = mp_size
        chips = dp_size // 2
        self.size = {
            PAIR: 2,
            PLANE: chips,
            COLUMN: mp_size,
            CROSS: chips * mp_size,
            ROW: dp_size,
            ALL: dp_size * mp_size,
        }[kind]

    def me(self):
        dp, mp = lax.axis_index("dp"), lax.axis_index("mp")
        if self.kind == PAIR:
            return lax.rem(dp, 2)
        if self.kind == PLANE:
            return lax.div(dp, 2)
        if self.kind == COLUMN:
            return mp
        if self.kind == CROSS:
            return lax.div(dp, 2) * self.mp_size + mp
        if self.kind == ROW:
            return dp
        return dp * self.mp_size + mp

    def device(self, member):
        dp, mp = lax.axis_index("dp"), lax.axis_index("mp")
        core = lax.rem(dp, 2)
        if self.kind == PAIR:
            return (dp - core + member, mp)
        if self.kind == PLANE:
            return (member * 2 + core, mp)
        if self.kind == COLUMN:
            return (dp, member)
        if self.kind == CROSS:
            return (lax.div(member, self.mp_size) * 2 + core, lax.rem(member, self.mp_size))
        if self.kind == ROW:
            return (member, mp)
        return (lax.div(member, self.mp_size), lax.rem(member, self.mp_size))


def repeat(low, high, body):
    if high - low <= 8:
        for step in range(low, high):
            body(step)
    else:
        lax.fori_loop(low, high, lambda step, none: (body(step), none)[1], None)


def exchange(group, operands, results, moves, collective_id):
    count = len(operands)
    size = group.size
    lanes = len(moves)

    def kernel(*refs):
        ins, outs = refs[:count], refs[count : count + len(results)]
        send_sems, recv_sems, own_sems = refs[count + len(results) :]
        me = group.me()
        barrier = pltpu.get_barrier_semaphore()

        def greet(step):
            other = lax.rem(me + step, size)
            pl.semaphore_signal(
                barrier, inc=1, device_id=group.device(other), device_id_type=pl.DeviceIdType.MESH
            )

        repeat(1, size, greet)
        pl.semaphore_wait(barrier, size - 1)

        def remote(move, lane, step, sender, target, device):
            return pltpu.make_async_remote_copy(
                src_ref=move(ins, outs, me, target)[0],
                dst_ref=move(ins, outs, sender, me)[1],
                send_sem=send_sems.at[lane, step],
                recv_sem=recv_sems.at[lane, step],
                device_id=group.device(device),
                device_id_type=pl.DeviceIdType.MESH,
            )

        def launch(step):
            other = lax.rem(me + step, size)
            for lane, move in enumerate(moves):
                remote(move, lane, step, me, other, other).start()

        repeat(1, size, launch)
        own = []
        for lane, move in enumerate(moves):
            source, target = move(ins, outs, me, me)
            own.append(pltpu.make_async_copy(source, target, own_sems.at[lane]))
            own[-1].start()

        def finish(step):
            other = lax.rem(me + step, size)
            sender = lax.rem(me + size - step, size)
            for lane, move in enumerate(moves):
                remote(move, lane, step, sender, other, other).wait()

        repeat(1, size, finish)
        for copy in own:
            copy.wait()

    any_space = pl.BlockSpec(memory_space=pl.ANY)
    return pl.pallas_call(
        kernel,
        out_shape=results,
        in_specs=[any_space] * count,
        out_specs=[any_space] * len(results),
        scratch_shapes=[
            pltpu.SemaphoreType.DMA((lanes, size)),
            pltpu.SemaphoreType.DMA((lanes, size)),
            pltpu.SemaphoreType.DMA((lanes,)),
        ],
        compiler_params=pltpu.CompilerParams(collective_id=collective_id, has_side_effects=True),
    )(*operands)


def shape(dims, dtype=BF16):
    return jax.ShapeDtypeStruct(dims, dtype)


def part(index, width):
    return pl.ds(pl.multiple_of(index * width, width), width)


def allowed_pairs(seg_row, seg_col, length):
    places = lax.broadcasted_iota(jnp.int32, (length, length), 0)
    keys = lax.broadcasted_iota(jnp.int32, (length, length), 1)
    return (seg_col[...] == seg_row[...]) & (keys <= places)


def probabilities(query, key, allowed):
    scores = jnp.where(allowed, mul(query, key, COLS_COLS) * SCALE, MASKED_SCORE)
    exponent = jnp.exp(scores - jnp.max(scores, axis=-1, keepdims=True))
    return exponent / jnp.sum(exponent, axis=-1, keepdims=True)


def attend_kernel(width, joint, seg_row, seg_col, out_weight, attended, partial):
    allowed = allowed_pairs(seg_row, seg_col, joint.shape[0])
    for start in range(0, width, HEAD_DIM):
        head = pl.ds(start, HEAD_DIM)
        query, key, value = (joint[:, pl.ds(c * width + start, HEAD_DIM)] for c in range(3))
        prob = probabilities(query, key, allowed)
        attended[:, head] = mul(prob.astype(BF16), value).astype(BF16)
    partial[...] = mul(attended[...], out_weight[...]).astype(BF16)


def attend_back_kernel(
    width, joint, seg_row, seg_col, out_weight, attended, branch, d_joint, grad_out, d_attended
):
    allowed = allowed_pairs(seg_row, seg_col, joint.shape[0])
    d_attended[...] = mul(branch[...], out_weight[...], COLS_COLS).astype(BF16)
    for start in range(0, width, HEAD_DIM):
        query, key, value = (joint[:, pl.ds(c * width + start, HEAD_DIM)] for c in range(3))
        d_out = d_attended[:, pl.ds(start, HEAD_DIM)]
        prob = probabilities(query, key, allowed)
        d_joint[:, pl.ds(2 * width + start, HEAD_DIM)] = mul(
            prob.astype(BF16), d_out, ROWS_ROWS
        ).astype(BF16)
        d_prob = mul(d_out, value, COLS_COLS)
        row_delta = jnp.sum(d_prob * prob, axis=-1, keepdims=True)
        d_raw = (prob * (d_prob - row_delta) * SCALE).astype(BF16)
        d_joint[:, pl.ds(start, HEAD_DIM)] = mul(d_raw, key).astype(BF16)
        d_joint[:, pl.ds(width + start, HEAD_DIM)] = mul(d_raw, query, ROWS_ROWS).astype(BF16)
    grad_out[...] = mul(attended[...], branch[...], ROWS_ROWS).astype(BF16)


def local_steps(
    dp_size,
    mp_size,
    inputs,
    segment_ids,
    cotangent,
    query_key_value,
    attention_out,
    expand_weight,
    contract_weight,
    norm_params,
    first_query_key_value,
    first_attention_out,
    first_expand_weight,
    first_contract_weight,
    first_norm_params,
    second_query_key_value,
    second_attention_out,
    second_expand_weight,
    second_contract_weight,
    second_norm_params,
):
    params = (query_key_value, attention_out, expand_weight, contract_weight, norm_params)
    firsts = (
        first_query_key_value,
        first_attention_out,
        first_expand_weight,
        first_contract_weight,
        first_norm_params,
    )
    seconds = (
        second_query_key_value,
        second_attention_out,
        second_expand_weight,
        second_contract_weight,
        second_norm_params,
    )
    chips = dp_size // 2
    pair, plane, column, cross, row, everyone = (
        Group(kind, dp_size, mp_size)
        for kind in (PAIR, PLANE, COLUMN, CROSS, ROW, ALL)
    )
    dp, mp = lax.axis_index("dp"), lax.axis_index("mp")
    core = dp % 2
    length, model = inputs.shape
    width = query_key_value.shape[2]
    shard = query_key_value.shape[1]
    slab = 2 * shard
    hidden_units = expand_weight.shape[1]
    own_units = contract_weight.shape[0]
    units = 2 * own_units
    out_rows = attention_out.shape[0]
    strip = length // mp_size
    tokens = chips * length

    (norm_all,) = exchange(
        row,
        [norm_params],
        [shape((dp_size, 4, shard), F32)],
        [lambda ins, outs, me, other: (ins[0], outs[0].at[me])],
        0,
    )
    norm_weights = jnp.swapaxes(norm_all.astype(BF16).astype(F32), 0, 1).reshape(4, model)

    def shared(column_block):
        def move(ins, outs, me, other):
            return (ins[0].at[column_block], outs[0].at[part(me, shard), pl.ds(column_block * width, width)])

        return move

    joint_weight, expand_pair, contract_pair = exchange(
        pair,
        [query_key_value.astype(BF16), expand_weight.astype(BF16), contract_weight.astype(BF16)],
        [shape((slab, 3 * width)), shape((slab, hidden_units)), shape((units, model))],
        [
            shared(0),
            shared(1),
            shared(2),
            lambda ins, outs, me, other: (ins[1], outs[1].at[part(me, shard), :]),
            lambda ins, outs, me, other: (ins[2], outs[2].at[part(me, own_units), :]),
        ],
        1,
    )
    (output_all,) = exchange(
        row,
        [attention_out.astype(BF16)],
        [shape((dp_size * out_rows, model))],
        [lambda ins, outs, me, other: (ins[0], outs[0].at[part(me, out_rows), :])],
        2,
    )
    (grad_rows,) = exchange(
        plane,
        [cotangent],
        [shape((chips, length, model))],
        [lambda ins, outs, me, other: (ins[0], outs[0].at[me])],
        3,
    )
    grad_rows = grad_rows.reshape(tokens, model)

    values = inputs.astype(F32)
    normed = layer_norm(values, norm_weights[0], norm_weights[1]).astype(BF16)
    (normed_low,) = exchange(
        plane,
        [normed],
        [shape((chips, length, slab))],
        [lambda ins, outs, me, other: (ins[0].at[:, part(other, slab)], outs[0].at[me])],
        4,
    )
    normed_low = normed_low.reshape(tokens, slab)
    joint_part = mul(normed_low, joint_weight).astype(BF16).reshape(chips, length, 3 * width)
    (joint_parts,) = exchange(
        plane,
        [joint_part],
        [shape((chips, length, 3 * width))],
        [lambda ins, outs, me, other: (ins[0].at[other], outs[0].at[me])],
        5,
    )
    joint = jnp.sum(joint_parts.astype(F32), axis=0).astype(BF16)

    seg_row = segment_ids
    seg_col = segment_ids.reshape(length, 1)
    attended, branch_part = pl.pallas_call(
        functools.partial(attend_kernel, width),
        out_shape=[shape((length, width)), shape((length, model))],
        compiler_params=pltpu.CompilerParams(vmem_limit_bytes=48 * 2**20),
    )(joint, seg_row, seg_col, output_all)

    (branch_parts,) = exchange(
        column,
        [branch_part.reshape(mp_size, strip, model)],
        [shape((mp_size, strip, model))],
        [lambda ins, outs, me, other: (ins[0].at[other], outs[0].at[me])],
        6,
    )
    own_values = lax.dynamic_slice_in_dim(values, mp * strip, strip, 0)
    hidden = own_values + jnp.sum(branch_parts.astype(F32), axis=0)
    normed_two, pull_two = jax.vjp(layer_norm, hidden, norm_weights[2], norm_weights[3])
    (second_low,) = exchange(
        cross,
        [normed_two.astype(BF16)],
        [shape((chips * mp_size, strip, slab))],
        [
            lambda ins, outs, me, other: (
                ins[0].at[:, part(lax.div(other, mp_size), slab)],
                outs[0].at[me],
            )
        ],
        7,
    )
    second_low = second_low.reshape(tokens, slab)
    pre_part = mul(second_low, expand_pair).astype(BF16)
    (pre_parts,) = exchange(
        plane,
        [pre_part],
        [shape((chips, tokens, units))],
        [lambda ins, outs, me, other: (ins[0].at[:, part(other, units)], outs[0].at[me])],
        8,
    )
    pre_gelu = jnp.sum(pre_parts.astype(F32), axis=0)
    activated, pull_gelu = jax.vjp(gelu_tanh, pre_gelu)
    activated_low = activated.astype(BF16)
    d_activated = mul(grad_rows, contract_pair, COLS_COLS)
    (d_pre,) = pull_gelu(d_activated)
    (d_pre_all,) = exchange(
        plane,
        [d_pre.astype(BF16)],
        [shape((tokens, hidden_units))],
        [lambda ins, outs, me, other: (ins[0], outs[0].at[:, part(me, units)])],
        9,
    )

    def scatter_rows(partial, collective_id):
        (blocks,) = exchange(
            cross,
            [partial.reshape(chips * mp_size, strip, slab)],
            [shape((chips * mp_size, strip, slab))],
            [lambda ins, outs, me, other: (ins[0].at[other], outs[0].at[me])],
            collective_id,
        )
        total = jnp.sum(blocks.reshape(chips, mp_size, strip, slab).astype(F32), axis=1)
        return jnp.swapaxes(total, 0, 1).reshape(strip, model)

    d_normed_two = scatter_rows(mul(d_pre_all, expand_pair, COLS_COLS).astype(BF16), 10)
    d_hidden_norm, gain_two, shift_two = pull_two(d_normed_two)
    own_grad = lax.dynamic_slice_in_dim(cotangent, mp * strip, strip, 0).astype(F32)
    d_hidden = own_grad + d_hidden_norm

    def gather_rows(block, collective_id):
        (rows,) = exchange(
            column,
            [block],
            [shape((mp_size, strip, model))],
            [lambda ins, outs, me, other: (ins[0], outs[0].at[me])],
            collective_id,
        )
        return rows.reshape(length, model)

    branch_grad = gather_rows(d_hidden.astype(BF16), 11)
    d_joint, grad_output_part, _ = pl.pallas_call(
        functools.partial(attend_back_kernel, width),
        out_shape=[shape((length, 3 * width)), shape((width, model)), shape((length, width))],
        compiler_params=pltpu.CompilerParams(vmem_limit_bytes=48 * 2**20),
    )(joint, seg_row, seg_col, output_all, attended, branch_grad)
    (d_joint_all,) = exchange(
        plane,
        [d_joint],
        [shape((chips, length, 3 * width))],
        [lambda ins, outs, me, other: (ins[0], outs[0].at[me])],
        12,
    )
    d_joint_all = d_joint_all.reshape(tokens, 3 * width)
    d_normed_one = scatter_rows(mul(d_joint_all, joint_weight, COLS_COLS).astype(BF16), 13)
    _, pull_one = jax.vjp(layer_norm, own_values, norm_weights[0], norm_weights[1])
    d_values_norm, gain_one, shift_one = pull_one(d_normed_one)
    input_grad = gather_rows((d_hidden + d_values_norm).astype(BF16), 14).astype(F32)

    out_part = mul(activated_low, contract_pair).astype(BF16).reshape(chips, length, model)
    (out_parts,) = exchange(
        plane,
        [out_part],
        [shape((chips, length, model))],
        [lambda ins, outs, me, other: (ins[0].at[other], outs[0].at[me])],
        15,
    )
    out_rows_sum = jnp.sum(out_parts.astype(F32), axis=0).astype(BF16)
    (out_strips,) = exchange(
        column,
        [out_rows_sum.reshape(mp_size, strip, model)],
        [shape((mp_size, strip, model))],
        [lambda ins, outs, me, other: (ins[0].at[other], outs[0].at[me])],
        16,
    )
    layer_output = gather_rows(
        (hidden + jnp.sum(out_strips.astype(F32), axis=0)).astype(BF16), 17
    )

    (grad_output_parts,) = exchange(
        row,
        [grad_output_part.reshape(dp_size, out_rows, model)],
        [shape((dp_size, out_rows, model))],
        [lambda ins, outs, me, other: (ins[0].at[other], outs[0].at[me])],
        18,
    )
    reduced_output = jnp.sum(grad_output_parts.astype(F32), axis=0)
    own_joint, other_joint = [], []
    grad_joint = mul(normed_low, d_joint_all, ROWS_ROWS)
    grad_expand = mul(second_low, d_pre_all, ROWS_ROWS)
    grad_contract = mul(activated_low, grad_rows, ROWS_ROWS)

    def halves(array, index):
        return lax.dynamic_slice_in_dim(array, index * (array.shape[0] // 2), array.shape[0] // 2, 0)

    pieces = (grad_joint, grad_expand, grad_contract)
    sent = [halves(entry, 1 - core).astype(BF16) for entry in pieces]
    got = exchange_pair(pair, sent, 19)
    reduced_joint, reduced_expand, reduced_contract = (
        halves(entry, core) + other.astype(F32) for entry, other in zip(pieces, got)
    )
    reduced_joint = jnp.swapaxes(reduced_joint.reshape(shard, 3, width), 0, 1)

    zero_row = jnp.zeros((model,), F32)
    norm_rows = jnp.stack([gain_one, shift_one, gain_two, shift_two] + [zero_row] * 4)
    norm_rows = jnp.swapaxes(norm_rows.reshape(8, dp_size, shard), 0, 1)
    (norm_parts,) = exchange(
        everyone,
        [norm_rows],
        [shape((dp_size * mp_size, 8, shard), F32)],
        [
            lambda ins, outs, me, other: (
                ins[0].at[lax.div(other, mp_size)],
                outs[0].at[me],
            )
        ],
        20,
    )
    reduced_norms = jnp.sum(norm_parts, axis=0)[:4]

    grads = (reduced_joint, reduced_output, reduced_expand, reduced_contract, reduced_norms)
    squares = sum((jnp.sum(entry * entry) for entry in grads[:4])) + jnp.sum(
        reduced_norms * reduced_norms
    ) / mp_size
    (square_parts,) = exchange(
        everyone,
        [jnp.full((8, 128), squares, F32)],
        [shape((dp_size * mp_size, 8, 128), F32)],
        [lambda ins, outs, me, other: (ins[0], outs[0].at[me])],
        21,
    )
    gradient_norm = jnp.sqrt(jnp.sum(square_parts[:, 0, 0]))
    clip_factor = jnp.minimum(1.0, MAX_NORM / (gradient_norm + CLIP_EPSILON))
    updates = [
        adam_update(params[k], grads[k], firsts[k], seconds[k], LEARN_RATES[k], clip_factor)
        for k in range(5)
    ]
    copies = [entry[2].astype(BF16) for entry in updates]
    return (
        layer_output,
        input_grad,
        *grads,
        *[entry[0] for entry in updates],
        *[entry[1] for entry in updates],
        *[entry[2] for entry in updates],
        *copies,
        gradient_norm,
    )


def exchange_pair(pair, sent, collective_id):
    moves = [
        lambda ins, outs, me, other, lane=lane: (ins[lane], outs[lane]) for lane in range(len(sent))
    ]
    return swap(pair, sent, moves, collective_id)


def swap(pair, sent, moves, collective_id):
    count = len(sent)

    def kernel(*refs):
        ins, outs = refs[:count], refs[count : 2 * count]
        send_sems, recv_sems = refs[2 * count :]
        other = pair.device(1 - pair.me())
        barrier = pltpu.get_barrier_semaphore()
        pl.semaphore_signal(barrier, inc=1, device_id=other, device_id_type=pl.DeviceIdType.MESH)
        pl.semaphore_wait(barrier, 1)
        copies = [
            pltpu.make_async_remote_copy(
                src_ref=ins[lane],
                dst_ref=outs[lane],
                send_sem=send_sems.at[lane],
                recv_sem=recv_sems.at[lane],
                device_id=other,
                device_id_type=pl.DeviceIdType.MESH,
            )
            for lane in range(count)
        ]
        for copy in copies:
            copy.start()
        for copy in copies:
            copy.wait()

    any_space = pl.BlockSpec(memory_space=pl.ANY)
    return pl.pallas_call(
        kernel,
        out_shape=[shape(entry.shape, entry.dtype) for entry in sent],
        in_specs=[any_space] * count,
        out_specs=[any_space] * count,
        scratch_shapes=[pltpu.SemaphoreType.DMA((count,)), pltpu.SemaphoreType.DMA((count,))],
        compiler_params=pltpu.CompilerParams(collective_id=collective_id, has_side_effects=True),
    )(*sent)


class Lane:
    def __init__(self, group, me, sems, view):
        self.group, self.me, self.view = group, me, view
        self.send_sems, self.recv_sems = sems
        self.size = group.size

    def copy(self, step):
        to = lax.rem(self.me + step, self.size)
        return pltpu.make_async_remote_copy(
            src_ref=self.view(self.me, to)[0],
            dst_ref=self.view(self.me, to)[1],
            send_sem=self.send_sems.at[step],
            recv_sem=self.recv_sems.at[step],
            device_id=self.group.device(to),
            device_id_type=pl.DeviceIdType.MESH,
        )

    def start(self, step):
        self.copy(step).start()

    def start_all(self):
        repeat(1, self.size, self.start)

    def source(self, step):
        return lax.rem(self.me + self.size - step, self.size)

    def take(self, step):
        to = lax.rem(self.me + step, self.size)
        pltpu.make_async_remote_copy(
            src_ref=self.view(self.me, to)[0],
            dst_ref=self.view(self.source(step), self.me)[1],
            send_sem=self.send_sems.at[step],
            recv_sem=self.recv_sems.at[step],
            device_id=self.group.device(to),
            device_id_type=pl.DeviceIdType.MESH,
        ).wait_recv()

    def take_all(self):
        repeat(1, self.size, self.take)

    def sent(self, step):
        self.copy(step).wait_send()

    def sent_all(self):
        repeat(1, self.size, self.sent)


class Hop:
    def __init__(self, dp, mp):
        core, self.me = lax.rem(dp, 2), lax.div(dp, 2)
        x_next = self.me + 1 - 2 * lax.rem(self.me, 2)
        self.chips = (x_next, lax.rem(self.me + 2, 4))
        self.far = 3 - self.me
        self.devices = tuple((chip * 2 + core, mp) for chip in self.chips)

    def copy(self, source, target, sems, index, way):
        return pltpu.make_async_remote_copy(
            src_ref=source,
            dst_ref=target,
            send_sem=sems[0].at[index],
            recv_sem=sems[1].at[index],
            device_id=self.devices[way],
            device_id_type=pl.DeviceIdType.MESH,
        )


class PlaneGather:
    def __init__(self, hop, sems, own, block, half):
        self.hop, self.sems, self.own, self.block, self.half = hop, sems, own, block, half

    def first(self, way):
        return self.hop.copy(self.own, self.block(self.hop.me), self.sems, way, way)

    def second(self, way):
        piece = self.half(self.block(self.hop.chips[way]), way)
        return self.hop.copy(piece, piece, self.sems, 2 + way, 1 - way)

    def start(self):
        for way in range(2):
            self.first(way).start()

    def near(self, way):
        near = self.block(self.hop.chips[way])
        self.hop.copy(near, near, self.sems, way, way).wait_recv()

    def forward(self):
        for way in range(2):
            self.near(way)
            self.second(way).start()

    def finish(self):
        for way in range(2):
            piece = self.half(self.block(self.hop.far), way)
            self.hop.copy(piece, piece, self.sems, 2 + way, 1 - way).wait_recv()

    def sent_all(self):
        for way in range(2):
            self.first(way).wait_send()
            self.second(way).wait_send()


class PlaneReduce:
    def __init__(self, hop, sems, parts, inbox, middle):
        self.hop, self.sems = hop, sems
        self.parts, self.inbox, self.middle = parts, inbox, middle

    def copy(self, stage, way):
        hop = self.hop
        chip = (hop.far, hop.chips[way])[stage] if stage < 2 else None
        source = self.parts.at[chip, way] if stage < 2 else self.middle.at[way]
        along = way if stage < 2 else 1 - way
        return hop.copy(source, self.inbox.at[stage, way], self.sems, 2 * stage + way, along)

    def start(self, stage):
        for way in range(2):
            self.copy(stage, way).start()

    def forward(self):
        for way in range(2):
            self.copy(0, way).wait_recv()
            onward = self.hop.chips[1 - way]
            total = self.parts[onward, way].astype(F32) + self.inbox[0, way].astype(F32)
            self.middle[way] = total.astype(BF16)
            self.copy(2, way).start()

    def take(self, way):
        self.copy(1, way).wait_recv()
        self.copy(2, way).wait_recv()

    def total(self, way, rows=slice(None)):
        own = self.parts[self.hop.me, way, rows].astype(F32)
        near = self.inbox[1, way, rows].astype(F32)
        return own + near + self.inbox[2, way, rows].astype(F32)

    def sent_all(self):
        for stage in range(3):
            for way in range(2):
                self.copy(stage, way).wait_send()


def standardise(values):
    row_mean = jnp.mean(values, axis=-1, keepdims=True)
    centered = values - row_mean
    spread = jnp.mean(centered * centered, axis=-1, keepdims=True)
    return centered, lax.rsqrt(spread + NORM_EPSILON)


def norm_back(grad, values, gain_row):
    centered, inverse = standardise(values)
    unit = centered * inverse
    scaled = grad * gain_row
    inner = jnp.mean(scaled * unit, axis=-1, keepdims=True)
    back = inverse * (scaled - jnp.mean(scaled, axis=-1, keepdims=True) - unit * inner)
    gain_grad = jnp.sum(grad * unit, axis=0, keepdims=True)
    shift_grad = jnp.sum(grad, axis=0, keepdims=True)
    return back, gain_grad, shift_grad


ROOT = math.sqrt(2.0 / math.pi)
CUBE = 0.044715

LANES = dict(
    norms=ROW,
    normed=PLANE,
    joint_weight=PAIR,
    out_own=PAIR,
    expand=PAIR,
    contract=PAIR,
    branch=COLUMN,
    second=CROSS,
    g_contract=PAIR,
    d_second=CROSS,
    g_expand=PAIR,
    d_hidden=COLUMN,
    g_out_pair=PAIR,
    out_strip=COLUMN,
    d_first=CROSS,
    g_joint=PAIR,
    out_rows=COLUMN,
    in_rows=COLUMN,
    g_norms=CROSS,
    g_norms_pair=PAIR,
    squares=CROSS,
    squares_pair=PAIR,
)


def layer(dp_size, mp_size, operands):
    x, segments, cotangent, joint_w, out_w, expand_w, contract_w, norms = operands
    chips = dp_size // 2
    groups = SimpleNamespace(
        **{kind: Group(kind, dp_size, mp_size) for kind in (PAIR, PLANE, COLUMN, CROSS, ROW)}
    )
    length, model = x.shape
    width, shard = joint_w.shape[2], joint_w.shape[1]
    slab = 2 * shard
    hidden = expand_w.shape[1]
    own_units = contract_w.shape[0]
    units = 2 * own_units
    out_rows = out_w.shape[0]
    strip = length // mp_size
    tokens = chips * length
    wide = 3 * width
    pieces = max(1, width // (2 * HEAD_DIM))
    piece = width // pieces

    outs = dict(
        layer_output=shape((length, model)),
        input_grad=shape((length, model), F32),
        own_joint=shape((3, shard, width), F32),
        own_out=shape((out_rows, model), F32),
        own_expand=shape((shard, hidden), F32),
        own_contract=shape((own_units, model), F32),
        own_norms=shape((8, shard), F32),
        square_sum=shape((8, 128), F32),
        far_joint=shape((3, shard, width)),
        far_out=shape((out_rows, model)),
        far_expand=shape((shard, hidden)),
        far_contract=shape((own_units, model)),
    )
    scratch = dict(
        norm_all=((dp_size, 4, shard), F32),
        a_mine=((chips, length, slab), BF16),
        a_all=((chips, length, slab), BF16),
        wq=((3, slab, width), BF16),
        wo=((dp_size, out_rows, model), BF16),
        wu=((chips, slab, units), BF16),
        wd=((units, model), BF16),
        j_send=((pieces, chips, 2, length // 2, 3 * piece), BF16),
        j_recv=((pieces, 3, 2, length // 2, 3 * piece), BF16),
        j_mid=((pieces, 2, length // 2, 3 * piece), BF16),
        joint=((pieces, length, 3 * piece), BF16),
        dy_all=((chips, length, model), BF16),
        attended=((length, width), BF16),
        b_send=((mp_size, strip, model), BF16),
        b_recv=((mp_size, strip, model), BF16),
        hid=((strip, model), F32),
        c_mine=((chips, strip, slab), BF16),
        c_all=((chips, mp_size, strip, slab), BF16),
        u_send=((chips, 2, tokens // 2, units), BF16),
        u_recv=((3, 2, tokens // 2, units), BF16),
        u_mid=((2, tokens // 2, units), BF16),
        dz=((tokens, units), F32),
        z=((tokens, units), BF16),
        du_all=((chips, tokens, units), BF16),
        y_send=((chips, 2, length // 2, model), BF16),
        y_recv=((3, 2, length // 2, model), BF16),
        y_mid=((2, length // 2, model), BF16),
        gc_send=((own_units, model), BF16),
        dc_send=((chips, mp_size, strip, slab), BF16),
        dc_recv=((chips, mp_size, strip, slab), BF16),
        ge_send=((shard, hidden), BF16),
        dh=((strip, model), F32),
        da_mine=((strip, model), BF16),
        da_rows=((mp_size, strip, model), BF16),
        dq_mine=((pieces, length, 3 * piece), BF16),
        dq_all=((pieces, chips, length, 3 * piece), BF16),
        go_send=((chips, 2, out_rows, model), BF16),
        go_recv=((3, 2, out_rows, model), BF16),
        go_mid=((2, out_rows, model), BF16),
        go_pair=((2, out_rows, model), BF16),
        y2_send=((mp_size, strip, model), BF16),
        y2_recv=((mp_size, strip, model), BF16),
        y_mine=((strip, model), BF16),
        y_rows=((mp_size, strip, model), BF16),
        df_send=((chips, mp_size, strip, slab), BF16),
        df_recv=((chips, mp_size, strip, slab), BF16),
        gj_send=((3, shard, width), BF16),
        ig_mine=((strip, model), BF16),
        ig_rows=((mp_size, strip, model), BF16),
        gn_send=((chips, 8, slab), F32),
        gn_recv=((chips * mp_size, 8, slab), F32),
        gn_pair=((8, shard), F32),
        gn_far=((8, shard), F32),
        sq_mine=((8, 128), F32),
        sq_recv=((chips * mp_size, 8, 128), F32),
        sq_pair=((8, 128), F32),
        sq_far=((8, 128), F32),
    )
    in_names = dict(
        x=0, seg_row=1, cot=2, f_joint=3, f_out=4, f_expand=5, f_contract=6, norm_own=7
    )
    names = list(in_names) + list(outs) + list(scratch)

    def kernel(*refs):
        r = SimpleNamespace(**dict(zip(names, refs)))
        sems = refs[len(names) :]
        load_sems = sems[0]
        dp, mp = lax.axis_index("dp"), lax.axis_index("mp")
        core, chip = lax.rem(dp, 2), lax.div(dp, 2)
        mine, other = part(core, shard), part(1 - core, shard)
        cross_me = groups.cross.me()

        def flat(ref, columns=slice(None)):
            values = ref[(slice(None),) * (len(ref.shape) - 1) + (columns,)]
            return values.reshape(-1, values.shape[-1])

        views = dict(
            norms=lambda s, t: (r.norm_own, r.norm_all.at[s]),
            normed=lambda s, t: (r.a_mine.at[t], r.a_all.at[s]),
            joint_weight=lambda s, t: (
                r.wq.at[:, part(s, shard), :],
                r.wq.at[:, part(s, shard), :],
            ),
            out_own=lambda s, t: (r.wo.at[dp - core + s], r.wo.at[dp - core + s]),
            expand=lambda s, t: (
                r.wu.at[:, part(s, shard), :],
                r.wu.at[:, part(s, shard), :],
            ),
            contract=lambda s, t: (
                r.wd.at[part(s, own_units), :],
                r.wd.at[part(s, own_units), :],
            ),
            branch=lambda s, t: (r.b_send.at[t], r.b_recv.at[s]),
            second=lambda s, t: (
                r.c_mine.at[lax.div(t, mp_size)],
                r.c_all.at[lax.div(s, mp_size), lax.rem(s, mp_size)],
            ),
            g_contract=lambda s, t: (r.gc_send, r.far_contract),
            d_second=lambda s, t: (
                r.dc_send.at[lax.div(t, mp_size), lax.rem(t, mp_size)],
                r.dc_recv.at[lax.div(s, mp_size), lax.rem(s, mp_size)],
            ),
            g_expand=lambda s, t: (r.ge_send, r.far_expand),
            d_hidden=lambda s, t: (r.da_mine, r.da_rows.at[s]),
            g_out_pair=lambda s, t: (r.go_pair.at[t], r.far_out),
            out_strip=lambda s, t: (r.y2_send.at[t], r.y2_recv.at[s]),
            d_first=lambda s, t: (
                r.df_send.at[lax.div(t, mp_size), lax.rem(t, mp_size)],
                r.df_recv.at[lax.div(s, mp_size), lax.rem(s, mp_size)],
            ),
            g_joint=lambda s, t: (r.gj_send, r.far_joint),
            out_rows=lambda s, t: (r.y_mine, r.y_rows.at[s]),
            in_rows=lambda s, t: (r.ig_mine, r.ig_rows.at[s]),
            g_norms=lambda s, t: (r.gn_send.at[lax.div(t, mp_size)], r.gn_recv.at[s]),
            g_norms_pair=lambda s, t: (r.gn_pair, r.gn_far),
            squares=lambda s, t: (r.sq_mine, r.sq_recv.at[s]),
            squares_pair=lambda s, t: (r.sq_pair, r.sq_far),
        )
        lane = SimpleNamespace()
        every_lane = []
        used = iter(sems[1:])

        def pair_of():
            return (next(used), next(used))

        for name, kind in LANES.items():
            group = vars(groups)[kind]
            setattr(lane, name, Lane(group, group.me(), pair_of(), views[name]))
            every_lane.append(vars(lane)[name])
        hop = Hop(dp, mp)

        def gather(own, block, half):
            every_lane.append(PlaneGather(hop, pair_of(), own, block, half))
            return every_lane[-1]

        def reduce(parts, inbox, middle):
            every_lane.append(PlaneReduce(hop, pair_of(), parts, inbox, middle))
            return every_lane[-1]

        def row_half(ref, way):
            rows = ref.shape[0] // 2
            return ref.at[pl.ds(way * rows, rows), :]

        out_plane = gather(r.wo.at[dp], lambda c: r.wo.at[2 * c + core], row_half)
        cot_plane = gather(r.cot, lambda c: r.dy_all.at[c], row_half)
        d_pre = gather(r.du_all.at[chip], lambda c: r.du_all.at[c], row_half)
        d_joint = [
            gather(r.dq_mine.at[p], lambda c, p=p: r.dq_all.at[p, c], row_half)
            for p in range(pieces)
        ]
        joint = [reduce(r.j_send.at[p], r.j_recv.at[p], r.j_mid.at[p]) for p in range(pieces)]
        pre_sum = reduce(r.u_send, r.u_recv, r.u_mid)
        out_sum = reduce(r.y_send, r.y_recv, r.y_mid)
        g_out_sum = reduce(r.go_send, r.go_recv, r.go_mid)
        pass_sems = pair_of()

        def passing(index, to_me):
            source = (*hop.chips, hop.far)[index]
            block = r.wo.at[2 * source + (1 - core if to_me else core)]
            return pltpu.make_async_remote_copy(
                src_ref=block,
                dst_ref=block,
                send_sem=pass_sems[0].at[index],
                recv_sem=pass_sems[1].at[index],
                device_id=(dp + 1 - 2 * core, mp),
                device_id_type=pl.DeviceIdType.MESH,
            )

        loads = [
            pltpu.make_async_copy(source, target, load_sems.at[i])
            for i, (source, target) in enumerate(
                (
                    (r.f_joint, r.own_joint),
                    (r.f_out, r.own_out),
                    (r.f_expand, r.own_expand),
                    (r.f_contract, r.own_contract),
                )
            )
        ]
        for load in (loads[1], loads[0], loads[2], loads[3]):
            load.start()

        barrier = pltpu.get_barrier_semaphore()

        def greet(device):
            pl.semaphore_signal(
                barrier, inc=1, device_id=device, device_id_type=pl.DeviceIdType.MESH
            )

        cross = groups.cross
        repeat(1, cross.size, lambda s: greet(cross.device(lax.rem(cross_me + s, cross.size))))
        repeat(0, chips, lambda s: greet((s * 2 + 1 - core, mp)))

        r.norm_all[dp] = r.norm_own[...]
        loads[1].wait()
        r.wo[dp] = r.own_out[...].astype(BF16)
        values = r.x[...].astype(F32)
        centered, inverse = standardise(values)
        unit = centered * inverse
        loads[0].wait()
        for c in range(3):
            r.wq[c, mine, :] = r.own_joint[c].astype(BF16)
        ids = jnp.broadcast_to(r.seg_row[...].astype(F32), (length, length))
        places = lax.broadcasted_iota(jnp.int32, (length, length), 0)
        keys = lax.broadcasted_iota(jnp.int32, (length, length), 1)
        allowed = (ids == ids.T) & (keys <= places)
        pl.semaphore_wait(barrier, cross.size - 1 + chips)

        lane.norms.start_all()
        lane.joint_weight.start_all()
        out_plane.start()
        lane.out_own.start_all()
        lane.norms.take_all()

        def norm_row(index, block=None):
            blocks = range(dp_size) if block is None else (block,)
            rows = [r.norm_all[b, pl.ds(index, 1), :] for b in blocks]
            whole = rows[0] if len(rows) == 1 else jnp.concatenate(rows, axis=1)
            return whole.astype(BF16).astype(F32)

        for b in range(dp_size):
            columns = slice(b * shard, (b + 1) * shard)
            r.a_mine[b // 2, :, (b % 2) * shard : (b % 2 + 1) * shard] = (
                unit[:, columns] * norm_row(0, b) + norm_row(1, b)
            ).astype(BF16)
        lane.normed.start_all()
        r.a_all[chip] = r.a_mine[chip]

        lane.joint_weight.take_all()

        half_rows = length // 2

        def joint_part(p, block):
            rows = r.a_all[block]
            for c in range(3):
                columns = slice(c * piece, (c + 1) * piece)
                third = mul(rows, r.wq[c, :, p * piece : (p + 1) * piece]).astype(BF16)
                for way in range(2):
                    r.j_send[p, block, way, :, columns] = third[
                        way * half_rows : (way + 1) * half_rows
                    ]

        def chip_step(block):
            return lax.rem(chip + chips - block, chips)

        for p in range(pieces):
            for way in range(2):
                if p == 0:
                    lane.normed.take(chip_step(hop.chips[way]))
                joint_part(p, hop.chips[way])
            joint[p].start(1)
            if p == 0:
                lane.normed.take(chip_step(hop.far))
            joint_part(p, hop.far)
            joint[p].start(0)
            joint_part(p, chip)
        out_plane.forward()
        for index in range(2):
            passing(index, False).start()
        for p in range(pieces):
            joint[p].forward()

        loads[2].wait()
        for c in range(chips):
            r.wu[c, mine, :] = r.own_expand[:, c * units : (c + 1) * units].astype(BF16)
        lane.expand.start_all()
        loads[3].wait()
        r.wd[part(core, own_units), :] = r.own_contract[...].astype(BF16)
        lane.contract.start_all()
        def query_key_value(start):
            p, first = start // piece, start % piece
            return (
                r.joint[p, :, c * piece + first : c * piece + first + HEAD_DIM] for c in range(3)
            )

        for p in range(pieces):
            for way in range(2):
                joint[p].take(way)
                r.joint[p, way * half_rows : (way + 1) * half_rows, :] = (
                    joint[p].total(way).astype(BF16)
                )
            if p == pieces - 1:
                cot_plane.start()
            for start in range(p * piece, (p + 1) * piece, HEAD_DIM):
                query, key, value = query_key_value(start)
                prob = probabilities(query, key, allowed)
                r.attended[:, start : start + HEAD_DIM] = mul(prob.astype(BF16), value).astype(BF16)

        lane.out_own.take_all()
        out_plane.finish()
        passing(2, False).start()
        for index in range(3):
            passing(index, True).wait_recv()
        branch = mul(r.attended[...], flat(r.wo)).astype(BF16)
        for m in range(mp_size):
            r.b_send[m] = branch[m * strip : (m + 1) * strip]
        lane.branch.start_all()
        r.dy_all[chip] = r.cot[...]
        cot_plane.forward()
        lane.branch.take_all()
        here = part(mp, strip)
        total = r.x[here, :].astype(F32) + r.b_send[mp].astype(F32)
        for step in range(1, mp_size):
            total = total + r.b_recv[lane.branch.source(step)].astype(F32)
        r.hid[...] = total
        centered, inverse = standardise(total)
        for b in range(dp_size):
            columns = slice(b * shard, (b + 1) * shard)
            r.c_mine[b // 2, :, (b % 2) * shard : (b % 2 + 1) * shard] = (
                centered[:, columns] * inverse * norm_row(2, b) + norm_row(3, b)
            ).astype(BF16)
        lane.second.start_all()
        r.c_all[chip, mp] = r.c_mine[chip]
        lane.expand.take_all()
        lane.second.take_all()

        half_tokens = tokens // 2

        def pre_part(to):
            part_sum = mul(flat(r.c_all), r.wu[to]).astype(BF16)
            for way in range(2):
                r.u_send[to, way] = part_sum[way * half_tokens : (way + 1) * half_tokens]

        pre_part(hop.far)
        pre_sum.start(0)
        for way in range(2):
            pre_part(hop.chips[way])
        pre_sum.start(1)
        pre_part(chip)
        pre_sum.forward()
        lane.contract.take_all()
        cot_plane.finish()
        r.dz[...] = mul(flat(r.dy_all), r.wd[...], COLS_COLS)
        tile = 64

        for way in range(2):
            pre_sum.take(way)

            def gelu_tile(i, none, way=way):
                rows = part(i, tile)
                pre = pre_sum.total(way, rows)
                square = pre * pre
                curve = jnp.tanh(ROOT * pre * (1.0 + CUBE * square))
                half = 0.5 * (1.0 + curve)
                slope = half + 0.5 * pre * (1.0 - curve * curve) * (
                    ROOT * (1.0 + 3.0 * CUBE * square)
                )
                rows = part(i + way * (half_tokens // tile), tile)
                r.z[rows, :] = (pre * half).astype(BF16)
                r.du_all[chip, rows, :] = (r.dz[rows, :] * slope).astype(BF16)
                return none

            lax.fori_loop(0, half_tokens // tile, gelu_tile, None)
        d_pre.start()

        def out_part(c):
            rows = r.z[c * length : (c + 1) * length, :]
            part_sum = mul(rows, r.wd[...]).astype(BF16)
            for way in range(2):
                r.y_send[c, way] = part_sum[way * half_rows : (way + 1) * half_rows]

        out_part(0)
        out_part(1)
        total = mul(r.du_all[chip], r.wu[chip], COLS_COLS)
        d_pre.forward()
        out_part(2)
        out_part(3)
        r.gc_send[...] = mul(r.z[:, part(1 - core, own_units)], flat(r.dy_all), ROWS_ROWS).astype(BF16)
        lane.g_contract.start_all()

        for way in range(2):
            total = total + mul(r.du_all[hop.chips[way]], r.wu[hop.chips[way]], COLS_COLS)
        d_pre.finish()
        total = total + mul(r.du_all[hop.far], r.wu[hop.far], COLS_COLS)
        total = total.astype(BF16)
        for c in range(chips):
            for m in range(mp_size):
                first = c * length + m * strip
                r.dc_send[c, m] = total[first : first + strip]
        lane.d_second.start_all()
        out_sum.start(0)
        out_sum.start(1)
        r.own_contract[...] = mul(r.z[:, part(core, own_units)], flat(r.dy_all), ROWS_ROWS)
        for c in range(chips):
            r.ge_send[:, c * units : (c + 1) * units] = mul(flat(r.c_all, other), r.du_all[c], ROWS_ROWS).astype(BF16)
        lane.g_expand.start_all()
        for c in range(chips):
            r.own_expand[:, c * units : (c + 1) * units] = mul(
                flat(r.c_all, mine), r.du_all[c], ROWS_ROWS
            )
        out_sum.forward()
        lane.d_second.take_all()

        def gathered(send, recv):
            blocks = []
            for c in range(chips):
                block = jnp.zeros((strip, slab), F32)
                for m in range(mp_size):
                    block = block + recv[c, m].astype(F32)
                blocks.append(block)
            return jnp.concatenate(blocks, axis=1)

        r.dc_recv[chip, mp] = r.dc_send[chip, mp]
        d_normed = gathered(r.dc_send, r.dc_recv)
        back, gain_two, shift_two = norm_back(d_normed, r.hid[...], norm_row(2))
        d_hidden = r.cot[here, :].astype(F32) + back
        r.dh[...] = d_hidden
        r.da_mine[...] = d_hidden.astype(BF16)
        lane.d_hidden.start_all()
        r.da_rows[mp] = r.da_mine[...]
        lane.d_hidden.take_all()
        grad_out = mul(r.attended[...], flat(r.da_rows), ROWS_ROWS).astype(BF16)
        for c in range(chips):
            for k in range(2):
                first = (2 * c + k) * out_rows
                r.go_send[c, k] = grad_out[first : first + out_rows]
        g_out_sum.start(0)
        g_out_sum.start(1)
        d_attended = mul(flat(r.da_rows), flat(r.wo), COLS_COLS).astype(BF16)
        for p in range(pieces):
            for start in range(p * piece, (p + 1) * piece, HEAD_DIM):
                query, key, value = query_key_value(start)
                d_out = d_attended[:, start : start + HEAD_DIM]
                prob = probabilities(query, key, allowed)
                d_prob = mul(d_out, value, COLS_COLS)
                row_delta = jnp.sum(d_prob * prob, axis=-1, keepdims=True)
                d_raw = (prob * (d_prob - row_delta) * SCALE).astype(BF16)
                thirds = (
                    mul(d_raw, key),
                    mul(d_raw, query, ROWS_ROWS),
                    mul(prob.astype(BF16), d_out, ROWS_ROWS),
                )
                for c in range(3):
                    first = c * piece + start % piece
                    r.dq_mine[p, :, first : first + HEAD_DIM] = thirds[c].astype(BF16)
            d_joint[p].start()
            r.dq_all[p, chip] = r.dq_mine[p]

        g_out_sum.forward()
        for way in range(2):
            out_sum.take(way)
            total = out_sum.total(way).astype(BF16)
            for m in range(mp_size // 2):
                r.y2_send[way * (mp_size // 2) + m] = total[m * strip : (m + 1) * strip]
        lane.out_strip.start_all()
        for p in range(pieces):
            d_joint[p].forward()

        def first_block(block):
            total = jnp.zeros((length, slab), F32)
            for p in range(pieces):
                for c in range(3):
                    total = total + mul(
                        r.dq_all[p, block, :, c * piece : (c + 1) * piece],
                        r.wq[c, :, p * piece : (p + 1) * piece],
                        COLS_COLS,
                    )
            total = total.astype(BF16)
            for m in range(mp_size):
                r.df_send[block, m] = total[m * strip : (m + 1) * strip]

        def first_send(block, others):
            for j in others:
                to = block * mp_size + lax.rem(mp + j, mp_size)
                lane.d_first.start(lax.rem(to + cross.size - cross_me, cross.size))

        first_block(chip)
        first_send(chip, range(1, mp_size))
        for way in range(2):
            first_block(hop.chips[way])
            first_send(hop.chips[way], range(mp_size))
        for p in range(pieces):
            d_joint[p].finish()
        first_block(hop.far)
        first_send(hop.far, range(mp_size))

        def joint_grad(c, columns, target):
            for p in range(pieces):
                target[c, :, p * piece : (p + 1) * piece] = mul(
                    flat(r.a_all, columns),
                    r.dq_all[p, :, :, c * piece : (c + 1) * piece].reshape(tokens, piece),
                    ROWS_ROWS,
                ).astype(target.dtype)

        for c in range(3):
            joint_grad(c, other, r.gj_send)
        lane.g_joint.start_all()
        for c in range(3):
            joint_grad(c, mine, r.own_joint)
        lane.out_strip.take_all()
        total = r.hid[...] + r.y2_send[mp].astype(F32)
        for step in range(1, mp_size):
            total = total + r.y2_recv[lane.out_strip.source(step)].astype(F32)
        r.y_mine[...] = total.astype(BF16)
        lane.out_rows.start_all()
        r.layer_output[here, :] = r.y_mine[...]

        lane.d_first.take_all()
        r.df_recv[chip, mp] = r.df_send[chip, mp]
        d_normed = gathered(r.df_send, r.df_recv)
        back, gain_one, shift_one = norm_back(d_normed, r.x[here, :].astype(F32), norm_row(0))
        grad = r.dh[...] + back
        r.ig_mine[...] = grad.astype(BF16)
        lane.in_rows.start_all()
        r.input_grad[here, :] = grad
        for c in range(chips):
            columns = slice(c * slab, (c + 1) * slab)
            for index, row in enumerate((gain_one, shift_one, gain_two, shift_two)):
                r.gn_send[c, index : index + 1, :] = row[:, columns]
            r.gn_send[c, 4:8, :] = jnp.zeros((4, slab), F32)
        lane.g_norms.start_all()
        r.gn_recv[cross_me] = r.gn_send[chip]

        def square(own, distant):
            whole = own + distant.astype(F32)
            return jnp.sum(whole * whole, axis=0, keepdims=True)

        def folded(row):
            return sum(row[:, i : i + 128] for i in range(0, row.shape[1], 128))

        lane.g_contract.take_all()
        squares = folded(square(r.own_contract[...], r.far_contract[...]))
        lane.g_expand.take_all()
        squares = squares + folded(square(r.own_expand[...], r.far_expand[...]))
        lane.g_joint.take_all()
        for c in range(3):
            squares = squares + folded(square(r.own_joint[c], r.far_joint[c]))

        for k in range(2):
            g_out_sum.take(k)
            total = g_out_sum.total(k)

            @pl.when(core == k)
            def _():
                r.own_out[...] = total

            r.go_pair[k] = total.astype(BF16)
        lane.g_out_pair.start_all()

        lane.g_norms.take_all()
        summed = r.gn_recv[0]
        for index in range(1, chips * mp_size):
            summed = summed + r.gn_recv[index]
        low, high = summed[:, :shard], summed[:, shard:]
        first = core == 0
        r.gn_pair[...] = jnp.where(first, high, low)
        lane.g_norms_pair.start_all()
        lane.g_out_pair.take_all()
        squares = squares + folded(square(r.own_out[...], r.far_out[...]))
        lane.g_norms_pair.take_all()
        own_norms = jnp.where(first, low, high) + r.gn_far[...]
        r.own_norms[...] = own_norms
        own_norms = jnp.sum(own_norms * own_norms, axis=0, keepdims=True) * (1.0 / mp_size)
        squares = squares + folded(own_norms)
        r.sq_mine[...] = jnp.broadcast_to(jnp.sum(squares), (8, 128))
        lane.squares.start_all()
        r.sq_recv[cross_me] = r.sq_mine[...]

        def place(rows_lane, rows, output):
            rows_lane.take_all()
            for step in range(1, mp_size):
                source = rows_lane.source(step)
                output[part(source, strip), :] = rows[source].astype(output.dtype)

        place(lane.out_rows, r.y_rows, r.layer_output)
        place(lane.in_rows, r.ig_rows, r.input_grad)
        lane.squares.take_all()
        total = r.sq_recv[0]
        for index in range(1, chips * mp_size):
            total = total + r.sq_recv[index]
        r.sq_pair[...] = total
        lane.squares_pair.start_all()
        lane.squares_pair.take_all()
        r.square_sum[...] = total + r.sq_far[...]
        for entry in every_lane:
            entry.sent_all()
        for index in range(3):
            passing(index, False).wait_send()

    vmem = pl.BlockSpec(memory_space=pltpu.VMEM)
    any_space = pl.BlockSpec(memory_space=pl.ANY)
    sem_shapes = [pltpu.SemaphoreType.DMA((4,))]
    for kind in LANES.values():
        sem_shapes += [pltpu.SemaphoreType.DMA((vars(groups)[kind].size,))] * 2
    sem_shapes += [pltpu.SemaphoreType.DMA((4,))] * 2 * (3 + pieces)
    sem_shapes += [pltpu.SemaphoreType.DMA((6,))] * 2 * (3 + pieces)
    sem_shapes += [pltpu.SemaphoreType.DMA((3,))] * 2
    results = pl.pallas_call(
        kernel,
        out_shape=list(outs.values()),
        in_specs=[vmem] * 3 + [any_space] * 4 + [vmem],
        out_specs=[vmem] * len(outs),
        scratch_shapes=[pltpu.VMEM(*entry) for entry in scratch.values()] + sem_shapes,
        compiler_params=pltpu.CompilerParams(
            collective_id=30, has_side_effects=True, vmem_limit_bytes=VMEM_LIMIT
        ),
    )(x, segments, cotangent, joint_w, out_w, expand_w, contract_w, norms)
    return SimpleNamespace(**dict(zip(outs, results)))


VMEM_LIMIT = 60 * 2**20


def local(dp_size, mp_size, *arrays):
    params, firsts, seconds = arrays[3:8], arrays[8:13], arrays[13:18]
    r = layer(dp_size, mp_size, arrays[:8])
    grads = (
        r.own_joint + r.far_joint.astype(F32),
        r.own_out + r.far_out.astype(F32),
        r.own_expand + r.far_expand.astype(F32),
        r.own_contract + r.far_contract.astype(F32),
        r.own_norms[:4],
    )
    gradient_norm = jnp.sqrt(r.square_sum[0, 0])
    clip_factor = jnp.minimum(1.0, MAX_NORM / (gradient_norm + CLIP_EPSILON))
    updates = [
        adam_update(params[k], grads[k], firsts[k], seconds[k], LEARN_RATES[k], clip_factor)
        for k in range(5)
    ]
    copies = [entry[2].astype(BF16) for entry in updates]
    return (
        r.layer_output,
        r.input_grad,
        *grads,
        *[entry[0] for entry in updates],
        *[entry[1] for entry in updates],
        *[entry[2] for entry in updates],
        *copies,
        gradient_norm,
    )


def solution(mesh):
    rows = P("dp", None)
    sets = (
        P(None, "dp", "mp"),
        P(("mp", "dp"), None),
        P("dp", "mp"),
        P(("mp", "dp"), None),
        P(None, "dp"),
    )
    form = local if mesh.shape["dp"] == 8 else local_steps
    return jax.shard_map(
        functools.partial(form, mesh.shape["dp"], mesh.shape["mp"]),
        mesh=mesh,
        in_specs=(rows, rows, rows) + sets * 3,
        out_specs=(rows, rows) + sets * 5 + (P(),),
        check_vma=False,
    )
```

```python
import functools
import math
from types import SimpleNamespace

import jax
import jax.numpy as jnp
from jax import lax
from jax.experimental import pallas as pl
from jax.experimental.pallas import tpu as pltpu
from jax.sharding import PartitionSpec as P

HEAD_DIM = 128
ADAM_STEP = 5
MAX_NORM = 8192


BETA_ONE = 0.9
BETA_TWO = 0.95
ADAM_EPSILON = 1e-08
WEIGHT_DECAY = 0.1
NORM_EPSILON = 1e-05
CLIP_EPSILON = 1e-06
LEARN_RATES = (0.01, 0.08, 0.012, 0.02, 0.3)
MASKED_SCORE = -1e30
SCALE = 1.0 / math.sqrt(HEAD_DIM)
F32 = jnp.float32
BF16 = jnp.bfloat16
ROWS_COLS = (((1,), (0,)), ((), ()))
COLS_COLS = (((1,), (1,)), ((), ()))
ROWS_ROWS = (((0,), (0,)), ((), ()))


def mul(left, right, dims=ROWS_COLS):
    return lax.dot_general(left, right, dims, preferred_element_type=F32)


def layer_norm(values, gain_row, shift_row):
    row_mean = jnp.mean(values, axis=-1, keepdims=True)
    centered = values - row_mean
    spread = jnp.mean(centered * centered, axis=-1, keepdims=True)
    return centered * lax.rsqrt(spread + NORM_EPSILON) * gain_row + shift_row


def gelu_tanh(values):
    return jax.nn.gelu(values, approximate=True)


def adam_update(weight, grad, first, second, rate, clip_factor):
    clipped = grad * clip_factor
    new_first = BETA_ONE * first + (1.0 - BETA_ONE) * clipped
    new_second = BETA_TWO * second + (1.0 - BETA_TWO) * clipped * clipped
    first_hat = new_first / (1.0 - BETA_ONE**ADAM_STEP)
    second_hat = new_second / (1.0 - BETA_TWO**ADAM_STEP)
    new_weight = weight - rate * (
        first_hat / (jnp.sqrt(second_hat) + ADAM_EPSILON) + WEIGHT_DECAY * weight
    )
    return (new_first, new_second, new_weight)


PAIR, PLANE, COLUMN, CROSS, ROW, ALL = ("pair", "plane", "column", "cross", "row", "all")


class Group:
    def __init__(self, kind, dp_size, mp_size):
        self.kind = kind
        self.mp_size = mp_size
        chips = dp_size // 2
        self.size = {
            PAIR: 2,
            PLANE: chips,
            COLUMN: mp_size,
            CROSS: chips * mp_size,
            ROW: dp_size,
            ALL: dp_size * mp_size,
        }[kind]

    def me(self):
        dp, mp = lax.axis_index("dp"), lax.axis_index("mp")
        if self.kind == PAIR:
            return lax.rem(dp, 2)
        if self.kind == PLANE:
            return lax.div(dp, 2)
        if self.kind == COLUMN:
            return mp
        if self.kind == CROSS:
            return lax.div(dp, 2) * self.mp_size + mp
        if self.kind == ROW:
            return dp
        return dp * self.mp_size + mp

    def device(self, member):
        dp, mp = lax.axis_index("dp"), lax.axis_index("mp")
        core = lax.rem(dp, 2)
        if self.kind == PAIR:
            return (dp - core + member, mp)
        if self.kind == PLANE:
            return (member * 2 + core, mp)
        if self.kind == COLUMN:
            return (dp, member)
        if self.kind == CROSS:
            return (lax.div(member, self.mp_size) * 2 + core, lax.rem(member, self.mp_size))
        if self.kind == ROW:
            return (member, mp)
        return (lax.div(member, self.mp_size), lax.rem(member, self.mp_size))


def repeat(low, high, body):
    if high - low <= 8:
        for step in range(low, high):
            body(step)
    else:
        lax.fori_loop(low, high, lambda step, none: (body(step), none)[1], None)


def exchange(group, operands, results, moves, collective_id):
    count = len(operands)
    size = group.size
    lanes = len(moves)

    def kernel(*refs):
        ins, outs = refs[:count], refs[count : count + len(results)]
        send_sems, recv_sems, own_sems = refs[count + len(results) :]
        me = group.me()
        barrier = pltpu.get_barrier_semaphore()

        def greet(step):
            other = lax.rem(me + step, size)
            pl.semaphore_signal(
                barrier, inc=1, device_id=group.device(other), device_id_type=pl.DeviceIdType.MESH
            )

        repeat(1, size, greet)
        pl.semaphore_wait(barrier, size - 1)

        def remote(move, lane, step, sender, target, device):
            return pltpu.make_async_remote_copy(
                src_ref=move(ins, outs, me, target)[0],
                dst_ref=move(ins, outs, sender, me)[1],
                send_sem=send_sems.at[lane, step],
                recv_sem=recv_sems.at[lane, step],
                device_id=group.device(device),
                device_id_type=pl.DeviceIdType.MESH,
            )

        def launch(step):
            other = lax.rem(me + step, size)
            for lane, move in enumerate(moves):
                remote(move, lane, step, me, other, other).start()

        repeat(1, size, launch)
        own = []
        for lane, move in enumerate(moves):
            source, target = move(ins, outs, me, me)
            own.append(pltpu.make_async_copy(source, target, own_sems.at[lane]))
            own[-1].start()

        def finish(step):
            other = lax.rem(me + step, size)
            sender = lax.rem(me + size - step, size)
            for lane, move in enumerate(moves):
                remote(move, lane, step, sender, other, other).wait()

        repeat(1, size, finish)
        for copy in own:
            copy.wait()

    any_space = pl.BlockSpec(memory_space=pl.ANY)
    return pl.pallas_call(
        kernel,
        out_shape=results,
        in_specs=[any_space] * count,
        out_specs=[any_space] * len(results),
        scratch_shapes=[
            pltpu.SemaphoreType.DMA((lanes, size)),
            pltpu.SemaphoreType.DMA((lanes, size)),
            pltpu.SemaphoreType.DMA((lanes,)),
        ],
        compiler_params=pltpu.CompilerParams(collective_id=collective_id, has_side_effects=True),
    )(*operands)


def shape(dims, dtype=BF16):
    return jax.ShapeDtypeStruct(dims, dtype)


def part(index, width):
    return pl.ds(pl.multiple_of(index * width, width), width)


def allowed_pairs(seg_row, seg_col, length):
    places = lax.broadcasted_iota(jnp.int32, (length, length), 0)
    keys = lax.broadcasted_iota(jnp.int32, (length, length), 1)
    return (seg_col[...] == seg_row[...]) & (keys <= places)


def probabilities(query, key, allowed):
    scores = jnp.where(allowed, mul(query, key, COLS_COLS) * SCALE, MASKED_SCORE)
    exponent = jnp.exp(scores - jnp.max(scores, axis=-1, keepdims=True))
    return exponent / jnp.sum(exponent, axis=-1, keepdims=True)


def attend_kernel(width, joint, seg_row, seg_col, out_weight, attended, partial):
    allowed = allowed_pairs(seg_row, seg_col, joint.shape[0])
    for start in range(0, width, HEAD_DIM):
        head = pl.ds(start, HEAD_DIM)
        query, key, value = (joint[:, pl.ds(c * width + start, HEAD_DIM)] for c in range(3))
        prob = probabilities(query, key, allowed)
        attended[:, head] = mul(prob.astype(BF16), value).astype(BF16)
    partial[...] = mul(attended[...], out_weight[...]).astype(BF16)


def attend_back_kernel(
    width, joint, seg_row, seg_col, out_weight, attended, branch, d_joint, grad_out, d_attended
):
    allowed = allowed_pairs(seg_row, seg_col, joint.shape[0])
    d_attended[...] = mul(branch[...], out_weight[...], COLS_COLS).astype(BF16)
    for start in range(0, width, HEAD_DIM):
        query, key, value = (joint[:, pl.ds(c * width + start, HEAD_DIM)] for c in range(3))
        d_out = d_attended[:, pl.ds(start, HEAD_DIM)]
        prob = probabilities(query, key, allowed)
        d_joint[:, pl.ds(2 * width + start, HEAD_DIM)] = mul(
            prob.astype(BF16), d_out, ROWS_ROWS
        ).astype(BF16)
        d_prob = mul(d_out, value, COLS_COLS)
        row_delta = jnp.sum(d_prob * prob, axis=-1, keepdims=True)
        d_raw = (prob * (d_prob - row_delta) * SCALE).astype(BF16)
        d_joint[:, pl.ds(start, HEAD_DIM)] = mul(d_raw, key).astype(BF16)
        d_joint[:, pl.ds(width + start, HEAD_DIM)] = mul(d_raw, query, ROWS_ROWS).astype(BF16)
    grad_out[...] = mul(attended[...], branch[...], ROWS_ROWS).astype(BF16)


def local_steps(
    dp_size,
    mp_size,
    inputs,
    segment_ids,
    cotangent,
    query_key_value,
    attention_out,
    expand_weight,
    contract_weight,
    norm_params,
    first_query_key_value,
    first_attention_out,
    first_expand_weight,
    first_contract_weight,
    first_norm_params,
    second_query_key_value,
    second_attention_out,
    second_expand_weight,
    second_contract_weight,
    second_norm_params,
):
    params = (query_key_value, attention_out, expand_weight, contract_weight, norm_params)
    firsts = (
        first_query_key_value,
        first_attention_out,
        first_expand_weight,
        first_contract_weight,
        first_norm_params,
    )
    seconds = (
        second_query_key_value,
        second_attention_out,
        second_expand_weight,
        second_contract_weight,
        second_norm_params,
    )
    chips = dp_size // 2
    pair, plane, column, cross, row, everyone = (
        Group(kind, dp_size, mp_size)
        for kind in (PAIR, PLANE, COLUMN, CROSS, ROW, ALL)
    )
    dp, mp = lax.axis_index("dp"), lax.axis_index("mp")
    core = dp % 2
    length, model = inputs.shape
    width = query_key_value.shape[2]
    shard = query_key_value.shape[1]
    slab = 2 * shard
    hidden_units = expand_weight.shape[1]
    own_units = contract_weight.shape[0]
    units = 2 * own_units
    out_rows = attention_out.shape[0]
    strip = length // mp_size
    tokens = chips * length

    (norm_all,) = exchange(
        row,
        [norm_params],
        [shape((dp_size, 4, shard), F32)],
        [lambda ins, outs, me, other: (ins[0], outs[0].at[me])],
        0,
    )
    norm_weights = jnp.swapaxes(norm_all.astype(BF16).astype(F32), 0, 1).reshape(4, model)

    def shared(column_block):
        def move(ins, outs, me, other):
            return (ins[0].at[column_block], outs[0].at[part(me, shard), pl.ds(column_block * width, width)])

        return move

    joint_weight, expand_pair, contract_pair = exchange(
        pair,
        [query_key_value.astype(BF16), expand_weight.astype(BF16), contract_weight.astype(BF16)],
        [shape((slab, 3 * width)), shape((slab, hidden_units)), shape((units, model))],
        [
            shared(0),
            shared(1),
            shared(2),
            lambda ins, outs, me, other: (ins[1], outs[1].at[part(me, shard), :]),
            lambda ins, outs, me, other: (ins[2], outs[2].at[part(me, own_units), :]),
        ],
        1,
    )
    (output_all,) = exchange(
        row,
        [attention_out.astype(BF16)],
        [shape((dp_size * out_rows, model))],
        [lambda ins, outs, me, other: (ins[0], outs[0].at[part(me, out_rows), :])],
        2,
    )
    (grad_rows,) = exchange(
        plane,
        [cotangent],
        [shape((chips, length, model))],
        [lambda ins, outs, me, other: (ins[0], outs[0].at[me])],
        3,
    )
    grad_rows = grad_rows.reshape(tokens, model)

    values = inputs.astype(F32)
    normed = layer_norm(values, norm_weights[0], norm_weights[1]).astype(BF16)
    (normed_low,) = exchange(
        plane,
        [normed],
        [shape((chips, length, slab))],
        [lambda ins, outs, me, other: (ins[0].at[:, part(other, slab)], outs[0].at[me])],
        4,
    )
    normed_low = normed_low.reshape(tokens, slab)
    joint_part = mul(normed_low, joint_weight).astype(BF16).reshape(chips, length, 3 * width)
    (joint_parts,) = exchange(
        plane,
        [joint_part],
        [shape((chips, length, 3 * width))],
        [lambda ins, outs, me, other: (ins[0].at[other], outs[0].at[me])],
        5,
    )
    joint = jnp.sum(joint_parts.astype(F32), axis=0).astype(BF16)

    seg_row = segment_ids
    seg_col = segment_ids.reshape(length, 1)
    attended, branch_part = pl.pallas_call(
        functools.partial(attend_kernel, width),
        out_shape=[shape((length, width)), shape((length, model))],
        compiler_params=pltpu.CompilerParams(vmem_limit_bytes=48 * 2**20),
    )(joint, seg_row, seg_col, output_all)

    (branch_parts,) = exchange(
        column,
        [branch_part.reshape(mp_size, strip, model)],
        [shape((mp_size, strip, model))],
        [lambda ins, outs, me, other: (ins[0].at[other], outs[0].at[me])],
        6,
    )
    own_values = lax.dynamic_slice_in_dim(values, mp * strip, strip, 0)
    hidden = own_values + jnp.sum(branch_parts.astype(F32), axis=0)
    normed_two, pull_two = jax.vjp(layer_norm, hidden, norm_weights[2], norm_weights[3])
    (second_low,) = exchange(
        cross,
        [normed_two.astype(BF16)],
        [shape((chips * mp_size, strip, slab))],
        [
            lambda ins, outs, me, other: (
                ins[0].at[:, part(lax.div(other, mp_size), slab)],
                outs[0].at[me],
            )
        ],
        7,
    )
    second_low = second_low.reshape(tokens, slab)
    pre_part = mul(second_low, expand_pair).astype(BF16)
    (pre_parts,) = exchange(
        plane,
        [pre_part],
        [shape((chips, tokens, units))],
        [lambda ins, outs, me, other: (ins[0].at[:, part(other, units)], outs[0].at[me])],
        8,
    )
    pre_gelu = jnp.sum(pre_parts.astype(F32), axis=0)
    activated, pull_gelu = jax.vjp(gelu_tanh, pre_gelu)
    activated_low = activated.astype(BF16)
    d_activated = mul(grad_rows, contract_pair, COLS_COLS)
    (d_pre,) = pull_gelu(d_activated)
    (d_pre_all,) = exchange(
        plane,
        [d_pre.astype(BF16)],
        [shape((tokens, hidden_units))],
        [lambda ins, outs, me, other: (ins[0], outs[0].at[:, part(me, units)])],
        9,
    )

    def scatter_rows(partial, collective_id):
        (blocks,) = exchange(
            cross,
            [partial.reshape(chips * mp_size, strip, slab)],
            [shape((chips * mp_size, strip, slab))],
            [lambda ins, outs, me, other: (ins[0].at[other], outs[0].at[me])],
            collective_id,
        )
        total = jnp.sum(blocks.reshape(chips, mp_size, strip, slab).astype(F32), axis=1)
        return jnp.swapaxes(total, 0, 1).reshape(strip, model)

    d_normed_two = scatter_rows(mul(d_pre_all, expand_pair, COLS_COLS).astype(BF16), 10)
    d_hidden_norm, gain_two, shift_two = pull_two(d_normed_two)
    own_grad = lax.dynamic_slice_in_dim(cotangent, mp * strip, strip, 0).astype(F32)
    d_hidden = own_grad + d_hidden_norm

    def gather_rows(block, collective_id):
        (rows,) = exchange(
            column,
            [block],
            [shape((mp_size, strip, model))],
            [lambda ins, outs, me, other: (ins[0], outs[0].at[me])],
            collective_id,
        )
        return rows.reshape(length, model)

    branch_grad = gather_rows(d_hidden.astype(BF16), 11)
    d_joint, grad_output_part, _ = pl.pallas_call(
        functools.partial(attend_back_kernel, width),
        out_shape=[shape((length, 3 * width)), shape((width, model)), shape((length, width))],
        compiler_params=pltpu.CompilerParams(vmem_limit_bytes=48 * 2**20),
    )(joint, seg_row, seg_col, output_all, attended, branch_grad)
    (d_joint_all,) = exchange(
        plane,
        [d_joint],
        [shape((chips, length, 3 * width))],
        [lambda ins, outs, me, other: (ins[0], outs[0].at[me])],
        12,
    )
    d_joint_all = d_joint_all.reshape(tokens, 3 * width)
    d_normed_one = scatter_rows(mul(d_joint_all, joint_weight, COLS_COLS).astype(BF16), 13)
    _, pull_one = jax.vjp(layer_norm, own_values, norm_weights[0], norm_weights[1])
    d_values_norm, gain_one, shift_one = pull_one(d_normed_one)
    input_grad = gather_rows((d_hidden + d_values_norm).astype(BF16), 14).astype(F32)

    out_part = mul(activated_low, contract_pair).astype(BF16).reshape(chips, length, model)
    (out_parts,) = exchange(
        plane,
        [out_part],
        [shape((chips, length, model))],
        [lambda ins, outs, me, other: (ins[0].at[other], outs[0].at[me])],
        15,
    )
    out_rows_sum = jnp.sum(out_parts.astype(F32), axis=0).astype(BF16)
    (out_strips,) = exchange(
        column,
        [out_rows_sum.reshape(mp_size, strip, model)],
        [shape((mp_size, strip, model))],
        [lambda ins, outs, me, other: (ins[0].at[other], outs[0].at[me])],
        16,
    )
    layer_output = gather_rows(
        (hidden + jnp.sum(out_strips.astype(F32), axis=0)).astype(BF16), 17
    )

    (grad_output_parts,) = exchange(
        row,
        [grad_output_part.reshape(dp_size, out_rows, model)],
        [shape((dp_size, out_rows, model))],
        [lambda ins, outs, me, other: (ins[0].at[other], outs[0].at[me])],
        18,
    )
    reduced_output = jnp.sum(grad_output_parts.astype(F32), axis=0)
    own_joint, other_joint = [], []
    grad_joint = mul(normed_low, d_joint_all, ROWS_ROWS)
    grad_expand = mul(second_low, d_pre_all, ROWS_ROWS)
    grad_contract = mul(activated_low, grad_rows, ROWS_ROWS)

    def halves(array, index):
        return lax.dynamic_slice_in_dim(array, index * (array.shape[0] // 2), array.shape[0] // 2, 0)

    pieces = (grad_joint, grad_expand, grad_contract)
    sent = [halves(entry, 1 - core).astype(BF16) for entry in pieces]
    got = exchange_pair(pair, sent, 19)
    reduced_joint, reduced_expand, reduced_contract = (
        halves(entry, core) + other.astype(F32) for entry, other in zip(pieces, got)
    )
    reduced_joint = jnp.swapaxes(reduced_joint.reshape(shard, 3, width), 0, 1)

    zero_row = jnp.zeros((model,), F32)
    norm_rows = jnp.stack([gain_one, shift_one, gain_two, shift_two] + [zero_row] * 4)
    norm_rows = jnp.swapaxes(norm_rows.reshape(8, dp_size, shard), 0, 1)
    (norm_parts,) = exchange(
        everyone,
        [norm_rows],
        [shape((dp_size * mp_size, 8, shard), F32)],
        [
            lambda ins, outs, me, other: (
                ins[0].at[lax.div(other, mp_size)],
                outs[0].at[me],
            )
        ],
        20,
    )
    reduced_norms = jnp.sum(norm_parts, axis=0)[:4]

    grads = (reduced_joint, reduced_output, reduced_expand, reduced_contract, reduced_norms)
    squares = sum((jnp.sum(entry * entry) for entry in grads[:4])) + jnp.sum(
        reduced_norms * reduced_norms
    ) / mp_size
    (square_parts,) = exchange(
        everyone,
        [jnp.full((8, 128), squares, F32)],
        [shape((dp_size * mp_size, 8, 128), F32)],
        [lambda ins, outs, me, other: (ins[0], outs[0].at[me])],
        21,
    )
    gradient_norm = jnp.sqrt(jnp.sum(square_parts[:, 0, 0]))
    clip_factor = jnp.minimum(1.0, MAX_NORM / (gradient_norm + CLIP_EPSILON))
    updates = [
        adam_update(params[k], grads[k], firsts[k], seconds[k], LEARN_RATES[k], clip_factor)
        for k in range(5)
    ]
    copies = [entry[2].astype(BF16) for entry in updates]
    return (
        layer_output,
        input_grad,
        *grads,
        *[entry[0] for entry in updates],
        *[entry[1] for entry in updates],
        *[entry[2] for entry in updates],
        *copies,
        gradient_norm,
    )


def exchange_pair(pair, sent, collective_id):
    moves = [
        lambda ins, outs, me, other, lane=lane: (ins[lane], outs[lane]) for lane in range(len(sent))
    ]
    return swap(pair, sent, moves, collective_id)


def swap(pair, sent, moves, collective_id):
    count = len(sent)

    def kernel(*refs):
        ins, outs = refs[:count], refs[count : 2 * count]
        send_sems, recv_sems = refs[2 * count :]
        other = pair.device(1 - pair.me())
        barrier = pltpu.get_barrier_semaphore()
        pl.semaphore_signal(barrier, inc=1, device_id=other, device_id_type=pl.DeviceIdType.MESH)
        pl.semaphore_wait(barrier, 1)
        copies = [
            pltpu.make_async_remote_copy(
                src_ref=ins[lane],
                dst_ref=outs[lane],
                send_sem=send_sems.at[lane],
                recv_sem=recv_sems.at[lane],
                device_id=other,
                device_id_type=pl.DeviceIdType.MESH,
            )
            for lane in range(count)
        ]
        for copy in copies:
            copy.start()
        for copy in copies:
            copy.wait()

    any_space = pl.BlockSpec(memory_space=pl.ANY)
    return pl.pallas_call(
        kernel,
        out_shape=[shape(entry.shape, entry.dtype) for entry in sent],
        in_specs=[any_space] * count,
        out_specs=[any_space] * count,
        scratch_shapes=[pltpu.SemaphoreType.DMA((count,)), pltpu.SemaphoreType.DMA((count,))],
        compiler_params=pltpu.CompilerParams(collective_id=collective_id, has_side_effects=True),
    )(*sent)


class Lane:
    def __init__(self, group, me, sems, view):
        self.group, self.me, self.view = group, me, view
        self.send_sems, self.recv_sems = sems
        self.size = group.size

    def copy(self, step):
        to = lax.rem(self.me + step, self.size)
        return pltpu.make_async_remote_copy(
            src_ref=self.view(self.me, to)[0],
            dst_ref=self.view(self.me, to)[1],
            send_sem=self.send_sems.at[step],
            recv_sem=self.recv_sems.at[step],
            device_id=self.group.device(to),
            device_id_type=pl.DeviceIdType.MESH,
        )

    def start(self, step):
        self.copy(step).start()

    def start_all(self):
        repeat(1, self.size, self.start)

    def source(self, step):
        return lax.rem(self.me + self.size - step, self.size)

    def take(self, step):
        to = lax.rem(self.me + step, self.size)
        pltpu.make_async_remote_copy(
            src_ref=self.view(self.me, to)[0],
            dst_ref=self.view(self.source(step), self.me)[1],
            send_sem=self.send_sems.at[step],
            recv_sem=self.recv_sems.at[step],
            device_id=self.group.device(to),
            device_id_type=pl.DeviceIdType.MESH,
        ).wait_recv()

    def take_all(self):
        repeat(1, self.size, self.take)

    def sent(self, step):
        self.copy(step).wait_send()

    def sent_all(self):
        repeat(1, self.size, self.sent)


class Hop:
    def __init__(self, dp, mp):
        core, self.me = lax.rem(dp, 2), lax.div(dp, 2)
        x_next = self.me + 1 - 2 * lax.rem(self.me, 2)
        self.chips = (x_next, lax.rem(self.me + 2, 4))
        self.far = 3 - self.me
        self.devices = tuple((chip * 2 + core, mp) for chip in self.chips)

    def copy(self, source, target, sems, index, way):
        return pltpu.make_async_remote_copy(
            src_ref=source,
            dst_ref=target,
            send_sem=sems[0].at[index],
            recv_sem=sems[1].at[index],
            device_id=self.devices[way],
            device_id_type=pl.DeviceIdType.MESH,
        )


class PlaneGather:
    def __init__(self, hop, sems, own, block, half):
        self.hop, self.sems, self.own, self.block, self.half = hop, sems, own, block, half

    def first(self, way):
        return self.hop.copy(self.own, self.block(self.hop.me), self.sems, way, way)

    def second(self, way):
        piece = self.half(self.block(self.hop.chips[way]), way)
        return self.hop.copy(piece, piece, self.sems, 2 + way, 1 - way)

    def start(self):
        for way in range(2):
            self.first(way).start()

    def near(self, way):
        near = self.block(self.hop.chips[way])
        self.hop.copy(near, near, self.sems, way, way).wait_recv()

    def forward(self):
        for way in range(2):
            self.near(way)
            self.second(way).start()

    def finish(self):
        for way in range(2):
            piece = self.half(self.block(self.hop.far), way)
            self.hop.copy(piece, piece, self.sems, 2 + way, 1 - way).wait_recv()

    def sent_all(self):
        for way in range(2):
            self.first(way).wait_send()
            self.second(way).wait_send()


class PlaneReduce:
    def __init__(self, hop, sems, parts, inbox, middle):
        self.hop, self.sems = hop, sems
        self.parts, self.inbox, self.middle = parts, inbox, middle

    def copy(self, stage, way):
        hop = self.hop
        chip = (hop.far, hop.chips[way])[stage] if stage < 2 else None
        source = self.parts.at[chip, way] if stage < 2 else self.middle.at[way]
        along = way if stage < 2 else 1 - way
        return hop.copy(source, self.inbox.at[stage, way], self.sems, 2 * stage + way, along)

    def start(self, stage):
        for way in range(2):
            self.copy(stage, way).start()

    def forward(self):
        for way in range(2):
            self.copy(0, way).wait_recv()
            onward = self.hop.chips[1 - way]
            total = self.parts[onward, way].astype(F32) + self.inbox[0, way].astype(F32)
            self.middle[way] = total.astype(BF16)
            self.copy(2, way).start()

    def take(self, way):
        self.copy(1, way).wait_recv()
        self.copy(2, way).wait_recv()

    def total(self, way, rows=slice(None)):
        own = self.parts[self.hop.me, way, rows].astype(F32)
        near = self.inbox[1, way, rows].astype(F32)
        return own + near + self.inbox[2, way, rows].astype(F32)

    def sent_all(self):
        for stage in range(3):
            for way in range(2):
                self.copy(stage, way).wait_send()


def standardise(values):
    row_mean = jnp.mean(values, axis=-1, keepdims=True)
    centered = values - row_mean
    spread = jnp.mean(centered * centered, axis=-1, keepdims=True)
    return centered, lax.rsqrt(spread + NORM_EPSILON)


def norm_back(grad, values, gain_row):
    centered, inverse = standardise(values)
    unit = centered * inverse
    scaled = grad * gain_row
    inner = jnp.mean(scaled * unit, axis=-1, keepdims=True)
    back = inverse * (scaled - jnp.mean(scaled, axis=-1, keepdims=True) - unit * inner)
    gain_grad = jnp.sum(grad * unit, axis=0, keepdims=True)
    shift_grad = jnp.sum(grad, axis=0, keepdims=True)
    return back, gain_grad, shift_grad


ROOT = math.sqrt(2.0 / math.pi)
CUBE = 0.044715

LANES = dict(
    norms=ROW,
    normed=PLANE,
    joint_weight=PAIR,
    out_own=PAIR,
    expand=PAIR,
    contract=PAIR,
    branch=COLUMN,
    second=CROSS,
    g_contract=PAIR,
    d_second=CROSS,
    g_expand=PAIR,
    d_hidden=COLUMN,
    g_out_pair=PAIR,
    out_strip=COLUMN,
    d_first=CROSS,
    g_joint=PAIR,
    out_rows=COLUMN,
    in_rows=COLUMN,
    g_norms=CROSS,
    g_norms_pair=PAIR,
    squares=CROSS,
    squares_pair=PAIR,
)

HALVED = dict(branch=2, second=2, d_second=2, d_hidden=2)


def layer(dp_size, mp_size, operands):
    x, segments, cotangent, joint_w, out_w, expand_w, contract_w, norms = operands
    chips = dp_size // 2
    groups = SimpleNamespace(
        **{kind: Group(kind, dp_size, mp_size) for kind in (PAIR, PLANE, COLUMN, CROSS, ROW)}
    )
    length, model = x.shape
    width, shard = joint_w.shape[2], joint_w.shape[1]
    slab = 2 * shard
    hidden = expand_w.shape[1]
    own_units = contract_w.shape[0]
    units = 2 * own_units
    out_rows = out_w.shape[0]
    strip = length // mp_size
    tokens = chips * length
    half_strip = strip // 2
    half_rows = length // 2
    half_tokens = tokens // 2
    pieces = max(1, width // (2 * HEAD_DIM))
    piece = width // pieces

    outs = dict(
        layer_output=shape((length, model)),
        input_grad=shape((length, model), F32),
        own_norms=shape((4, shard), F32),
        square_sum=shape((8, 128), F32),
    )
    homes = dict(
        home_joint=shape((3, shard, width), F32),
        home_out=shape((out_rows, model), F32),
        home_expand=shape((shard, hidden), F32),
        home_contract=shape((own_units, model), F32),
        home_far_joint=shape((3, shard, width)),
        home_far_out=shape((out_rows, model)),
        home_far_expand=shape((shard, hidden)),
        home_far_contract=shape((own_units, model)),
    )
    scratch = dict(
        own_joint=((3, shard, width), F32),
        own_out=((out_rows, model), F32),
        own_expand=((shard, hidden), F32),
        own_contract=((own_units, model), F32),
        far_joint=((3, shard, width), BF16),
        far_out=((out_rows, model), BF16),
        far_expand=((shard, hidden), BF16),
        far_contract=((own_units, model), BF16),
        norm_all=((dp_size, 4, shard), F32),
        a_mine=((chips, length, slab), BF16),
        a_all=((chips, length, slab), BF16),
        wq=((3, slab, width), BF16),
        wo=((dp_size, out_rows, model), BF16),
        wu=((chips, slab, units), BF16),
        wd=((units, model), BF16),
        j_send=((pieces, chips, 2, length // 2, 3 * piece), BF16),
        j_recv=((pieces, 3, 2, length // 2, 3 * piece), BF16),
        j_mid=((pieces, 2, length // 2, 3 * piece), BF16),
        joint=((pieces, length, 3 * piece), BF16),
        dy_mine=((2, half_rows, model), BF16),
        dy_all=((chips, 2, half_rows, model), BF16),
        attended=((length, width), BF16),
        b_send=((2, mp_size, half_strip, model), BF16),
        b_recv=((2, mp_size, half_strip, model), BF16),
        hid=((2, half_strip, model), F32),
        c_mine=((2, chips, half_strip, slab), BF16),
        c_all=((2, chips, mp_size, half_strip, slab), BF16),
        u_send=((2, chips, 2, tokens // 4, units), BF16),
        u_recv=((2, 3, 2, tokens // 4, units), BF16),
        u_mid=((2, 2, tokens // 4, units), BF16),
        dz=((2, half_tokens, units), F32),
        z=((2, half_tokens, units), BF16),
        du_all=((2, chips, half_tokens, units), BF16),
        y_send=((chips, 2, length // 2, model), BF16),
        y_recv=((3, 2, length // 2, model), BF16),
        y_mid=((2, length // 2, model), BF16),
        gc_send=((own_units, model), BF16),
        dc_send=((2, chips, mp_size, half_strip, slab), BF16),
        dc_recv=((2, chips, mp_size, half_strip, slab), BF16),
        ge_send=((shard, hidden), BF16),
        dh=((2, half_strip, model), F32),
        da_mine=((2, half_strip, model), BF16),
        da_rows=((mp_size, 2, half_strip, model), BF16),
        dq_mine=((pieces, length, 3 * piece), BF16),
        dq_all=((pieces, chips, length, 3 * piece), BF16),
        go_send=((chips, 2, out_rows, model), BF16),
        go_recv=((3, 2, out_rows, model), BF16),
        go_mid=((2, out_rows, model), BF16),
        go_pair=((2, out_rows, model), BF16),
        y2_send=((mp_size, strip, model), BF16),
        y2_recv=((mp_size, strip, model), BF16),
        y_mine=((strip, model), BF16),
        y_rows=((mp_size, strip, model), BF16),
        df_send=((chips, mp_size, strip, slab), BF16),
        df_recv=((chips, mp_size, strip, slab), BF16),
        gj_send=((3, shard, width), BF16),
        ig_mine=((strip, model), BF16),
        ig_rows=((mp_size, strip, model), BF16),
        gn_send=((chips, 8, shard), F32),
        gn_recv=((chips * mp_size, 8, shard), F32),
        gn_pair=((8, shard), F32),
        gn_far=((8, shard), F32),
        sq_mine=((8, 128), F32),
        sq_recv=((chips * mp_size, 8, 128), F32),
        sq_pair=((8, 128), F32),
        sq_far=((8, 128), F32),
    )
    in_names = dict(
        x=0, seg_row=1, cot=2, f_joint=3, f_out=4, f_expand=5, f_contract=6, norm_own=7
    )
    names = list(in_names) + list(outs) + list(homes) + list(scratch)

    def kernel(*refs):
        r = SimpleNamespace(**dict(zip(names, refs)))
        sems = refs[len(names) :]
        load_sems, home_sems = sems[:2]
        dp, mp = lax.axis_index("dp"), lax.axis_index("mp")
        core, chip = lax.rem(dp, 2), lax.div(dp, 2)
        mine, other = part(core, shard), part(1 - core, shard)
        cross_me = groups.cross.me()

        def flat(ref, columns=slice(None)):
            values = ref[(slice(None),) * (len(ref.shape) - 1) + (columns,)]
            return values.reshape(-1, values.shape[-1])

        views = dict(
            norms=lambda s, t: (r.norm_own, r.norm_all.at[s]),
            normed=lambda s, t: (r.a_mine.at[t], r.a_all.at[s]),
            joint_weight=lambda s, t: (
                r.wq.at[:, part(s, shard), :],
                r.wq.at[:, part(s, shard), :],
            ),
            out_own=lambda s, t: (r.wo.at[dp - core + s], r.wo.at[dp - core + s]),
            expand=lambda s, t: (
                r.wu.at[:, part(s, shard), :],
                r.wu.at[:, part(s, shard), :],
            ),
            contract=lambda s, t: (
                r.wd.at[part(s, own_units), :],
                r.wd.at[part(s, own_units), :],
            ),
            branch=[
                lambda s, t, h=h: (r.b_send.at[h, t], r.b_recv.at[h, s]) for h in range(2)
            ],
            second=[
                lambda s, t, h=h: (
                    r.c_mine.at[h, lax.div(t, mp_size)],
                    r.c_all.at[h, lax.div(s, mp_size), lax.rem(s, mp_size)],
                )
                for h in range(2)
            ],
            g_contract=lambda s, t: (r.gc_send, r.far_contract),
            d_second=[
                lambda s, t, h=h: (
                    r.dc_send.at[h, lax.div(t, mp_size), lax.rem(t, mp_size)],
                    r.dc_recv.at[h, lax.div(s, mp_size), lax.rem(s, mp_size)],
                )
                for h in range(2)
            ],
            g_expand=lambda s, t: (r.ge_send, r.far_expand),
            d_hidden=[
                lambda s, t, h=h: (r.da_mine.at[h], r.da_rows.at[s, h]) for h in range(2)
            ],
            g_out_pair=lambda s, t: (r.go_pair.at[t], r.far_out),
            out_strip=lambda s, t: (r.y2_send.at[t], r.y2_recv.at[s]),
            d_first=lambda s, t: (
                r.df_send.at[lax.div(t, mp_size), lax.rem(t, mp_size)],
                r.df_recv.at[lax.div(s, mp_size), lax.rem(s, mp_size)],
            ),
            g_joint=lambda s, t: (r.gj_send, r.far_joint),
            out_rows=lambda s, t: (r.y_mine, r.y_rows.at[s]),
            in_rows=lambda s, t: (r.ig_mine, r.ig_rows.at[s]),
            g_norms=lambda s, t: (r.gn_send.at[lax.div(t, mp_size)], r.gn_recv.at[s]),
            g_norms_pair=lambda s, t: (r.gn_pair, r.gn_far),
            squares=lambda s, t: (r.sq_mine, r.sq_recv.at[s]),
            squares_pair=lambda s, t: (r.sq_pair, r.sq_far),
        )
        lane = SimpleNamespace()
        every_lane = []
        used = iter(sems[2:])

        def pair_of():
            return (next(used), next(used))

        for name, kind in LANES.items():
            group = vars(groups)[kind]
            several = name in HALVED
            lanes = [
                Lane(group, group.me(), pair_of(), view)
                for view in (views[name] if several else [views[name]])
            ]
            every_lane += lanes
            setattr(lane, name, lanes if several else lanes[0])
        hop = Hop(dp, mp)

        def gather(own, block, half):
            every_lane.append(PlaneGather(hop, pair_of(), own, block, half))
            return every_lane[-1]

        def reduce(parts, inbox, middle):
            every_lane.append(PlaneReduce(hop, pair_of(), parts, inbox, middle))
            return every_lane[-1]

        def row_half(ref, way):
            rows = ref.shape[0] // 2
            return ref.at[pl.ds(way * rows, rows), :]

        out_plane = gather(r.wo.at[dp], lambda c: r.wo.at[2 * c + core], row_half)
        cot_plane = gather(r.dy_mine, lambda c: r.dy_all.at[c], lambda ref, way: ref.at[way])
        d_pre = [
            gather(r.du_all.at[h, chip], lambda c, h=h: r.du_all.at[h, c], row_half)
            for h in range(2)
        ]
        d_joint = [
            gather(r.dq_mine.at[p], lambda c, p=p: r.dq_all.at[p, c], row_half)
            for p in range(pieces)
        ]
        joint = [reduce(r.j_send.at[p], r.j_recv.at[p], r.j_mid.at[p]) for p in range(pieces)]
        pre_sum = [reduce(r.u_send.at[h], r.u_recv.at[h], r.u_mid.at[h]) for h in range(2)]
        out_sum = reduce(r.y_send, r.y_recv, r.y_mid)
        g_out_sum = reduce(r.go_send, r.go_recv, r.go_mid)
        pass_sems = pair_of()

        def passing(index, to_me):
            source = (*hop.chips, hop.far)[index]
            block = r.wo.at[2 * source + (1 - core if to_me else core)]
            return pltpu.make_async_remote_copy(
                src_ref=block,
                dst_ref=block,
                send_sem=pass_sems[0].at[index],
                recv_sem=pass_sems[1].at[index],
                device_id=(dp + 1 - 2 * core, mp),
                device_id_type=pl.DeviceIdType.MESH,
            )

        loads = [
            pltpu.make_async_copy(source, target, load_sems.at[i])
            for i, (source, target) in enumerate(
                (
                    (r.f_joint, r.own_joint),
                    (r.f_out, r.own_out),
                    (r.f_expand, r.own_expand),
                    (r.f_contract, r.own_contract),
                )
            )
        ]
        for load in (loads[1], loads[0], loads[2], loads[3]):
            load.start()

        leaving = []

        def send_home(index, source, target):
            leaving.append(pltpu.make_async_copy(source, target, home_sems.at[index]))
            leaving[-1].start()

        barrier = pltpu.get_barrier_semaphore()

        def greet(device):
            pl.semaphore_signal(
                barrier, inc=1, device_id=device, device_id_type=pl.DeviceIdType.MESH
            )

        cross = groups.cross
        repeat(1, cross.size, lambda s: greet(cross.device(lax.rem(cross_me + s, cross.size))))
        repeat(0, chips, lambda s: greet((s * 2 + 1 - core, mp)))

        r.norm_all[dp] = r.norm_own[...]
        loads[1].wait()
        r.wo[dp] = r.own_out[...].astype(BF16)
        values = r.x[...].astype(F32)
        centered, inverse = standardise(values)
        unit = centered * inverse
        loads[0].wait()
        for c in range(3):
            r.wq[c, mine, :] = r.own_joint[c].astype(BF16)
        ids = jnp.broadcast_to(r.seg_row[...].astype(F32), (length, length))
        places = lax.broadcasted_iota(jnp.int32, (length, length), 0)
        keys = lax.broadcasted_iota(jnp.int32, (length, length), 1)
        allowed = (ids == ids.T) & (keys <= places)
        pl.semaphore_wait(barrier, cross.size - 1 + chips)

        lane.norms.start_all()
        lane.joint_weight.start_all()
        out_plane.start()
        lane.out_own.start_all()
        lane.norms.take_all()

        def norm_row(index, block=None):
            blocks = range(dp_size) if block is None else (block,)
            rows = [r.norm_all[b, pl.ds(index, 1), :] for b in blocks]
            whole = rows[0] if len(rows) == 1 else jnp.concatenate(rows, axis=1)
            return whole.astype(BF16).astype(F32)

        for b in range(dp_size):
            columns = slice(b * shard, (b + 1) * shard)
            r.a_mine[b // 2, :, (b % 2) * shard : (b % 2 + 1) * shard] = (
                unit[:, columns] * norm_row(0, b) + norm_row(1, b)
            ).astype(BF16)
        lane.normed.start_all()
        r.a_all[chip] = r.a_mine[chip]

        lane.joint_weight.take_all()

        def joint_part(p, block):
            rows = r.a_all[block]
            for c in range(3):
                columns = slice(c * piece, (c + 1) * piece)
                third = mul(rows, r.wq[c, :, p * piece : (p + 1) * piece]).astype(BF16)
                for way in range(2):
                    r.j_send[p, block, way, :, columns] = third[
                        way * half_rows : (way + 1) * half_rows
                    ]

        def chip_step(block):
            return lax.rem(chip + chips - block, chips)

        for p in range(pieces):
            for way in range(2):
                if p == 0:
                    lane.normed.take(chip_step(hop.chips[way]))
                joint_part(p, hop.chips[way])
            joint[p].start(1)
            if p == 0:
                lane.normed.take(chip_step(hop.far))
            joint_part(p, hop.far)
            joint[p].start(0)
            joint_part(p, chip)
        for h in range(2):
            for m in range(mp_size):
                first = m * strip + h * half_strip
                r.dy_mine[h, m * half_strip : (m + 1) * half_strip, :] = r.cot[
                    first : first + half_strip, :
                ]
        out_plane.forward()
        for index in range(2):
            passing(index, False).start()
        for p in range(pieces):
            joint[p].forward()

        loads[2].wait()
        for c in range(chips):
            r.wu[c, mine, :] = r.own_expand[:, c * units : (c + 1) * units].astype(BF16)
        lane.expand.start_all()
        loads[3].wait()
        r.wd[part(core, own_units), :] = r.own_contract[...].astype(BF16)
        lane.contract.start_all()
        def query_key_value(start):
            p, first = start // piece, start % piece
            return (
                r.joint[p, :, c * piece + first : c * piece + first + HEAD_DIM] for c in range(3)
            )

        for p in range(pieces):
            for way in range(2):
                joint[p].take(way)
                r.joint[p, way * half_rows : (way + 1) * half_rows, :] = (
                    joint[p].total(way).astype(BF16)
                )
            if p == pieces - 1:
                cot_plane.start()
            for start in range(p * piece, (p + 1) * piece, HEAD_DIM):
                query, key, value = query_key_value(start)
                prob = probabilities(query, key, allowed)
                r.attended[:, start : start + HEAD_DIM] = mul(prob.astype(BF16), value).astype(BF16)

        lane.out_own.take_all()
        out_plane.finish()
        passing(2, False).start()
        for index in range(3):
            passing(index, True).wait_recv()
        branch = mul(r.attended[...], flat(r.wo)).astype(BF16)
        for h in range(2):
            for m in range(mp_size):
                first = m * strip + h * half_strip
                r.b_send[h, m] = branch[first : first + half_strip]
            lane.branch[h].start_all()
        r.dy_all[chip] = r.dy_mine[...]
        cot_plane.forward()

        def here(h):
            return pl.ds(pl.multiple_of(mp * strip + h * half_strip, half_strip), half_strip)

        for h in range(2):
            lane.branch[h].take_all()
            total = r.x[here(h), :].astype(F32) + r.b_send[h, mp].astype(F32)
            for step in range(1, mp_size):
                total = total + r.b_recv[h, lane.branch[h].source(step)].astype(F32)
            r.hid[h] = total
            centered, inverse = standardise(total)
            for b in range(dp_size):
                columns = slice(b * shard, (b + 1) * shard)
                r.c_mine[h, b // 2, :, (b % 2) * shard : (b % 2 + 1) * shard] = (
                    centered[:, columns] * inverse * norm_row(2, b) + norm_row(3, b)
                ).astype(BF16)
            lane.second[h].start_all()
            r.c_all[h, chip, mp] = r.c_mine[h, chip]
        lane.expand.take_all()

        def dy_half(h):
            return r.dy_all[:, h].reshape(half_tokens, model)

        quarter = half_tokens // 2

        def pre_part(h, to):
            part_sum = mul(flat(r.c_all.at[h]), r.wu[to]).astype(BF16)
            for way in range(2):
                r.u_send[h, to, way] = part_sum[way * quarter : (way + 1) * quarter]

        for h in range(2):
            lane.second[h].take_all()
            pre_part(h, hop.far)
            pre_sum[h].start(0)
            for way in range(2):
                pre_part(h, hop.chips[way])
            pre_sum[h].start(1)
            pre_part(h, chip)
            if h == 0:
                lane.contract.take_all()
                cot_plane.finish()
            r.dz[h] = mul(dy_half(h), r.wd[...], COLS_COLS)
            pre_sum[h].forward()
        tile = 64

        for h in range(2):
            for way in range(2):
                pre_sum[h].take(way)

                def gelu_tile(i, none, h=h, way=way):
                    rows = part(i, tile)
                    pre = pre_sum[h].total(way, rows)
                    square = pre * pre
                    curve = jnp.tanh(ROOT * pre * (1.0 + CUBE * square))
                    half = 0.5 * (1.0 + curve)
                    slope = half + 0.5 * pre * (1.0 - curve * curve) * (
                        ROOT * (1.0 + 3.0 * CUBE * square)
                    )
                    rows = part(i + way * (quarter // tile), tile)
                    r.z[h, rows, :] = (pre * half).astype(BF16)
                    r.du_all[h, chip, rows, :] = (r.dz[h, rows, :] * slope).astype(BF16)
                    return none

                lax.fori_loop(0, quarter // tile, gelu_tile, None)
            d_pre[h].start()

        def out_part(h):
            part_sum = mul(r.z[h], r.wd[...]).astype(BF16)
            for c in range(chips):
                r.y_send[c, h] = part_sum[c * half_rows : (c + 1) * half_rows]

        def second_part(h, source):
            return mul(r.du_all[h, source], r.wu[source], COLS_COLS)

        d_pre[0].forward()
        for h in range(2):
            out_part(h)
            total = second_part(h, chip)
            for way in range(2):
                total = total + second_part(h, hop.chips[way])
            if h == 0:
                d_pre[1].forward()
            d_pre[h].finish()
            total = (total + second_part(h, hop.far)).astype(BF16)
            for c in range(chips):
                for m in range(mp_size):
                    first = (c * mp_size + m) * half_strip
                    r.dc_send[h, c, m] = total[first : first + half_strip]
            lane.d_second[h].start_all()
        out_sum.start(0)
        out_sum.start(1)

        def contract_grad(columns):
            return sum(mul(r.z[h, :, columns], dy_half(h), ROWS_ROWS) for h in range(2))

        def gathered(recv, rows):
            blocks = []
            for c in range(chips):
                block = jnp.zeros((rows, slab), F32)
                for m in range(mp_size):
                    block = block + recv[c, m].astype(F32)
                blocks.append(block)
            return jnp.concatenate(blocks, axis=1)

        r.gc_send[...] = contract_grad(part(1 - core, own_units)).astype(BF16)
        lane.g_contract.start_all()
        gain_two, shift_two = 0.0, 0.0
        for h in range(2):
            lane.d_second[h].take_all()
            r.dc_recv[h, chip, mp] = r.dc_send[h, chip, mp]
            d_normed = gathered(r.dc_recv.at[h], half_strip)
            back, gain, shift = norm_back(d_normed, r.hid[h], norm_row(2))
            gain_two, shift_two = gain_two + gain, shift_two + shift
            d_hidden = r.cot[here(h), :].astype(F32) + back
            r.dh[h] = d_hidden
            r.da_mine[h] = d_hidden.astype(BF16)
            lane.d_hidden[h].start_all()
            r.da_rows[mp, h] = r.da_mine[h]
        out_sum.forward()
        for c in range(chips):
            r.ge_send[:, c * units : (c + 1) * units] = mul(
                flat(r.c_all, other), flat(r.du_all.at[:, c]), ROWS_ROWS
            ).astype(BF16)
        lane.g_expand.start_all()
        r.own_contract[...] = contract_grad(part(core, own_units))
        send_home(3, r.own_contract, r.home_contract)
        for h in range(2):
            lane.d_hidden[h].take_all()

        for way in range(2):
            out_sum.take(way)
            total = out_sum.total(way).astype(BF16)
            for m in range(mp_size):
                r.y2_send[m, way * half_strip : (way + 1) * half_strip, :] = total[
                    m * half_strip : (m + 1) * half_strip
                ]
        lane.out_strip.start_all()
        d_attended = mul(flat(r.da_rows), flat(r.wo), COLS_COLS).astype(BF16)
        for p in range(pieces):
            for start in range(p * piece, (p + 1) * piece, HEAD_DIM):
                query, key, value = query_key_value(start)
                d_out = d_attended[:, start : start + HEAD_DIM]
                prob = probabilities(query, key, allowed)
                d_prob = mul(d_out, value, COLS_COLS)
                row_delta = jnp.sum(d_prob * prob, axis=-1, keepdims=True)
                d_raw = (prob * (d_prob - row_delta) * SCALE).astype(BF16)
                thirds = (
                    mul(d_raw, key),
                    mul(d_raw, query, ROWS_ROWS),
                    mul(prob.astype(BF16), d_out, ROWS_ROWS),
                )
                for c in range(3):
                    first = c * piece + start % piece
                    r.dq_mine[p, :, first : first + HEAD_DIM] = thirds[c].astype(BF16)
            d_joint[p].start()
            r.dq_all[p, chip] = r.dq_mine[p]

        grad_out = mul(r.attended[...], flat(r.da_rows), ROWS_ROWS).astype(BF16)
        for c in range(chips):
            for k in range(2):
                first = (2 * c + k) * out_rows
                r.go_send[c, k] = grad_out[first : first + out_rows]
        for p in range(pieces):
            d_joint[p].forward()
        lane.out_strip.take_all()
        total = r.hid[...].reshape(strip, model) + r.y2_send[mp].astype(F32)
        for step in range(1, mp_size):
            total = total + r.y2_recv[lane.out_strip.source(step)].astype(F32)
        r.y_mine[...] = total.astype(BF16)
        lane.out_rows.start_all()
        r.layer_output[part(mp, strip), :] = r.y_mine[...]
        for c in range(chips):
            r.own_expand[:, c * units : (c + 1) * units] = mul(
                flat(r.c_all, mine), flat(r.du_all.at[:, c]), ROWS_ROWS
            )
        send_home(2, r.own_expand, r.home_expand)

        def first_block(block):
            total = jnp.zeros((length, slab), F32)
            for p in range(pieces):
                for c in range(3):
                    total = total + mul(
                        r.dq_all[p, block, :, c * piece : (c + 1) * piece],
                        r.wq[c, :, p * piece : (p + 1) * piece],
                        COLS_COLS,
                    )
            total = total.astype(BF16)
            for m in range(mp_size):
                r.df_send[block, m] = total[m * strip : (m + 1) * strip]

        def first_send(block, others):
            for j in others:
                to = block * mp_size + lax.rem(mp + j, mp_size)
                lane.d_first.start(lax.rem(to + cross.size - cross_me, cross.size))

        first_block(chip)
        first_send(chip, range(1, mp_size))
        for way in range(2):
            first_block(hop.chips[way])
            first_send(hop.chips[way], range(mp_size))
        for p in range(pieces):
            d_joint[p].finish()
        first_block(hop.far)
        first_send(hop.far, range(mp_size))
        g_out_sum.start(0)
        g_out_sum.start(1)

        def joint_grad(c, columns, target):
            for p in range(pieces):
                target[c, :, p * piece : (p + 1) * piece] = mul(
                    flat(r.a_all, columns),
                    r.dq_all[p, :, :, c * piece : (c + 1) * piece].reshape(tokens, piece),
                    ROWS_ROWS,
                ).astype(target.dtype)

        for c in range(3):
            joint_grad(c, other, r.gj_send)
        lane.g_joint.start_all()
        for c in range(3):
            joint_grad(c, mine, r.own_joint)
        send_home(0, r.own_joint, r.home_joint)
        g_out_sum.forward()

        lane.d_first.take_all()
        r.df_recv[chip, mp] = r.df_send[chip, mp]
        d_normed = gathered(r.df_recv, strip)
        back, gain_one, shift_one = norm_back(d_normed, r.x[part(mp, strip), :].astype(F32), norm_row(0))
        grad = r.dh[...].reshape(strip, model) + back
        r.ig_mine[...] = grad.astype(BF16)
        lane.in_rows.start_all()
        r.input_grad[part(mp, strip), :] = grad
        for index, row in enumerate((gain_one, shift_one, gain_two, shift_two)):
            for b in range(dp_size):
                place = (b % 2) * 4 + index
                r.gn_send[b // 2, place : place + 1, :] = row[:, b * shard : (b + 1) * shard]
        lane.g_norms.start_all()
        r.gn_recv[cross_me] = r.gn_send[chip]

        def square(own, distant):
            whole = own + distant.astype(F32)
            return jnp.sum(whole * whole, axis=0, keepdims=True)

        def folded(row):
            return sum(row[:, i : i + 128] for i in range(0, row.shape[1], 128))

        lane.g_contract.take_all()
        send_home(7, r.far_contract, r.home_far_contract)
        squares = folded(square(r.own_contract[...], r.far_contract[...]))
        lane.g_expand.take_all()
        send_home(6, r.far_expand, r.home_far_expand)
        squares = squares + folded(square(r.own_expand[...], r.far_expand[...]))
        lane.g_joint.take_all()
        send_home(4, r.far_joint, r.home_far_joint)
        for c in range(3):
            squares = squares + folded(square(r.own_joint[c], r.far_joint[c]))

        for k in range(2):
            g_out_sum.take(k)
            total = g_out_sum.total(k)

            @pl.when(core == k)
            def _():
                r.own_out[...] = total

            r.go_pair[k] = total.astype(BF16)
        lane.g_out_pair.start_all()
        send_home(1, r.own_out, r.home_out)

        lane.g_norms.take_all()
        summed = r.gn_recv[0]
        for index in range(1, chips * mp_size):
            summed = summed + r.gn_recv[index]
        r.gn_pair[...] = summed
        lane.g_norms_pair.start_all()
        lane.g_out_pair.take_all()
        send_home(5, r.far_out, r.home_far_out)
        squares = squares + folded(square(r.own_out[...], r.far_out[...]))
        lane.g_norms_pair.take_all()
        summed = summed + r.gn_far[...]
        own_norms = jnp.where(core == 0, summed[:4], summed[4:])
        r.own_norms[...] = own_norms
        own_norms = jnp.sum(own_norms * own_norms, axis=0, keepdims=True) * (1.0 / mp_size)
        squares = squares + folded(own_norms)
        r.sq_mine[...] = jnp.broadcast_to(jnp.sum(squares), (8, 128))
        lane.squares.start_all()
        r.sq_recv[cross_me] = r.sq_mine[...]

        def place(rows_lane, rows, output):
            rows_lane.take_all()
            for step in range(1, mp_size):
                source = rows_lane.source(step)
                output[part(source, strip), :] = rows[source].astype(output.dtype)

        place(lane.out_rows, r.y_rows, r.layer_output)
        place(lane.in_rows, r.ig_rows, r.input_grad)
        lane.squares.take_all()
        total = r.sq_recv[0]
        for index in range(1, chips * mp_size):
            total = total + r.sq_recv[index]
        r.sq_pair[...] = total
        lane.squares_pair.start_all()
        lane.squares_pair.take_all()
        r.square_sum[...] = total + r.sq_far[...]
        for entry in every_lane:
            entry.sent_all()
        for index in range(3):
            passing(index, False).wait_send()
        for entry in leaving:
            entry.wait()

    vmem = pl.BlockSpec(memory_space=pltpu.VMEM)
    any_space = pl.BlockSpec(memory_space=pl.ANY)
    sem_shapes = [pltpu.SemaphoreType.DMA((4,)), pltpu.SemaphoreType.DMA((8,))]
    for name, kind in LANES.items():
        count = 2 * HALVED.get(name, 1)
        sem_shapes += [pltpu.SemaphoreType.DMA((vars(groups)[kind].size,))] * count
    sem_shapes += [pltpu.SemaphoreType.DMA((4,))] * 2 * (4 + pieces)
    sem_shapes += [pltpu.SemaphoreType.DMA((6,))] * 2 * (4 + pieces)
    sem_shapes += [pltpu.SemaphoreType.DMA((3,))] * 2
    results = pl.pallas_call(
        kernel,
        out_shape=list(outs.values()) + list(homes.values()),
        in_specs=[vmem] * 3 + [any_space] * 4 + [vmem],
        out_specs=[vmem] * len(outs) + [any_space] * len(homes),
        scratch_shapes=[pltpu.VMEM(*entry) for entry in scratch.values()] + sem_shapes,
        compiler_params=pltpu.CompilerParams(
            collective_id=30, has_side_effects=True, vmem_limit_bytes=VMEM_LIMIT
        ),
    )(x, segments, cotangent, joint_w, out_w, expand_w, contract_w, norms)
    return SimpleNamespace(**dict(zip(list(outs) + list(homes), results)))


VMEM_LIMIT = 60 * 2**20


def local(dp_size, mp_size, *arrays):
    params, firsts, seconds = arrays[3:8], arrays[8:13], arrays[13:18]
    r = layer(dp_size, mp_size, arrays[:8])
    grads = (
        r.home_joint + r.home_far_joint.astype(F32),
        r.home_out + r.home_far_out.astype(F32),
        r.home_expand + r.home_far_expand.astype(F32),
        r.home_contract + r.home_far_contract.astype(F32),
        r.own_norms,
    )
    gradient_norm = jnp.sqrt(r.square_sum[0, 0])
    clip_factor = jnp.minimum(1.0, MAX_NORM / (gradient_norm + CLIP_EPSILON))
    updates = [
        adam_update(params[k], grads[k], firsts[k], seconds[k], LEARN_RATES[k], clip_factor)
        for k in range(5)
    ]
    copies = [entry[2].astype(BF16) for entry in updates]
    return (
        r.layer_output,
        r.input_grad,
        *grads,
        *[entry[0] for entry in updates],
        *[entry[1] for entry in updates],
        *[entry[2] for entry in updates],
        *copies,
        gradient_norm,
    )


def solution(mesh):
    rows = P("dp", None)
    sets = (
        P(None, "dp", "mp"),
        P(("mp", "dp"), None),
        P("dp", "mp"),
        P(("mp", "dp"), None),
        P(None, "dp"),
    )
    form = local if mesh.shape["dp"] == 8 else local_steps
    return jax.shard_map(
        functools.partial(form, mesh.shape["dp"], mesh.shape["mp"]),
        mesh=mesh,
        in_specs=(rows, rows, rows) + sets * 3,
        out_specs=(rows, rows) + sets * 5 + (P(),),
        check_vma=False,
    )
```

```python
import functools
import math
from types import SimpleNamespace

import jax
import jax.numpy as jnp
from jax import lax
from jax.experimental import pallas as pl
from jax.experimental.pallas import tpu as pltpu
from jax.sharding import PartitionSpec as P

HEAD_DIM = 128
ADAM_STEP = 5
MAX_NORM = 8192


BETA_ONE = 0.9
BETA_TWO = 0.95
ADAM_EPSILON = 1e-08
WEIGHT_DECAY = 0.1
NORM_EPSILON = 1e-05
CLIP_EPSILON = 1e-06
LEARN_RATES = (0.01, 0.08, 0.012, 0.02, 0.3)
MASKED_SCORE = -1e30
SCALE = 1.0 / math.sqrt(HEAD_DIM)
F32 = jnp.float32
BF16 = jnp.bfloat16
ROWS_COLS = (((1,), (0,)), ((), ()))
COLS_COLS = (((1,), (1,)), ((), ()))
ROWS_ROWS = (((0,), (0,)), ((), ()))


def mul(left, right, dims=ROWS_COLS):
    return lax.dot_general(left, right, dims, preferred_element_type=F32)


def layer_norm(values, gain_row, shift_row):
    row_mean = jnp.mean(values, axis=-1, keepdims=True)
    centered = values - row_mean
    spread = jnp.mean(centered * centered, axis=-1, keepdims=True)
    return centered * lax.rsqrt(spread + NORM_EPSILON) * gain_row + shift_row


def gelu_tanh(values):
    return jax.nn.gelu(values, approximate=True)


def adam_update(weight, grad, first, second, rate, clip_factor):
    clipped = grad * clip_factor
    new_first = BETA_ONE * first + (1.0 - BETA_ONE) * clipped
    new_second = BETA_TWO * second + (1.0 - BETA_TWO) * clipped * clipped
    first_hat = new_first / (1.0 - BETA_ONE**ADAM_STEP)
    second_hat = new_second / (1.0 - BETA_TWO**ADAM_STEP)
    new_weight = weight - rate * (
        first_hat / (jnp.sqrt(second_hat) + ADAM_EPSILON) + WEIGHT_DECAY * weight
    )
    return (new_first, new_second, new_weight)


PAIR, PLANE, COLUMN, CROSS, ROW, ALL = ("pair", "plane", "column", "cross", "row", "all")


class Group:
    def __init__(self, kind, dp_size, mp_size):
        self.kind = kind
        self.mp_size = mp_size
        chips = dp_size // 2
        self.size = {
            PAIR: 2,
            PLANE: chips,
            COLUMN: mp_size,
            CROSS: chips * mp_size,
            ROW: dp_size,
            ALL: dp_size * mp_size,
        }[kind]

    def me(self):
        dp, mp = lax.axis_index("dp"), lax.axis_index("mp")
        if self.kind == PAIR:
            return lax.rem(dp, 2)
        if self.kind == PLANE:
            return lax.div(dp, 2)
        if self.kind == COLUMN:
            return mp
        if self.kind == CROSS:
            return lax.div(dp, 2) * self.mp_size + mp
        if self.kind == ROW:
            return dp
        return dp * self.mp_size + mp

    def device(self, member):
        dp, mp = lax.axis_index("dp"), lax.axis_index("mp")
        core = lax.rem(dp, 2)
        if self.kind == PAIR:
            return (dp - core + member, mp)
        if self.kind == PLANE:
            return (member * 2 + core, mp)
        if self.kind == COLUMN:
            return (dp, member)
        if self.kind == CROSS:
            return (lax.div(member, self.mp_size) * 2 + core, lax.rem(member, self.mp_size))
        if self.kind == ROW:
            return (member, mp)
        return (lax.div(member, self.mp_size), lax.rem(member, self.mp_size))


def repeat(low, high, body):
    if high - low <= 8:
        for step in range(low, high):
            body(step)
    else:
        lax.fori_loop(low, high, lambda step, none: (body(step), none)[1], None)


def exchange(group, operands, results, moves, collective_id):
    count = len(operands)
    size = group.size
    lanes = len(moves)

    def kernel(*refs):
        ins, outs = refs[:count], refs[count : count + len(results)]
        send_sems, recv_sems, own_sems = refs[count + len(results) :]
        me = group.me()
        barrier = pltpu.get_barrier_semaphore()

        def greet(step):
            other = lax.rem(me + step, size)
            pl.semaphore_signal(
                barrier, inc=1, device_id=group.device(other), device_id_type=pl.DeviceIdType.MESH
            )

        repeat(1, size, greet)
        pl.semaphore_wait(barrier, size - 1)

        def remote(move, lane, step, sender, target, device):
            return pltpu.make_async_remote_copy(
                src_ref=move(ins, outs, me, target)[0],
                dst_ref=move(ins, outs, sender, me)[1],
                send_sem=send_sems.at[lane, step],
                recv_sem=recv_sems.at[lane, step],
                device_id=group.device(device),
                device_id_type=pl.DeviceIdType.MESH,
            )

        def launch(step):
            other = lax.rem(me + step, size)
            for lane, move in enumerate(moves):
                remote(move, lane, step, me, other, other).start()

        repeat(1, size, launch)
        own = []
        for lane, move in enumerate(moves):
            source, target = move(ins, outs, me, me)
            own.append(pltpu.make_async_copy(source, target, own_sems.at[lane]))
            own[-1].start()

        def finish(step):
            other = lax.rem(me + step, size)
            sender = lax.rem(me + size - step, size)
            for lane, move in enumerate(moves):
                remote(move, lane, step, sender, other, other).wait()

        repeat(1, size, finish)
        for copy in own:
            copy.wait()

    any_space = pl.BlockSpec(memory_space=pl.ANY)
    return pl.pallas_call(
        kernel,
        out_shape=results,
        in_specs=[any_space] * count,
        out_specs=[any_space] * len(results),
        scratch_shapes=[
            pltpu.SemaphoreType.DMA((lanes, size)),
            pltpu.SemaphoreType.DMA((lanes, size)),
            pltpu.SemaphoreType.DMA((lanes,)),
        ],
        compiler_params=pltpu.CompilerParams(collective_id=collective_id, has_side_effects=True),
    )(*operands)


def shape(dims, dtype=BF16):
    return jax.ShapeDtypeStruct(dims, dtype)


def part(index, width):
    return pl.ds(pl.multiple_of(index * width, width), width)


def allowed_pairs(seg_row, seg_col, length):
    places = lax.broadcasted_iota(jnp.int32, (length, length), 0)
    keys = lax.broadcasted_iota(jnp.int32, (length, length), 1)
    return (seg_col[...] == seg_row[...]) & (keys <= places)


def probabilities(query, key, allowed):
    scores = jnp.where(allowed, mul(query, key, COLS_COLS) * SCALE, MASKED_SCORE)
    exponent = jnp.exp(scores - jnp.max(scores, axis=-1, keepdims=True))
    return exponent / jnp.sum(exponent, axis=-1, keepdims=True)


def attend_kernel(width, joint, seg_row, seg_col, out_weight, attended, partial):
    allowed = allowed_pairs(seg_row, seg_col, joint.shape[0])
    for start in range(0, width, HEAD_DIM):
        head = pl.ds(start, HEAD_DIM)
        query, key, value = (joint[:, pl.ds(c * width + start, HEAD_DIM)] for c in range(3))
        prob = probabilities(query, key, allowed)
        attended[:, head] = mul(prob.astype(BF16), value).astype(BF16)
    partial[...] = mul(attended[...], out_weight[...]).astype(BF16)


def attend_back_kernel(
    width, joint, seg_row, seg_col, out_weight, attended, branch, d_joint, grad_out, d_attended
):
    allowed = allowed_pairs(seg_row, seg_col, joint.shape[0])
    d_attended[...] = mul(branch[...], out_weight[...], COLS_COLS).astype(BF16)
    for start in range(0, width, HEAD_DIM):
        query, key, value = (joint[:, pl.ds(c * width + start, HEAD_DIM)] for c in range(3))
        d_out = d_attended[:, pl.ds(start, HEAD_DIM)]
        prob = probabilities(query, key, allowed)
        d_joint[:, pl.ds(2 * width + start, HEAD_DIM)] = mul(
            prob.astype(BF16), d_out, ROWS_ROWS
        ).astype(BF16)
        d_prob = mul(d_out, value, COLS_COLS)
        row_delta = jnp.sum(d_prob * prob, axis=-1, keepdims=True)
        d_raw = (prob * (d_prob - row_delta) * SCALE).astype(BF16)
        d_joint[:, pl.ds(start, HEAD_DIM)] = mul(d_raw, key).astype(BF16)
        d_joint[:, pl.ds(width + start, HEAD_DIM)] = mul(d_raw, query, ROWS_ROWS).astype(BF16)
    grad_out[...] = mul(attended[...], branch[...], ROWS_ROWS).astype(BF16)


def local_steps(
    dp_size,
    mp_size,
    inputs,
    segment_ids,
    cotangent,
    query_key_value,
    attention_out,
    expand_weight,
    contract_weight,
    norm_params,
    first_query_key_value,
    first_attention_out,
    first_expand_weight,
    first_contract_weight,
    first_norm_params,
    second_query_key_value,
    second_attention_out,
    second_expand_weight,
    second_contract_weight,
    second_norm_params,
):
    params = (query_key_value, attention_out, expand_weight, contract_weight, norm_params)
    firsts = (
        first_query_key_value,
        first_attention_out,
        first_expand_weight,
        first_contract_weight,
        first_norm_params,
    )
    seconds = (
        second_query_key_value,
        second_attention_out,
        second_expand_weight,
        second_contract_weight,
        second_norm_params,
    )
    chips = dp_size // 2
    pair, plane, column, cross, row, everyone = (
        Group(kind, dp_size, mp_size)
        for kind in (PAIR, PLANE, COLUMN, CROSS, ROW, ALL)
    )
    dp, mp = lax.axis_index("dp"), lax.axis_index("mp")
    core = dp % 2
    length, model = inputs.shape
    width = query_key_value.shape[2]
    shard = query_key_value.shape[1]
    slab = 2 * shard
    hidden_units = expand_weight.shape[1]
    own_units = contract_weight.shape[0]
    units = 2 * own_units
    out_rows = attention_out.shape[0]
    strip = length // mp_size
    tokens = chips * length

    (norm_all,) = exchange(
        row,
        [norm_params],
        [shape((dp_size, 4, shard), F32)],
        [lambda ins, outs, me, other: (ins[0], outs[0].at[me])],
        0,
    )
    norm_weights = jnp.swapaxes(norm_all.astype(BF16).astype(F32), 0, 1).reshape(4, model)

    def shared(column_block):
        def move(ins, outs, me, other):
            return (ins[0].at[column_block], outs[0].at[part(me, shard), pl.ds(column_block * width, width)])

        return move

    joint_weight, expand_pair, contract_pair = exchange(
        pair,
        [query_key_value.astype(BF16), expand_weight.astype(BF16), contract_weight.astype(BF16)],
        [shape((slab, 3 * width)), shape((slab, hidden_units)), shape((units, model))],
        [
            shared(0),
            shared(1),
            shared(2),
            lambda ins, outs, me, other: (ins[1], outs[1].at[part(me, shard), :]),
            lambda ins, outs, me, other: (ins[2], outs[2].at[part(me, own_units), :]),
        ],
        1,
    )
    (output_all,) = exchange(
        row,
        [attention_out.astype(BF16)],
        [shape((dp_size * out_rows, model))],
        [lambda ins, outs, me, other: (ins[0], outs[0].at[part(me, out_rows), :])],
        2,
    )
    (grad_rows,) = exchange(
        plane,
        [cotangent],
        [shape((chips, length, model))],
        [lambda ins, outs, me, other: (ins[0], outs[0].at[me])],
        3,
    )
    grad_rows = grad_rows.reshape(tokens, model)

    values = inputs.astype(F32)
    normed = layer_norm(values, norm_weights[0], norm_weights[1]).astype(BF16)
    (normed_low,) = exchange(
        plane,
        [normed],
        [shape((chips, length, slab))],
        [lambda ins, outs, me, other: (ins[0].at[:, part(other, slab)], outs[0].at[me])],
        4,
    )
    normed_low = normed_low.reshape(tokens, slab)
    joint_part = mul(normed_low, joint_weight).astype(BF16).reshape(chips, length, 3 * width)
    (joint_parts,) = exchange(
        plane,
        [joint_part],
        [shape((chips, length, 3 * width))],
        [lambda ins, outs, me, other: (ins[0].at[other], outs[0].at[me])],
        5,
    )
    joint = jnp.sum(joint_parts.astype(F32), axis=0).astype(BF16)

    seg_row = segment_ids
    seg_col = segment_ids.reshape(length, 1)
    attended, branch_part = pl.pallas_call(
        functools.partial(attend_kernel, width),
        out_shape=[shape((length, width)), shape((length, model))],
        compiler_params=pltpu.CompilerParams(vmem_limit_bytes=48 * 2**20),
    )(joint, seg_row, seg_col, output_all)

    (branch_parts,) = exchange(
        column,
        [branch_part.reshape(mp_size, strip, model)],
        [shape((mp_size, strip, model))],
        [lambda ins, outs, me, other: (ins[0].at[other], outs[0].at[me])],
        6,
    )
    own_values = lax.dynamic_slice_in_dim(values, mp * strip, strip, 0)
    hidden = own_values + jnp.sum(branch_parts.astype(F32), axis=0)
    normed_two, pull_two = jax.vjp(layer_norm, hidden, norm_weights[2], norm_weights[3])
    (second_low,) = exchange(
        cross,
        [normed_two.astype(BF16)],
        [shape((chips * mp_size, strip, slab))],
        [
            lambda ins, outs, me, other: (
                ins[0].at[:, part(lax.div(other, mp_size), slab)],
                outs[0].at[me],
            )
        ],
        7,
    )
    second_low = second_low.reshape(tokens, slab)
    pre_part = mul(second_low, expand_pair).astype(BF16)
    (pre_parts,) = exchange(
        plane,
        [pre_part],
        [shape((chips, tokens, units))],
        [lambda ins, outs, me, other: (ins[0].at[:, part(other, units)], outs[0].at[me])],
        8,
    )
    pre_gelu = jnp.sum(pre_parts.astype(F32), axis=0)
    activated, pull_gelu = jax.vjp(gelu_tanh, pre_gelu)
    activated_low = activated.astype(BF16)
    d_activated = mul(grad_rows, contract_pair, COLS_COLS)
    (d_pre,) = pull_gelu(d_activated)
    (d_pre_all,) = exchange(
        plane,
        [d_pre.astype(BF16)],
        [shape((tokens, hidden_units))],
        [lambda ins, outs, me, other: (ins[0], outs[0].at[:, part(me, units)])],
        9,
    )

    def scatter_rows(partial, collective_id):
        (blocks,) = exchange(
            cross,
            [partial.reshape(chips * mp_size, strip, slab)],
            [shape((chips * mp_size, strip, slab))],
            [lambda ins, outs, me, other: (ins[0].at[other], outs[0].at[me])],
            collective_id,
        )
        total = jnp.sum(blocks.reshape(chips, mp_size, strip, slab).astype(F32), axis=1)
        return jnp.swapaxes(total, 0, 1).reshape(strip, model)

    d_normed_two = scatter_rows(mul(d_pre_all, expand_pair, COLS_COLS).astype(BF16), 10)
    d_hidden_norm, gain_two, shift_two = pull_two(d_normed_two)
    own_grad = lax.dynamic_slice_in_dim(cotangent, mp * strip, strip, 0).astype(F32)
    d_hidden = own_grad + d_hidden_norm

    def gather_rows(block, collective_id):
        (rows,) = exchange(
            column,
            [block],
            [shape((mp_size, strip, model))],
            [lambda ins, outs, me, other: (ins[0], outs[0].at[me])],
            collective_id,
        )
        return rows.reshape(length, model)

    branch_grad = gather_rows(d_hidden.astype(BF16), 11)
    d_joint, grad_output_part, _ = pl.pallas_call(
        functools.partial(attend_back_kernel, width),
        out_shape=[shape((length, 3 * width)), shape((width, model)), shape((length, width))],
        compiler_params=pltpu.CompilerParams(vmem_limit_bytes=48 * 2**20),
    )(joint, seg_row, seg_col, output_all, attended, branch_grad)
    (d_joint_all,) = exchange(
        plane,
        [d_joint],
        [shape((chips, length, 3 * width))],
        [lambda ins, outs, me, other: (ins[0], outs[0].at[me])],
        12,
    )
    d_joint_all = d_joint_all.reshape(tokens, 3 * width)
    d_normed_one = scatter_rows(mul(d_joint_all, joint_weight, COLS_COLS).astype(BF16), 13)
    _, pull_one = jax.vjp(layer_norm, own_values, norm_weights[0], norm_weights[1])
    d_values_norm, gain_one, shift_one = pull_one(d_normed_one)
    input_grad = gather_rows((d_hidden + d_values_norm).astype(BF16), 14).astype(F32)

    out_part = mul(activated_low, contract_pair).astype(BF16).reshape(chips, length, model)
    (out_parts,) = exchange(
        plane,
        [out_part],
        [shape((chips, length, model))],
        [lambda ins, outs, me, other: (ins[0].at[other], outs[0].at[me])],
        15,
    )
    out_rows_sum = jnp.sum(out_parts.astype(F32), axis=0).astype(BF16)
    (out_strips,) = exchange(
        column,
        [out_rows_sum.reshape(mp_size, strip, model)],
        [shape((mp_size, strip, model))],
        [lambda ins, outs, me, other: (ins[0].at[other], outs[0].at[me])],
        16,
    )
    layer_output = gather_rows(
        (hidden + jnp.sum(out_strips.astype(F32), axis=0)).astype(BF16), 17
    )

    (grad_output_parts,) = exchange(
        row,
        [grad_output_part.reshape(dp_size, out_rows, model)],
        [shape((dp_size, out_rows, model))],
        [lambda ins, outs, me, other: (ins[0].at[other], outs[0].at[me])],
        18,
    )
    reduced_output = jnp.sum(grad_output_parts.astype(F32), axis=0)
    own_joint, other_joint = [], []
    grad_joint = mul(normed_low, d_joint_all, ROWS_ROWS)
    grad_expand = mul(second_low, d_pre_all, ROWS_ROWS)
    grad_contract = mul(activated_low, grad_rows, ROWS_ROWS)

    def halves(array, index):
        return lax.dynamic_slice_in_dim(array, index * (array.shape[0] // 2), array.shape[0] // 2, 0)

    pieces = (grad_joint, grad_expand, grad_contract)
    sent = [halves(entry, 1 - core).astype(BF16) for entry in pieces]
    got = exchange_pair(pair, sent, 19)
    reduced_joint, reduced_expand, reduced_contract = (
        halves(entry, core) + other.astype(F32) for entry, other in zip(pieces, got)
    )
    reduced_joint = jnp.swapaxes(reduced_joint.reshape(shard, 3, width), 0, 1)

    zero_row = jnp.zeros((model,), F32)
    norm_rows = jnp.stack([gain_one, shift_one, gain_two, shift_two] + [zero_row] * 4)
    norm_rows = jnp.swapaxes(norm_rows.reshape(8, dp_size, shard), 0, 1)
    (norm_parts,) = exchange(
        everyone,
        [norm_rows],
        [shape((dp_size * mp_size, 8, shard), F32)],
        [
            lambda ins, outs, me, other: (
                ins[0].at[lax.div(other, mp_size)],
                outs[0].at[me],
            )
        ],
        20,
    )
    reduced_norms = jnp.sum(norm_parts, axis=0)[:4]

    grads = (reduced_joint, reduced_output, reduced_expand, reduced_contract, reduced_norms)
    squares = sum((jnp.sum(entry * entry) for entry in grads[:4])) + jnp.sum(
        reduced_norms * reduced_norms
    ) / mp_size
    (square_parts,) = exchange(
        everyone,
        [jnp.full((8, 128), squares, F32)],
        [shape((dp_size * mp_size, 8, 128), F32)],
        [lambda ins, outs, me, other: (ins[0], outs[0].at[me])],
        21,
    )
    gradient_norm = jnp.sqrt(jnp.sum(square_parts[:, 0, 0]))
    clip_factor = jnp.minimum(1.0, MAX_NORM / (gradient_norm + CLIP_EPSILON))
    updates = [
        adam_update(params[k], grads[k], firsts[k], seconds[k], LEARN_RATES[k], clip_factor)
        for k in range(5)
    ]
    copies = [entry[2].astype(BF16) for entry in updates]
    return (
        layer_output,
        input_grad,
        *grads,
        *[entry[0] for entry in updates],
        *[entry[1] for entry in updates],
        *[entry[2] for entry in updates],
        *copies,
        gradient_norm,
    )


def exchange_pair(pair, sent, collective_id):
    moves = [
        lambda ins, outs, me, other, lane=lane: (ins[lane], outs[lane]) for lane in range(len(sent))
    ]
    return swap(pair, sent, moves, collective_id)


def swap(pair, sent, moves, collective_id):
    count = len(sent)

    def kernel(*refs):
        ins, outs = refs[:count], refs[count : 2 * count]
        send_sems, recv_sems = refs[2 * count :]
        other = pair.device(1 - pair.me())
        barrier = pltpu.get_barrier_semaphore()
        pl.semaphore_signal(barrier, inc=1, device_id=other, device_id_type=pl.DeviceIdType.MESH)
        pl.semaphore_wait(barrier, 1)
        copies = [
            pltpu.make_async_remote_copy(
                src_ref=ins[lane],
                dst_ref=outs[lane],
                send_sem=send_sems.at[lane],
                recv_sem=recv_sems.at[lane],
                device_id=other,
                device_id_type=pl.DeviceIdType.MESH,
            )
            for lane in range(count)
        ]
        for copy in copies:
            copy.start()
        for copy in copies:
            copy.wait()

    any_space = pl.BlockSpec(memory_space=pl.ANY)
    return pl.pallas_call(
        kernel,
        out_shape=[shape(entry.shape, entry.dtype) for entry in sent],
        in_specs=[any_space] * count,
        out_specs=[any_space] * count,
        scratch_shapes=[pltpu.SemaphoreType.DMA((count,)), pltpu.SemaphoreType.DMA((count,))],
        compiler_params=pltpu.CompilerParams(collective_id=collective_id, has_side_effects=True),
    )(*sent)


class Lane:
    def __init__(self, group, me, sems, view, bulk=None):
        self.group, self.me, self.view, self.bulk = group, me, view, bulk
        self.sems = sems
        self.size = group.size

    def remote(self, source, target, step):
        index = step - 1 if self.bulk is None else 0
        return pltpu.make_async_remote_copy(
            src_ref=source,
            dst_ref=target,
            send_sem=self.sems[0].at[index],
            recv_sem=self.sems[1].at[index],
            device_id=self.group.device(lax.rem(self.me + step, self.size)),
            device_id_type=pl.DeviceIdType.MESH,
        )

    def copy(self, step):
        return self.remote(*self.view(self.me, lax.rem(self.me + step, self.size)), step)

    def start(self, step):
        self.copy(step).start()

    def start_all(self):
        repeat(1, self.size, self.start)

    def source(self, step):
        return lax.rem(self.me + self.size - step, self.size)

    def take(self, step):
        to = lax.rem(self.me + step, self.size)
        source, target = self.view(self.me, to)[0], self.view(self.source(step), self.me)[1]
        self.remote(source, target, step).wait_recv()

    def take_all(self):
        if self.bulk is None:
            repeat(1, self.size, self.take)
        else:
            self.remote(self.bulk, self.bulk, 1).wait_recv()

    def sent_all(self):
        if self.bulk is None:
            repeat(1, self.size, lambda step: self.copy(step).wait_send())
        else:
            self.remote(self.bulk, self.bulk, 1).wait_send()


class Hop:
    def __init__(self, dp, mp):
        core, self.me = lax.rem(dp, 2), lax.div(dp, 2)
        x_next = self.me + 1 - 2 * lax.rem(self.me, 2)
        self.chips = (x_next, lax.rem(self.me + 2, 4))
        self.far = 3 - self.me
        self.devices = tuple((chip * 2 + core, mp) for chip in self.chips)

    def copy(self, source, target, sems, index, way):
        return pltpu.make_async_remote_copy(
            src_ref=source,
            dst_ref=target,
            send_sem=sems[0].at[index],
            recv_sem=sems[1].at[index],
            device_id=self.devices[way],
            device_id_type=pl.DeviceIdType.MESH,
        )


class PlaneGather:
    def __init__(self, hop, sems, own, block, half):
        self.hop, self.sems, self.own, self.block, self.half = hop, sems, own, block, half

    def first(self, way):
        return self.hop.copy(self.own, self.block(self.hop.me), self.sems, way, way)

    def second(self, way):
        piece = self.half(self.block(self.hop.chips[way]), way)
        return self.hop.copy(piece, piece, self.sems, 2 + way, 1 - way)

    def start(self):
        for way in range(2):
            self.first(way).start()

    def near(self, way):
        near = self.block(self.hop.chips[way])
        self.hop.copy(near, near, self.sems, way, way).wait_recv()

    def forward(self):
        for way in range(2):
            self.near(way)
            self.second(way).start()

    def finish(self):
        for way in range(2):
            piece = self.half(self.block(self.hop.far), way)
            self.hop.copy(piece, piece, self.sems, 2 + way, 1 - way).wait_recv()

    def sent_all(self):
        for way in range(2):
            self.first(way).wait_send()
            self.second(way).wait_send()


class PlaneReduce:
    def __init__(self, hop, sems, parts, inbox, middle):
        self.hop, self.sems = hop, sems
        self.parts, self.inbox, self.middle = parts, inbox, middle

    def copy(self, stage, way):
        hop = self.hop
        chip = (hop.far, hop.chips[way])[stage] if stage < 2 else None
        source = self.parts.at[chip, way] if stage < 2 else self.middle.at[way]
        along = way if stage < 2 else 1 - way
        return hop.copy(source, self.inbox.at[stage, way], self.sems, 2 * stage + way, along)

    def start(self, stage):
        for way in range(2):
            self.copy(stage, way).start()

    def forward(self):
        for way in range(2):
            self.copy(0, way).wait_recv()
            onward = self.hop.chips[1 - way]
            total = self.parts[onward, way].astype(F32) + self.inbox[0, way].astype(F32)
            self.middle[way] = total.astype(BF16)
            self.copy(2, way).start()

    def take(self, way):
        self.copy(1, way).wait_recv()
        self.copy(2, way).wait_recv()

    def total(self, way, rows=slice(None)):
        own = self.parts[self.hop.me, way, rows].astype(F32)
        near = self.inbox[1, way, rows].astype(F32)
        return own + near + self.inbox[2, way, rows].astype(F32)

    def sent_all(self):
        for stage in range(3):
            for way in range(2):
                self.copy(stage, way).wait_send()


def standardise(values):
    row_mean = jnp.mean(values, axis=-1, keepdims=True)
    centered = values - row_mean
    spread = jnp.mean(centered * centered, axis=-1, keepdims=True)
    return centered, lax.rsqrt(spread + NORM_EPSILON)


def norm_back(grad, values, gain_row):
    centered, inverse = standardise(values)
    unit = centered * inverse
    scaled = grad * gain_row
    inner = jnp.mean(scaled * unit, axis=-1, keepdims=True)
    back = inverse * (scaled - jnp.mean(scaled, axis=-1, keepdims=True) - unit * inner)
    gain_grad = jnp.sum(grad * unit, axis=0, keepdims=True)
    shift_grad = jnp.sum(grad, axis=0, keepdims=True)
    return back, gain_grad, shift_grad


ROOT = math.sqrt(2.0 / math.pi)
CUBE = 0.044715

LANES = dict(
    norms=ROW,
    normed=PLANE,
    joint_weight=PAIR,
    out_own=PAIR,
    expand=PAIR,
    contract=PAIR,
    branch=COLUMN,
    second=CROSS,
    g_contract=PAIR,
    d_second=CROSS,
    g_expand=PAIR,
    d_hidden=COLUMN,
    g_out_pair=PAIR,
    out_strip=COLUMN,
    d_first=CROSS,
    g_joint=PAIR,
    out_rows=COLUMN,
    in_rows=COLUMN,
    g_norms=CROSS,
    g_norms_pair=PAIR,
    squares=CROSS,
    squares_pair=PAIR,
)

STEPWISE = dict(normed=True)
HALVED = dict(branch=2, second=2, d_second=2, d_hidden=2)


def layer(dp_size, mp_size, operands):
    x, segments, cotangent, joint_w, out_w, expand_w, contract_w, norms = operands
    chips = dp_size // 2
    groups = SimpleNamespace(
        **{kind: Group(kind, dp_size, mp_size) for kind in (PAIR, PLANE, COLUMN, CROSS, ROW)}
    )
    length, model = x.shape
    width, shard = joint_w.shape[2], joint_w.shape[1]
    slab = 2 * shard
    hidden = expand_w.shape[1]
    own_units = contract_w.shape[0]
    units = 2 * own_units
    out_rows = out_w.shape[0]
    strip = length // mp_size
    tokens = chips * length
    half_strip = strip // 2
    half_rows = length // 2
    half_tokens = tokens // 2
    pieces = max(1, width // (2 * HEAD_DIM))
    piece = width // pieces

    outs = dict(
        layer_output=shape((length, model)),
        input_grad=shape((length, model), F32),
        own_norms=shape((4, shard), F32),
        square_sum=shape((1, 1), F32),
    )
    homes = dict(
        home_joint=shape((3, shard, width), F32),
        home_out=shape((out_rows, model), F32),
        home_expand=shape((shard, hidden), F32),
        home_contract=shape((own_units, model), F32),
        home_far_joint=shape((3, shard, width)),
        home_far_out=shape((out_rows, model)),
        home_far_expand=shape((shard, hidden)),
        home_far_contract=shape((own_units, model)),
    )
    scratch = dict(
        own_joint=((3, shard, width), F32),
        own_out=((out_rows, model), F32),
        own_expand=((shard, hidden), F32),
        own_contract=((own_units, model), F32),
        far_joint=((3, shard, width), BF16),
        far_out=((out_rows, model), BF16),
        far_expand=((shard, hidden), BF16),
        far_contract=((own_units, model), BF16),
        norm_all=((dp_size, 4, shard), F32),
        a_mine=((chips, length, slab), BF16),
        a_all=((chips, length, slab), BF16),
        wq=((3, slab, width), BF16),
        wo=((dp_size, out_rows, model), BF16),
        wu=((chips, slab, units), BF16),
        wd=((units, model), BF16),
        j_send=((pieces, chips, 2, length // 2, 3 * piece), BF16),
        j_recv=((pieces, 3, 2, length // 2, 3 * piece), BF16),
        j_mid=((pieces, 2, length // 2, 3 * piece), BF16),
        joint=((pieces, length, 3 * piece), BF16),
        dy_mine=((2, half_rows, model), BF16),
        dy_all=((chips, 2, half_rows, model), BF16),
        attended=((length, width), BF16),
        b_send=((2, mp_size, half_strip, model), BF16),
        b_recv=((2, mp_size, half_strip, model), BF16),
        hid=((2, half_strip, model), F32),
        bulk=(((chips * mp_size - 1) * strip, slab), BF16),
        c_mine=((2, chips, half_strip, slab), BF16),
        c_all=((2, chips, mp_size, half_strip, slab), BF16),
        u_send=((2, chips, 2, tokens // 4, units), BF16),
        u_recv=((2, 3, 2, tokens // 4, units), BF16),
        u_mid=((2, 2, tokens // 4, units), BF16),
        dz=((2, half_tokens, units), F32),
        z=((2, half_tokens, units), BF16),
        du_all=((2, chips, half_tokens, units), BF16),
        y_send=((chips, 2, length // 2, model), BF16),
        y_recv=((3, 2, length // 2, model), BF16),
        y_mid=((2, length // 2, model), BF16),
        gc_send=((own_units, model), BF16),
        dc_send=((2, chips, mp_size, half_strip, slab), BF16),
        dc_recv=((2, chips, mp_size, half_strip, slab), BF16),
        ge_send=((shard, hidden), BF16),
        dh=((2, half_strip, model), F32),
        da_mine=((2, half_strip, model), BF16),
        da_rows=((mp_size, 2, half_strip, model), BF16),
        dq_mine=((pieces, length, 3 * piece), BF16),
        dq_all=((pieces, chips, length, 3 * piece), BF16),
        go_send=((chips, 2, out_rows, model), BF16),
        go_recv=((3, 2, out_rows, model), BF16),
        go_mid=((2, out_rows, model), BF16),
        go_pair=((2, out_rows, model), BF16),
        y2_send=((mp_size, strip, model), BF16),
        y2_recv=((mp_size, strip, model), BF16),
        y_mine=((strip, model), BF16),
        y_rows=((mp_size, strip, model), BF16),
        df_send=((chips, mp_size, strip, slab), BF16),
        df_recv=((chips, mp_size, strip, slab), BF16),
        gj_send=((3, shard, width), BF16),
        ig_mine=((strip, model), BF16),
        ig_rows=((mp_size, strip, model), BF16),
        gn_send=((chips, 8, shard), F32),
        gn_recv=((chips * mp_size, 8, shard), F32),
        gn_pair=((8, shard), F32),
        gn_far=((8, shard), F32),
        sq_mine=((8, 128), F32),
        sq_recv=((chips * mp_size, 8, 128), F32),
        sq_pair=((8, 128), F32),
        sq_far=((8, 128), F32),
    )
    in_names = dict(
        x=0, seg_row=1, cot=2, f_joint=3, f_out=4, f_expand=5, f_contract=6, norm_own=7
    )
    names = list(in_names) + list(outs) + list(homes) + list(scratch)

    def kernel(*refs):
        r = SimpleNamespace(**dict(zip(names, refs)))
        sems = refs[len(names) :]
        load_sems, home_sems = sems[:2]
        dp, mp = lax.axis_index("dp"), lax.axis_index("mp")
        core, chip = lax.rem(dp, 2), lax.div(dp, 2)
        mine, other = part(core, shard), part(1 - core, shard)
        cross_me = groups.cross.me()

        def flat(ref, columns=slice(None)):
            values = ref[(slice(None),) * (len(ref.shape) - 1) + (columns,)]
            return values.reshape(-1, values.shape[-1])

        views = dict(
            norms=lambda s, t: (r.norm_own, r.norm_all.at[s]),
            normed=lambda s, t: (r.a_mine.at[t], r.a_all.at[s]),
            joint_weight=lambda s, t: (
                r.wq.at[:, part(s, shard), :],
                r.wq.at[:, part(s, shard), :],
            ),
            out_own=lambda s, t: (r.wo.at[dp - core + s], r.wo.at[dp - core + s]),
            expand=lambda s, t: (
                r.wu.at[:, part(s, shard), :],
                r.wu.at[:, part(s, shard), :],
            ),
            contract=lambda s, t: (
                r.wd.at[part(s, own_units), :],
                r.wd.at[part(s, own_units), :],
            ),
            branch=[
                lambda s, t, h=h: (r.b_send.at[h, t], r.b_recv.at[h, s]) for h in range(2)
            ],
            second=[
                lambda s, t, h=h: (
                    r.c_mine.at[h, lax.div(t, mp_size)],
                    r.c_all.at[h, lax.div(s, mp_size), lax.rem(s, mp_size)],
                )
                for h in range(2)
            ],
            g_contract=lambda s, t: (r.gc_send, r.far_contract),
            d_second=[
                lambda s, t, h=h: (
                    r.dc_send.at[h, lax.div(t, mp_size), lax.rem(t, mp_size)],
                    r.dc_recv.at[h, lax.div(s, mp_size), lax.rem(s, mp_size)],
                )
                for h in range(2)
            ],
            g_expand=lambda s, t: (r.ge_send, r.far_expand),
            d_hidden=[
                lambda s, t, h=h: (r.da_mine.at[h], r.da_rows.at[s, h]) for h in range(2)
            ],
            g_out_pair=lambda s, t: (r.go_pair.at[t], r.far_out),
            out_strip=lambda s, t: (r.y2_send.at[t], r.y2_recv.at[s]),
            d_first=lambda s, t: (
                r.df_send.at[lax.div(t, mp_size), lax.rem(t, mp_size)],
                r.df_recv.at[lax.div(s, mp_size), lax.rem(s, mp_size)],
            ),
            g_joint=lambda s, t: (r.gj_send, r.far_joint),
            out_rows=lambda s, t: (r.y_mine, r.y_rows.at[s]),
            in_rows=lambda s, t: (r.ig_mine, r.ig_rows.at[s]),
            g_norms=lambda s, t: (r.gn_send.at[lax.div(t, mp_size)], r.gn_recv.at[s]),
            g_norms_pair=lambda s, t: (r.gn_pair, r.gn_far),
            squares=lambda s, t: (r.sq_mine, r.sq_recv.at[s]),
            squares_pair=lambda s, t: (r.sq_pair, r.sq_far),
        )
        others = chips * mp_size - 1
        column_blocks = pl.ds(0, mp_size - 1)
        bulks = dict(
            norms=r.norm_all.at[pl.ds(0, dp_size - 1)],
            branch=[r.b_recv.at[h, column_blocks] for h in range(2)],
            second=[r.bulk.at[pl.ds(0, others * half_strip), :]] * 2,
            d_second=[r.bulk.at[pl.ds(0, others * half_strip), :]] * 2,
            d_hidden=[r.da_rows.at[column_blocks, h] for h in range(2)],
            out_strip=r.y2_recv.at[column_blocks],
            d_first=r.bulk,
            out_rows=r.y_rows.at[column_blocks],
            in_rows=r.ig_rows.at[column_blocks],
            g_norms=r.gn_recv.at[pl.ds(0, others)],
            squares=r.sq_recv.at[pl.ds(0, others)],
        )
        lane = SimpleNamespace()
        every_lane = []
        used = iter(sems[2:])

        def pair_of():
            return (next(used), next(used))

        for name, kind in LANES.items():
            group = vars(groups)[kind]
            several = name in HALVED
            bulk = bulks.get(name, None)
            lanes = [
                Lane(group, group.me(), pair_of(), view, one)
                for view, one in (
                    zip(views[name], bulk) if several else [(views[name], bulk)]
                )
            ]
            every_lane += lanes
            setattr(lane, name, lanes if several else lanes[0])
        hop = Hop(dp, mp)

        def gather(own, block, half):
            every_lane.append(PlaneGather(hop, pair_of(), own, block, half))
            return every_lane[-1]

        def reduce(parts, inbox, middle):
            every_lane.append(PlaneReduce(hop, pair_of(), parts, inbox, middle))
            return every_lane[-1]

        def row_half(ref, way):
            rows = ref.shape[0] // 2
            return ref.at[pl.ds(way * rows, rows), :]

        out_plane = gather(r.wo.at[dp], lambda c: r.wo.at[2 * c + core], row_half)
        cot_plane = gather(r.dy_mine, lambda c: r.dy_all.at[c], lambda ref, way: ref.at[way])
        d_pre = [
            gather(r.du_all.at[h, chip], lambda c, h=h: r.du_all.at[h, c], row_half)
            for h in range(2)
        ]
        d_joint = [
            gather(r.dq_mine.at[p], lambda c, p=p: r.dq_all.at[p, c], row_half)
            for p in range(pieces)
        ]
        joint = [reduce(r.j_send.at[p], r.j_recv.at[p], r.j_mid.at[p]) for p in range(pieces)]
        pre_sum = [reduce(r.u_send.at[h], r.u_recv.at[h], r.u_mid.at[h]) for h in range(2)]
        out_sum = reduce(r.y_send, r.y_recv, r.y_mid)
        g_out_sum = reduce(r.go_send, r.go_recv, r.go_mid)
        pass_sems = pair_of()

        def passing(index, to_me):
            source = (*hop.chips, hop.far)[index]
            block = r.wo.at[2 * source + (1 - core if to_me else core)]
            return pltpu.make_async_remote_copy(
                src_ref=block,
                dst_ref=block,
                send_sem=pass_sems[0].at[index],
                recv_sem=pass_sems[1].at[index],
                device_id=(dp + 1 - 2 * core, mp),
                device_id_type=pl.DeviceIdType.MESH,
            )

        loads = [
            pltpu.make_async_copy(source, target, load_sems.at[i])
            for i, (source, target) in enumerate(
                (
                    (r.f_joint, r.own_joint),
                    (r.f_out, r.own_out),
                    (r.f_expand, r.own_expand),
                    (r.f_contract, r.own_contract),
                )
            )
        ]
        for load in (loads[1], loads[0], loads[2], loads[3]):
            load.start()

        leaving = []

        def send_home(index, source, target):
            leaving.append(pltpu.make_async_copy(source, target, home_sems.at[index]))
            leaving[-1].start()

        barrier = pltpu.get_barrier_semaphore()

        def greet(device):
            pl.semaphore_signal(
                barrier, inc=1, device_id=device, device_id_type=pl.DeviceIdType.MESH
            )

        cross = groups.cross
        repeat(1, cross.size, lambda s: greet(cross.device(lax.rem(cross_me + s, cross.size))))
        repeat(0, chips, lambda s: greet((s * 2 + 1 - core, mp)))

        r.norm_all[dp] = r.norm_own[...]
        loads[1].wait()
        r.wo[dp] = r.own_out[...].astype(BF16)
        values = r.x[...].astype(F32)
        centered, inverse = standardise(values)
        unit = centered * inverse
        loads[0].wait()
        for c in range(3):
            r.wq[c, mine, :] = r.own_joint[c].astype(BF16)
        ids = jnp.broadcast_to(r.seg_row[...].astype(F32), (length, length))
        places = lax.broadcasted_iota(jnp.int32, (length, length), 0)
        keys = lax.broadcasted_iota(jnp.int32, (length, length), 1)
        allowed = (ids == ids.T) & (keys <= places)
        pl.semaphore_wait(barrier, cross.size - 1 + chips)

        lane.norms.start_all()
        lane.joint_weight.start_all()
        out_plane.start()
        lane.out_own.start_all()
        lane.norms.take_all()

        def norm_row(index, block=None):
            blocks = range(dp_size) if block is None else (block,)
            rows = [r.norm_all[b, pl.ds(index, 1), :] for b in blocks]
            whole = rows[0] if len(rows) == 1 else jnp.concatenate(rows, axis=1)
            return whole.astype(BF16).astype(F32)

        for b in range(dp_size):
            columns = slice(b * shard, (b + 1) * shard)
            r.a_mine[b // 2, :, (b % 2) * shard : (b % 2 + 1) * shard] = (
                unit[:, columns] * norm_row(0, b) + norm_row(1, b)
            ).astype(BF16)
        lane.normed.start_all()
        r.a_all[chip] = r.a_mine[chip]

        lane.joint_weight.take_all()

        def joint_part(p, block):
            rows = r.a_all[block]
            for c in range(3):
                columns = slice(c * piece, (c + 1) * piece)
                third = mul(rows, r.wq[c, :, p * piece : (p + 1) * piece]).astype(BF16)
                for way in range(2):
                    r.j_send[p, block, way, :, columns] = third[
                        way * half_rows : (way + 1) * half_rows
                    ]

        def chip_step(block):
            return lax.rem(chip + chips - block, chips)

        for p in range(pieces):
            for way in range(2):
                if p == 0:
                    lane.normed.take(chip_step(hop.chips[way]))
                joint_part(p, hop.chips[way])
            joint[p].start(1)
            if p == 0:
                lane.normed.take(chip_step(hop.far))
            joint_part(p, hop.far)
            joint[p].start(0)
            joint_part(p, chip)
        for h in range(2):
            for m in range(mp_size):
                first = m * strip + h * half_strip
                r.dy_mine[h, m * half_strip : (m + 1) * half_strip, :] = r.cot[
                    first : first + half_strip, :
                ]
        out_plane.forward()
        for index in range(2):
            passing(index, False).start()
        for p in range(pieces):
            joint[p].forward()

        loads[2].wait()
        for c in range(chips):
            r.wu[c, mine, :] = r.own_expand[:, c * units : (c + 1) * units].astype(BF16)
        lane.expand.start_all()
        loads[3].wait()
        r.wd[part(core, own_units), :] = r.own_contract[...].astype(BF16)
        lane.contract.start_all()
        def query_key_value(start):
            p, first = start // piece, start % piece
            return (
                r.joint[p, :, c * piece + first : c * piece + first + HEAD_DIM] for c in range(3)
            )

        for p in range(pieces):
            for way in range(2):
                joint[p].take(way)
                r.joint[p, way * half_rows : (way + 1) * half_rows, :] = (
                    joint[p].total(way).astype(BF16)
                )
            if p == pieces - 1:
                cot_plane.start()
            for start in range(p * piece, (p + 1) * piece, HEAD_DIM):
                query, key, value = query_key_value(start)
                prob = probabilities(query, key, allowed)
                r.attended[:, start : start + HEAD_DIM] = mul(prob.astype(BF16), value).astype(BF16)

        lane.out_own.take_all()
        out_plane.finish()
        passing(2, False).start()
        for index in range(3):
            passing(index, True).wait_recv()
        branch = mul(r.attended[...], flat(r.wo)).astype(BF16)
        for h in range(2):
            for m in range(mp_size):
                first = m * strip + h * half_strip
                r.b_send[h, m] = branch[first : first + half_strip]
            lane.branch[h].start_all()
        r.dy_all[chip] = r.dy_mine[...]
        cot_plane.forward()

        def here(h):
            return pl.ds(pl.multiple_of(mp * strip + h * half_strip, half_strip), half_strip)

        for h in range(2):
            lane.branch[h].take_all()
            total = r.x[here(h), :].astype(F32) + r.b_send[h, mp].astype(F32)
            for step in range(1, mp_size):
                total = total + r.b_recv[h, lane.branch[h].source(step)].astype(F32)
            r.hid[h] = total
            centered, inverse = standardise(total)
            for b in range(dp_size):
                columns = slice(b * shard, (b + 1) * shard)
                r.c_mine[h, b // 2, :, (b % 2) * shard : (b % 2 + 1) * shard] = (
                    centered[:, columns] * inverse * norm_row(2, b) + norm_row(3, b)
                ).astype(BF16)
            lane.second[h].start_all()
            r.c_all[h, chip, mp] = r.c_mine[h, chip]
        lane.expand.take_all()

        def dy_half(h):
            return r.dy_all[:, h].reshape(half_tokens, model)

        quarter = half_tokens // 2

        def pre_part(h, to):
            part_sum = mul(flat(r.c_all.at[h]), r.wu[to]).astype(BF16)
            for way in range(2):
                r.u_send[h, to, way] = part_sum[way * quarter : (way + 1) * quarter]

        for h in range(2):
            lane.second[h].take_all()
            pre_part(h, hop.far)
            pre_sum[h].start(0)
            for way in range(2):
                pre_part(h, hop.chips[way])
            pre_sum[h].start(1)
            pre_part(h, chip)
            if h == 0:
                lane.contract.take_all()
                cot_plane.finish()
            r.dz[h] = mul(dy_half(h), r.wd[...], COLS_COLS)
            pre_sum[h].forward()
        tile = 64

        for h in range(2):
            for way in range(2):
                pre_sum[h].take(way)

                def gelu_tile(i, none, h=h, way=way):
                    rows = part(i, tile)
                    pre = pre_sum[h].total(way, rows)
                    square = pre * pre
                    curve = jnp.tanh(ROOT * pre * (1.0 + CUBE * square))
                    half = 0.5 * (1.0 + curve)
                    slope = half + 0.5 * pre * (1.0 - curve * curve) * (
                        ROOT * (1.0 + 3.0 * CUBE * square)
                    )
                    rows = part(i + way * (quarter // tile), tile)
                    r.z[h, rows, :] = (pre * half).astype(BF16)
                    r.du_all[h, chip, rows, :] = (r.dz[h, rows, :] * slope).astype(BF16)
                    return none

                lax.fori_loop(0, quarter // tile, gelu_tile, None)
            d_pre[h].start()

        def out_part(h):
            part_sum = mul(r.z[h], r.wd[...]).astype(BF16)
            for c in range(chips):
                r.y_send[c, h] = part_sum[c * half_rows : (c + 1) * half_rows]

        def second_part(h, source):
            return mul(r.du_all[h, source], r.wu[source], COLS_COLS)

        d_pre[0].forward()
        for h in range(2):
            out_part(h)
            total = second_part(h, chip)
            for way in range(2):
                total = total + second_part(h, hop.chips[way])
            if h == 0:
                d_pre[1].forward()
            d_pre[h].finish()
            total = (total + second_part(h, hop.far)).astype(BF16)
            for c in range(chips):
                for m in range(mp_size):
                    first = (c * mp_size + m) * half_strip
                    r.dc_send[h, c, m] = total[first : first + half_strip]
            lane.d_second[h].start_all()
        out_sum.start(0)
        out_sum.start(1)

        def contract_grad(columns):
            return sum(mul(r.z[h, :, columns], dy_half(h), ROWS_ROWS) for h in range(2))

        def gathered(recv, rows):
            blocks = []
            for c in range(chips):
                block = jnp.zeros((rows, slab), F32)
                for m in range(mp_size):
                    block = block + recv[c, m].astype(F32)
                blocks.append(block)
            return jnp.concatenate(blocks, axis=1)

        r.gc_send[...] = contract_grad(part(1 - core, own_units)).astype(BF16)
        lane.g_contract.start_all()
        gain_two, shift_two = 0.0, 0.0
        for h in range(2):
            lane.d_second[h].take_all()
            r.dc_recv[h, chip, mp] = r.dc_send[h, chip, mp]
            d_normed = gathered(r.dc_recv.at[h], half_strip)
            back, gain, shift = norm_back(d_normed, r.hid[h], norm_row(2))
            gain_two, shift_two = gain_two + gain, shift_two + shift
            d_hidden = r.cot[here(h), :].astype(F32) + back
            r.dh[h] = d_hidden
            r.da_mine[h] = d_hidden.astype(BF16)
            lane.d_hidden[h].start_all()
            r.da_rows[mp, h] = r.da_mine[h]
        out_sum.forward()
        for c in range(chips):
            r.ge_send[:, c * units : (c + 1) * units] = mul(
                flat(r.c_all, other), flat(r.du_all.at[:, c]), ROWS_ROWS
            ).astype(BF16)
        lane.g_expand.start_all()
        r.own_contract[...] = contract_grad(part(core, own_units))
        send_home(3, r.own_contract, r.home_contract)
        for h in range(2):
            lane.d_hidden[h].take_all()

        for way in range(2):
            out_sum.take(way)
            total = out_sum.total(way).astype(BF16)
            for m in range(mp_size):
                r.y2_send[m, way * half_strip : (way + 1) * half_strip, :] = total[
                    m * half_strip : (m + 1) * half_strip
                ]
        lane.out_strip.start_all()
        d_attended = mul(flat(r.da_rows), flat(r.wo), COLS_COLS).astype(BF16)
        for p in range(pieces):
            for start in range(p * piece, (p + 1) * piece, HEAD_DIM):
                query, key, value = query_key_value(start)
                d_out = d_attended[:, start : start + HEAD_DIM]
                prob = probabilities(query, key, allowed)
                d_prob = mul(d_out, value, COLS_COLS)
                row_delta = jnp.sum(d_prob * prob, axis=-1, keepdims=True)
                d_raw = (prob * (d_prob - row_delta) * SCALE).astype(BF16)
                thirds = (
                    mul(d_raw, key),
                    mul(d_raw, query, ROWS_ROWS),
                    mul(prob.astype(BF16), d_out, ROWS_ROWS),
                )
                for c in range(3):
                    first = c * piece + start % piece
                    r.dq_mine[p, :, first : first + HEAD_DIM] = thirds[c].astype(BF16)
            d_joint[p].start()
            r.dq_all[p, chip] = r.dq_mine[p]

        grad_out = mul(r.attended[...], flat(r.da_rows), ROWS_ROWS).astype(BF16)
        for c in range(chips):
            for k in range(2):
                first = (2 * c + k) * out_rows
                r.go_send[c, k] = grad_out[first : first + out_rows]
        for p in range(pieces):
            d_joint[p].forward()
        lane.out_strip.take_all()
        total = r.hid[...].reshape(strip, model) + r.y2_send[mp].astype(F32)
        for step in range(1, mp_size):
            total = total + r.y2_recv[lane.out_strip.source(step)].astype(F32)
        r.y_mine[...] = total.astype(BF16)
        lane.out_rows.start_all()
        r.layer_output[part(mp, strip), :] = r.y_mine[...]
        for c in range(chips):
            r.own_expand[:, c * units : (c + 1) * units] = mul(
                flat(r.c_all, mine), flat(r.du_all.at[:, c]), ROWS_ROWS
            )
        send_home(2, r.own_expand, r.home_expand)

        def first_block(block):
            total = jnp.zeros((length, slab), F32)
            for p in range(pieces):
                for c in range(3):
                    total = total + mul(
                        r.dq_all[p, block, :, c * piece : (c + 1) * piece],
                        r.wq[c, :, p * piece : (p + 1) * piece],
                        COLS_COLS,
                    )
            total = total.astype(BF16)
            for m in range(mp_size):
                r.df_send[block, m] = total[m * strip : (m + 1) * strip]

        def first_send(block, others):
            for j in others:
                to = block * mp_size + lax.rem(mp + j, mp_size)
                lane.d_first.start(lax.rem(to + cross.size - cross_me, cross.size))

        first_block(chip)
        first_send(chip, range(1, mp_size))
        for way in range(2):
            first_block(hop.chips[way])
            first_send(hop.chips[way], range(mp_size))
        for p in range(pieces):
            d_joint[p].finish()
        first_block(hop.far)
        first_send(hop.far, range(mp_size))
        g_out_sum.start(0)
        g_out_sum.start(1)

        def joint_grad(c, columns, target):
            for p in range(pieces):
                target[c, :, p * piece : (p + 1) * piece] = mul(
                    flat(r.a_all, columns),
                    r.dq_all[p, :, :, c * piece : (c + 1) * piece].reshape(tokens, piece),
                    ROWS_ROWS,
                ).astype(target.dtype)

        for c in range(3):
            joint_grad(c, other, r.gj_send)
        lane.g_joint.start_all()
        for c in range(3):
            joint_grad(c, mine, r.own_joint)
        send_home(0, r.own_joint, r.home_joint)
        g_out_sum.forward()

        lane.d_first.take_all()
        r.df_recv[chip, mp] = r.df_send[chip, mp]
        d_normed = gathered(r.df_recv, strip)
        back, gain_one, shift_one = norm_back(d_normed, r.x[part(mp, strip), :].astype(F32), norm_row(0))
        grad = r.dh[...].reshape(strip, model) + back
        r.ig_mine[...] = grad.astype(BF16)
        for index, row in enumerate((gain_one, shift_one, gain_two, shift_two)):
            for b in range(dp_size):
                place = (b % 2) * 4 + index
                r.gn_send[b // 2, place : place + 1, :] = row[:, b * shard : (b + 1) * shard]
        lane.g_norms.start_all()
        lane.in_rows.start_all()
        r.input_grad[part(mp, strip), :] = grad
        r.gn_recv[cross_me] = r.gn_send[chip]

        def square(own, distant):
            whole = own + distant.astype(F32)
            return jnp.sum(whole * whole, axis=0, keepdims=True)

        def folded(row):
            return sum(row[:, i : i + 128] for i in range(0, row.shape[1], 128))

        lane.g_contract.take_all()
        send_home(7, r.far_contract, r.home_far_contract)
        squares = folded(square(r.own_contract[...], r.far_contract[...]))
        lane.g_expand.take_all()
        send_home(6, r.far_expand, r.home_far_expand)
        squares = squares + folded(square(r.own_expand[...], r.far_expand[...]))
        lane.g_joint.take_all()
        send_home(4, r.far_joint, r.home_far_joint)
        for c in range(3):
            squares = squares + folded(square(r.own_joint[c], r.far_joint[c]))

        for k in range(2):
            g_out_sum.take(k)
            total = g_out_sum.total(k)

            @pl.when(core == k)
            def _():
                r.own_out[...] = total

            r.go_pair[k] = total.astype(BF16)
        lane.g_out_pair.start_all()
        send_home(1, r.own_out, r.home_out)

        lane.g_norms.take_all()
        summed = r.gn_recv[0]
        for index in range(1, chips * mp_size):
            summed = summed + r.gn_recv[index]
        r.gn_pair[...] = summed
        lane.g_norms_pair.start_all()
        lane.g_out_pair.take_all()
        send_home(5, r.far_out, r.home_far_out)
        squares = squares + folded(square(r.own_out[...], r.far_out[...]))
        lane.g_norms_pair.take_all()
        summed = summed + r.gn_far[...]
        own_norms = jnp.where(core == 0, summed[:4], summed[4:])
        r.own_norms[...] = own_norms
        own_norms = jnp.sum(own_norms * own_norms, axis=0, keepdims=True) * (1.0 / mp_size)
        squares = squares + folded(own_norms)
        r.sq_mine[...] = jnp.broadcast_to(jnp.sum(squares), (8, 128))
        lane.squares.start_all()
        r.sq_recv[cross_me] = r.sq_mine[...]

        def place(rows_lane, rows, output):
            rows_lane.take_all()
            for step in range(1, mp_size):
                source = rows_lane.source(step)
                output[part(source, strip), :] = rows[source].astype(output.dtype)

        place(lane.out_rows, r.y_rows, r.layer_output)
        place(lane.in_rows, r.ig_rows, r.input_grad)
        lane.squares.take_all()
        total = r.sq_recv[0]
        for index in range(1, chips * mp_size):
            total = total + r.sq_recv[index]
        r.sq_pair[...] = total
        lane.squares_pair.start_all()
        lane.squares_pair.take_all()
        r.square_sum[...] = (total + r.sq_far[...])[:1, :1]
        for entry in every_lane:
            entry.sent_all()
        for index in range(3):
            passing(index, False).wait_send()
        for entry in leaving:
            entry.wait()

    vmem = pl.BlockSpec(memory_space=pltpu.VMEM)
    any_space = pl.BlockSpec(memory_space=pl.ANY)
    sem_shapes = [pltpu.SemaphoreType.DMA((4,)), pltpu.SemaphoreType.DMA((8,))]
    for name, kind in LANES.items():
        count = 2 * HALVED.get(name, 1)
        slots = vars(groups)[kind].size - 1 if kind == PAIR or name in STEPWISE else 1
        sem_shapes += [pltpu.SemaphoreType.DMA((slots,))] * count
    sem_shapes += [pltpu.SemaphoreType.DMA((4,))] * 2 * (4 + pieces)
    sem_shapes += [pltpu.SemaphoreType.DMA((6,))] * 2 * (4 + pieces)
    sem_shapes += [pltpu.SemaphoreType.DMA((3,))] * 2
    results = pl.pallas_call(
        kernel,
        out_shape=list(outs.values()) + list(homes.values()),
        in_specs=[vmem] * 3 + [any_space] * 4 + [vmem],
        out_specs=[vmem] * len(outs) + [any_space] * len(homes),
        scratch_shapes=[pltpu.VMEM(*entry) for entry in scratch.values()] + sem_shapes,
        compiler_params=pltpu.CompilerParams(
            collective_id=30, has_side_effects=True, vmem_limit_bytes=VMEM_LIMIT
        ),
    )(x, segments, cotangent, joint_w, out_w, expand_w, contract_w, norms)
    return SimpleNamespace(**dict(zip(list(outs) + list(homes), results)))


VMEM_LIMIT = 60 * 2**20


def local(dp_size, mp_size, *arrays):
    params, firsts, seconds = arrays[3:8], arrays[8:13], arrays[13:18]
    r = layer(dp_size, mp_size, arrays[:8])
    grads = (
        r.home_joint + r.home_far_joint.astype(F32),
        r.home_out + r.home_far_out.astype(F32),
        r.home_expand + r.home_far_expand.astype(F32),
        r.home_contract + r.home_far_contract.astype(F32),
        r.own_norms,
    )
    gradient_norm = jnp.sqrt(r.square_sum.reshape(()))
    clip_factor = jnp.minimum(1.0, MAX_NORM / (gradient_norm + CLIP_EPSILON))
    updates = [
        adam_update(params[k], grads[k], firsts[k], seconds[k], LEARN_RATES[k], clip_factor)
        for k in range(5)
    ]
    copies = [entry[2].astype(BF16) for entry in updates]
    return (
        r.layer_output,
        r.input_grad,
        *grads,
        *[entry[0] for entry in updates],
        *[entry[1] for entry in updates],
        *[entry[2] for entry in updates],
        *copies,
        gradient_norm,
    )


def solution(mesh):
    rows = P("dp", None)
    sets = (
        P(None, "dp", "mp"),
        P(("mp", "dp"), None),
        P("dp", "mp"),
        P(("mp", "dp"), None),
        P(None, "dp"),
    )
    form = local if mesh.shape["dp"] == 8 else local_steps
    return jax.shard_map(
        functools.partial(form, mesh.shape["dp"], mesh.shape["mp"]),
        mesh=mesh,
        in_specs=(rows, rows, rows) + sets * 3,
        out_specs=(rows, rows) + sets * 5 + (P(),),
        check_vma=False,
    )
```

```python
import functools
import math
from types import SimpleNamespace

import jax
import jax.numpy as jnp
from jax import lax
from jax.experimental import pallas as pl
from jax.experimental.pallas import tpu as pltpu
from jax.sharding import PartitionSpec as P

HEAD_DIM = 128
ADAM_STEP = 5
MAX_NORM = 8192


BETA_ONE = 0.9
BETA_TWO = 0.95
ADAM_EPSILON = 1e-08
WEIGHT_DECAY = 0.1
NORM_EPSILON = 1e-05
CLIP_EPSILON = 1e-06
LEARN_RATES = (0.01, 0.08, 0.012, 0.02, 0.3)
MASKED_SCORE = -1e30
SCALE = 1.0 / math.sqrt(HEAD_DIM)
F32 = jnp.float32
BF16 = jnp.bfloat16
ROWS_COLS = (((1,), (0,)), ((), ()))
COLS_COLS = (((1,), (1,)), ((), ()))
ROWS_ROWS = (((0,), (0,)), ((), ()))


def mul(left, right, dims=ROWS_COLS):
    return lax.dot_general(left, right, dims, preferred_element_type=F32)


def layer_norm(values, gain_row, shift_row):
    row_mean = jnp.mean(values, axis=-1, keepdims=True)
    centered = values - row_mean
    spread = jnp.mean(centered * centered, axis=-1, keepdims=True)
    return centered * lax.rsqrt(spread + NORM_EPSILON) * gain_row + shift_row


def gelu_tanh(values):
    return jax.nn.gelu(values, approximate=True)


def adam_update(weight, grad, first, second, rate, clip_factor):
    clipped = grad * clip_factor
    new_first = BETA_ONE * first + (1.0 - BETA_ONE) * clipped
    new_second = BETA_TWO * second + (1.0 - BETA_TWO) * clipped * clipped
    first_hat = new_first / (1.0 - BETA_ONE**ADAM_STEP)
    second_hat = new_second / (1.0 - BETA_TWO**ADAM_STEP)
    new_weight = weight - rate * (
        first_hat / (jnp.sqrt(second_hat) + ADAM_EPSILON) + WEIGHT_DECAY * weight
    )
    return (new_first, new_second, new_weight)


PAIR, PLANE, COLUMN, CROSS, ROW, ALL = ("pair", "plane", "column", "cross", "row", "all")


class Group:
    def __init__(self, kind, dp_size, mp_size):
        self.kind = kind
        self.mp_size = mp_size
        chips = dp_size // 2
        self.size = {
            PAIR: 2,
            PLANE: chips,
            COLUMN: mp_size,
            CROSS: chips * mp_size,
            ROW: dp_size,
            ALL: dp_size * mp_size,
        }[kind]

    def me(self):
        dp, mp = lax.axis_index("dp"), lax.axis_index("mp")
        if self.kind == PAIR:
            return lax.rem(dp, 2)
        if self.kind == PLANE:
            return lax.div(dp, 2)
        if self.kind == COLUMN:
            return mp
        if self.kind == CROSS:
            return lax.div(dp, 2) * self.mp_size + mp
        if self.kind == ROW:
            return dp
        return dp * self.mp_size + mp

    def device(self, member):
        dp, mp = lax.axis_index("dp"), lax.axis_index("mp")
        core = lax.rem(dp, 2)
        if self.kind == PAIR:
            return (dp - core + member, mp)
        if self.kind == PLANE:
            return (member * 2 + core, mp)
        if self.kind == COLUMN:
            return (dp, member)
        if self.kind == CROSS:
            return (lax.div(member, self.mp_size) * 2 + core, lax.rem(member, self.mp_size))
        if self.kind == ROW:
            return (member, mp)
        return (lax.div(member, self.mp_size), lax.rem(member, self.mp_size))


def repeat(low, high, body):
    if high - low <= 8:
        for step in range(low, high):
            body(step)
    else:
        lax.fori_loop(low, high, lambda step, none: (body(step), none)[1], None)


def exchange(group, operands, results, moves, collective_id):
    count = len(operands)
    size = group.size
    lanes = len(moves)

    def kernel(*refs):
        ins, outs = refs[:count], refs[count : count + len(results)]
        send_sems, recv_sems, own_sems = refs[count + len(results) :]
        me = group.me()
        barrier = pltpu.get_barrier_semaphore()

        def greet(step):
            other = lax.rem(me + step, size)
            pl.semaphore_signal(
                barrier, inc=1, device_id=group.device(other), device_id_type=pl.DeviceIdType.MESH
            )

        repeat(1, size, greet)
        pl.semaphore_wait(barrier, size - 1)

        def remote(move, lane, step, sender, target, device):
            return pltpu.make_async_remote_copy(
                src_ref=move(ins, outs, me, target)[0],
                dst_ref=move(ins, outs, sender, me)[1],
                send_sem=send_sems.at[lane, step],
                recv_sem=recv_sems.at[lane, step],
                device_id=group.device(device),
                device_id_type=pl.DeviceIdType.MESH,
            )

        def launch(step):
            other = lax.rem(me + step, size)
            for lane, move in enumerate(moves):
                remote(move, lane, step, me, other, other).start()

        repeat(1, size, launch)
        own = []
        for lane, move in enumerate(moves):
            source, target = move(ins, outs, me, me)
            own.append(pltpu.make_async_copy(source, target, own_sems.at[lane]))
            own[-1].start()

        def finish(step):
            other = lax.rem(me + step, size)
            sender = lax.rem(me + size - step, size)
            for lane, move in enumerate(moves):
                remote(move, lane, step, sender, other, other).wait()

        repeat(1, size, finish)
        for copy in own:
            copy.wait()

    any_space = pl.BlockSpec(memory_space=pl.ANY)
    return pl.pallas_call(
        kernel,
        out_shape=results,
        in_specs=[any_space] * count,
        out_specs=[any_space] * len(results),
        scratch_shapes=[
            pltpu.SemaphoreType.DMA((lanes, size)),
            pltpu.SemaphoreType.DMA((lanes, size)),
            pltpu.SemaphoreType.DMA((lanes,)),
        ],
        compiler_params=pltpu.CompilerParams(collective_id=collective_id, has_side_effects=True),
    )(*operands)


def shape(dims, dtype=BF16):
    return jax.ShapeDtypeStruct(dims, dtype)


def part(index, width):
    return pl.ds(pl.multiple_of(index * width, width), width)


def allowed_pairs(seg_row, seg_col, length):
    places = lax.broadcasted_iota(jnp.int32, (length, length), 0)
    keys = lax.broadcasted_iota(jnp.int32, (length, length), 1)
    return (seg_col[...] == seg_row[...]) & (keys <= places)


def probabilities(query, key, allowed):
    scores = jnp.where(allowed, mul(query, key, COLS_COLS) * SCALE, MASKED_SCORE)
    exponent = jnp.exp(scores - jnp.max(scores, axis=-1, keepdims=True))
    return exponent / jnp.sum(exponent, axis=-1, keepdims=True)


def attend_kernel(width, joint, seg_row, seg_col, out_weight, attended, partial):
    allowed = allowed_pairs(seg_row, seg_col, joint.shape[0])
    for start in range(0, width, HEAD_DIM):
        head = pl.ds(start, HEAD_DIM)
        query, key, value = (joint[:, pl.ds(c * width + start, HEAD_DIM)] for c in range(3))
        prob = probabilities(query, key, allowed)
        attended[:, head] = mul(prob.astype(BF16), value).astype(BF16)
    partial[...] = mul(attended[...], out_weight[...]).astype(BF16)


def attend_back_kernel(
    width, joint, seg_row, seg_col, out_weight, attended, branch, d_joint, grad_out, d_attended
):
    allowed = allowed_pairs(seg_row, seg_col, joint.shape[0])
    d_attended[...] = mul(branch[...], out_weight[...], COLS_COLS).astype(BF16)
    for start in range(0, width, HEAD_DIM):
        query, key, value = (joint[:, pl.ds(c * width + start, HEAD_DIM)] for c in range(3))
        d_out = d_attended[:, pl.ds(start, HEAD_DIM)]
        prob = probabilities(query, key, allowed)
        d_joint[:, pl.ds(2 * width + start, HEAD_DIM)] = mul(
            prob.astype(BF16), d_out, ROWS_ROWS
        ).astype(BF16)
        d_prob = mul(d_out, value, COLS_COLS)
        row_delta = jnp.sum(d_prob * prob, axis=-1, keepdims=True)
        d_raw = (prob * (d_prob - row_delta) * SCALE).astype(BF16)
        d_joint[:, pl.ds(start, HEAD_DIM)] = mul(d_raw, key).astype(BF16)
        d_joint[:, pl.ds(width + start, HEAD_DIM)] = mul(d_raw, query, ROWS_ROWS).astype(BF16)
    grad_out[...] = mul(attended[...], branch[...], ROWS_ROWS).astype(BF16)


def local_steps(
    dp_size,
    mp_size,
    inputs,
    segment_ids,
    cotangent,
    query_key_value,
    attention_out,
    expand_weight,
    contract_weight,
    norm_params,
    first_query_key_value,
    first_attention_out,
    first_expand_weight,
    first_contract_weight,
    first_norm_params,
    second_query_key_value,
    second_attention_out,
    second_expand_weight,
    second_contract_weight,
    second_norm_params,
):
    params = (query_key_value, attention_out, expand_weight, contract_weight, norm_params)
    firsts = (
        first_query_key_value,
        first_attention_out,
        first_expand_weight,
        first_contract_weight,
        first_norm_params,
    )
    seconds = (
        second_query_key_value,
        second_attention_out,
        second_expand_weight,
        second_contract_weight,
        second_norm_params,
    )
    chips = dp_size // 2
    pair, plane, column, cross, row, everyone = (
        Group(kind, dp_size, mp_size)
        for kind in (PAIR, PLANE, COLUMN, CROSS, ROW, ALL)
    )
    dp, mp = lax.axis_index("dp"), lax.axis_index("mp")
    core = dp % 2
    length, model = inputs.shape
    width = query_key_value.shape[2]
    shard = query_key_value.shape[1]
    slab = 2 * shard
    hidden_units = expand_weight.shape[1]
    own_units = contract_weight.shape[0]
    units = 2 * own_units
    out_rows = attention_out.shape[0]
    strip = length // mp_size
    tokens = chips * length

    (norm_all,) = exchange(
        row,
        [norm_params],
        [shape((dp_size, 4, shard), F32)],
        [lambda ins, outs, me, other: (ins[0], outs[0].at[me])],
        0,
    )
    norm_weights = jnp.swapaxes(norm_all.astype(BF16).astype(F32), 0, 1).reshape(4, model)

    def shared(column_block):
        def move(ins, outs, me, other):
            return (ins[0].at[column_block], outs[0].at[part(me, shard), pl.ds(column_block * width, width)])

        return move

    joint_weight, expand_pair, contract_pair = exchange(
        pair,
        [query_key_value.astype(BF16), expand_weight.astype(BF16), contract_weight.astype(BF16)],
        [shape((slab, 3 * width)), shape((slab, hidden_units)), shape((units, model))],
        [
            shared(0),
            shared(1),
            shared(2),
            lambda ins, outs, me, other: (ins[1], outs[1].at[part(me, shard), :]),
            lambda ins, outs, me, other: (ins[2], outs[2].at[part(me, own_units), :]),
        ],
        1,
    )
    (output_all,) = exchange(
        row,
        [attention_out.astype(BF16)],
        [shape((dp_size * out_rows, model))],
        [lambda ins, outs, me, other: (ins[0], outs[0].at[part(me, out_rows), :])],
        2,
    )
    (grad_rows,) = exchange(
        plane,
        [cotangent],
        [shape((chips, length, model))],
        [lambda ins, outs, me, other: (ins[0], outs[0].at[me])],
        3,
    )
    grad_rows = grad_rows.reshape(tokens, model)

    values = inputs.astype(F32)
    normed = layer_norm(values, norm_weights[0], norm_weights[1]).astype(BF16)
    (normed_low,) = exchange(
        plane,
        [normed],
        [shape((chips, length, slab))],
        [lambda ins, outs, me, other: (ins[0].at[:, part(other, slab)], outs[0].at[me])],
        4,
    )
    normed_low = normed_low.reshape(tokens, slab)
    joint_part = mul(normed_low, joint_weight).astype(BF16).reshape(chips, length, 3 * width)
    (joint_parts,) = exchange(
        plane,
        [joint_part],
        [shape((chips, length, 3 * width))],
        [lambda ins, outs, me, other: (ins[0].at[other], outs[0].at[me])],
        5,
    )
    joint = jnp.sum(joint_parts.astype(F32), axis=0).astype(BF16)

    seg_row = segment_ids
    seg_col = segment_ids.reshape(length, 1)
    attended, branch_part = pl.pallas_call(
        functools.partial(attend_kernel, width),
        out_shape=[shape((length, width)), shape((length, model))],
        compiler_params=pltpu.CompilerParams(vmem_limit_bytes=48 * 2**20),
    )(joint, seg_row, seg_col, output_all)

    (branch_parts,) = exchange(
        column,
        [branch_part.reshape(mp_size, strip, model)],
        [shape((mp_size, strip, model))],
        [lambda ins, outs, me, other: (ins[0].at[other], outs[0].at[me])],
        6,
    )
    own_values = lax.dynamic_slice_in_dim(values, mp * strip, strip, 0)
    hidden = own_values + jnp.sum(branch_parts.astype(F32), axis=0)
    normed_two, pull_two = jax.vjp(layer_norm, hidden, norm_weights[2], norm_weights[3])
    (second_low,) = exchange(
        cross,
        [normed_two.astype(BF16)],
        [shape((chips * mp_size, strip, slab))],
        [
            lambda ins, outs, me, other: (
                ins[0].at[:, part(lax.div(other, mp_size), slab)],
                outs[0].at[me],
            )
        ],
        7,
    )
    second_low = second_low.reshape(tokens, slab)
    pre_part = mul(second_low, expand_pair).astype(BF16)
    (pre_parts,) = exchange(
        plane,
        [pre_part],
        [shape((chips, tokens, units))],
        [lambda ins, outs, me, other: (ins[0].at[:, part(other, units)], outs[0].at[me])],
        8,
    )
    pre_gelu = jnp.sum(pre_parts.astype(F32), axis=0)
    activated, pull_gelu = jax.vjp(gelu_tanh, pre_gelu)
    activated_low = activated.astype(BF16)
    d_activated = mul(grad_rows, contract_pair, COLS_COLS)
    (d_pre,) = pull_gelu(d_activated)
    (d_pre_all,) = exchange(
        plane,
        [d_pre.astype(BF16)],
        [shape((tokens, hidden_units))],
        [lambda ins, outs, me, other: (ins[0], outs[0].at[:, part(me, units)])],
        9,
    )

    def scatter_rows(partial, collective_id):
        (blocks,) = exchange(
            cross,
            [partial.reshape(chips * mp_size, strip, slab)],
            [shape((chips * mp_size, strip, slab))],
            [lambda ins, outs, me, other: (ins[0].at[other], outs[0].at[me])],
            collective_id,
        )
        total = jnp.sum(blocks.reshape(chips, mp_size, strip, slab).astype(F32), axis=1)
        return jnp.swapaxes(total, 0, 1).reshape(strip, model)

    d_normed_two = scatter_rows(mul(d_pre_all, expand_pair, COLS_COLS).astype(BF16), 10)
    d_hidden_norm, gain_two, shift_two = pull_two(d_normed_two)
    own_grad = lax.dynamic_slice_in_dim(cotangent, mp * strip, strip, 0).astype(F32)
    d_hidden = own_grad + d_hidden_norm

    def gather_rows(block, collective_id):
        (rows,) = exchange(
            column,
            [block],
            [shape((mp_size, strip, model))],
            [lambda ins, outs, me, other: (ins[0], outs[0].at[me])],
            collective_id,
        )
        return rows.reshape(length, model)

    branch_grad = gather_rows(d_hidden.astype(BF16), 11)
    d_joint, grad_output_part, _ = pl.pallas_call(
        functools.partial(attend_back_kernel, width),
        out_shape=[shape((length, 3 * width)), shape((width, model)), shape((length, width))],
        compiler_params=pltpu.CompilerParams(vmem_limit_bytes=48 * 2**20),
    )(joint, seg_row, seg_col, output_all, attended, branch_grad)
    (d_joint_all,) = exchange(
        plane,
        [d_joint],
        [shape((chips, length, 3 * width))],
        [lambda ins, outs, me, other: (ins[0], outs[0].at[me])],
        12,
    )
    d_joint_all = d_joint_all.reshape(tokens, 3 * width)
    d_normed_one = scatter_rows(mul(d_joint_all, joint_weight, COLS_COLS).astype(BF16), 13)
    _, pull_one = jax.vjp(layer_norm, own_values, norm_weights[0], norm_weights[1])
    d_values_norm, gain_one, shift_one = pull_one(d_normed_one)
    input_grad = gather_rows((d_hidden + d_values_norm).astype(BF16), 14).astype(F32)

    out_part = mul(activated_low, contract_pair).astype(BF16).reshape(chips, length, model)
    (out_parts,) = exchange(
        plane,
        [out_part],
        [shape((chips, length, model))],
        [lambda ins, outs, me, other: (ins[0].at[other], outs[0].at[me])],
        15,
    )
    out_rows_sum = jnp.sum(out_parts.astype(F32), axis=0).astype(BF16)
    (out_strips,) = exchange(
        column,
        [out_rows_sum.reshape(mp_size, strip, model)],
        [shape((mp_size, strip, model))],
        [lambda ins, outs, me, other: (ins[0].at[other], outs[0].at[me])],
        16,
    )
    layer_output = gather_rows(
        (hidden + jnp.sum(out_strips.astype(F32), axis=0)).astype(BF16), 17
    )

    (grad_output_parts,) = exchange(
        row,
        [grad_output_part.reshape(dp_size, out_rows, model)],
        [shape((dp_size, out_rows, model))],
        [lambda ins, outs, me, other: (ins[0].at[other], outs[0].at[me])],
        18,
    )
    reduced_output = jnp.sum(grad_output_parts.astype(F32), axis=0)
    own_joint, other_joint = [], []
    grad_joint = mul(normed_low, d_joint_all, ROWS_ROWS)
    grad_expand = mul(second_low, d_pre_all, ROWS_ROWS)
    grad_contract = mul(activated_low, grad_rows, ROWS_ROWS)

    def halves(array, index):
        return lax.dynamic_slice_in_dim(array, index * (array.shape[0] // 2), array.shape[0] // 2, 0)

    pieces = (grad_joint, grad_expand, grad_contract)
    sent = [halves(entry, 1 - core).astype(BF16) for entry in pieces]
    got = exchange_pair(pair, sent, 19)
    reduced_joint, reduced_expand, reduced_contract = (
        halves(entry, core) + other.astype(F32) for entry, other in zip(pieces, got)
    )
    reduced_joint = jnp.swapaxes(reduced_joint.reshape(shard, 3, width), 0, 1)

    zero_row = jnp.zeros((model,), F32)
    norm_rows = jnp.stack([gain_one, shift_one, gain_two, shift_two] + [zero_row] * 4)
    norm_rows = jnp.swapaxes(norm_rows.reshape(8, dp_size, shard), 0, 1)
    (norm_parts,) = exchange(
        everyone,
        [norm_rows],
        [shape((dp_size * mp_size, 8, shard), F32)],
        [
            lambda ins, outs, me, other: (
                ins[0].at[lax.div(other, mp_size)],
                outs[0].at[me],
            )
        ],
        20,
    )
    reduced_norms = jnp.sum(norm_parts, axis=0)[:4]

    grads = (reduced_joint, reduced_output, reduced_expand, reduced_contract, reduced_norms)
    squares = sum((jnp.sum(entry * entry) for entry in grads[:4])) + jnp.sum(
        reduced_norms * reduced_norms
    ) / mp_size
    (square_parts,) = exchange(
        everyone,
        [jnp.full((8, 128), squares, F32)],
        [shape((dp_size * mp_size, 8, 128), F32)],
        [lambda ins, outs, me, other: (ins[0], outs[0].at[me])],
        21,
    )
    gradient_norm = jnp.sqrt(jnp.sum(square_parts[:, 0, 0]))
    clip_factor = jnp.minimum(1.0, MAX_NORM / (gradient_norm + CLIP_EPSILON))
    updates = [
        adam_update(params[k], grads[k], firsts[k], seconds[k], LEARN_RATES[k], clip_factor)
        for k in range(5)
    ]
    copies = [entry[2].astype(BF16) for entry in updates]
    return (
        layer_output,
        input_grad,
        *grads,
        *[entry[0] for entry in updates],
        *[entry[1] for entry in updates],
        *[entry[2] for entry in updates],
        *copies,
        gradient_norm,
    )


def exchange_pair(pair, sent, collective_id):
    moves = [
        lambda ins, outs, me, other, lane=lane: (ins[lane], outs[lane]) for lane in range(len(sent))
    ]
    return swap(pair, sent, moves, collective_id)


def swap(pair, sent, moves, collective_id):
    count = len(sent)

    def kernel(*refs):
        ins, outs = refs[:count], refs[count : 2 * count]
        send_sems, recv_sems = refs[2 * count :]
        other = pair.device(1 - pair.me())
        barrier = pltpu.get_barrier_semaphore()
        pl.semaphore_signal(barrier, inc=1, device_id=other, device_id_type=pl.DeviceIdType.MESH)
        pl.semaphore_wait(barrier, 1)
        copies = [
            pltpu.make_async_remote_copy(
                src_ref=ins[lane],
                dst_ref=outs[lane],
                send_sem=send_sems.at[lane],
                recv_sem=recv_sems.at[lane],
                device_id=other,
                device_id_type=pl.DeviceIdType.MESH,
            )
            for lane in range(count)
        ]
        for copy in copies:
            copy.start()
        for copy in copies:
            copy.wait()

    any_space = pl.BlockSpec(memory_space=pl.ANY)
    return pl.pallas_call(
        kernel,
        out_shape=[shape(entry.shape, entry.dtype) for entry in sent],
        in_specs=[any_space] * count,
        out_specs=[any_space] * count,
        scratch_shapes=[pltpu.SemaphoreType.DMA((count,)), pltpu.SemaphoreType.DMA((count,))],
        compiler_params=pltpu.CompilerParams(collective_id=collective_id, has_side_effects=True),
    )(*sent)


class Lane:
    def __init__(self, group, me, sems, view, bulk=None):
        self.group, self.me, self.view, self.bulk = group, me, view, bulk
        self.sems = sems
        self.size = group.size

    def remote(self, source, target, step):
        index = step - 1 if self.bulk is None else 0
        return pltpu.make_async_remote_copy(
            src_ref=source,
            dst_ref=target,
            send_sem=self.sems[0].at[index],
            recv_sem=self.sems[1].at[index],
            device_id=self.group.device(lax.rem(self.me + step, self.size)),
            device_id_type=pl.DeviceIdType.MESH,
        )

    def copy(self, step):
        return self.remote(*self.view(self.me, lax.rem(self.me + step, self.size)), step)

    def start(self, step):
        self.copy(step).start()

    def start_all(self):
        repeat(1, self.size, self.start)

    def source(self, step):
        return lax.rem(self.me + self.size - step, self.size)

    def take(self, step):
        to = lax.rem(self.me + step, self.size)
        source, target = self.view(self.me, to)[0], self.view(self.source(step), self.me)[1]
        self.remote(source, target, step).wait_recv()

    def take_all(self):
        if self.bulk is None:
            repeat(1, self.size, self.take)
        else:
            self.remote(self.bulk, self.bulk, 1).wait_recv()

    def sent_all(self):
        if self.bulk is None:
            repeat(1, self.size, lambda step: self.copy(step).wait_send())
        else:
            self.remote(self.bulk, self.bulk, 1).wait_send()


class Hop:
    def __init__(self, dp, mp):
        core, self.me = lax.rem(dp, 2), lax.div(dp, 2)
        x_next = self.me + 1 - 2 * lax.rem(self.me, 2)
        self.chips = (x_next, lax.rem(self.me + 2, 4))
        self.far = 3 - self.me
        self.devices = tuple((chip * 2 + core, mp) for chip in self.chips)

    def copy(self, source, target, sems, index, way):
        return pltpu.make_async_remote_copy(
            src_ref=source,
            dst_ref=target,
            send_sem=sems[0].at[index],
            recv_sem=sems[1].at[index],
            device_id=self.devices[way],
            device_id_type=pl.DeviceIdType.MESH,
        )


class PlaneGather:
    def __init__(self, hop, sems, own, block, half):
        self.hop, self.sems, self.own, self.block, self.half = hop, sems, own, block, half

    def first(self, way):
        return self.hop.copy(self.own, self.block(self.hop.me), self.sems, way, way)

    def second(self, way):
        piece = self.half(self.block(self.hop.chips[way]), way)
        return self.hop.copy(piece, piece, self.sems, 2 + way, 1 - way)

    def start(self):
        for way in range(2):
            self.first(way).start()

    def near(self, way):
        near = self.block(self.hop.chips[way])
        self.hop.copy(near, near, self.sems, way, way).wait_recv()

    def forward(self):
        for way in range(2):
            self.near(way)
            self.second(way).start()

    def finish(self):
        for way in range(2):
            piece = self.half(self.block(self.hop.far), way)
            self.hop.copy(piece, piece, self.sems, 2 + way, 1 - way).wait_recv()

    def sent_all(self):
        for way in range(2):
            self.first(way).wait_send()
            self.second(way).wait_send()


class PlaneReduce:
    def __init__(self, hop, sems, parts, inbox, middle):
        self.hop, self.sems = hop, sems
        self.parts, self.inbox, self.middle = parts, inbox, middle

    def copy(self, stage, way):
        hop = self.hop
        chip = (hop.far, hop.chips[way])[stage] if stage < 2 else None
        source = self.parts.at[chip, way] if stage < 2 else self.middle.at[way]
        along = way if stage < 2 else 1 - way
        return hop.copy(source, self.inbox.at[stage, way], self.sems, 2 * stage + way, along)

    def start(self, stage):
        for way in range(2):
            self.copy(stage, way).start()

    def forward(self):
        for way in range(2):
            self.copy(0, way).wait_recv()
            onward = self.hop.chips[1 - way]
            total = self.parts[onward, way].astype(F32) + self.inbox[0, way].astype(F32)
            self.middle[way] = total.astype(BF16)
            self.copy(2, way).start()

    def take(self, way):
        self.copy(1, way).wait_recv()
        self.copy(2, way).wait_recv()

    def total(self, way, rows=slice(None)):
        own = self.parts[self.hop.me, way, rows].astype(F32)
        near = self.inbox[1, way, rows].astype(F32)
        return own + near + self.inbox[2, way, rows].astype(F32)

    def sent_all(self):
        for stage in range(3):
            for way in range(2):
                self.copy(stage, way).wait_send()


def standardise(values):
    row_mean = jnp.mean(values, axis=-1, keepdims=True)
    centered = values - row_mean
    spread = jnp.mean(centered * centered, axis=-1, keepdims=True)
    return centered, lax.rsqrt(spread + NORM_EPSILON)


def norm_back(grad, values, gain_row):
    centered, inverse = standardise(values)
    unit = centered * inverse
    scaled = grad * gain_row
    inner = jnp.mean(scaled * unit, axis=-1, keepdims=True)
    back = inverse * (scaled - jnp.mean(scaled, axis=-1, keepdims=True) - unit * inner)
    gain_grad = jnp.sum(grad * unit, axis=0, keepdims=True)
    shift_grad = jnp.sum(grad, axis=0, keepdims=True)
    return back, gain_grad, shift_grad


ROOT = math.sqrt(2.0 / math.pi)
CUBE = 0.044715

LANES = dict(
    norms=ROW,
    normed=PLANE,
    joint_weight=PAIR,
    out_own=PAIR,
    expand=PAIR,
    contract=PAIR,
    branch=COLUMN,
    second=CROSS,
    g_contract=PAIR,
    d_second=CROSS,
    g_expand=PAIR,
    d_hidden=COLUMN,
    g_out_pair=PAIR,
    out_strip=COLUMN,
    d_first=CROSS,
    g_joint=PAIR,
    in_rows=COLUMN,
    g_norms=CROSS,
    g_norms_pair=PAIR,
    squares=CROSS,
    squares_pair=PAIR,
)

STEPWISE = dict(normed=True)
HALVED = dict(branch=2, second=2, d_second=2, d_hidden=2)


def layer(dp_size, mp_size, operands):
    x, segments, cotangent, joint_w, out_w, expand_w, contract_w, norms = operands
    chips = dp_size // 2
    groups = SimpleNamespace(
        **{kind: Group(kind, dp_size, mp_size) for kind in (PAIR, PLANE, COLUMN, CROSS, ROW)}
    )
    length, model = x.shape
    width, shard = joint_w.shape[2], joint_w.shape[1]
    slab = 2 * shard
    hidden = expand_w.shape[1]
    own_units = contract_w.shape[0]
    units = 2 * own_units
    out_rows = out_w.shape[0]
    strip = length // mp_size
    tokens = chips * length
    half_strip = strip // 2
    half_rows = length // 2
    half_tokens = tokens // 2
    pieces = max(1, width // (2 * HEAD_DIM))
    piece = width // pieces

    outs = dict(
        out_mine=shape((strip, model)),
        grad_rows=shape((mp_size, strip, model)),
        own_norms=shape((4, shard), F32),
        square_sum=shape((1, 1), F32),
    )
    homes = dict(
        home_joint=shape((3, shard, width), F32),
        home_out=shape((out_rows, model), F32),
        home_expand=shape((shard, hidden), F32),
        home_contract=shape((own_units, model), F32),
        home_far_joint=shape((3, shard, width)),
        home_far_out=shape((out_rows, model)),
        home_far_expand=shape((shard, hidden)),
        home_far_contract=shape((own_units, model)),
    )
    scratch = dict(
        own_joint=((3, shard, width), F32),
        own_out=((out_rows, model), F32),
        own_expand=((shard, hidden), F32),
        own_contract=((own_units, model), F32),
        far_joint=((3, shard, width), BF16),
        far_out=((out_rows, model), BF16),
        far_expand=((shard, hidden), BF16),
        far_contract=((own_units, model), BF16),
        norm_all=((dp_size, 4, shard), F32),
        a_mine=((chips, length, slab), BF16),
        a_all=((chips, length, slab), BF16),
        wq=((3, slab, width), BF16),
        wo=((dp_size, out_rows, model), BF16),
        wu=((chips, slab, units), BF16),
        wd=((units, model), BF16),
        j_send=((pieces, chips, 2, length // 2, 3 * piece), BF16),
        j_recv=((pieces, 3, 2, length // 2, 3 * piece), BF16),
        j_mid=((pieces, 2, length // 2, 3 * piece), BF16),
        joint=((pieces, length, 3 * piece), BF16),
        dy_mine=((2, half_rows, model), BF16),
        dy_all=((chips, 2, half_rows, model), BF16),
        attended=((length, width), BF16),
        b_send=((2, mp_size, half_strip, model), BF16),
        b_recv=((2, mp_size, half_strip, model), BF16),
        hid=((2, half_strip, model), F32),
        bulk=(((chips * mp_size - 1) * strip, slab), BF16),
        c_mine=((2, chips, half_strip, slab), BF16),
        c_all=((2, chips, mp_size, half_strip, slab), BF16),
        u_send=((2, chips, 2, tokens // 4, units), BF16),
        u_recv=((2, 3, 2, tokens // 4, units), BF16),
        u_mid=((2, 2, tokens // 4, units), BF16),
        dz=((2, half_tokens, units), F32),
        z=((2, half_tokens, units), BF16),
        du_all=((2, chips, half_tokens, units), BF16),
        y_send=((chips, 2, length // 2, model), BF16),
        y_recv=((3, 2, length // 2, model), BF16),
        y_mid=((2, length // 2, model), BF16),
        gc_send=((own_units, model), BF16),
        dc_send=((2, chips, mp_size, half_strip, slab), BF16),
        dc_recv=((2, chips, mp_size, half_strip, slab), BF16),
        ge_send=((shard, hidden), BF16),
        dh=((2, half_strip, model), F32),
        da_mine=((2, half_strip, model), BF16),
        da_rows=((mp_size, 2, half_strip, model), BF16),
        dq_mine=((pieces, length, 3 * piece), BF16),
        dq_all=((pieces, chips, length, 3 * piece), BF16),
        go_pair=((2, out_rows, model), BF16),
        y2_send=((mp_size, strip, model), BF16),
        y2_recv=((mp_size, strip, model), BF16),
        df_send=((chips, mp_size, strip, slab), BF16),
        df_recv=((chips, mp_size, strip, slab), BF16),
        gj_send=((3, shard, width), BF16),
        ig_mine=((strip, model), BF16),
        gn_send=((chips, 8, shard), F32),
        gn_recv=((chips * mp_size, 8, shard), F32),
        gn_pair=((8, shard), F32),
        gn_far=((8, shard), F32),
        sq_mine=((8, 128), F32),
        sq_recv=((chips * mp_size, 8, 128), F32),
        sq_pair=((8, 128), F32),
        sq_far=((8, 128), F32),
    )
    in_names = dict(
        x=0, seg_row=1, cot=2, f_joint=3, f_out=4, f_expand=5, f_contract=6, norm_own=7
    )
    names = list(in_names) + list(outs) + list(homes) + list(scratch)

    def kernel(*refs):
        r = SimpleNamespace(**dict(zip(names, refs)))
        sems = refs[len(names) :]
        load_sems, home_sems = sems[:2]
        dp, mp = lax.axis_index("dp"), lax.axis_index("mp")
        core, chip = lax.rem(dp, 2), lax.div(dp, 2)
        mine, other = part(core, shard), part(1 - core, shard)
        cross_me = groups.cross.me()

        def flat(ref, columns=slice(None)):
            values = ref[(slice(None),) * (len(ref.shape) - 1) + (columns,)]
            return values.reshape(-1, values.shape[-1])

        views = dict(
            norms=lambda s, t: (r.norm_own, r.norm_all.at[s]),
            normed=lambda s, t: (r.a_mine.at[t], r.a_all.at[s]),
            joint_weight=lambda s, t: (
                r.wq.at[:, part(s, shard), :],
                r.wq.at[:, part(s, shard), :],
            ),
            out_own=lambda s, t: (r.wo.at[dp - core + s], r.wo.at[dp - core + s]),
            expand=lambda s, t: (
                r.wu.at[:, part(s, shard), :],
                r.wu.at[:, part(s, shard), :],
            ),
            contract=lambda s, t: (
                r.wd.at[part(s, own_units), :],
                r.wd.at[part(s, own_units), :],
            ),
            branch=[
                lambda s, t, h=h: (r.b_send.at[h, t], r.b_recv.at[h, s]) for h in range(2)
            ],
            second=[
                lambda s, t, h=h: (
                    r.c_mine.at[h, lax.div(t, mp_size)],
                    r.c_all.at[h, lax.div(s, mp_size), lax.rem(s, mp_size)],
                )
                for h in range(2)
            ],
            g_contract=lambda s, t: (r.gc_send, r.far_contract),
            d_second=[
                lambda s, t, h=h: (
                    r.dc_send.at[h, lax.div(t, mp_size), lax.rem(t, mp_size)],
                    r.dc_recv.at[h, lax.div(s, mp_size), lax.rem(s, mp_size)],
                )
                for h in range(2)
            ],
            g_expand=lambda s, t: (r.ge_send, r.far_expand),
            d_hidden=[
                lambda s, t, h=h: (r.da_mine.at[h], r.da_rows.at[s, h]) for h in range(2)
            ],
            g_out_pair=lambda s, t: (r.go_pair.at[t], r.far_out),
            out_strip=lambda s, t: (r.y2_send.at[t], r.y2_recv.at[s]),
            d_first=lambda s, t: (
                r.df_send.at[lax.div(t, mp_size), lax.rem(t, mp_size)],
                r.df_recv.at[lax.div(s, mp_size), lax.rem(s, mp_size)],
            ),
            g_joint=lambda s, t: (r.gj_send, r.far_joint),
            in_rows=lambda s, t: (r.ig_mine, r.grad_rows.at[s]),
            g_norms=lambda s, t: (r.gn_send.at[lax.div(t, mp_size)], r.gn_recv.at[s]),
            g_norms_pair=lambda s, t: (r.gn_pair, r.gn_far),
            squares=lambda s, t: (r.sq_mine, r.sq_recv.at[s]),
            squares_pair=lambda s, t: (r.sq_pair, r.sq_far),
        )
        others = chips * mp_size - 1
        column_blocks = pl.ds(0, mp_size - 1)
        bulks = dict(
            norms=r.norm_all.at[pl.ds(0, dp_size - 1)],
            branch=[r.b_recv.at[h, column_blocks] for h in range(2)],
            second=[r.bulk.at[pl.ds(0, others * half_strip), :]] * 2,
            d_second=[r.bulk.at[pl.ds(0, others * half_strip), :]] * 2,
            d_hidden=[r.da_rows.at[column_blocks, h] for h in range(2)],
            out_strip=r.y2_recv.at[column_blocks],
            d_first=r.bulk,
            in_rows=r.grad_rows.at[column_blocks],
            g_norms=r.gn_recv.at[pl.ds(0, others)],
            squares=r.sq_recv.at[pl.ds(0, others)],
        )
        lane = SimpleNamespace()
        every_lane = []
        used = iter(sems[2:])

        def pair_of():
            return (next(used), next(used))

        for name, kind in LANES.items():
            group = vars(groups)[kind]
            several = name in HALVED
            bulk = bulks.get(name, None)
            lanes = [
                Lane(group, group.me(), pair_of(), view, one)
                for view, one in (
                    zip(views[name], bulk) if several else [(views[name], bulk)]
                )
            ]
            every_lane += lanes
            setattr(lane, name, lanes if several else lanes[0])
        hop = Hop(dp, mp)

        def gather(own, block, half):
            every_lane.append(PlaneGather(hop, pair_of(), own, block, half))
            return every_lane[-1]

        def reduce(parts, inbox, middle):
            every_lane.append(PlaneReduce(hop, pair_of(), parts, inbox, middle))
            return every_lane[-1]

        def row_half(ref, way):
            rows = ref.shape[0] // 2
            return ref.at[pl.ds(way * rows, rows), :]

        out_plane = gather(r.wo.at[dp], lambda c: r.wo.at[2 * c + core], row_half)
        cot_plane = gather(r.dy_mine, lambda c: r.dy_all.at[c], lambda ref, way: ref.at[way])
        d_pre = [
            gather(r.du_all.at[h, chip], lambda c, h=h: r.du_all.at[h, c], row_half)
            for h in range(2)
        ]
        d_joint = [
            gather(r.dq_mine.at[p], lambda c, p=p: r.dq_all.at[p, c], row_half)
            for p in range(pieces)
        ]
        joint = [reduce(r.j_send.at[p], r.j_recv.at[p], r.j_mid.at[p]) for p in range(pieces)]
        pre_sum = [reduce(r.u_send.at[h], r.u_recv.at[h], r.u_mid.at[h]) for h in range(2)]
        out_sum = reduce(r.y_send, r.y_recv, r.y_mid)
        g_out_sum = reduce(r.y_send, r.y_recv, r.y_mid)
        pass_sems = pair_of()

        def passing(index, to_me):
            source = (*hop.chips, hop.far)[index]
            block = r.wo.at[2 * source + (1 - core if to_me else core)]
            return pltpu.make_async_remote_copy(
                src_ref=block,
                dst_ref=block,
                send_sem=pass_sems[0].at[index],
                recv_sem=pass_sems[1].at[index],
                device_id=(dp + 1 - 2 * core, mp),
                device_id_type=pl.DeviceIdType.MESH,
            )

        loads = [
            pltpu.make_async_copy(source, target, load_sems.at[i])
            for i, (source, target) in enumerate(
                (
                    (r.f_joint, r.own_joint),
                    (r.f_out, r.own_out),
                    (r.f_expand, r.own_expand),
                    (r.f_contract, r.own_contract),
                )
            )
        ]
        for load in (loads[1], loads[0], loads[2], loads[3]):
            load.start()

        leaving = []

        def send_home(index, source, target):
            leaving.append(pltpu.make_async_copy(source, target, home_sems.at[index]))
            leaving[-1].start()

        barrier = pltpu.get_barrier_semaphore()

        def greet(device):
            pl.semaphore_signal(
                barrier, inc=1, device_id=device, device_id_type=pl.DeviceIdType.MESH
            )

        cross = groups.cross
        repeat(1, cross.size, lambda s: greet(cross.device(lax.rem(cross_me + s, cross.size))))
        repeat(0, chips, lambda s: greet((s * 2 + 1 - core, mp)))

        r.norm_all[dp] = r.norm_own[...]
        loads[1].wait()
        r.wo[dp] = r.own_out[...].astype(BF16)
        values = r.x[...].astype(F32)
        centered, inverse = standardise(values)
        unit = centered * inverse
        loads[0].wait()
        for c in range(3):
            r.wq[c, mine, :] = r.own_joint[c].astype(BF16)
        ids = jnp.broadcast_to(r.seg_row[...].astype(F32), (length, length))
        places = lax.broadcasted_iota(jnp.int32, (length, length), 0)
        keys = lax.broadcasted_iota(jnp.int32, (length, length), 1)
        allowed = (ids == ids.T) & (keys <= places)
        pl.semaphore_wait(barrier, cross.size - 1 + chips)

        lane.norms.start_all()
        lane.joint_weight.start_all()
        out_plane.start()
        lane.out_own.start_all()
        lane.norms.take_all()

        def norm_row(index, block=None):
            blocks = range(dp_size) if block is None else (block,)
            rows = [r.norm_all[b, pl.ds(index, 1), :] for b in blocks]
            whole = rows[0] if len(rows) == 1 else jnp.concatenate(rows, axis=1)
            return whole.astype(BF16).astype(F32)

        for b in range(dp_size):
            columns = slice(b * shard, (b + 1) * shard)
            r.a_mine[b // 2, :, (b % 2) * shard : (b % 2 + 1) * shard] = (
                unit[:, columns] * norm_row(0, b) + norm_row(1, b)
            ).astype(BF16)
        lane.normed.start_all()
        r.a_all[chip] = r.a_mine[chip]

        lane.joint_weight.take_all()

        def joint_part(p, block):
            rows = r.a_all[block]
            for c in range(3):
                columns = slice(c * piece, (c + 1) * piece)
                third = mul(rows, r.wq[c, :, p * piece : (p + 1) * piece]).astype(BF16)
                for way in range(2):
                    r.j_send[p, block, way, :, columns] = third[
                        way * half_rows : (way + 1) * half_rows
                    ]

        def chip_step(block):
            return lax.rem(chip + chips - block, chips)

        for p in range(pieces):
            for way in range(2):
                if p == 0:
                    lane.normed.take(chip_step(hop.chips[way]))
                joint_part(p, hop.chips[way])
            joint[p].start(1)
            if p == 0:
                lane.normed.take(chip_step(hop.far))
            joint_part(p, hop.far)
            joint[p].start(0)
            joint_part(p, chip)
        for h in range(2):
            for m in range(mp_size):
                first = m * strip + h * half_strip
                r.dy_mine[h, m * half_strip : (m + 1) * half_strip, :] = r.cot[
                    first : first + half_strip, :
                ]
        out_plane.forward()
        for index in range(2):
            passing(index, False).start()
        for p in range(pieces):
            joint[p].forward()

        loads[2].wait()
        for c in range(chips):
            r.wu[c, mine, :] = r.own_expand[:, c * units : (c + 1) * units].astype(BF16)
        lane.expand.start_all()
        loads[3].wait()
        r.wd[part(core, own_units), :] = r.own_contract[...].astype(BF16)
        lane.contract.start_all()
        def query_key_value(start):
            p, first = start // piece, start % piece
            return (
                r.joint[p, :, c * piece + first : c * piece + first + HEAD_DIM] for c in range(3)
            )

        for p in range(pieces):
            for way in range(2):
                joint[p].take(way)
                r.joint[p, way * half_rows : (way + 1) * half_rows, :] = (
                    joint[p].total(way).astype(BF16)
                )
            if p == pieces - 1:
                cot_plane.start()
            for start in range(p * piece, (p + 1) * piece, HEAD_DIM):
                query, key, value = query_key_value(start)
                prob = probabilities(query, key, allowed)
                r.attended[:, start : start + HEAD_DIM] = mul(prob.astype(BF16), value).astype(BF16)

        lane.out_own.take_all()
        out_plane.finish()
        passing(2, False).start()
        for index in range(3):
            passing(index, True).wait_recv()
        branch = mul(r.attended[...], flat(r.wo)).astype(BF16)
        for h in range(2):
            for m in range(mp_size):
                first = m * strip + h * half_strip
                r.b_send[h, m] = branch[first : first + half_strip]
            lane.branch[h].start_all()
        r.dy_all[chip] = r.dy_mine[...]
        cot_plane.forward()

        def here(h):
            return pl.ds(pl.multiple_of(mp * strip + h * half_strip, half_strip), half_strip)

        for h in range(2):
            lane.branch[h].take_all()
            total = r.x[here(h), :].astype(F32) + r.b_send[h, mp].astype(F32)
            for step in range(1, mp_size):
                total = total + r.b_recv[h, lane.branch[h].source(step)].astype(F32)
            r.hid[h] = total
            centered, inverse = standardise(total)
            for b in range(dp_size):
                columns = slice(b * shard, (b + 1) * shard)
                r.c_mine[h, b // 2, :, (b % 2) * shard : (b % 2 + 1) * shard] = (
                    centered[:, columns] * inverse * norm_row(2, b) + norm_row(3, b)
                ).astype(BF16)
            lane.second[h].start_all()
            r.c_all[h, chip, mp] = r.c_mine[h, chip]
        lane.expand.take_all()

        def dy_half(h):
            return r.dy_all[:, h].reshape(half_tokens, model)

        quarter = half_tokens // 2

        def pre_part(h, to):
            part_sum = mul(flat(r.c_all.at[h]), r.wu[to]).astype(BF16)
            for way in range(2):
                r.u_send[h, to, way] = part_sum[way * quarter : (way + 1) * quarter]

        for h in range(2):
            lane.second[h].take_all()
            pre_part(h, hop.far)
            pre_sum[h].start(0)
            for way in range(2):
                pre_part(h, hop.chips[way])
            pre_sum[h].start(1)
            pre_part(h, chip)
            if h == 0:
                lane.contract.take_all()
                cot_plane.finish()
            r.dz[h] = mul(dy_half(h), r.wd[...], COLS_COLS)
            pre_sum[h].forward()
        tile = 64

        for h in range(2):
            for way in range(2):
                pre_sum[h].take(way)

                def gelu_tile(i, none, h=h, way=way):
                    rows = part(i, tile)
                    pre = pre_sum[h].total(way, rows)
                    square = pre * pre
                    curve = jnp.tanh(ROOT * pre * (1.0 + CUBE * square))
                    half = 0.5 * (1.0 + curve)
                    slope = half + 0.5 * pre * (1.0 - curve * curve) * (
                        ROOT * (1.0 + 3.0 * CUBE * square)
                    )
                    rows = part(i + way * (quarter // tile), tile)
                    r.z[h, rows, :] = (pre * half).astype(BF16)
                    r.du_all[h, chip, rows, :] = (r.dz[h, rows, :] * slope).astype(BF16)
                    return none

                lax.fori_loop(0, quarter // tile, gelu_tile, None)
            d_pre[h].start()

        def out_part(h):
            part_sum = mul(r.z[h], r.wd[...]).astype(BF16)
            for c in range(chips):
                r.y_send[c, h] = part_sum[c * half_rows : (c + 1) * half_rows]

        def second_part(h, source):
            return mul(r.du_all[h, source], r.wu[source], COLS_COLS)

        d_pre[0].forward()
        for h in range(2):
            out_part(h)
            total = second_part(h, chip)
            for way in range(2):
                total = total + second_part(h, hop.chips[way])
            if h == 0:
                d_pre[1].forward()
            d_pre[h].finish()
            total = (total + second_part(h, hop.far)).astype(BF16)
            for c in range(chips):
                for m in range(mp_size):
                    first = (c * mp_size + m) * half_strip
                    r.dc_send[h, c, m] = total[first : first + half_strip]
            lane.d_second[h].start_all()
        out_sum.start(0)
        out_sum.start(1)

        def contract_grad(columns):
            return sum(mul(r.z[h, :, columns], dy_half(h), ROWS_ROWS) for h in range(2))

        def gathered(recv, rows):
            blocks = []
            for c in range(chips):
                block = jnp.zeros((rows, slab), F32)
                for m in range(mp_size):
                    block = block + recv[c, m].astype(F32)
                blocks.append(block)
            return jnp.concatenate(blocks, axis=1)

        r.gc_send[...] = contract_grad(part(1 - core, own_units)).astype(BF16)
        lane.g_contract.start_all()
        gain_two, shift_two = 0.0, 0.0
        for h in range(2):
            lane.d_second[h].take_all()
            r.dc_recv[h, chip, mp] = r.dc_send[h, chip, mp]
            d_normed = gathered(r.dc_recv.at[h], half_strip)
            back, gain, shift = norm_back(d_normed, r.hid[h], norm_row(2))
            gain_two, shift_two = gain_two + gain, shift_two + shift
            d_hidden = r.cot[here(h), :].astype(F32) + back
            r.dh[h] = d_hidden
            r.da_mine[h] = d_hidden.astype(BF16)
            lane.d_hidden[h].start_all()
            r.da_rows[mp, h] = r.da_mine[h]
        out_sum.forward()
        for c in range(chips):
            r.ge_send[:, c * units : (c + 1) * units] = mul(
                flat(r.c_all, other), flat(r.du_all.at[:, c]), ROWS_ROWS
            ).astype(BF16)
        lane.g_expand.start_all()
        r.own_contract[...] = contract_grad(part(core, own_units))
        send_home(3, r.own_contract, r.home_contract)
        for h in range(2):
            lane.d_hidden[h].take_all()

        for way in range(2):
            out_sum.take(way)
            total = out_sum.total(way).astype(BF16)
            for m in range(mp_size):
                r.y2_send[m, way * half_strip : (way + 1) * half_strip, :] = total[
                    m * half_strip : (m + 1) * half_strip
                ]
        lane.out_strip.start_all()
        d_attended = mul(flat(r.da_rows), flat(r.wo), COLS_COLS).astype(BF16)
        for p in range(pieces):
            for start in range(p * piece, (p + 1) * piece, HEAD_DIM):
                query, key, value = query_key_value(start)
                d_out = d_attended[:, start : start + HEAD_DIM]
                prob = probabilities(query, key, allowed)
                d_prob = mul(d_out, value, COLS_COLS)
                row_delta = jnp.sum(d_prob * prob, axis=-1, keepdims=True)
                d_raw = (prob * (d_prob - row_delta) * SCALE).astype(BF16)
                thirds = (
                    mul(d_raw, key),
                    mul(d_raw, query, ROWS_ROWS),
                    mul(prob.astype(BF16), d_out, ROWS_ROWS),
                )
                for c in range(3):
                    first = c * piece + start % piece
                    r.dq_mine[p, :, first : first + HEAD_DIM] = thirds[c].astype(BF16)
            d_joint[p].start()
            r.dq_all[p, chip] = r.dq_mine[p]

        out_sum.sent_all()
        every_lane.remove(out_sum)
        grad_out = mul(r.attended[...], flat(r.da_rows), ROWS_ROWS).astype(BF16)
        for c in range(chips):
            for k in range(2):
                first = (2 * c + k) * out_rows
                r.y_send[c, k] = grad_out[first : first + out_rows]

        def first_block(block):
            total = jnp.zeros((length, slab), F32)
            for p in range(pieces):
                for c in range(3):
                    total = total + mul(
                        r.dq_all[p, block, :, c * piece : (c + 1) * piece],
                        r.wq[c, :, p * piece : (p + 1) * piece],
                        COLS_COLS,
                    )
            total = total.astype(BF16)
            for m in range(mp_size):
                r.df_send[block, m] = total[m * strip : (m + 1) * strip]

        def first_send(block, others):
            for j in others:
                to = block * mp_size + lax.rem(mp + j, mp_size)
                lane.d_first.start(lax.rem(to + cross.size - cross_me, cross.size))

        first_block(chip)
        first_send(chip, range(1, mp_size))
        for p in range(pieces):
            d_joint[p].forward()
        for way in range(2):
            first_block(hop.chips[way])
            first_send(hop.chips[way], range(mp_size))
        for p in range(pieces):
            d_joint[p].finish()
        first_block(hop.far)
        first_send(hop.far, range(mp_size))
        g_out_sum.start(0)
        g_out_sum.start(1)

        def joint_grad(c, columns, target):
            for p in range(pieces):
                target[c, :, p * piece : (p + 1) * piece] = mul(
                    flat(r.a_all, columns),
                    r.dq_all[p, :, :, c * piece : (c + 1) * piece].reshape(tokens, piece),
                    ROWS_ROWS,
                ).astype(target.dtype)

        for c in range(3):
            joint_grad(c, other, r.gj_send)
        lane.g_joint.start_all()
        for c in range(3):
            joint_grad(c, mine, r.own_joint)
        send_home(0, r.own_joint, r.home_joint)
        for c in range(chips):
            r.own_expand[:, c * units : (c + 1) * units] = mul(
                flat(r.c_all, mine), flat(r.du_all.at[:, c]), ROWS_ROWS
            )
        send_home(2, r.own_expand, r.home_expand)
        lane.out_strip.take_all()
        total = r.hid[...].reshape(strip, model) + r.y2_send[mp].astype(F32)
        for step in range(1, mp_size):
            total = total + r.y2_recv[lane.out_strip.source(step)].astype(F32)
        r.out_mine[...] = total.astype(BF16)
        g_out_sum.forward()

        lane.d_first.take_all()
        r.df_recv[chip, mp] = r.df_send[chip, mp]
        d_normed = gathered(r.df_recv, strip)
        back, gain_one, shift_one = norm_back(d_normed, r.x[part(mp, strip), :].astype(F32), norm_row(0))
        grad = r.dh[...].reshape(strip, model) + back
        r.ig_mine[...] = grad.astype(BF16)
        for index, row in enumerate((gain_one, shift_one, gain_two, shift_two)):
            for b in range(dp_size):
                place = (b % 2) * 4 + index
                r.gn_send[b // 2, place : place + 1, :] = row[:, b * shard : (b + 1) * shard]
        lane.g_norms.start_all()
        lane.in_rows.start_all()
        r.grad_rows[mp] = r.ig_mine[...]
        r.gn_recv[cross_me] = r.gn_send[chip]

        def square(own, distant):
            whole = own + distant.astype(F32)
            return jnp.sum(whole * whole, axis=0, keepdims=True)

        def folded(row):
            return sum(row[:, i : i + 128] for i in range(0, row.shape[1], 128))

        lane.g_contract.take_all()
        send_home(7, r.far_contract, r.home_far_contract)
        squares = folded(square(r.own_contract[...], r.far_contract[...]))
        lane.g_expand.take_all()
        send_home(6, r.far_expand, r.home_far_expand)
        squares = squares + folded(square(r.own_expand[...], r.far_expand[...]))
        lane.g_joint.take_all()
        send_home(4, r.far_joint, r.home_far_joint)
        for c in range(3):
            squares = squares + folded(square(r.own_joint[c], r.far_joint[c]))

        for k in range(2):
            g_out_sum.take(k)
            total = g_out_sum.total(k)

            @pl.when(core == k)
            def _():
                r.own_out[...] = total

            r.go_pair[k] = total.astype(BF16)
        lane.g_out_pair.start_all()
        send_home(1, r.own_out, r.home_out)

        lane.g_norms.take_all()
        summed = r.gn_recv[0]
        for index in range(1, chips * mp_size):
            summed = summed + r.gn_recv[index]
        r.gn_pair[...] = summed
        lane.g_norms_pair.start_all()
        lane.g_out_pair.take_all()
        send_home(5, r.far_out, r.home_far_out)
        squares = squares + folded(square(r.own_out[...], r.far_out[...]))
        lane.g_norms_pair.take_all()
        summed = summed + r.gn_far[...]
        own_norms = jnp.where(core == 0, summed[:4], summed[4:])
        r.own_norms[...] = own_norms
        own_norms = jnp.sum(own_norms * own_norms, axis=0, keepdims=True) * (1.0 / mp_size)
        squares = squares + folded(own_norms)
        r.sq_mine[...] = jnp.broadcast_to(jnp.sum(squares), (8, 128))
        lane.squares.start_all()
        r.sq_recv[cross_me] = r.sq_mine[...]

        lane.in_rows.take_all()
        lane.squares.take_all()
        total = r.sq_recv[0]
        for index in range(1, chips * mp_size):
            total = total + r.sq_recv[index]
        r.sq_pair[...] = total
        lane.squares_pair.start_all()
        lane.squares_pair.take_all()
        r.square_sum[...] = (total + r.sq_far[...])[:1, :1]
        for entry in every_lane:
            entry.sent_all()
        for index in range(3):
            passing(index, False).wait_send()
        for entry in leaving:
            entry.wait()

    vmem = pl.BlockSpec(memory_space=pltpu.VMEM)
    any_space = pl.BlockSpec(memory_space=pl.ANY)
    sem_shapes = [pltpu.SemaphoreType.DMA((4,)), pltpu.SemaphoreType.DMA((8,))]
    for name, kind in LANES.items():
        count = 2 * HALVED.get(name, 1)
        slots = vars(groups)[kind].size - 1 if kind == PAIR or name in STEPWISE else 1
        sem_shapes += [pltpu.SemaphoreType.DMA((slots,))] * count
    sem_shapes += [pltpu.SemaphoreType.DMA((4,))] * 2 * (4 + pieces)
    sem_shapes += [pltpu.SemaphoreType.DMA((6,))] * 2 * (4 + pieces)
    sem_shapes += [pltpu.SemaphoreType.DMA((3,))] * 2
    results = pl.pallas_call(
        kernel,
        out_shape=list(outs.values()) + list(homes.values()),
        in_specs=[vmem] * 3 + [any_space] * 4 + [vmem],
        out_specs=[vmem] * len(outs) + [any_space] * len(homes),
        scratch_shapes=[pltpu.VMEM(*entry) for entry in scratch.values()] + sem_shapes,
        compiler_params=pltpu.CompilerParams(
            collective_id=30, has_side_effects=True, vmem_limit_bytes=VMEM_LIMIT
        ),
    )(x, segments, cotangent, joint_w, out_w, expand_w, contract_w, norms)
    return SimpleNamespace(**dict(zip(list(outs) + list(homes), results)))


VMEM_LIMIT = 60 * 2**20


def finish_kernel(mp_size, *refs):
    blocks, (grad_rows, norms, output, input_grad, grad_norms) = refs[:mp_size], refs[mp_size:]
    strip = blocks[0].shape[0]
    for step, block in enumerate(blocks):
        source = lax.rem(lax.axis_index("mp") + mp_size - step, mp_size)
        output[part(source, strip), :] = block[...]
    for m in range(mp_size):
        input_grad[m * strip : (m + 1) * strip, :] = grad_rows[m].astype(F32)
    grad_norms[...] = norms[...]


def finish(r, mp_size):
    blocks = [r.out_mine] + [
        lax.ppermute(r.out_mine, "mp", [(i, (i + step) % mp_size) for i in range(mp_size)])
        for step in range(1, mp_size)
    ]
    strip, model = r.out_mine.shape
    return pl.pallas_call(
        functools.partial(finish_kernel, mp_size),
        out_shape=[
            shape((mp_size * strip, model)),
            shape((mp_size * strip, model), F32),
            shape(r.own_norms.shape, F32),
        ],
    )(*blocks, r.grad_rows, r.own_norms)


def local(dp_size, mp_size, *arrays):
    params, firsts, seconds = arrays[3:8], arrays[8:13], arrays[13:18]
    r = layer(dp_size, mp_size, arrays[:8])
    grads = (
        r.home_joint + r.home_far_joint.astype(F32),
        r.home_out + r.home_far_out.astype(F32),
        r.home_expand + r.home_far_expand.astype(F32),
        r.home_contract + r.home_far_contract.astype(F32),
        r.own_norms,
    )
    gradient_norm = jnp.sqrt(r.square_sum.reshape(()))
    clip_factor = jnp.minimum(1.0, MAX_NORM / (gradient_norm + CLIP_EPSILON))
    updates = [
        adam_update(params[k], grads[k], firsts[k], seconds[k], LEARN_RATES[k], clip_factor)
        for k in range(5)
    ]
    copies = [entry[2].astype(BF16) for entry in updates]
    layer_output, input_grad, grad_norms = finish(r, mp_size)
    return (
        layer_output,
        input_grad,
        *grads[:4],
        grad_norms,
        *[entry[0] for entry in updates],
        *[entry[1] for entry in updates],
        *[entry[2] for entry in updates],
        *copies,
        gradient_norm,
    )


def solution(mesh):
    rows = P("dp", None)
    sets = (
        P(None, "dp", "mp"),
        P(("mp", "dp"), None),
        P("dp", "mp"),
        P(("mp", "dp"), None),
        P(None, "dp"),
    )
    form = local if mesh.shape["dp"] == 8 else local_steps
    return jax.shard_map(
        functools.partial(form, mesh.shape["dp"], mesh.shape["mp"]),
        mesh=mesh,
        in_specs=(rows, rows, rows) + sets * 3,
        out_specs=(rows, rows) + sets * 5 + (P(),),
        check_vma=False,
    )
```

```python
import functools
import math
from types import SimpleNamespace

import jax
import jax.numpy as jnp
from jax import lax
from jax.experimental import pallas as pl
from jax.experimental.pallas import tpu as pltpu
from jax.sharding import PartitionSpec as P

HEAD_DIM = 128
ADAM_STEP = 5
MAX_NORM = 8192


BETA_ONE = 0.9
BETA_TWO = 0.95
ADAM_EPSILON = 1e-08
WEIGHT_DECAY = 0.1
NORM_EPSILON = 1e-05
CLIP_EPSILON = 1e-06
LEARN_RATES = (0.01, 0.08, 0.012, 0.02, 0.3)
MASKED_SCORE = -1e30
SCALE = 1.0 / math.sqrt(HEAD_DIM)
F32 = jnp.float32
BF16 = jnp.bfloat16
ROWS_COLS = (((1,), (0,)), ((), ()))
COLS_COLS = (((1,), (1,)), ((), ()))
ROWS_ROWS = (((0,), (0,)), ((), ()))


def mul(left, right, dims=ROWS_COLS):
    return lax.dot_general(left, right, dims, preferred_element_type=F32)


def layer_norm(values, gain_row, shift_row):
    row_mean = jnp.mean(values, axis=-1, keepdims=True)
    centered = values - row_mean
    spread = jnp.mean(centered * centered, axis=-1, keepdims=True)
    return centered * lax.rsqrt(spread + NORM_EPSILON) * gain_row + shift_row


def gelu_tanh(values):
    return jax.nn.gelu(values, approximate=True)


def adam_update(weight, grad, first, second, rate, clip_factor):
    clipped = grad * clip_factor
    new_first = BETA_ONE * first + (1.0 - BETA_ONE) * clipped
    new_second = BETA_TWO * second + (1.0 - BETA_TWO) * clipped * clipped
    first_hat = new_first / (1.0 - BETA_ONE**ADAM_STEP)
    second_hat = new_second / (1.0 - BETA_TWO**ADAM_STEP)
    new_weight = weight - rate * (
        first_hat / (jnp.sqrt(second_hat) + ADAM_EPSILON) + WEIGHT_DECAY * weight
    )
    return (new_first, new_second, new_weight)


PAIR, PLANE, COLUMN, CROSS, ROW, ALL = ("pair", "plane", "column", "cross", "row", "all")


class Group:
    def __init__(self, kind, dp_size, mp_size):
        self.kind = kind
        self.mp_size = mp_size
        chips = dp_size // 2
        self.size = {
            PAIR: 2,
            PLANE: chips,
            COLUMN: mp_size,
            CROSS: chips * mp_size,
            ROW: dp_size,
            ALL: dp_size * mp_size,
        }[kind]

    def me(self):
        dp, mp = lax.axis_index("dp"), lax.axis_index("mp")
        if self.kind == PAIR:
            return lax.rem(dp, 2)
        if self.kind == PLANE:
            return lax.div(dp, 2)
        if self.kind == COLUMN:
            return mp
        if self.kind == CROSS:
            return lax.div(dp, 2) * self.mp_size + mp
        if self.kind == ROW:
            return dp
        return dp * self.mp_size + mp

    def device(self, member):
        dp, mp = lax.axis_index("dp"), lax.axis_index("mp")
        core = lax.rem(dp, 2)
        if self.kind == PAIR:
            return (dp - core + member, mp)
        if self.kind == PLANE:
            return (member * 2 + core, mp)
        if self.kind == COLUMN:
            return (dp, member)
        if self.kind == CROSS:
            return (lax.div(member, self.mp_size) * 2 + core, lax.rem(member, self.mp_size))
        if self.kind == ROW:
            return (member, mp)
        return (lax.div(member, self.mp_size), lax.rem(member, self.mp_size))


def repeat(low, high, body):
    if high - low <= 8:
        for step in range(low, high):
            body(step)
    else:
        lax.fori_loop(low, high, lambda step, none: (body(step), none)[1], None)


def exchange(group, operands, results, moves, collective_id):
    count = len(operands)
    size = group.size
    lanes = len(moves)

    def kernel(*refs):
        ins, outs = refs[:count], refs[count : count + len(results)]
        send_sems, recv_sems, own_sems = refs[count + len(results) :]
        me = group.me()
        barrier = pltpu.get_barrier_semaphore()

        def greet(step):
            other = lax.rem(me + step, size)
            pl.semaphore_signal(
                barrier, inc=1, device_id=group.device(other), device_id_type=pl.DeviceIdType.MESH
            )

        repeat(1, size, greet)
        pl.semaphore_wait(barrier, size - 1)

        def remote(move, lane, step, sender, target, device):
            return pltpu.make_async_remote_copy(
                src_ref=move(ins, outs, me, target)[0],
                dst_ref=move(ins, outs, sender, me)[1],
                send_sem=send_sems.at[lane, step],
                recv_sem=recv_sems.at[lane, step],
                device_id=group.device(device),
                device_id_type=pl.DeviceIdType.MESH,
            )

        def launch(step):
            other = lax.rem(me + step, size)
            for lane, move in enumerate(moves):
                remote(move, lane, step, me, other, other).start()

        repeat(1, size, launch)
        own = []
        for lane, move in enumerate(moves):
            source, target = move(ins, outs, me, me)
            own.append(pltpu.make_async_copy(source, target, own_sems.at[lane]))
            own[-1].start()

        def finish(step):
            other = lax.rem(me + step, size)
            sender = lax.rem(me + size - step, size)
            for lane, move in enumerate(moves):
                remote(move, lane, step, sender, other, other).wait()

        repeat(1, size, finish)
        for copy in own:
            copy.wait()

    any_space = pl.BlockSpec(memory_space=pl.ANY)
    return pl.pallas_call(
        kernel,
        out_shape=results,
        in_specs=[any_space] * count,
        out_specs=[any_space] * len(results),
        scratch_shapes=[
            pltpu.SemaphoreType.DMA((lanes, size)),
            pltpu.SemaphoreType.DMA((lanes, size)),
            pltpu.SemaphoreType.DMA((lanes,)),
        ],
        compiler_params=pltpu.CompilerParams(collective_id=collective_id, has_side_effects=True),
    )(*operands)


def shape(dims, dtype=BF16):
    return jax.ShapeDtypeStruct(dims, dtype)


def part(index, width):
    return pl.ds(pl.multiple_of(index * width, width), width)


def allowed_pairs(seg_row, seg_col, length):
    places = lax.broadcasted_iota(jnp.int32, (length, length), 0)
    keys = lax.broadcasted_iota(jnp.int32, (length, length), 1)
    return (seg_col[...] == seg_row[...]) & (keys <= places)


def probabilities(query, key, allowed):
    scores = jnp.where(allowed, mul(query, key, COLS_COLS) * SCALE, MASKED_SCORE)
    exponent = jnp.exp(scores - jnp.max(scores, axis=-1, keepdims=True))
    return exponent / jnp.sum(exponent, axis=-1, keepdims=True)


def attend_kernel(width, joint, seg_row, seg_col, out_weight, attended, partial):
    allowed = allowed_pairs(seg_row, seg_col, joint.shape[0])
    for start in range(0, width, HEAD_DIM):
        head = pl.ds(start, HEAD_DIM)
        query, key, value = (joint[:, pl.ds(c * width + start, HEAD_DIM)] for c in range(3))
        prob = probabilities(query, key, allowed)
        attended[:, head] = mul(prob.astype(BF16), value).astype(BF16)
    partial[...] = mul(attended[...], out_weight[...]).astype(BF16)


def attend_back_kernel(
    width, joint, seg_row, seg_col, out_weight, attended, branch, d_joint, grad_out, d_attended
):
    allowed = allowed_pairs(seg_row, seg_col, joint.shape[0])
    d_attended[...] = mul(branch[...], out_weight[...], COLS_COLS).astype(BF16)
    for start in range(0, width, HEAD_DIM):
        query, key, value = (joint[:, pl.ds(c * width + start, HEAD_DIM)] for c in range(3))
        d_out = d_attended[:, pl.ds(start, HEAD_DIM)]
        prob = probabilities(query, key, allowed)
        d_joint[:, pl.ds(2 * width + start, HEAD_DIM)] = mul(
            prob.astype(BF16), d_out, ROWS_ROWS
        ).astype(BF16)
        d_prob = mul(d_out, value, COLS_COLS)
        row_delta = jnp.sum(d_prob * prob, axis=-1, keepdims=True)
        d_raw = (prob * (d_prob - row_delta) * SCALE).astype(BF16)
        d_joint[:, pl.ds(start, HEAD_DIM)] = mul(d_raw, key).astype(BF16)
        d_joint[:, pl.ds(width + start, HEAD_DIM)] = mul(d_raw, query, ROWS_ROWS).astype(BF16)
    grad_out[...] = mul(attended[...], branch[...], ROWS_ROWS).astype(BF16)


def local_steps(
    dp_size,
    mp_size,
    inputs,
    segment_ids,
    cotangent,
    query_key_value,
    attention_out,
    expand_weight,
    contract_weight,
    norm_params,
    first_query_key_value,
    first_attention_out,
    first_expand_weight,
    first_contract_weight,
    first_norm_params,
    second_query_key_value,
    second_attention_out,
    second_expand_weight,
    second_contract_weight,
    second_norm_params,
):
    params = (query_key_value, attention_out, expand_weight, contract_weight, norm_params)
    firsts = (
        first_query_key_value,
        first_attention_out,
        first_expand_weight,
        first_contract_weight,
        first_norm_params,
    )
    seconds = (
        second_query_key_value,
        second_attention_out,
        second_expand_weight,
        second_contract_weight,
        second_norm_params,
    )
    chips = dp_size // 2
    pair, plane, column, cross, row, everyone = (
        Group(kind, dp_size, mp_size)
        for kind in (PAIR, PLANE, COLUMN, CROSS, ROW, ALL)
    )
    dp, mp = lax.axis_index("dp"), lax.axis_index("mp")
    core = dp % 2
    length, model = inputs.shape
    width = query_key_value.shape[2]
    shard = query_key_value.shape[1]
    slab = 2 * shard
    hidden_units = expand_weight.shape[1]
    own_units = contract_weight.shape[0]
    units = 2 * own_units
    out_rows = attention_out.shape[0]
    strip = length // mp_size
    tokens = chips * length

    (norm_all,) = exchange(
        row,
        [norm_params],
        [shape((dp_size, 4, shard), F32)],
        [lambda ins, outs, me, other: (ins[0], outs[0].at[me])],
        0,
    )
    norm_weights = jnp.swapaxes(norm_all.astype(BF16).astype(F32), 0, 1).reshape(4, model)

    def shared(column_block):
        def move(ins, outs, me, other):
            return (ins[0].at[column_block], outs[0].at[part(me, shard), pl.ds(column_block * width, width)])

        return move

    joint_weight, expand_pair, contract_pair = exchange(
        pair,
        [query_key_value.astype(BF16), expand_weight.astype(BF16), contract_weight.astype(BF16)],
        [shape((slab, 3 * width)), shape((slab, hidden_units)), shape((units, model))],
        [
            shared(0),
            shared(1),
            shared(2),
            lambda ins, outs, me, other: (ins[1], outs[1].at[part(me, shard), :]),
            lambda ins, outs, me, other: (ins[2], outs[2].at[part(me, own_units), :]),
        ],
        1,
    )
    (output_all,) = exchange(
        row,
        [attention_out.astype(BF16)],
        [shape((dp_size * out_rows, model))],
        [lambda ins, outs, me, other: (ins[0], outs[0].at[part(me, out_rows), :])],
        2,
    )
    (grad_rows,) = exchange(
        plane,
        [cotangent],
        [shape((chips, length, model))],
        [lambda ins, outs, me, other: (ins[0], outs[0].at[me])],
        3,
    )
    grad_rows = grad_rows.reshape(tokens, model)

    values = inputs.astype(F32)
    normed = layer_norm(values, norm_weights[0], norm_weights[1]).astype(BF16)
    (normed_low,) = exchange(
        plane,
        [normed],
        [shape((chips, length, slab))],
        [lambda ins, outs, me, other: (ins[0].at[:, part(other, slab)], outs[0].at[me])],
        4,
    )
    normed_low = normed_low.reshape(tokens, slab)
    joint_part = mul(normed_low, joint_weight).astype(BF16).reshape(chips, length, 3 * width)
    (joint_parts,) = exchange(
        plane,
        [joint_part],
        [shape((chips, length, 3 * width))],
        [lambda ins, outs, me, other: (ins[0].at[other], outs[0].at[me])],
        5,
    )
    joint = jnp.sum(joint_parts.astype(F32), axis=0).astype(BF16)

    seg_row = segment_ids
    seg_col = segment_ids.reshape(length, 1)
    attended, branch_part = pl.pallas_call(
        functools.partial(attend_kernel, width),
        out_shape=[shape((length, width)), shape((length, model))],
        compiler_params=pltpu.CompilerParams(vmem_limit_bytes=48 * 2**20),
    )(joint, seg_row, seg_col, output_all)

    (branch_parts,) = exchange(
        column,
        [branch_part.reshape(mp_size, strip, model)],
        [shape((mp_size, strip, model))],
        [lambda ins, outs, me, other: (ins[0].at[other], outs[0].at[me])],
        6,
    )
    own_values = lax.dynamic_slice_in_dim(values, mp * strip, strip, 0)
    hidden = own_values + jnp.sum(branch_parts.astype(F32), axis=0)
    normed_two, pull_two = jax.vjp(layer_norm, hidden, norm_weights[2], norm_weights[3])
    (second_low,) = exchange(
        cross,
        [normed_two.astype(BF16)],
        [shape((chips * mp_size, strip, slab))],
        [
            lambda ins, outs, me, other: (
                ins[0].at[:, part(lax.div(other, mp_size), slab)],
                outs[0].at[me],
            )
        ],
        7,
    )
    second_low = second_low.reshape(tokens, slab)
    pre_part = mul(second_low, expand_pair).astype(BF16)
    (pre_parts,) = exchange(
        plane,
        [pre_part],
        [shape((chips, tokens, units))],
        [lambda ins, outs, me, other: (ins[0].at[:, part(other, units)], outs[0].at[me])],
        8,
    )
    pre_gelu = jnp.sum(pre_parts.astype(F32), axis=0)
    activated, pull_gelu = jax.vjp(gelu_tanh, pre_gelu)
    activated_low = activated.astype(BF16)
    d_activated = mul(grad_rows, contract_pair, COLS_COLS)
    (d_pre,) = pull_gelu(d_activated)
    (d_pre_all,) = exchange(
        plane,
        [d_pre.astype(BF16)],
        [shape((tokens, hidden_units))],
        [lambda ins, outs, me, other: (ins[0], outs[0].at[:, part(me, units)])],
        9,
    )

    def scatter_rows(partial, collective_id):
        (blocks,) = exchange(
            cross,
            [partial.reshape(chips * mp_size, strip, slab)],
            [shape((chips * mp_size, strip, slab))],
            [lambda ins, outs, me, other: (ins[0].at[other], outs[0].at[me])],
            collective_id,
        )
        total = jnp.sum(blocks.reshape(chips, mp_size, strip, slab).astype(F32), axis=1)
        return jnp.swapaxes(total, 0, 1).reshape(strip, model)

    d_normed_two = scatter_rows(mul(d_pre_all, expand_pair, COLS_COLS).astype(BF16), 10)
    d_hidden_norm, gain_two, shift_two = pull_two(d_normed_two)
    own_grad = lax.dynamic_slice_in_dim(cotangent, mp * strip, strip, 0).astype(F32)
    d_hidden = own_grad + d_hidden_norm

    def gather_rows(block, collective_id):
        (rows,) = exchange(
            column,
            [block],
            [shape((mp_size, strip, model))],
            [lambda ins, outs, me, other: (ins[0], outs[0].at[me])],
            collective_id,
        )
        return rows.reshape(length, model)

    branch_grad = gather_rows(d_hidden.astype(BF16), 11)
    d_joint, grad_output_part, _ = pl.pallas_call(
        functools.partial(attend_back_kernel, width),
        out_shape=[shape((length, 3 * width)), shape((width, model)), shape((length, width))],
        compiler_params=pltpu.CompilerParams(vmem_limit_bytes=48 * 2**20),
    )(joint, seg_row, seg_col, output_all, attended, branch_grad)
    (d_joint_all,) = exchange(
        plane,
        [d_joint],
        [shape((chips, length, 3 * width))],
        [lambda ins, outs, me, other: (ins[0], outs[0].at[me])],
        12,
    )
    d_joint_all = d_joint_all.reshape(tokens, 3 * width)
    d_normed_one = scatter_rows(mul(d_joint_all, joint_weight, COLS_COLS).astype(BF16), 13)
    _, pull_one = jax.vjp(layer_norm, own_values, norm_weights[0], norm_weights[1])
    d_values_norm, gain_one, shift_one = pull_one(d_normed_one)
    input_grad = gather_rows((d_hidden + d_values_norm).astype(BF16), 14).astype(F32)

    out_part = mul(activated_low, contract_pair).astype(BF16).reshape(chips, length, model)
    (out_parts,) = exchange(
        plane,
        [out_part],
        [shape((chips, length, model))],
        [lambda ins, outs, me, other: (ins[0].at[other], outs[0].at[me])],
        15,
    )
    out_rows_sum = jnp.sum(out_parts.astype(F32), axis=0).astype(BF16)
    (out_strips,) = exchange(
        column,
        [out_rows_sum.reshape(mp_size, strip, model)],
        [shape((mp_size, strip, model))],
        [lambda ins, outs, me, other: (ins[0].at[other], outs[0].at[me])],
        16,
    )
    layer_output = gather_rows(
        (hidden + jnp.sum(out_strips.astype(F32), axis=0)).astype(BF16), 17
    )

    (grad_output_parts,) = exchange(
        row,
        [grad_output_part.reshape(dp_size, out_rows, model)],
        [shape((dp_size, out_rows, model))],
        [lambda ins, outs, me, other: (ins[0].at[other], outs[0].at[me])],
        18,
    )
    reduced_output = jnp.sum(grad_output_parts.astype(F32), axis=0)
    own_joint, other_joint = [], []
    grad_joint = mul(normed_low, d_joint_all, ROWS_ROWS)
    grad_expand = mul(second_low, d_pre_all, ROWS_ROWS)
    grad_contract = mul(activated_low, grad_rows, ROWS_ROWS)

    def halves(array, index):
        return lax.dynamic_slice_in_dim(array, index * (array.shape[0] // 2), array.shape[0] // 2, 0)

    pieces = (grad_joint, grad_expand, grad_contract)
    sent = [halves(entry, 1 - core).astype(BF16) for entry in pieces]
    got = exchange_pair(pair, sent, 19)
    reduced_joint, reduced_expand, reduced_contract = (
        halves(entry, core) + other.astype(F32) for entry, other in zip(pieces, got)
    )
    reduced_joint = jnp.swapaxes(reduced_joint.reshape(shard, 3, width), 0, 1)

    zero_row = jnp.zeros((model,), F32)
    norm_rows = jnp.stack([gain_one, shift_one, gain_two, shift_two] + [zero_row] * 4)
    norm_rows = jnp.swapaxes(norm_rows.reshape(8, dp_size, shard), 0, 1)
    (norm_parts,) = exchange(
        everyone,
        [norm_rows],
        [shape((dp_size * mp_size, 8, shard), F32)],
        [
            lambda ins, outs, me, other: (
                ins[0].at[lax.div(other, mp_size)],
                outs[0].at[me],
            )
        ],
        20,
    )
    reduced_norms = jnp.sum(norm_parts, axis=0)[:4]

    grads = (reduced_joint, reduced_output, reduced_expand, reduced_contract, reduced_norms)
    squares = sum((jnp.sum(entry * entry) for entry in grads[:4])) + jnp.sum(
        reduced_norms * reduced_norms
    ) / mp_size
    (square_parts,) = exchange(
        everyone,
        [jnp.full((8, 128), squares, F32)],
        [shape((dp_size * mp_size, 8, 128), F32)],
        [lambda ins, outs, me, other: (ins[0], outs[0].at[me])],
        21,
    )
    gradient_norm = jnp.sqrt(jnp.sum(square_parts[:, 0, 0]))
    clip_factor = jnp.minimum(1.0, MAX_NORM / (gradient_norm + CLIP_EPSILON))
    updates = [
        adam_update(params[k], grads[k], firsts[k], seconds[k], LEARN_RATES[k], clip_factor)
        for k in range(5)
    ]
    copies = [entry[2].astype(BF16) for entry in updates]
    return (
        layer_output,
        input_grad,
        *grads,
        *[entry[0] for entry in updates],
        *[entry[1] for entry in updates],
        *[entry[2] for entry in updates],
        *copies,
        gradient_norm,
    )


def exchange_pair(pair, sent, collective_id):
    moves = [
        lambda ins, outs, me, other, lane=lane: (ins[lane], outs[lane]) for lane in range(len(sent))
    ]
    return swap(pair, sent, moves, collective_id)


def swap(pair, sent, moves, collective_id):
    count = len(sent)

    def kernel(*refs):
        ins, outs = refs[:count], refs[count : 2 * count]
        send_sems, recv_sems = refs[2 * count :]
        other = pair.device(1 - pair.me())
        barrier = pltpu.get_barrier_semaphore()
        pl.semaphore_signal(barrier, inc=1, device_id=other, device_id_type=pl.DeviceIdType.MESH)
        pl.semaphore_wait(barrier, 1)
        copies = [
            pltpu.make_async_remote_copy(
                src_ref=ins[lane],
                dst_ref=outs[lane],
                send_sem=send_sems.at[lane],
                recv_sem=recv_sems.at[lane],
                device_id=other,
                device_id_type=pl.DeviceIdType.MESH,
            )
            for lane in range(count)
        ]
        for copy in copies:
            copy.start()
        for copy in copies:
            copy.wait()

    any_space = pl.BlockSpec(memory_space=pl.ANY)
    return pl.pallas_call(
        kernel,
        out_shape=[shape(entry.shape, entry.dtype) for entry in sent],
        in_specs=[any_space] * count,
        out_specs=[any_space] * count,
        scratch_shapes=[pltpu.SemaphoreType.DMA((count,)), pltpu.SemaphoreType.DMA((count,))],
        compiler_params=pltpu.CompilerParams(collective_id=collective_id, has_side_effects=True),
    )(*sent)


class Lane:
    def __init__(self, group, me, sems, view, bulk=None):
        self.group, self.me, self.view, self.bulk = group, me, view, bulk
        self.sems = sems
        self.size = group.size

    def remote(self, source, target, step):
        index = step - 1 if self.bulk is None else 0
        return pltpu.make_async_remote_copy(
            src_ref=source,
            dst_ref=target,
            send_sem=self.sems[0].at[index],
            recv_sem=self.sems[1].at[index],
            device_id=self.group.device(lax.rem(self.me + step, self.size)),
            device_id_type=pl.DeviceIdType.MESH,
        )

    def copy(self, step):
        return self.remote(*self.view(self.me, lax.rem(self.me + step, self.size)), step)

    def start(self, step):
        self.copy(step).start()

    def start_all(self):
        repeat(1, self.size, self.start)

    def source(self, step):
        return lax.rem(self.me + self.size - step, self.size)

    def take(self, step):
        to = lax.rem(self.me + step, self.size)
        source, target = self.view(self.me, to)[0], self.view(self.source(step), self.me)[1]
        self.remote(source, target, step).wait_recv()

    def take_all(self):
        if self.bulk is None:
            repeat(1, self.size, self.take)
        else:
            self.remote(self.bulk, self.bulk, 1).wait_recv()

    def sent_all(self):
        if self.bulk is None:
            repeat(1, self.size, lambda step: self.copy(step).wait_send())
        else:
            self.remote(self.bulk, self.bulk, 1).wait_send()


class Hop:
    def __init__(self, dp, mp):
        core, self.me = lax.rem(dp, 2), lax.div(dp, 2)
        x_next = self.me + 1 - 2 * lax.rem(self.me, 2)
        self.chips = (x_next, lax.rem(self.me + 2, 4))
        self.far = 3 - self.me
        self.devices = tuple((chip * 2 + core, mp) for chip in self.chips)

    def copy(self, source, target, sems, index, way):
        return pltpu.make_async_remote_copy(
            src_ref=source,
            dst_ref=target,
            send_sem=sems[0].at[index],
            recv_sem=sems[1].at[index],
            device_id=self.devices[way],
            device_id_type=pl.DeviceIdType.MESH,
        )


class PlaneGather:
    def __init__(self, hop, sems, own, block, half):
        self.hop, self.sems, self.own, self.block, self.half = hop, sems, own, block, half

    def first(self, way):
        return self.hop.copy(self.own, self.block(self.hop.me), self.sems, way, way)

    def second(self, way):
        piece = self.half(self.block(self.hop.chips[way]), way)
        return self.hop.copy(piece, piece, self.sems, 2 + way, 1 - way)

    def start(self):
        for way in range(2):
            self.first(way).start()

    def near(self, way):
        near = self.block(self.hop.chips[way])
        self.hop.copy(near, near, self.sems, way, way).wait_recv()

    def forward(self):
        for way in range(2):
            self.near(way)
            self.second(way).start()

    def finish(self):
        for way in range(2):
            piece = self.half(self.block(self.hop.far), way)
            self.hop.copy(piece, piece, self.sems, 2 + way, 1 - way).wait_recv()

    def sent_all(self):
        for way in range(2):
            self.first(way).wait_send()
            self.second(way).wait_send()


class PlaneReduce:
    def __init__(self, hop, sems, parts, inbox, middle):
        self.hop, self.sems = hop, sems
        self.parts, self.inbox, self.middle = parts, inbox, middle

    def copy(self, stage, way):
        hop = self.hop
        chip = (hop.far, hop.chips[way])[stage] if stage < 2 else None
        source = self.parts.at[chip, way] if stage < 2 else self.middle.at[way]
        along = way if stage < 2 else 1 - way
        return hop.copy(source, self.inbox.at[stage, way], self.sems, 2 * stage + way, along)

    def start(self, stage):
        for way in range(2):
            self.copy(stage, way).start()

    def forward(self):
        for way in range(2):
            self.copy(0, way).wait_recv()
            onward = self.hop.chips[1 - way]
            total = self.parts[onward, way].astype(F32) + self.inbox[0, way].astype(F32)
            self.middle[way] = total.astype(BF16)
            self.copy(2, way).start()

    def take(self, way):
        self.copy(1, way).wait_recv()
        self.copy(2, way).wait_recv()

    def total(self, way, rows=slice(None)):
        own = self.parts[self.hop.me, way, rows].astype(F32)
        near = self.inbox[1, way, rows].astype(F32)
        return own + near + self.inbox[2, way, rows].astype(F32)

    def sent_all(self):
        for stage in range(3):
            for way in range(2):
                self.copy(stage, way).wait_send()


def standardise(values):
    row_mean = jnp.mean(values, axis=-1, keepdims=True)
    centered = values - row_mean
    spread = jnp.mean(centered * centered, axis=-1, keepdims=True)
    return centered, lax.rsqrt(spread + NORM_EPSILON)


def norm_back(grad, values, gain_row):
    centered, inverse = standardise(values)
    unit = centered * inverse
    scaled = grad * gain_row
    inner = jnp.mean(scaled * unit, axis=-1, keepdims=True)
    back = inverse * (scaled - jnp.mean(scaled, axis=-1, keepdims=True) - unit * inner)
    gain_grad = jnp.sum(grad * unit, axis=0, keepdims=True)
    shift_grad = jnp.sum(grad, axis=0, keepdims=True)
    return back, gain_grad, shift_grad


ROOT = math.sqrt(2.0 / math.pi)
CUBE = 0.044715

LANES = dict(
    norms=ROW,
    normed=PLANE,
    joint_weight=PAIR,
    out_own=PAIR,
    expand=PAIR,
    contract=PAIR,
    branch=COLUMN,
    second=CROSS,
    g_contract=PAIR,
    d_second=CROSS,
    g_expand=PAIR,
    d_hidden=COLUMN,
    g_out_pair=PAIR,
    out_strip=COLUMN,
    d_first=CROSS,
    g_joint=PAIR,
    out_rows=COLUMN,
    in_rows=COLUMN,
    g_norms=CROSS,
    g_norms_pair=PAIR,
    squares=CROSS,
    squares_pair=PAIR,
)

STEPWISE = dict(normed=True)
HALVED = dict(branch=2, second=2, d_second=2, d_hidden=2)


def layer(dp_size, mp_size, operands):
    x, segments, cotangent, joint_w, out_w, expand_w, contract_w, norms = operands
    chips = dp_size // 2
    groups = SimpleNamespace(
        **{kind: Group(kind, dp_size, mp_size) for kind in (PAIR, PLANE, COLUMN, CROSS, ROW)}
    )
    length, model = x.shape
    width, shard = joint_w.shape[2], joint_w.shape[1]
    slab = 2 * shard
    hidden = expand_w.shape[1]
    own_units = contract_w.shape[0]
    units = 2 * own_units
    out_rows = out_w.shape[0]
    strip = length // mp_size
    tokens = chips * length
    half_strip = strip // 2
    half_rows = length // 2
    half_tokens = tokens // 2
    pieces = max(1, width // (2 * HEAD_DIM))
    piece = width // pieces

    outs = dict(
        layer_output=shape((length, model)),
        grad_rows=shape((mp_size, strip, model)),
        own_norms=shape((4, shard), F32),
        square_sum=shape((1, 1), F32),
    )
    homes = dict(
        sum_joint=shape((3, shard, width)),
        sum_out=shape((out_rows, model)),
        sum_expand=shape((shard, hidden)),
        sum_contract=shape((own_units, model)),
    )
    scratch = dict(
        own_joint=((3, shard, width), F32),
        own_out=((out_rows, model), F32),
        own_expand=((shard, hidden), F32),
        own_contract=((own_units, model), F32),
        far_joint=((3, shard, width), BF16),
        far_out=((out_rows, model), BF16),
        far_expand=((shard, hidden), BF16),
        far_contract=((own_units, model), BF16),
        norm_all=((dp_size, 4, shard), F32),
        a_mine=((chips, length, slab), BF16),
        a_all=((chips, length, slab), BF16),
        wq=((3, slab, width), BF16),
        wo=((dp_size, out_rows, model), BF16),
        wu=((chips, slab, units), BF16),
        wd=((units, model), BF16),
        j_send=((pieces, chips, 2, length // 2, 3 * piece), BF16),
        j_recv=((pieces, 3, 2, length // 2, 3 * piece), BF16),
        j_mid=((pieces, 2, length // 2, 3 * piece), BF16),
        joint=((pieces, length, 3 * piece), BF16),
        dy_mine=((2, half_rows, model), BF16),
        dy_all=((chips, 2, half_rows, model), BF16),
        attended=((length, width), BF16),
        b_send=((2, mp_size, half_strip, model), BF16),
        b_recv=((2, mp_size, half_strip, model), BF16),
        hid=((2, half_strip, model), F32),
        bulk=(((chips * mp_size - 1) * strip, slab), BF16),
        c_mine=((2, chips, half_strip, slab), BF16),
        c_all=((2, chips, mp_size, half_strip, slab), BF16),
        u_send=((2, chips, 2, tokens // 4, units), BF16),
        u_recv=((2, 3, 2, tokens // 4, units), BF16),
        u_mid=((2, 2, tokens // 4, units), BF16),
        dz=((2, half_tokens, units), F32),
        z=((2, half_tokens, units), BF16),
        du_all=((2, chips, half_tokens, units), BF16),
        y_send=((chips, 2, length // 2, model), BF16),
        y_recv=((3, 2, length // 2, model), BF16),
        y_mid=((2, length // 2, model), BF16),
        gc_send=((own_units, model), BF16),
        dc_send=((2, chips, mp_size, half_strip, slab), BF16),
        dc_recv=((2, chips, mp_size, half_strip, slab), BF16),
        ge_send=((shard, hidden), BF16),
        dh=((2, half_strip, model), F32),
        da_mine=((2, half_strip, model), BF16),
        da_rows=((mp_size, 2, half_strip, model), BF16),
        dq_mine=((pieces, length, 3 * piece), BF16),
        dq_all=((pieces, chips, length, 3 * piece), BF16),
        go_send=((chips, 2, out_rows, model), BF16),
        go_recv=((3, 2, out_rows, model), BF16),
        go_mid=((2, out_rows, model), BF16),
        go_pair=((2, out_rows, model), BF16),
        y2_send=((mp_size, strip, model), BF16),
        y2_recv=((mp_size, strip, model), BF16),
        y_mine=((strip, model), BF16),
        y_rows=((mp_size, strip, model), BF16),
        df_send=((chips, mp_size, strip, slab), BF16),
        df_recv=((chips, mp_size, strip, slab), BF16),
        gj_send=((3, shard, width), BF16),
        ig_mine=((strip, model), BF16),
        gn_send=((chips, 8, shard), F32),
        gn_recv=((chips * mp_size, 8, shard), F32),
        gn_pair=((8, shard), F32),
        gn_far=((8, shard), F32),
        sq_mine=((8, 128), F32),
        sq_recv=((chips * mp_size, 8, 128), F32),
        sq_pair=((8, 128), F32),
        sq_far=((8, 128), F32),
    )
    in_names = dict(
        x=0, seg_row=1, cot=2, f_joint=3, f_out=4, f_expand=5, f_contract=6, norm_own=7
    )
    names = list(in_names) + list(outs) + list(homes) + list(scratch)

    def kernel(*refs):
        r = SimpleNamespace(**dict(zip(names, refs)))
        sems = refs[len(names) :]
        load_sems, home_sems = sems[:2]
        dp, mp = lax.axis_index("dp"), lax.axis_index("mp")
        core, chip = lax.rem(dp, 2), lax.div(dp, 2)
        mine, other = part(core, shard), part(1 - core, shard)
        cross_me = groups.cross.me()

        def flat(ref, columns=slice(None)):
            values = ref[(slice(None),) * (len(ref.shape) - 1) + (columns,)]
            return values.reshape(-1, values.shape[-1])

        views = dict(
            norms=lambda s, t: (r.norm_own, r.norm_all.at[s]),
            normed=lambda s, t: (r.a_mine.at[t], r.a_all.at[s]),
            joint_weight=lambda s, t: (
                r.wq.at[:, part(s, shard), :],
                r.wq.at[:, part(s, shard), :],
            ),
            out_own=lambda s, t: (r.wo.at[dp - core + s], r.wo.at[dp - core + s]),
            expand=lambda s, t: (
                r.wu.at[:, part(s, shard), :],
                r.wu.at[:, part(s, shard), :],
            ),
            contract=lambda s, t: (
                r.wd.at[part(s, own_units), :],
                r.wd.at[part(s, own_units), :],
            ),
            branch=[
                lambda s, t, h=h: (r.b_send.at[h, t], r.b_recv.at[h, s]) for h in range(2)
            ],
            second=[
                lambda s, t, h=h: (
                    r.c_mine.at[h, lax.div(t, mp_size)],
                    r.c_all.at[h, lax.div(s, mp_size), lax.rem(s, mp_size)],
                )
                for h in range(2)
            ],
            g_contract=lambda s, t: (r.gc_send, r.far_contract),
            d_second=[
                lambda s, t, h=h: (
                    r.dc_send.at[h, lax.div(t, mp_size), lax.rem(t, mp_size)],
                    r.dc_recv.at[h, lax.div(s, mp_size), lax.rem(s, mp_size)],
                )
                for h in range(2)
            ],
            g_expand=lambda s, t: (r.ge_send, r.far_expand),
            d_hidden=[
                lambda s, t, h=h: (r.da_mine.at[h], r.da_rows.at[s, h]) for h in range(2)
            ],
            g_out_pair=lambda s, t: (r.go_pair.at[t], r.far_out),
            out_strip=lambda s, t: (r.y2_send.at[t], r.y2_recv.at[s]),
            d_first=lambda s, t: (
                r.df_send.at[lax.div(t, mp_size), lax.rem(t, mp_size)],
                r.df_recv.at[lax.div(s, mp_size), lax.rem(s, mp_size)],
            ),
            g_joint=lambda s, t: (r.gj_send, r.far_joint),
            out_rows=lambda s, t: (r.y_mine, r.y_rows.at[s]),
            in_rows=lambda s, t: (r.ig_mine, r.grad_rows.at[s]),
            g_norms=lambda s, t: (r.gn_send.at[lax.div(t, mp_size)], r.gn_recv.at[s]),
            g_norms_pair=lambda s, t: (r.gn_pair, r.gn_far),
            squares=lambda s, t: (r.sq_mine, r.sq_recv.at[s]),
            squares_pair=lambda s, t: (r.sq_pair, r.sq_far),
        )
        others = chips * mp_size - 1
        column_blocks = pl.ds(0, mp_size - 1)
        bulks = dict(
            norms=r.norm_all.at[pl.ds(0, dp_size - 1)],
            branch=[r.b_recv.at[h, column_blocks] for h in range(2)],
            second=[r.bulk.at[pl.ds(0, others * half_strip), :]] * 2,
            d_second=[r.bulk.at[pl.ds(0, others * half_strip), :]] * 2,
            d_hidden=[r.da_rows.at[column_blocks, h] for h in range(2)],
            out_strip=r.y2_recv.at[column_blocks],
            d_first=r.bulk,
            out_rows=r.y_rows.at[column_blocks],
            in_rows=r.grad_rows.at[column_blocks],
            g_norms=r.gn_recv.at[pl.ds(0, others)],
            squares=r.sq_recv.at[pl.ds(0, others)],
        )
        lane = SimpleNamespace()
        every_lane = []
        used = iter(sems[2:])

        def pair_of():
            return (next(used), next(used))

        for name, kind in LANES.items():
            group = vars(groups)[kind]
            several = name in HALVED
            bulk = bulks.get(name, None)
            lanes = [
                Lane(group, group.me(), pair_of(), view, one)
                for view, one in (
                    zip(views[name], bulk) if several else [(views[name], bulk)]
                )
            ]
            every_lane += lanes
            setattr(lane, name, lanes if several else lanes[0])
        hop = Hop(dp, mp)

        def gather(own, block, half):
            every_lane.append(PlaneGather(hop, pair_of(), own, block, half))
            return every_lane[-1]

        def reduce(parts, inbox, middle):
            every_lane.append(PlaneReduce(hop, pair_of(), parts, inbox, middle))
            return every_lane[-1]

        def row_half(ref, way):
            rows = ref.shape[0] // 2
            return ref.at[pl.ds(way * rows, rows), :]

        out_plane = gather(r.wo.at[dp], lambda c: r.wo.at[2 * c + core], row_half)
        cot_plane = gather(r.dy_mine, lambda c: r.dy_all.at[c], lambda ref, way: ref.at[way])
        d_pre = [
            gather(r.du_all.at[h, chip], lambda c, h=h: r.du_all.at[h, c], row_half)
            for h in range(2)
        ]
        d_joint = [
            gather(r.dq_mine.at[p], lambda c, p=p: r.dq_all.at[p, c], row_half)
            for p in range(pieces)
        ]
        joint = [reduce(r.j_send.at[p], r.j_recv.at[p], r.j_mid.at[p]) for p in range(pieces)]
        pre_sum = [reduce(r.u_send.at[h], r.u_recv.at[h], r.u_mid.at[h]) for h in range(2)]
        out_sum = reduce(r.y_send, r.y_recv, r.y_mid)
        g_out_sum = reduce(r.go_send, r.go_recv, r.go_mid)
        pass_sems = pair_of()

        def passing(index, to_me):
            source = (*hop.chips, hop.far)[index]
            block = r.wo.at[2 * source + (1 - core if to_me else core)]
            return pltpu.make_async_remote_copy(
                src_ref=block,
                dst_ref=block,
                send_sem=pass_sems[0].at[index],
                recv_sem=pass_sems[1].at[index],
                device_id=(dp + 1 - 2 * core, mp),
                device_id_type=pl.DeviceIdType.MESH,
            )

        loads = [
            pltpu.make_async_copy(source, target, load_sems.at[i])
            for i, (source, target) in enumerate(
                (
                    (r.f_joint, r.own_joint),
                    (r.f_out, r.own_out),
                    (r.f_expand, r.own_expand),
                    (r.f_contract, r.own_contract),
                )
            )
        ]
        for load in (loads[1], loads[0], loads[2], loads[3]):
            load.start()

        leaving = []

        def send_home(index, source, target):
            leaving.append(pltpu.make_async_copy(source, target, home_sems.at[index]))
            leaving[-1].start()

        barrier = pltpu.get_barrier_semaphore()

        def greet(device):
            pl.semaphore_signal(
                barrier, inc=1, device_id=device, device_id_type=pl.DeviceIdType.MESH
            )

        cross = groups.cross
        repeat(1, cross.size, lambda s: greet(cross.device(lax.rem(cross_me + s, cross.size))))
        repeat(0, chips, lambda s: greet((s * 2 + 1 - core, mp)))

        r.norm_all[dp] = r.norm_own[...]
        loads[1].wait()
        r.wo[dp] = r.own_out[...].astype(BF16)
        values = r.x[...].astype(F32)
        centered, inverse = standardise(values)
        unit = centered * inverse
        loads[0].wait()
        for c in range(3):
            r.wq[c, mine, :] = r.own_joint[c].astype(BF16)
        ids = jnp.broadcast_to(r.seg_row[...].astype(F32), (length, length))
        places = lax.broadcasted_iota(jnp.int32, (length, length), 0)
        keys = lax.broadcasted_iota(jnp.int32, (length, length), 1)
        allowed = (ids == ids.T) & (keys <= places)
        pl.semaphore_wait(barrier, cross.size - 1 + chips)

        lane.norms.start_all()
        lane.joint_weight.start_all()
        out_plane.start()
        lane.out_own.start_all()
        lane.norms.take_all()

        def norm_row(index, block=None):
            blocks = range(dp_size) if block is None else (block,)
            rows = [r.norm_all[b, pl.ds(index, 1), :] for b in blocks]
            whole = rows[0] if len(rows) == 1 else jnp.concatenate(rows, axis=1)
            return whole.astype(BF16).astype(F32)

        for b in range(dp_size):
            columns = slice(b * shard, (b + 1) * shard)
            r.a_mine[b // 2, :, (b % 2) * shard : (b % 2 + 1) * shard] = (
                unit[:, columns] * norm_row(0, b) + norm_row(1, b)
            ).astype(BF16)
        lane.normed.start_all()
        r.a_all[chip] = r.a_mine[chip]

        lane.joint_weight.take_all()

        def joint_part(p, block):
            rows = r.a_all[block]
            for c in range(3):
                columns = slice(c * piece, (c + 1) * piece)
                third = mul(rows, r.wq[c, :, p * piece : (p + 1) * piece]).astype(BF16)
                for way in range(2):
                    r.j_send[p, block, way, :, columns] = third[
                        way * half_rows : (way + 1) * half_rows
                    ]

        def chip_step(block):
            return lax.rem(chip + chips - block, chips)

        for p in range(pieces):
            for way in range(2):
                if p == 0:
                    lane.normed.take(chip_step(hop.chips[way]))
                joint_part(p, hop.chips[way])
            joint[p].start(1)
            if p == 0:
                lane.normed.take(chip_step(hop.far))
            joint_part(p, hop.far)
            joint[p].start(0)
            joint_part(p, chip)
        for h in range(2):
            for m in range(mp_size):
                first = m * strip + h * half_strip
                r.dy_mine[h, m * half_strip : (m + 1) * half_strip, :] = r.cot[
                    first : first + half_strip, :
                ]
        out_plane.forward()
        for index in range(2):
            passing(index, False).start()
        for p in range(pieces):
            joint[p].forward()

        loads[2].wait()
        for c in range(chips):
            r.wu[c, mine, :] = r.own_expand[:, c * units : (c + 1) * units].astype(BF16)
        lane.expand.start_all()
        loads[3].wait()
        r.wd[part(core, own_units), :] = r.own_contract[...].astype(BF16)
        lane.contract.start_all()
        def query_key_value(start):
            p, first = start // piece, start % piece
            return (
                r.joint[p, :, c * piece + first : c * piece + first + HEAD_DIM] for c in range(3)
            )

        for p in range(pieces):
            for way in range(2):
                joint[p].take(way)
                r.joint[p, way * half_rows : (way + 1) * half_rows, :] = (
                    joint[p].total(way).astype(BF16)
                )
            if p == pieces - 1:
                cot_plane.start()
            for start in range(p * piece, (p + 1) * piece, HEAD_DIM):
                query, key, value = query_key_value(start)
                prob = probabilities(query, key, allowed)
                r.attended[:, start : start + HEAD_DIM] = mul(prob.astype(BF16), value).astype(BF16)

        lane.out_own.take_all()
        out_plane.finish()
        passing(2, False).start()
        for index in range(3):
            passing(index, True).wait_recv()
        branch = mul(r.attended[...], flat(r.wo)).astype(BF16)
        for h in range(2):
            for m in range(mp_size):
                first = m * strip + h * half_strip
                r.b_send[h, m] = branch[first : first + half_strip]
            lane.branch[h].start_all()
        r.dy_all[chip] = r.dy_mine[...]
        cot_plane.forward()

        def here(h):
            return pl.ds(pl.multiple_of(mp * strip + h * half_strip, half_strip), half_strip)

        for h in range(2):
            lane.branch[h].take_all()
            total = r.x[here(h), :].astype(F32) + r.b_send[h, mp].astype(F32)
            for step in range(1, mp_size):
                total = total + r.b_recv[h, lane.branch[h].source(step)].astype(F32)
            r.hid[h] = total
            centered, inverse = standardise(total)
            for b in range(dp_size):
                columns = slice(b * shard, (b + 1) * shard)
                r.c_mine[h, b // 2, :, (b % 2) * shard : (b % 2 + 1) * shard] = (
                    centered[:, columns] * inverse * norm_row(2, b) + norm_row(3, b)
                ).astype(BF16)
            lane.second[h].start_all()
            r.c_all[h, chip, mp] = r.c_mine[h, chip]
        lane.expand.take_all()

        def dy_half(h):
            return r.dy_all[:, h].reshape(half_tokens, model)

        quarter = half_tokens // 2

        def pre_part(h, to):
            part_sum = mul(flat(r.c_all.at[h]), r.wu[to]).astype(BF16)
            for way in range(2):
                r.u_send[h, to, way] = part_sum[way * quarter : (way + 1) * quarter]

        for h in range(2):
            lane.second[h].take_all()
            pre_part(h, hop.far)
            pre_sum[h].start(0)
            for way in range(2):
                pre_part(h, hop.chips[way])
            pre_sum[h].start(1)
            pre_part(h, chip)
            if h == 0:
                lane.contract.take_all()
                cot_plane.finish()
            r.dz[h] = mul(dy_half(h), r.wd[...], COLS_COLS)
            pre_sum[h].forward()
        tile = 64

        for h in range(2):
            for way in range(2):
                pre_sum[h].take(way)

                def gelu_tile(i, none, h=h, way=way):
                    rows = part(i, tile)
                    pre = pre_sum[h].total(way, rows)
                    square = pre * pre
                    curve = jnp.tanh(ROOT * pre * (1.0 + CUBE * square))
                    half = 0.5 * (1.0 + curve)
                    slope = half + 0.5 * pre * (1.0 - curve * curve) * (
                        ROOT * (1.0 + 3.0 * CUBE * square)
                    )
                    rows = part(i + way * (quarter // tile), tile)
                    r.z[h, rows, :] = (pre * half).astype(BF16)
                    r.du_all[h, chip, rows, :] = (r.dz[h, rows, :] * slope).astype(BF16)
                    return none

                lax.fori_loop(0, quarter // tile, gelu_tile, None)
            d_pre[h].start()

        def out_part(h):
            part_sum = mul(r.z[h], r.wd[...]).astype(BF16)
            for c in range(chips):
                r.y_send[c, h] = part_sum[c * half_rows : (c + 1) * half_rows]

        def second_part(h, source):
            return mul(r.du_all[h, source], r.wu[source], COLS_COLS)

        d_pre[0].forward()
        for h in range(2):
            out_part(h)
            total = second_part(h, chip)
            for way in range(2):
                total = total + second_part(h, hop.chips[way])
            if h == 0:
                d_pre[1].forward()
            d_pre[h].finish()
            total = (total + second_part(h, hop.far)).astype(BF16)
            for c in range(chips):
                for m in range(mp_size):
                    first = (c * mp_size + m) * half_strip
                    r.dc_send[h, c, m] = total[first : first + half_strip]
            lane.d_second[h].start_all()
        out_sum.start(0)
        out_sum.start(1)

        def contract_grad(columns):
            return sum(mul(r.z[h, :, columns], dy_half(h), ROWS_ROWS) for h in range(2))

        def gathered(recv, rows):
            blocks = []
            for c in range(chips):
                block = jnp.zeros((rows, slab), F32)
                for m in range(mp_size):
                    block = block + recv[c, m].astype(F32)
                blocks.append(block)
            return jnp.concatenate(blocks, axis=1)

        r.gc_send[...] = contract_grad(part(1 - core, own_units)).astype(BF16)
        lane.g_contract.start_all()
        gain_two, shift_two = 0.0, 0.0
        for h in range(2):
            lane.d_second[h].take_all()
            r.dc_recv[h, chip, mp] = r.dc_send[h, chip, mp]
            d_normed = gathered(r.dc_recv.at[h], half_strip)
            back, gain, shift = norm_back(d_normed, r.hid[h], norm_row(2))
            gain_two, shift_two = gain_two + gain, shift_two + shift
            d_hidden = r.cot[here(h), :].astype(F32) + back
            r.dh[h] = d_hidden
            r.da_mine[h] = d_hidden.astype(BF16)
            lane.d_hidden[h].start_all()
            r.da_rows[mp, h] = r.da_mine[h]
        out_sum.forward()
        for c in range(chips):
            r.ge_send[:, c * units : (c + 1) * units] = mul(
                flat(r.c_all, other), flat(r.du_all.at[:, c]), ROWS_ROWS
            ).astype(BF16)
        lane.g_expand.start_all()
        r.own_contract[...] = contract_grad(part(core, own_units))
        for h in range(2):
            lane.d_hidden[h].take_all()

        for way in range(2):
            out_sum.take(way)
            total = out_sum.total(way).astype(BF16)
            for m in range(mp_size):
                r.y2_send[m, way * half_strip : (way + 1) * half_strip, :] = total[
                    m * half_strip : (m + 1) * half_strip
                ]
        lane.out_strip.start_all()
        d_attended = mul(flat(r.da_rows), flat(r.wo), COLS_COLS).astype(BF16)
        for p in range(pieces):
            for start in range(p * piece, (p + 1) * piece, HEAD_DIM):
                query, key, value = query_key_value(start)
                d_out = d_attended[:, start : start + HEAD_DIM]
                prob = probabilities(query, key, allowed)
                d_prob = mul(d_out, value, COLS_COLS)
                row_delta = jnp.sum(d_prob * prob, axis=-1, keepdims=True)
                d_raw = (prob * (d_prob - row_delta) * SCALE).astype(BF16)
                thirds = (
                    mul(d_raw, key),
                    mul(d_raw, query, ROWS_ROWS),
                    mul(prob.astype(BF16), d_out, ROWS_ROWS),
                )
                for c in range(3):
                    first = c * piece + start % piece
                    r.dq_mine[p, :, first : first + HEAD_DIM] = thirds[c].astype(BF16)
            d_joint[p].start()
            r.dq_all[p, chip] = r.dq_mine[p]

        grad_out = mul(r.attended[...], flat(r.da_rows), ROWS_ROWS).astype(BF16)
        for c in range(chips):
            for k in range(2):
                first = (2 * c + k) * out_rows
                r.go_send[c, k] = grad_out[first : first + out_rows]

        def first_block(block):
            total = jnp.zeros((length, slab), F32)
            for p in range(pieces):
                for c in range(3):
                    total = total + mul(
                        r.dq_all[p, block, :, c * piece : (c + 1) * piece],
                        r.wq[c, :, p * piece : (p + 1) * piece],
                        COLS_COLS,
                    )
            total = total.astype(BF16)
            for m in range(mp_size):
                r.df_send[block, m] = total[m * strip : (m + 1) * strip]

        def first_send(block, others):
            for j in others:
                to = block * mp_size + lax.rem(mp + j, mp_size)
                lane.d_first.start(lax.rem(to + cross.size - cross_me, cross.size))

        first_block(chip)
        first_send(chip, range(1, mp_size))
        for p in range(pieces):
            d_joint[p].forward()
        for way in range(2):
            first_block(hop.chips[way])
            first_send(hop.chips[way], range(mp_size))
        for p in range(pieces):
            d_joint[p].finish()
        first_block(hop.far)
        first_send(hop.far, range(mp_size))
        lane.out_strip.take_all()
        total = r.hid[...].reshape(strip, model) + r.y2_send[mp].astype(F32)
        for step in range(1, mp_size):
            total = total + r.y2_recv[lane.out_strip.source(step)].astype(F32)
        r.y_mine[...] = total.astype(BF16)
        lane.out_rows.start_all()
        r.layer_output[part(mp, strip), :] = r.y_mine[...]
        g_out_sum.start(0)
        g_out_sum.start(1)

        def joint_grad(c, columns, target):
            for p in range(pieces):
                target[c, :, p * piece : (p + 1) * piece] = mul(
                    flat(r.a_all, columns),
                    r.dq_all[p, :, :, c * piece : (c + 1) * piece].reshape(tokens, piece),
                    ROWS_ROWS,
                ).astype(target.dtype)

        for c in range(3):
            joint_grad(c, other, r.gj_send)
        lane.g_joint.start_all()
        for c in range(3):
            joint_grad(c, mine, r.own_joint)
        for c in range(chips):
            r.own_expand[:, c * units : (c + 1) * units] = mul(
                flat(r.c_all, mine), flat(r.du_all.at[:, c]), ROWS_ROWS
            )
        g_out_sum.forward()

        lane.d_first.take_all()
        r.df_recv[chip, mp] = r.df_send[chip, mp]
        d_normed = gathered(r.df_recv, strip)
        back, gain_one, shift_one = norm_back(d_normed, r.x[part(mp, strip), :].astype(F32), norm_row(0))
        grad = r.dh[...].reshape(strip, model) + back
        r.ig_mine[...] = grad.astype(BF16)
        for index, row in enumerate((gain_one, shift_one, gain_two, shift_two)):
            for b in range(dp_size):
                place = (b % 2) * 4 + index
                r.gn_send[b // 2, place : place + 1, :] = row[:, b * shard : (b + 1) * shard]
        lane.g_norms.start_all()
        lane.in_rows.start_all()
        r.grad_rows[mp] = r.ig_mine[...]
        r.gn_recv[cross_me] = r.gn_send[chip]

        def settle(own, distant):
            whole = own[...] + distant[...].astype(F32)
            distant[...] = whole.astype(BF16)
            return jnp.sum(whole * whole, axis=0, keepdims=True)

        def folded(row):
            return sum(row[:, i : i + 128] for i in range(0, row.shape[1], 128))

        lane.g_contract.take_all()
        squares = folded(settle(r.own_contract, r.far_contract))
        send_home(3, r.far_contract, r.sum_contract)
        lane.g_expand.take_all()
        squares = squares + folded(settle(r.own_expand, r.far_expand))
        send_home(2, r.far_expand, r.sum_expand)
        lane.g_joint.take_all()
        for c in range(3):
            squares = squares + folded(settle(r.own_joint.at[c], r.far_joint.at[c]))
        send_home(0, r.far_joint, r.sum_joint)

        for k in range(2):
            g_out_sum.take(k)
            total = g_out_sum.total(k)

            @pl.when(core == k)
            def _():
                r.own_out[...] = total

            r.go_pair[k] = total.astype(BF16)
        lane.g_out_pair.start_all()

        lane.g_norms.take_all()
        summed = r.gn_recv[0]
        for index in range(1, chips * mp_size):
            summed = summed + r.gn_recv[index]
        r.gn_pair[...] = summed
        lane.g_norms_pair.start_all()
        lane.g_out_pair.take_all()
        squares = squares + folded(settle(r.own_out, r.far_out))
        send_home(1, r.far_out, r.sum_out)
        lane.g_norms_pair.take_all()
        summed = summed + r.gn_far[...]
        own_norms = jnp.where(core == 0, summed[:4], summed[4:])
        r.own_norms[...] = own_norms
        own_norms = jnp.sum(own_norms * own_norms, axis=0, keepdims=True) * (1.0 / mp_size)
        squares = squares + folded(own_norms)
        r.sq_mine[...] = jnp.broadcast_to(jnp.sum(squares), (8, 128))
        lane.squares.start_all()
        r.sq_recv[cross_me] = r.sq_mine[...]

        def place(rows_lane, rows, output):
            rows_lane.take_all()
            for step in range(1, mp_size):
                source = rows_lane.source(step)
                output[part(source, strip), :] = rows[source].astype(output.dtype)

        place(lane.out_rows, r.y_rows, r.layer_output)
        lane.in_rows.take_all()
        lane.squares.take_all()
        total = r.sq_recv[0]
        for index in range(1, chips * mp_size):
            total = total + r.sq_recv[index]
        r.sq_pair[...] = total
        lane.squares_pair.start_all()
        lane.squares_pair.take_all()
        r.square_sum[...] = (total + r.sq_far[...])[:1, :1]
        for entry in every_lane:
            entry.sent_all()
        for index in range(3):
            passing(index, False).wait_send()
        for entry in leaving:
            entry.wait()

    vmem = pl.BlockSpec(memory_space=pltpu.VMEM)
    any_space = pl.BlockSpec(memory_space=pl.ANY)
    sem_shapes = [pltpu.SemaphoreType.DMA((4,)), pltpu.SemaphoreType.DMA((4,))]
    for name, kind in LANES.items():
        count = 2 * HALVED.get(name, 1)
        slots = vars(groups)[kind].size - 1 if kind == PAIR or name in STEPWISE else 1
        sem_shapes += [pltpu.SemaphoreType.DMA((slots,))] * count
    sem_shapes += [pltpu.SemaphoreType.DMA((4,))] * 2 * (4 + pieces)
    sem_shapes += [pltpu.SemaphoreType.DMA((6,))] * 2 * (4 + pieces)
    sem_shapes += [pltpu.SemaphoreType.DMA((3,))] * 2
    results = pl.pallas_call(
        kernel,
        out_shape=list(outs.values()) + list(homes.values()),
        in_specs=[vmem] * 3 + [any_space] * 4 + [vmem],
        out_specs=[vmem] * len(outs) + [any_space] * len(homes),
        scratch_shapes=[pltpu.VMEM(*entry) for entry in scratch.values()] + sem_shapes,
        compiler_params=pltpu.CompilerParams(
            collective_id=30, has_side_effects=True, vmem_limit_bytes=VMEM_LIMIT
        ),
    )(x, segments, cotangent, joint_w, out_w, expand_w, contract_w, norms)
    return SimpleNamespace(**dict(zip(list(outs) + list(homes), results)))


VMEM_LIMIT = 60 * 2**20


CHUNKS = 4
TILE_ROWS = 16


def adam_kernel(shapes, *refs):
    squares, output, grad_rows = refs[:3]
    ins = [refs[3 + 4 * k : 7 + 4 * k] for k in range(4)]
    norm_ins = refs[19:23]
    norm_out, output_out, input_grad = refs[23:26]
    outs = [refs[26 + 5 * k : 31 + 5 * k] for k in range(5)]
    held = [refs[51 + 5 * k : 56 + 5 * k] for k in range(4)]
    output_held, rows_held, grad_held, in_sems, out_sems, row_sems = refs[71:]

    chunks = []
    for k in (2, 3, 0, 1):
        total = shapes[k][0]
        count = max(total // CHUNKS, 64)
        chunks += [(k, first, count) for first in range(0, total, count)]
    loads = [
        [
            pltpu.make_async_copy(
                ins[k][a].at[pl.ds(first, count), :],
                held[k][a].at[pl.ds(first, count), :],
                in_sems.at[4 * index + a],
            )
            for a in range(4)
        ]
        for index, (k, first, count) in enumerate(chunks)
    ]
    for group in loads:
        for load in group:
            load.start()
    row_loads = [
        pltpu.make_async_copy(output, output_held, row_sems.at[0]),
        pltpu.make_async_copy(grad_rows, rows_held, row_sems.at[1]),
    ]
    for load in row_loads:
        load.start()
    norm = jnp.sqrt(squares[...])
    norm_out[...] = norm
    clip = jnp.minimum(1.0, MAX_NORM / (norm + CLIP_EPSILON))

    stores = []
    for index, (k, first, count) in enumerate(chunks):
        for load in loads[index]:
            load.wait()
        low, weight, moment, square, whole = held[k]

        def tile(i, none, k=k, first=first, refs=held[k]):
            low, weight, moment, square, whole = refs
            here = pl.ds(pl.multiple_of(first + i * TILE_ROWS, TILE_ROWS), TILE_ROWS)
            grad = low[here, :].astype(F32)
            entries = adam_update(
                weight[here, :], grad, moment[here, :], square[here, :], LEARN_RATES[k], clip
            )
            whole[here, :] = grad
            moment[here, :], square[here, :], weight[here, :] = entries
            low[here, :] = entries[2].astype(BF16)
            return none

        lax.fori_loop(0, count // TILE_ROWS, tile, None)
        for a, source in enumerate((whole, moment, square, weight, low)):
            stores.append(
                pltpu.make_async_copy(
                    source.at[pl.ds(first, count), :],
                    outs[k][a].at[pl.ds(first, count), :],
                    out_sems.at[5 * index + a],
                )
            )
            stores[-1].start()
    for load in row_loads:
        load.wait()
    grad_held[...] = rows_held[...].astype(F32)
    stores.append(pltpu.make_async_copy(output_held, output_out, row_sems.at[2]))
    stores[-1].start()
    stores.append(pltpu.make_async_copy(grad_held, input_grad, row_sems.at[3]))
    stores[-1].start()
    own, weight, moment, square = (entry[...] for entry in norm_ins)
    entries = adam_update(weight, own, moment, square, LEARN_RATES[4], clip)
    for target, entry in zip(outs[4], (own, *entries, entries[2].astype(BF16))):
        target[...] = entry
    for store in stores:
        store.wait()


def optimizer(r, params, firsts, seconds):
    def rows(array):
        return array.reshape(-1, array.shape[-1])

    vmem, any_space = pl.BlockSpec(memory_space=pltpu.VMEM), pl.BlockSpec(memory_space=pl.ANY)
    sums = (r.sum_joint, r.sum_out, r.sum_expand, r.sum_contract)
    operands = [r.square_sum, r.layer_output, rows(r.grad_rows)]
    results = [shape((1, 1), F32), shape(operands[1].shape), shape(operands[2].shape, F32)]
    scratch, shapes = [], []
    for total, weight, first, second in zip(sums, params, firsts, seconds):
        arrays = [rows(a) for a in (total, weight, first, second)]
        operands += arrays
        shapes.append(arrays[0].shape)
        results += [shape(shapes[-1], F32)] * 4 + [shape(shapes[-1])]
        scratch += [pltpu.VMEM(a.shape, a.dtype) for a in arrays] + [pltpu.VMEM(shapes[-1], F32)]
    operands += [r.own_norms, params[4], firsts[4], seconds[4]]
    results += [shape(r.own_norms.shape, F32)] * 4 + [shape(r.own_norms.shape)]
    count = sum(entry[0] // max(entry[0] // CHUNKS, 64) for entry in shapes)
    out = pl.pallas_call(
        functools.partial(adam_kernel, shapes),
        in_specs=[vmem] + [any_space] * 18 + [vmem] * 4,
        out_specs=[vmem] + [any_space] * 22 + [vmem] * 5,
        out_shape=results,
        scratch_shapes=scratch
        + [pltpu.VMEM(entry.shape, entry.dtype) for entry in (operands[1], operands[2], results[2])]
        + [pltpu.SemaphoreType.DMA((4 * count,)), pltpu.SemaphoreType.DMA((5 * count,))]
        + [pltpu.SemaphoreType.DMA((4,))],
        compiler_params=pltpu.CompilerParams(vmem_limit_bytes=VMEM_LIMIT),
    )(*operands)
    sets = [
        [entry.reshape(params[k].shape) for entry in out[3 + 5 * k : 8 + 5 * k]] for k in range(5)
    ]
    return (out[1], out[2]), sets, out[0].reshape(())


def local(dp_size, mp_size, *arrays):
    params, firsts, seconds = arrays[3:8], arrays[8:13], arrays[13:18]
    r = layer(dp_size, mp_size, arrays[:8])
    rows, sets, gradient_norm = optimizer(r, params, firsts, seconds)
    return (*rows, *[sets[k][c] for c in range(5) for k in range(5)], gradient_norm)


def solution(mesh):
    rows = P("dp", None)
    sets = (
        P(None, "dp", "mp"),
        P(("mp", "dp"), None),
        P("dp", "mp"),
        P(("mp", "dp"), None),
        P(None, "dp"),
    )
    form = local if mesh.shape["dp"] == 8 else local_steps
    return jax.shard_map(
        functools.partial(form, mesh.shape["dp"], mesh.shape["mp"]),
        mesh=mesh,
        in_specs=(rows, rows, rows) + sets * 3,
        out_specs=(rows, rows) + sets * 5 + (P(),),
        check_vma=False,
    )
```

```python
import functools
import math
from types import SimpleNamespace

import jax
import jax.numpy as jnp
from jax import lax
from jax.experimental import pallas as pl
from jax.experimental.pallas import tpu as pltpu
from jax.sharding import PartitionSpec as P

HEAD_DIM = 128
ADAM_STEP = 5
MAX_NORM = 8192


BETA_ONE = 0.9
BETA_TWO = 0.95
ADAM_EPSILON = 1e-08
WEIGHT_DECAY = 0.1
NORM_EPSILON = 1e-05
CLIP_EPSILON = 1e-06
LEARN_RATES = (0.01, 0.08, 0.012, 0.02, 0.3)
MASKED_SCORE = -1e30
SCALE = 1.0 / math.sqrt(HEAD_DIM)
F32 = jnp.float32
BF16 = jnp.bfloat16
ROWS_COLS = (((1,), (0,)), ((), ()))
COLS_COLS = (((1,), (1,)), ((), ()))
ROWS_ROWS = (((0,), (0,)), ((), ()))


def mul(left, right, dims=ROWS_COLS):
    return lax.dot_general(left, right, dims, preferred_element_type=F32)


def layer_norm(values, gain_row, shift_row):
    row_mean = jnp.mean(values, axis=-1, keepdims=True)
    centered = values - row_mean
    spread = jnp.mean(centered * centered, axis=-1, keepdims=True)
    return centered * lax.rsqrt(spread + NORM_EPSILON) * gain_row + shift_row


def gelu_tanh(values):
    return jax.nn.gelu(values, approximate=True)


def adam_update(weight, grad, first, second, rate, clip_factor):
    clipped = grad * clip_factor
    new_first = BETA_ONE * first + (1.0 - BETA_ONE) * clipped
    new_second = BETA_TWO * second + (1.0 - BETA_TWO) * clipped * clipped
    first_hat = new_first / (1.0 - BETA_ONE**ADAM_STEP)
    second_hat = new_second / (1.0 - BETA_TWO**ADAM_STEP)
    new_weight = weight - rate * (
        first_hat / (jnp.sqrt(second_hat) + ADAM_EPSILON) + WEIGHT_DECAY * weight
    )
    return (new_first, new_second, new_weight)


PAIR, PLANE, COLUMN, CROSS, ROW, ALL = ("pair", "plane", "column", "cross", "row", "all")


class Group:
    def __init__(self, kind, dp_size, mp_size):
        self.kind = kind
        self.mp_size = mp_size
        chips = dp_size // 2
        self.size = {
            PAIR: 2,
            PLANE: chips,
            COLUMN: mp_size,
            CROSS: chips * mp_size,
            ROW: dp_size,
            ALL: dp_size * mp_size,
        }[kind]

    def me(self):
        dp, mp = lax.axis_index("dp"), lax.axis_index("mp")
        if self.kind == PAIR:
            return lax.rem(dp, 2)
        if self.kind == PLANE:
            return lax.div(dp, 2)
        if self.kind == COLUMN:
            return mp
        if self.kind == CROSS:
            return lax.div(dp, 2) * self.mp_size + mp
        if self.kind == ROW:
            return dp
        return dp * self.mp_size + mp

    def device(self, member):
        dp, mp = lax.axis_index("dp"), lax.axis_index("mp")
        core = lax.rem(dp, 2)
        if self.kind == PAIR:
            return (dp - core + member, mp)
        if self.kind == PLANE:
            return (member * 2 + core, mp)
        if self.kind == COLUMN:
            return (dp, member)
        if self.kind == CROSS:
            return (lax.div(member, self.mp_size) * 2 + core, lax.rem(member, self.mp_size))
        if self.kind == ROW:
            return (member, mp)
        return (lax.div(member, self.mp_size), lax.rem(member, self.mp_size))


def repeat(low, high, body):
    if high - low <= 8:
        for step in range(low, high):
            body(step)
    else:
        lax.fori_loop(low, high, lambda step, none: (body(step), none)[1], None)


def exchange(group, operands, results, moves, collective_id):
    count = len(operands)
    size = group.size
    lanes = len(moves)

    def kernel(*refs):
        ins, outs = refs[:count], refs[count : count + len(results)]
        send_sems, recv_sems, own_sems = refs[count + len(results) :]
        me = group.me()
        barrier = pltpu.get_barrier_semaphore()

        def greet(step):
            other = lax.rem(me + step, size)
            pl.semaphore_signal(
                barrier, inc=1, device_id=group.device(other), device_id_type=pl.DeviceIdType.MESH
            )

        repeat(1, size, greet)
        pl.semaphore_wait(barrier, size - 1)

        def remote(move, lane, step, sender, target, device):
            return pltpu.make_async_remote_copy(
                src_ref=move(ins, outs, me, target)[0],
                dst_ref=move(ins, outs, sender, me)[1],
                send_sem=send_sems.at[lane, step],
                recv_sem=recv_sems.at[lane, step],
                device_id=group.device(device),
                device_id_type=pl.DeviceIdType.MESH,
            )

        def launch(step):
            other = lax.rem(me + step, size)
            for lane, move in enumerate(moves):
                remote(move, lane, step, me, other, other).start()

        repeat(1, size, launch)
        own = []
        for lane, move in enumerate(moves):
            source, target = move(ins, outs, me, me)
            own.append(pltpu.make_async_copy(source, target, own_sems.at[lane]))
            own[-1].start()

        def finish(step):
            other = lax.rem(me + step, size)
            sender = lax.rem(me + size - step, size)
            for lane, move in enumerate(moves):
                remote(move, lane, step, sender, other, other).wait()

        repeat(1, size, finish)
        for copy in own:
            copy.wait()

    any_space = pl.BlockSpec(memory_space=pl.ANY)
    return pl.pallas_call(
        kernel,
        out_shape=results,
        in_specs=[any_space] * count,
        out_specs=[any_space] * len(results),
        scratch_shapes=[
            pltpu.SemaphoreType.DMA((lanes, size)),
            pltpu.SemaphoreType.DMA((lanes, size)),
            pltpu.SemaphoreType.DMA((lanes,)),
        ],
        compiler_params=pltpu.CompilerParams(collective_id=collective_id, has_side_effects=True),
    )(*operands)


def shape(dims, dtype=BF16):
    return jax.ShapeDtypeStruct(dims, dtype)


def part(index, width):
    return pl.ds(pl.multiple_of(index * width, width), width)


def allowed_pairs(seg_row, seg_col, length):
    places = lax.broadcasted_iota(jnp.int32, (length, length), 0)
    keys = lax.broadcasted_iota(jnp.int32, (length, length), 1)
    return (seg_col[...] == seg_row[...]) & (keys <= places)


def probabilities(query, key, allowed):
    scores = jnp.where(allowed, mul(query, key, COLS_COLS) * SCALE, MASKED_SCORE)
    exponent = jnp.exp(scores - jnp.max(scores, axis=-1, keepdims=True))
    return exponent / jnp.sum(exponent, axis=-1, keepdims=True)


def attend_kernel(width, joint, seg_row, seg_col, out_weight, attended, partial):
    allowed = allowed_pairs(seg_row, seg_col, joint.shape[0])
    for start in range(0, width, HEAD_DIM):
        head = pl.ds(start, HEAD_DIM)
        query, key, value = (joint[:, pl.ds(c * width + start, HEAD_DIM)] for c in range(3))
        prob = probabilities(query, key, allowed)
        attended[:, head] = mul(prob.astype(BF16), value).astype(BF16)
    partial[...] = mul(attended[...], out_weight[...]).astype(BF16)


def attend_back_kernel(
    width, joint, seg_row, seg_col, out_weight, attended, branch, d_joint, grad_out, d_attended
):
    allowed = allowed_pairs(seg_row, seg_col, joint.shape[0])
    d_attended[...] = mul(branch[...], out_weight[...], COLS_COLS).astype(BF16)
    for start in range(0, width, HEAD_DIM):
        query, key, value = (joint[:, pl.ds(c * width + start, HEAD_DIM)] for c in range(3))
        d_out = d_attended[:, pl.ds(start, HEAD_DIM)]
        prob = probabilities(query, key, allowed)
        d_joint[:, pl.ds(2 * width + start, HEAD_DIM)] = mul(
            prob.astype(BF16), d_out, ROWS_ROWS
        ).astype(BF16)
        d_prob = mul(d_out, value, COLS_COLS)
        row_delta = jnp.sum(d_prob * prob, axis=-1, keepdims=True)
        d_raw = (prob * (d_prob - row_delta) * SCALE).astype(BF16)
        d_joint[:, pl.ds(start, HEAD_DIM)] = mul(d_raw, key).astype(BF16)
        d_joint[:, pl.ds(width + start, HEAD_DIM)] = mul(d_raw, query, ROWS_ROWS).astype(BF16)
    grad_out[...] = mul(attended[...], branch[...], ROWS_ROWS).astype(BF16)


def local_steps(
    dp_size,
    mp_size,
    inputs,
    segment_ids,
    cotangent,
    query_key_value,
    attention_out,
    expand_weight,
    contract_weight,
    norm_params,
    first_query_key_value,
    first_attention_out,
    first_expand_weight,
    first_contract_weight,
    first_norm_params,
    second_query_key_value,
    second_attention_out,
    second_expand_weight,
    second_contract_weight,
    second_norm_params,
):
    params = (query_key_value, attention_out, expand_weight, contract_weight, norm_params)
    firsts = (
        first_query_key_value,
        first_attention_out,
        first_expand_weight,
        first_contract_weight,
        first_norm_params,
    )
    seconds = (
        second_query_key_value,
        second_attention_out,
        second_expand_weight,
        second_contract_weight,
        second_norm_params,
    )
    chips = dp_size // 2
    pair, plane, column, cross, row, everyone = (
        Group(kind, dp_size, mp_size)
        for kind in (PAIR, PLANE, COLUMN, CROSS, ROW, ALL)
    )
    dp, mp = lax.axis_index("dp"), lax.axis_index("mp")
    core = dp % 2
    length, model = inputs.shape
    width = query_key_value.shape[2]
    shard = query_key_value.shape[1]
    slab = 2 * shard
    hidden_units = expand_weight.shape[1]
    own_units = contract_weight.shape[0]
    units = 2 * own_units
    out_rows = attention_out.shape[0]
    strip = length // mp_size
    tokens = chips * length

    (norm_all,) = exchange(
        row,
        [norm_params],
        [shape((dp_size, 4, shard), F32)],
        [lambda ins, outs, me, other: (ins[0], outs[0].at[me])],
        0,
    )
    norm_weights = jnp.swapaxes(norm_all.astype(BF16).astype(F32), 0, 1).reshape(4, model)

    def shared(column_block):
        def move(ins, outs, me, other):
            return (ins[0].at[column_block], outs[0].at[part(me, shard), pl.ds(column_block * width, width)])

        return move

    joint_weight, expand_pair, contract_pair = exchange(
        pair,
        [query_key_value.astype(BF16), expand_weight.astype(BF16), contract_weight.astype(BF16)],
        [shape((slab, 3 * width)), shape((slab, hidden_units)), shape((units, model))],
        [
            shared(0),
            shared(1),
            shared(2),
            lambda ins, outs, me, other: (ins[1], outs[1].at[part(me, shard), :]),
            lambda ins, outs, me, other: (ins[2], outs[2].at[part(me, own_units), :]),
        ],
        1,
    )
    (output_all,) = exchange(
        row,
        [attention_out.astype(BF16)],
        [shape((dp_size * out_rows, model))],
        [lambda ins, outs, me, other: (ins[0], outs[0].at[part(me, out_rows), :])],
        2,
    )
    (grad_rows,) = exchange(
        plane,
        [cotangent],
        [shape((chips, length, model))],
        [lambda ins, outs, me, other: (ins[0], outs[0].at[me])],
        3,
    )
    grad_rows = grad_rows.reshape(tokens, model)

    values = inputs.astype(F32)
    normed = layer_norm(values, norm_weights[0], norm_weights[1]).astype(BF16)
    (normed_low,) = exchange(
        plane,
        [normed],
        [shape((chips, length, slab))],
        [lambda ins, outs, me, other: (ins[0].at[:, part(other, slab)], outs[0].at[me])],
        4,
    )
    normed_low = normed_low.reshape(tokens, slab)
    joint_part = mul(normed_low, joint_weight).astype(BF16).reshape(chips, length, 3 * width)
    (joint_parts,) = exchange(
        plane,
        [joint_part],
        [shape((chips, length, 3 * width))],
        [lambda ins, outs, me, other: (ins[0].at[other], outs[0].at[me])],
        5,
    )
    joint = jnp.sum(joint_parts.astype(F32), axis=0).astype(BF16)

    seg_row = segment_ids
    seg_col = segment_ids.reshape(length, 1)
    attended, branch_part = pl.pallas_call(
        functools.partial(attend_kernel, width),
        out_shape=[shape((length, width)), shape((length, model))],
        compiler_params=pltpu.CompilerParams(vmem_limit_bytes=48 * 2**20),
    )(joint, seg_row, seg_col, output_all)

    (branch_parts,) = exchange(
        column,
        [branch_part.reshape(mp_size, strip, model)],
        [shape((mp_size, strip, model))],
        [lambda ins, outs, me, other: (ins[0].at[other], outs[0].at[me])],
        6,
    )
    own_values = lax.dynamic_slice_in_dim(values, mp * strip, strip, 0)
    hidden = own_values + jnp.sum(branch_parts.astype(F32), axis=0)
    normed_two, pull_two = jax.vjp(layer_norm, hidden, norm_weights[2], norm_weights[3])
    (second_low,) = exchange(
        cross,
        [normed_two.astype(BF16)],
        [shape((chips * mp_size, strip, slab))],
        [
            lambda ins, outs, me, other: (
                ins[0].at[:, part(lax.div(other, mp_size), slab)],
                outs[0].at[me],
            )
        ],
        7,
    )
    second_low = second_low.reshape(tokens, slab)
    pre_part = mul(second_low, expand_pair).astype(BF16)
    (pre_parts,) = exchange(
        plane,
        [pre_part],
        [shape((chips, tokens, units))],
        [lambda ins, outs, me, other: (ins[0].at[:, part(other, units)], outs[0].at[me])],
        8,
    )
    pre_gelu = jnp.sum(pre_parts.astype(F32), axis=0)
    activated, pull_gelu = jax.vjp(gelu_tanh, pre_gelu)
    activated_low = activated.astype(BF16)
    d_activated = mul(grad_rows, contract_pair, COLS_COLS)
    (d_pre,) = pull_gelu(d_activated)
    (d_pre_all,) = exchange(
        plane,
        [d_pre.astype(BF16)],
        [shape((tokens, hidden_units))],
        [lambda ins, outs, me, other: (ins[0], outs[0].at[:, part(me, units)])],
        9,
    )

    def scatter_rows(partial, collective_id):
        (blocks,) = exchange(
            cross,
            [partial.reshape(chips * mp_size, strip, slab)],
            [shape((chips * mp_size, strip, slab))],
            [lambda ins, outs, me, other: (ins[0].at[other], outs[0].at[me])],
            collective_id,
        )
        total = jnp.sum(blocks.reshape(chips, mp_size, strip, slab).astype(F32), axis=1)
        return jnp.swapaxes(total, 0, 1).reshape(strip, model)

    d_normed_two = scatter_rows(mul(d_pre_all, expand_pair, COLS_COLS).astype(BF16), 10)
    d_hidden_norm, gain_two, shift_two = pull_two(d_normed_two)
    own_grad = lax.dynamic_slice_in_dim(cotangent, mp * strip, strip, 0).astype(F32)
    d_hidden = own_grad + d_hidden_norm

    def gather_rows(block, collective_id):
        (rows,) = exchange(
            column,
            [block],
            [shape((mp_size, strip, model))],
            [lambda ins, outs, me, other: (ins[0], outs[0].at[me])],
            collective_id,
        )
        return rows.reshape(length, model)

    branch_grad = gather_rows(d_hidden.astype(BF16), 11)
    d_joint, grad_output_part, _ = pl.pallas_call(
        functools.partial(attend_back_kernel, width),
        out_shape=[shape((length, 3 * width)), shape((width, model)), shape((length, width))],
        compiler_params=pltpu.CompilerParams(vmem_limit_bytes=48 * 2**20),
    )(joint, seg_row, seg_col, output_all, attended, branch_grad)
    (d_joint_all,) = exchange(
        plane,
        [d_joint],
        [shape((chips, length, 3 * width))],
        [lambda ins, outs, me, other: (ins[0], outs[0].at[me])],
        12,
    )
    d_joint_all = d_joint_all.reshape(tokens, 3 * width)
    d_normed_one = scatter_rows(mul(d_joint_all, joint_weight, COLS_COLS).astype(BF16), 13)
    _, pull_one = jax.vjp(layer_norm, own_values, norm_weights[0], norm_weights[1])
    d_values_norm, gain_one, shift_one = pull_one(d_normed_one)
    input_grad = gather_rows((d_hidden + d_values_norm).astype(BF16), 14).astype(F32)

    out_part = mul(activated_low, contract_pair).astype(BF16).reshape(chips, length, model)
    (out_parts,) = exchange(
        plane,
        [out_part],
        [shape((chips, length, model))],
        [lambda ins, outs, me, other: (ins[0].at[other], outs[0].at[me])],
        15,
    )
    out_rows_sum = jnp.sum(out_parts.astype(F32), axis=0).astype(BF16)
    (out_strips,) = exchange(
        column,
        [out_rows_sum.reshape(mp_size, strip, model)],
        [shape((mp_size, strip, model))],
        [lambda ins, outs, me, other: (ins[0].at[other], outs[0].at[me])],
        16,
    )
    layer_output = gather_rows(
        (hidden + jnp.sum(out_strips.astype(F32), axis=0)).astype(BF16), 17
    )

    (grad_output_parts,) = exchange(
        row,
        [grad_output_part.reshape(dp_size, out_rows, model)],
        [shape((dp_size, out_rows, model))],
        [lambda ins, outs, me, other: (ins[0].at[other], outs[0].at[me])],
        18,
    )
    reduced_output = jnp.sum(grad_output_parts.astype(F32), axis=0)
    own_joint, other_joint = [], []
    grad_joint = mul(normed_low, d_joint_all, ROWS_ROWS)
    grad_expand = mul(second_low, d_pre_all, ROWS_ROWS)
    grad_contract = mul(activated_low, grad_rows, ROWS_ROWS)

    def halves(array, index):
        return lax.dynamic_slice_in_dim(array, index * (array.shape[0] // 2), array.shape[0] // 2, 0)

    pieces = (grad_joint, grad_expand, grad_contract)
    sent = [halves(entry, 1 - core).astype(BF16) for entry in pieces]
    got = exchange_pair(pair, sent, 19)
    reduced_joint, reduced_expand, reduced_contract = (
        halves(entry, core) + other.astype(F32) for entry, other in zip(pieces, got)
    )
    reduced_joint = jnp.swapaxes(reduced_joint.reshape(shard, 3, width), 0, 1)

    zero_row = jnp.zeros((model,), F32)
    norm_rows = jnp.stack([gain_one, shift_one, gain_two, shift_two] + [zero_row] * 4)
    norm_rows = jnp.swapaxes(norm_rows.reshape(8, dp_size, shard), 0, 1)
    (norm_parts,) = exchange(
        everyone,
        [norm_rows],
        [shape((dp_size * mp_size, 8, shard), F32)],
        [
            lambda ins, outs, me, other: (
                ins[0].at[lax.div(other, mp_size)],
                outs[0].at[me],
            )
        ],
        20,
    )
    reduced_norms = jnp.sum(norm_parts, axis=0)[:4]

    grads = (reduced_joint, reduced_output, reduced_expand, reduced_contract, reduced_norms)
    squares = sum((jnp.sum(entry * entry) for entry in grads[:4])) + jnp.sum(
        reduced_norms * reduced_norms
    ) / mp_size
    (square_parts,) = exchange(
        everyone,
        [jnp.full((8, 128), squares, F32)],
        [shape((dp_size * mp_size, 8, 128), F32)],
        [lambda ins, outs, me, other: (ins[0], outs[0].at[me])],
        21,
    )
    gradient_norm = jnp.sqrt(jnp.sum(square_parts[:, 0, 0]))
    clip_factor = jnp.minimum(1.0, MAX_NORM / (gradient_norm + CLIP_EPSILON))
    updates = [
        adam_update(params[k], grads[k], firsts[k], seconds[k], LEARN_RATES[k], clip_factor)
        for k in range(5)
    ]
    copies = [entry[2].astype(BF16) for entry in updates]
    return (
        layer_output,
        input_grad,
        *grads,
        *[entry[0] for entry in updates],
        *[entry[1] for entry in updates],
        *[entry[2] for entry in updates],
        *copies,
        gradient_norm,
    )


def exchange_pair(pair, sent, collective_id):
    moves = [
        lambda ins, outs, me, other, lane=lane: (ins[lane], outs[lane]) for lane in range(len(sent))
    ]
    return swap(pair, sent, moves, collective_id)


def swap(pair, sent, moves, collective_id):
    count = len(sent)

    def kernel(*refs):
        ins, outs = refs[:count], refs[count : 2 * count]
        send_sems, recv_sems = refs[2 * count :]
        other = pair.device(1 - pair.me())
        barrier = pltpu.get_barrier_semaphore()
        pl.semaphore_signal(barrier, inc=1, device_id=other, device_id_type=pl.DeviceIdType.MESH)
        pl.semaphore_wait(barrier, 1)
        copies = [
            pltpu.make_async_remote_copy(
                src_ref=ins[lane],
                dst_ref=outs[lane],
                send_sem=send_sems.at[lane],
                recv_sem=recv_sems.at[lane],
                device_id=other,
                device_id_type=pl.DeviceIdType.MESH,
            )
            for lane in range(count)
        ]
        for copy in copies:
            copy.start()
        for copy in copies:
            copy.wait()

    any_space = pl.BlockSpec(memory_space=pl.ANY)
    return pl.pallas_call(
        kernel,
        out_shape=[shape(entry.shape, entry.dtype) for entry in sent],
        in_specs=[any_space] * count,
        out_specs=[any_space] * count,
        scratch_shapes=[pltpu.SemaphoreType.DMA((count,)), pltpu.SemaphoreType.DMA((count,))],
        compiler_params=pltpu.CompilerParams(collective_id=collective_id, has_side_effects=True),
    )(*sent)


class Lane:
    def __init__(self, group, me, sems, view, bulk=None):
        self.group, self.me, self.view, self.bulk = group, me, view, bulk
        self.sems = sems
        self.size = group.size

    def remote(self, source, target, step):
        index = step - 1 if self.bulk is None else 0
        return pltpu.make_async_remote_copy(
            src_ref=source,
            dst_ref=target,
            send_sem=self.sems[0].at[index],
            recv_sem=self.sems[1].at[index],
            device_id=self.group.device(lax.rem(self.me + step, self.size)),
            device_id_type=pl.DeviceIdType.MESH,
        )

    def copy(self, step):
        return self.remote(*self.view(self.me, lax.rem(self.me + step, self.size)), step)

    def start(self, step):
        self.copy(step).start()

    def start_all(self):
        repeat(1, self.size, self.start)

    def source(self, step):
        return lax.rem(self.me + self.size - step, self.size)

    def take(self, step):
        to = lax.rem(self.me + step, self.size)
        source, target = self.view(self.me, to)[0], self.view(self.source(step), self.me)[1]
        self.remote(source, target, step).wait_recv()

    def take_all(self):
        if self.bulk is None:
            repeat(1, self.size, self.take)
        else:
            self.remote(self.bulk, self.bulk, 1).wait_recv()

    def sent_all(self):
        if self.bulk is None:
            repeat(1, self.size, lambda step: self.copy(step).wait_send())
        else:
            self.remote(self.bulk, self.bulk, 1).wait_send()


class Hop:
    def __init__(self, dp, mp):
        core, self.me = lax.rem(dp, 2), lax.div(dp, 2)
        x_next = self.me + 1 - 2 * lax.rem(self.me, 2)
        self.chips = (x_next, lax.rem(self.me + 2, 4))
        self.far = 3 - self.me
        self.devices = tuple((chip * 2 + core, mp) for chip in self.chips)

    def copy(self, source, target, sems, index, way):
        return pltpu.make_async_remote_copy(
            src_ref=source,
            dst_ref=target,
            send_sem=sems[0].at[index],
            recv_sem=sems[1].at[index],
            device_id=self.devices[way],
            device_id_type=pl.DeviceIdType.MESH,
        )


class PlaneGather:
    def __init__(self, hop, sems, own, block, half):
        self.hop, self.sems, self.own, self.block, self.half = hop, sems, own, block, half

    def first(self, way):
        return self.hop.copy(self.own, self.block(self.hop.me), self.sems, way, way)

    def second(self, way):
        piece = self.half(self.block(self.hop.chips[way]), way)
        return self.hop.copy(piece, piece, self.sems, 2 + way, 1 - way)

    def start(self):
        for way in range(2):
            self.first(way).start()

    def near(self, way):
        near = self.block(self.hop.chips[way])
        self.hop.copy(near, near, self.sems, way, way).wait_recv()

    def forward(self):
        for way in range(2):
            self.near(way)
            self.second(way).start()

    def finish(self):
        for way in range(2):
            piece = self.half(self.block(self.hop.far), way)
            self.hop.copy(piece, piece, self.sems, 2 + way, 1 - way).wait_recv()

    def sent_all(self):
        for way in range(2):
            self.first(way).wait_send()
            self.second(way).wait_send()


class PlaneReduce:
    def __init__(self, hop, sems, parts, inbox, middle):
        self.hop, self.sems = hop, sems
        self.parts, self.inbox, self.middle = parts, inbox, middle

    def copy(self, stage, way):
        hop = self.hop
        chip = (hop.far, hop.chips[way])[stage] if stage < 2 else None
        source = self.parts.at[chip, way] if stage < 2 else self.middle.at[way]
        along = way if stage < 2 else 1 - way
        return hop.copy(source, self.inbox.at[stage, way], self.sems, 2 * stage + way, along)

    def start(self, stage):
        for way in range(2):
            self.copy(stage, way).start()

    def forward(self):
        for way in range(2):
            self.copy(0, way).wait_recv()
            onward = self.hop.chips[1 - way]
            total = self.parts[onward, way].astype(F32) + self.inbox[0, way].astype(F32)
            self.middle[way] = total.astype(BF16)
            self.copy(2, way).start()

    def take(self, way):
        self.copy(1, way).wait_recv()
        self.copy(2, way).wait_recv()

    def total(self, way, rows=slice(None)):
        own = self.parts[self.hop.me, way, rows].astype(F32)
        near = self.inbox[1, way, rows].astype(F32)
        return own + near + self.inbox[2, way, rows].astype(F32)

    def sent_all(self):
        for stage in range(3):
            for way in range(2):
                self.copy(stage, way).wait_send()


def standardise(values):
    row_mean = jnp.mean(values, axis=-1, keepdims=True)
    centered = values - row_mean
    spread = jnp.mean(centered * centered, axis=-1, keepdims=True)
    return centered, lax.rsqrt(spread + NORM_EPSILON)


def norm_back(grad, values, gain_row):
    centered, inverse = standardise(values)
    unit = centered * inverse
    scaled = grad * gain_row
    inner = jnp.mean(scaled * unit, axis=-1, keepdims=True)
    back = inverse * (scaled - jnp.mean(scaled, axis=-1, keepdims=True) - unit * inner)
    gain_grad = jnp.sum(grad * unit, axis=0, keepdims=True)
    shift_grad = jnp.sum(grad, axis=0, keepdims=True)
    return back, gain_grad, shift_grad


ROOT = math.sqrt(2.0 / math.pi)
CUBE = 0.044715

LANES = dict(
    norms=ROW,
    normed=PLANE,
    joint_weight=PAIR,
    out_own=PAIR,
    expand=PAIR,
    contract=PAIR,
    branch=COLUMN,
    second=CROSS,
    g_contract=PAIR,
    d_second=CROSS,
    g_expand=PAIR,
    d_hidden=COLUMN,
    g_out_pair=PAIR,
    out_strip=COLUMN,
    d_first=CROSS,
    g_joint=PAIR,
    out_rows=COLUMN,
    in_rows=COLUMN,
    g_norms=CROSS,
    g_norms_pair=PAIR,
    squares=CROSS,
    squares_pair=PAIR,
)

STEPWISE = dict(normed=True)
HALVED = dict(branch=2, second=2, d_second=2, d_hidden=2)


def layer(dp_size, mp_size, operands):
    x, segments, cotangent, joint_w, out_w, expand_w, contract_w, norms = operands
    chips = dp_size // 2
    groups = SimpleNamespace(
        **{kind: Group(kind, dp_size, mp_size) for kind in (PAIR, PLANE, COLUMN, CROSS, ROW)}
    )
    length, model = x.shape
    width, shard = joint_w.shape[2], joint_w.shape[1]
    slab = 2 * shard
    hidden = expand_w.shape[1]
    own_units = contract_w.shape[0]
    units = 2 * own_units
    out_rows = out_w.shape[0]
    strip = length // mp_size
    tokens = chips * length
    half_strip = strip // 2
    half_rows = length // 2
    half_tokens = tokens // 2
    pieces = max(1, width // (2 * HEAD_DIM))
    piece = width // pieces

    outs = dict(
        own_norms=shape((4, shard), F32),
        square_sum=shape((1, 1), F32),
    )
    homes = dict(
        home_output=shape((length, model)),
        home_rows=shape((mp_size, strip, model)),
        sum_joint=shape((3, shard, width)),
        sum_out=shape((out_rows, model)),
        sum_expand=shape((shard, hidden)),
        sum_contract=shape((own_units, model)),
    )
    scratch = dict(
        layer_output=((length, model), BF16),
        grad_rows=((mp_size, strip, model), BF16),
        cot=((length, model), BF16),
        own_joint=((3, shard, width), F32),
        own_out=((out_rows, model), F32),
        own_expand=((shard, hidden), F32),
        own_contract=((own_units, model), F32),
        far_joint=((3, shard, width), BF16),
        far_out=((out_rows, model), BF16),
        far_expand=((shard, hidden), BF16),
        far_contract=((own_units, model), BF16),
        norm_all=((dp_size, 4, shard), F32),
        a_mine=((chips, length, slab), BF16),
        a_all=((chips, length, slab), BF16),
        wq=((3, slab, width), BF16),
        wo=((dp_size, out_rows, model), BF16),
        wu=((chips, slab, units), BF16),
        wd=((units, model), BF16),
        j_send=((pieces, chips, 2, length // 2, 3 * piece), BF16),
        j_recv=((pieces, 3, 2, length // 2, 3 * piece), BF16),
        j_mid=((pieces, 2, length // 2, 3 * piece), BF16),
        joint=((pieces, length, 3 * piece), BF16),
        dy_mine=((2, half_rows, model), BF16),
        dy_all=((chips, 2, half_rows, model), BF16),
        attended=((length, width), BF16),
        b_send=((2, mp_size, half_strip, model), BF16),
        b_recv=((2, mp_size, half_strip, model), BF16),
        hid=((2, half_strip, model), F32),
        bulk=(((chips * mp_size - 1) * strip, slab), BF16),
        c_mine=((2, chips, half_strip, slab), BF16),
        c_all=((2, chips, mp_size, half_strip, slab), BF16),
        u_send=((2, chips, 2, tokens // 4, units), BF16),
        u_recv=((2, 3, 2, tokens // 4, units), BF16),
        u_mid=((2, 2, tokens // 4, units), BF16),
        dz=((2, half_tokens, units), F32),
        z=((2, half_tokens, units), BF16),
        du_all=((2, chips, half_tokens, units), BF16),
        y_send=((chips, 2, length // 2, model), BF16),
        y_recv=((3, 2, length // 2, model), BF16),
        y_mid=((2, length // 2, model), BF16),
        gc_send=((own_units, model), BF16),
        dc_send=((2, chips, mp_size, half_strip, slab), BF16),
        dc_recv=((2, chips, mp_size, half_strip, slab), BF16),
        ge_send=((shard, hidden), BF16),
        dh=((2, half_strip, model), F32),
        da_mine=((2, half_strip, model), BF16),
        da_rows=((mp_size, 2, half_strip, model), BF16),
        dq_mine=((pieces, length, 3 * piece), BF16),
        dq_all=((pieces, chips, length, 3 * piece), BF16),
        go_send=((chips, 2, out_rows, model), BF16),
        go_recv=((3, 2, out_rows, model), BF16),
        go_mid=((2, out_rows, model), BF16),
        go_pair=((2, out_rows, model), BF16),
        y2_send=((mp_size, strip, model), BF16),
        y2_recv=((mp_size, strip, model), BF16),
        y_mine=((strip, model), BF16),
        y_rows=((mp_size, strip, model), BF16),
        df_send=((chips, mp_size, strip, slab), BF16),
        df_recv=((chips, mp_size, strip, slab), BF16),
        gj_send=((3, shard, width), BF16),
        ig_mine=((strip, model), BF16),
        gn_send=((chips, 8, shard), F32),
        gn_recv=((chips * mp_size, 8, shard), F32),
        gn_pair=((8, shard), F32),
        gn_far=((8, shard), F32),
        sq_mine=((8, 128), F32),
        sq_recv=((chips * mp_size, 8, 128), F32),
        sq_pair=((8, 128), F32),
        sq_far=((8, 128), F32),
    )
    in_names = dict(
        x=0, seg_row=1, f_cot=2, f_joint=3, f_out=4, f_expand=5, f_contract=6, norm_own=7
    )
    names = list(in_names) + list(outs) + list(homes) + list(scratch)

    def kernel(*refs):
        r = SimpleNamespace(**dict(zip(names, refs)))
        sems = refs[len(names) :]
        load_sems, home_sems = sems[:2]
        dp, mp = lax.axis_index("dp"), lax.axis_index("mp")
        core, chip = lax.rem(dp, 2), lax.div(dp, 2)
        mine, other = part(core, shard), part(1 - core, shard)
        cross_me = groups.cross.me()

        def flat(ref, columns=slice(None)):
            values = ref[(slice(None),) * (len(ref.shape) - 1) + (columns,)]
            return values.reshape(-1, values.shape[-1])

        views = dict(
            norms=lambda s, t: (r.norm_own, r.norm_all.at[s]),
            normed=lambda s, t: (r.a_mine.at[t], r.a_all.at[s]),
            joint_weight=lambda s, t: (
                r.wq.at[:, part(s, shard), :],
                r.wq.at[:, part(s, shard), :],
            ),
            out_own=lambda s, t: (r.wo.at[dp - core + s], r.wo.at[dp - core + s]),
            expand=lambda s, t: (
                r.wu.at[:, part(s, shard), :],
                r.wu.at[:, part(s, shard), :],
            ),
            contract=lambda s, t: (
                r.wd.at[part(s, own_units), :],
                r.wd.at[part(s, own_units), :],
            ),
            branch=[
                lambda s, t, h=h: (r.b_send.at[h, t], r.b_recv.at[h, s]) for h in range(2)
            ],
            second=[
                lambda s, t, h=h: (
                    r.c_mine.at[h, lax.div(t, mp_size)],
                    r.c_all.at[h, lax.div(s, mp_size), lax.rem(s, mp_size)],
                )
                for h in range(2)
            ],
            g_contract=lambda s, t: (r.gc_send, r.far_contract),
            d_second=[
                lambda s, t, h=h: (
                    r.dc_send.at[h, lax.div(t, mp_size), lax.rem(t, mp_size)],
                    r.dc_recv.at[h, lax.div(s, mp_size), lax.rem(s, mp_size)],
                )
                for h in range(2)
            ],
            g_expand=lambda s, t: (r.ge_send, r.far_expand),
            d_hidden=[
                lambda s, t, h=h: (r.da_mine.at[h], r.da_rows.at[s, h]) for h in range(2)
            ],
            g_out_pair=lambda s, t: (r.go_pair.at[t], r.far_out),
            out_strip=lambda s, t: (r.y2_send.at[t], r.y2_recv.at[s]),
            d_first=lambda s, t: (
                r.df_send.at[lax.div(t, mp_size), lax.rem(t, mp_size)],
                r.df_recv.at[lax.div(s, mp_size), lax.rem(s, mp_size)],
            ),
            g_joint=lambda s, t: (r.gj_send, r.far_joint),
            out_rows=lambda s, t: (r.y_mine, r.y_rows.at[s]),
            in_rows=lambda s, t: (r.ig_mine, r.grad_rows.at[s]),
            g_norms=lambda s, t: (r.gn_send.at[lax.div(t, mp_size)], r.gn_recv.at[s]),
            g_norms_pair=lambda s, t: (r.gn_pair, r.gn_far),
            squares=lambda s, t: (r.sq_mine, r.sq_recv.at[s]),
            squares_pair=lambda s, t: (r.sq_pair, r.sq_far),
        )
        others = chips * mp_size - 1
        column_blocks = pl.ds(0, mp_size - 1)
        bulks = dict(
            norms=r.norm_all.at[pl.ds(0, dp_size - 1)],
            branch=[r.b_recv.at[h, column_blocks] for h in range(2)],
            second=[r.bulk.at[pl.ds(0, others * half_strip), :]] * 2,
            d_second=[r.bulk.at[pl.ds(0, others * half_strip), :]] * 2,
            d_hidden=[r.da_rows.at[column_blocks, h] for h in range(2)],
            out_strip=r.y2_recv.at[column_blocks],
            d_first=r.bulk,
            out_rows=r.y_rows.at[column_blocks],
            in_rows=r.grad_rows.at[column_blocks],
            g_norms=r.gn_recv.at[pl.ds(0, others)],
            squares=r.sq_recv.at[pl.ds(0, others)],
        )
        lane = SimpleNamespace()
        every_lane = []
        used = iter(sems[2:])

        def pair_of():
            return (next(used), next(used))

        for name, kind in LANES.items():
            group = vars(groups)[kind]
            several = name in HALVED
            bulk = bulks.get(name, None)
            lanes = [
                Lane(group, group.me(), pair_of(), view, one)
                for view, one in (
                    zip(views[name], bulk) if several else [(views[name], bulk)]
                )
            ]
            every_lane += lanes
            setattr(lane, name, lanes if several else lanes[0])
        hop = Hop(dp, mp)

        def gather(own, block, half):
            every_lane.append(PlaneGather(hop, pair_of(), own, block, half))
            return every_lane[-1]

        def reduce(parts, inbox, middle):
            every_lane.append(PlaneReduce(hop, pair_of(), parts, inbox, middle))
            return every_lane[-1]

        def row_half(ref, way):
            rows = ref.shape[0] // 2
            return ref.at[pl.ds(way * rows, rows), :]

        out_plane = gather(r.wo.at[dp], lambda c: r.wo.at[2 * c + core], row_half)
        cot_plane = gather(r.dy_mine, lambda c: r.dy_all.at[c], lambda ref, way: ref.at[way])
        d_pre = [
            gather(r.du_all.at[h, chip], lambda c, h=h: r.du_all.at[h, c], row_half)
            for h in range(2)
        ]
        d_joint = [
            gather(r.dq_mine.at[p], lambda c, p=p: r.dq_all.at[p, c], row_half)
            for p in range(pieces)
        ]
        joint = [reduce(r.j_send.at[p], r.j_recv.at[p], r.j_mid.at[p]) for p in range(pieces)]
        pre_sum = [reduce(r.u_send.at[h], r.u_recv.at[h], r.u_mid.at[h]) for h in range(2)]
        out_sum = reduce(r.y_send, r.y_recv, r.y_mid)
        g_out_sum = reduce(r.go_send, r.go_recv, r.go_mid)
        pass_sems = pair_of()

        def passing(index, to_me):
            source = (*hop.chips, hop.far)[index]
            block = r.wo.at[2 * source + (1 - core if to_me else core)]
            return pltpu.make_async_remote_copy(
                src_ref=block,
                dst_ref=block,
                send_sem=pass_sems[0].at[index],
                recv_sem=pass_sems[1].at[index],
                device_id=(dp + 1 - 2 * core, mp),
                device_id_type=pl.DeviceIdType.MESH,
            )

        loads = [
            pltpu.make_async_copy(source, target, load_sems.at[i])
            for i, (source, target) in enumerate(
                (
                    (r.f_joint, r.own_joint),
                    (r.f_out, r.own_out),
                    (r.f_expand, r.own_expand),
                    (r.f_contract, r.own_contract),
                    (r.f_cot, r.cot),
                )
            )
        ]
        for load in (loads[1], loads[0], loads[2], loads[3], loads[4]):
            load.start()

        leaving = []

        def send_home(index, source, target):
            leaving.append(pltpu.make_async_copy(source, target, home_sems.at[index]))
            leaving[-1].start()

        barrier = pltpu.get_barrier_semaphore()

        def greet(device):
            pl.semaphore_signal(
                barrier, inc=1, device_id=device, device_id_type=pl.DeviceIdType.MESH
            )

        cross = groups.cross
        repeat(1, cross.size, lambda s: greet(cross.device(lax.rem(cross_me + s, cross.size))))
        repeat(0, chips, lambda s: greet((s * 2 + 1 - core, mp)))

        r.norm_all[dp] = r.norm_own[...]
        loads[1].wait()
        r.wo[dp] = r.own_out[...].astype(BF16)
        values = r.x[...].astype(F32)
        centered, inverse = standardise(values)
        unit = centered * inverse
        loads[0].wait()
        for c in range(3):
            r.wq[c, mine, :] = r.own_joint[c].astype(BF16)
        ids = jnp.broadcast_to(r.seg_row[...].astype(F32), (length, length))
        places = lax.broadcasted_iota(jnp.int32, (length, length), 0)
        keys = lax.broadcasted_iota(jnp.int32, (length, length), 1)
        allowed = (ids == ids.T) & (keys <= places)
        pl.semaphore_wait(barrier, cross.size - 1 + chips)

        lane.norms.start_all()
        lane.joint_weight.start_all()
        out_plane.start()
        lane.out_own.start_all()
        lane.norms.take_all()

        def norm_row(index, block=None):
            blocks = range(dp_size) if block is None else (block,)
            rows = [r.norm_all[b, pl.ds(index, 1), :] for b in blocks]
            whole = rows[0] if len(rows) == 1 else jnp.concatenate(rows, axis=1)
            return whole.astype(BF16).astype(F32)

        for b in range(dp_size):
            columns = slice(b * shard, (b + 1) * shard)
            r.a_mine[b // 2, :, (b % 2) * shard : (b % 2 + 1) * shard] = (
                unit[:, columns] * norm_row(0, b) + norm_row(1, b)
            ).astype(BF16)
        lane.normed.start_all()
        r.a_all[chip] = r.a_mine[chip]

        lane.joint_weight.take_all()

        def joint_part(p, block):
            rows = r.a_all[block]
            for c in range(3):
                columns = slice(c * piece, (c + 1) * piece)
                third = mul(rows, r.wq[c, :, p * piece : (p + 1) * piece]).astype(BF16)
                for way in range(2):
                    r.j_send[p, block, way, :, columns] = third[
                        way * half_rows : (way + 1) * half_rows
                    ]

        def chip_step(block):
            return lax.rem(chip + chips - block, chips)

        for p in range(pieces):
            for way in range(2):
                if p == 0:
                    lane.normed.take(chip_step(hop.chips[way]))
                joint_part(p, hop.chips[way])
            joint[p].start(1)
            if p == 0:
                lane.normed.take(chip_step(hop.far))
            joint_part(p, hop.far)
            joint[p].start(0)
            joint_part(p, chip)
        loads[4].wait()
        for h in range(2):
            for m in range(mp_size):
                first = m * strip + h * half_strip
                r.dy_mine[h, m * half_strip : (m + 1) * half_strip, :] = r.cot[
                    first : first + half_strip, :
                ]
        out_plane.forward()
        for index in range(2):
            passing(index, False).start()
        for p in range(pieces):
            joint[p].forward()

        loads[2].wait()
        for c in range(chips):
            r.wu[c, mine, :] = r.own_expand[:, c * units : (c + 1) * units].astype(BF16)
        lane.expand.start_all()
        loads[3].wait()
        r.wd[part(core, own_units), :] = r.own_contract[...].astype(BF16)
        lane.contract.start_all()
        def query_key_value(start):
            p, first = start // piece, start % piece
            return (
                r.joint[p, :, c * piece + first : c * piece + first + HEAD_DIM] for c in range(3)
            )

        for p in range(pieces):
            for way in range(2):
                joint[p].take(way)
                r.joint[p, way * half_rows : (way + 1) * half_rows, :] = (
                    joint[p].total(way).astype(BF16)
                )
            if p == pieces - 1:
                cot_plane.start()
            for start in range(p * piece, (p + 1) * piece, HEAD_DIM):
                query, key, value = query_key_value(start)
                prob = probabilities(query, key, allowed)
                r.attended[:, start : start + HEAD_DIM] = mul(prob.astype(BF16), value).astype(BF16)

        lane.out_own.take_all()
        out_plane.finish()
        passing(2, False).start()
        for index in range(3):
            passing(index, True).wait_recv()
        branch = mul(r.attended[...], flat(r.wo)).astype(BF16)
        for h in range(2):
            for m in range(mp_size):
                first = m * strip + h * half_strip
                r.b_send[h, m] = branch[first : first + half_strip]
            lane.branch[h].start_all()
        r.dy_all[chip] = r.dy_mine[...]
        cot_plane.forward()

        def here(h):
            return pl.ds(pl.multiple_of(mp * strip + h * half_strip, half_strip), half_strip)

        for h in range(2):
            lane.branch[h].take_all()
            total = r.x[here(h), :].astype(F32) + r.b_send[h, mp].astype(F32)
            for step in range(1, mp_size):
                total = total + r.b_recv[h, lane.branch[h].source(step)].astype(F32)
            r.hid[h] = total
            centered, inverse = standardise(total)
            for b in range(dp_size):
                columns = slice(b * shard, (b + 1) * shard)
                r.c_mine[h, b // 2, :, (b % 2) * shard : (b % 2 + 1) * shard] = (
                    centered[:, columns] * inverse * norm_row(2, b) + norm_row(3, b)
                ).astype(BF16)
            lane.second[h].start_all()
            r.c_all[h, chip, mp] = r.c_mine[h, chip]
        lane.expand.take_all()

        def dy_half(h):
            return r.dy_all[:, h].reshape(half_tokens, model)

        quarter = half_tokens // 2

        def pre_part(h, to):
            part_sum = mul(flat(r.c_all.at[h]), r.wu[to]).astype(BF16)
            for way in range(2):
                r.u_send[h, to, way] = part_sum[way * quarter : (way + 1) * quarter]

        for h in range(2):
            lane.second[h].take_all()
            pre_part(h, hop.far)
            pre_sum[h].start(0)
            for way in range(2):
                pre_part(h, hop.chips[way])
            pre_sum[h].start(1)
            pre_part(h, chip)
            if h == 0:
                lane.contract.take_all()
                cot_plane.finish()
            r.dz[h] = mul(dy_half(h), r.wd[...], COLS_COLS)
            pre_sum[h].forward()
        tile = 64

        for h in range(2):
            for way in range(2):
                pre_sum[h].take(way)

                def gelu_tile(i, none, h=h, way=way):
                    rows = part(i, tile)
                    pre = pre_sum[h].total(way, rows)
                    square = pre * pre
                    curve = jnp.tanh(ROOT * pre * (1.0 + CUBE * square))
                    half = 0.5 * (1.0 + curve)
                    slope = half + 0.5 * pre * (1.0 - curve * curve) * (
                        ROOT * (1.0 + 3.0 * CUBE * square)
                    )
                    rows = part(i + way * (quarter // tile), tile)
                    r.z[h, rows, :] = (pre * half).astype(BF16)
                    r.du_all[h, chip, rows, :] = (r.dz[h, rows, :] * slope).astype(BF16)
                    return none

                lax.fori_loop(0, quarter // tile, gelu_tile, None)
            d_pre[h].start()

        def out_part(h):
            part_sum = mul(r.z[h], r.wd[...]).astype(BF16)
            for c in range(chips):
                r.y_send[c, h] = part_sum[c * half_rows : (c + 1) * half_rows]

        def second_part(h, source):
            return mul(r.du_all[h, source], r.wu[source], COLS_COLS)

        d_pre[0].forward()
        for h in range(2):
            out_part(h)
            total = second_part(h, chip)
            for way in range(2):
                total = total + second_part(h, hop.chips[way])
            if h == 0:
                d_pre[1].forward()
            d_pre[h].finish()
            total = (total + second_part(h, hop.far)).astype(BF16)
            for c in range(chips):
                for m in range(mp_size):
                    first = (c * mp_size + m) * half_strip
                    r.dc_send[h, c, m] = total[first : first + half_strip]
            lane.d_second[h].start_all()
        out_sum.start(0)
        out_sum.start(1)

        def contract_grad(columns):
            return sum(mul(r.z[h, :, columns], dy_half(h), ROWS_ROWS) for h in range(2))

        def gathered(recv, rows):
            blocks = []
            for c in range(chips):
                block = jnp.zeros((rows, slab), F32)
                for m in range(mp_size):
                    block = block + recv[c, m].astype(F32)
                blocks.append(block)
            return jnp.concatenate(blocks, axis=1)

        r.gc_send[...] = contract_grad(part(1 - core, own_units)).astype(BF16)
        lane.g_contract.start_all()
        gain_two, shift_two = 0.0, 0.0
        for h in range(2):
            lane.d_second[h].take_all()
            r.dc_recv[h, chip, mp] = r.dc_send[h, chip, mp]
            d_normed = gathered(r.dc_recv.at[h], half_strip)
            back, gain, shift = norm_back(d_normed, r.hid[h], norm_row(2))
            gain_two, shift_two = gain_two + gain, shift_two + shift
            d_hidden = r.cot[here(h), :].astype(F32) + back
            r.dh[h] = d_hidden
            r.da_mine[h] = d_hidden.astype(BF16)
            lane.d_hidden[h].start_all()
            r.da_rows[mp, h] = r.da_mine[h]
        out_sum.forward()
        for c in range(chips):
            r.ge_send[:, c * units : (c + 1) * units] = mul(
                flat(r.c_all, other), flat(r.du_all.at[:, c]), ROWS_ROWS
            ).astype(BF16)
        lane.g_expand.start_all()
        r.own_contract[...] = contract_grad(part(core, own_units))
        for h in range(2):
            lane.d_hidden[h].take_all()

        for way in range(2):
            out_sum.take(way)
            total = out_sum.total(way).astype(BF16)
            for m in range(mp_size):
                r.y2_send[m, way * half_strip : (way + 1) * half_strip, :] = total[
                    m * half_strip : (m + 1) * half_strip
                ]
        lane.out_strip.start_all()
        d_attended = mul(flat(r.da_rows), flat(r.wo), COLS_COLS).astype(BF16)
        for p in range(pieces):
            for start in range(p * piece, (p + 1) * piece, HEAD_DIM):
                query, key, value = query_key_value(start)
                d_out = d_attended[:, start : start + HEAD_DIM]
                prob = probabilities(query, key, allowed)
                d_prob = mul(d_out, value, COLS_COLS)
                row_delta = jnp.sum(d_prob * prob, axis=-1, keepdims=True)
                d_raw = (prob * (d_prob - row_delta) * SCALE).astype(BF16)
                thirds = (
                    mul(d_raw, key),
                    mul(d_raw, query, ROWS_ROWS),
                    mul(prob.astype(BF16), d_out, ROWS_ROWS),
                )
                for c in range(3):
                    first = c * piece + start % piece
                    r.dq_mine[p, :, first : first + HEAD_DIM] = thirds[c].astype(BF16)
            d_joint[p].start()
            r.dq_all[p, chip] = r.dq_mine[p]

        grad_out = mul(r.attended[...], flat(r.da_rows), ROWS_ROWS).astype(BF16)
        for c in range(chips):
            for k in range(2):
                first = (2 * c + k) * out_rows
                r.go_send[c, k] = grad_out[first : first + out_rows]

        def first_block(block):
            total = jnp.zeros((length, slab), F32)
            for p in range(pieces):
                for c in range(3):
                    total = total + mul(
                        r.dq_all[p, block, :, c * piece : (c + 1) * piece],
                        r.wq[c, :, p * piece : (p + 1) * piece],
                        COLS_COLS,
                    )
            total = total.astype(BF16)
            for m in range(mp_size):
                r.df_send[block, m] = total[m * strip : (m + 1) * strip]

        def first_send(block, others):
            for j in others:
                to = block * mp_size + lax.rem(mp + j, mp_size)
                lane.d_first.start(lax.rem(to + cross.size - cross_me, cross.size))

        first_block(chip)
        first_send(chip, range(1, mp_size))
        for p in range(pieces):
            d_joint[p].forward()
        for way in range(2):
            first_block(hop.chips[way])
            first_send(hop.chips[way], range(mp_size))
        for p in range(pieces):
            d_joint[p].finish()
        first_block(hop.far)
        first_send(hop.far, range(mp_size))
        lane.out_strip.take_all()
        total = r.hid[...].reshape(strip, model) + r.y2_send[mp].astype(F32)
        for step in range(1, mp_size):
            total = total + r.y2_recv[lane.out_strip.source(step)].astype(F32)
        r.y_mine[...] = total.astype(BF16)
        lane.out_rows.start_all()
        r.layer_output[part(mp, strip), :] = r.y_mine[...]
        g_out_sum.start(0)
        g_out_sum.start(1)

        def joint_grad(c, columns, target):
            for p in range(pieces):
                target[c, :, p * piece : (p + 1) * piece] = mul(
                    flat(r.a_all, columns),
                    r.dq_all[p, :, :, c * piece : (c + 1) * piece].reshape(tokens, piece),
                    ROWS_ROWS,
                ).astype(target.dtype)

        for c in range(3):
            joint_grad(c, other, r.gj_send)
        lane.g_joint.start_all()
        for c in range(3):
            joint_grad(c, mine, r.own_joint)
        for c in range(chips):
            r.own_expand[:, c * units : (c + 1) * units] = mul(
                flat(r.c_all, mine), flat(r.du_all.at[:, c]), ROWS_ROWS
            )
        g_out_sum.forward()

        lane.d_first.take_all()
        r.df_recv[chip, mp] = r.df_send[chip, mp]
        d_normed = gathered(r.df_recv, strip)
        back, gain_one, shift_one = norm_back(d_normed, r.x[part(mp, strip), :].astype(F32), norm_row(0))
        grad = r.dh[...].reshape(strip, model) + back
        r.ig_mine[...] = grad.astype(BF16)
        for index, row in enumerate((gain_one, shift_one, gain_two, shift_two)):
            for b in range(dp_size):
                place = (b % 2) * 4 + index
                r.gn_send[b // 2, place : place + 1, :] = row[:, b * shard : (b + 1) * shard]
        lane.g_norms.start_all()
        lane.in_rows.start_all()
        r.grad_rows[mp] = r.ig_mine[...]
        r.gn_recv[cross_me] = r.gn_send[chip]

        def settle(own, distant):
            whole = own[...] + distant[...].astype(F32)
            distant[...] = whole.astype(BF16)
            return jnp.sum(whole * whole, axis=0, keepdims=True)

        def folded(row):
            return sum(row[:, i : i + 128] for i in range(0, row.shape[1], 128))

        lane.g_contract.take_all()
        squares = folded(settle(r.own_contract, r.far_contract))
        send_home(3, r.far_contract, r.sum_contract)
        lane.g_expand.take_all()
        squares = squares + folded(settle(r.own_expand, r.far_expand))
        send_home(2, r.far_expand, r.sum_expand)
        lane.g_joint.take_all()
        for c in range(3):
            squares = squares + folded(settle(r.own_joint.at[c], r.far_joint.at[c]))
        send_home(0, r.far_joint, r.sum_joint)

        for k in range(2):
            g_out_sum.take(k)
            total = g_out_sum.total(k)

            @pl.when(core == k)
            def _():
                r.own_out[...] = total

            r.go_pair[k] = total.astype(BF16)
        lane.g_out_pair.start_all()

        lane.g_norms.take_all()
        summed = r.gn_recv[0]
        for index in range(1, chips * mp_size):
            summed = summed + r.gn_recv[index]
        r.gn_pair[...] = summed
        lane.g_norms_pair.start_all()
        lane.g_out_pair.take_all()
        squares = squares + folded(settle(r.own_out, r.far_out))
        send_home(1, r.far_out, r.sum_out)
        lane.g_norms_pair.take_all()
        summed = summed + r.gn_far[...]
        own_norms = jnp.where(core == 0, summed[:4], summed[4:])
        r.own_norms[...] = own_norms
        own_norms = jnp.sum(own_norms * own_norms, axis=0, keepdims=True) * (1.0 / mp_size)
        squares = squares + folded(own_norms)
        r.sq_mine[...] = jnp.broadcast_to(jnp.sum(squares), (8, 128))
        lane.squares.start_all()
        r.sq_recv[cross_me] = r.sq_mine[...]

        def place(rows_lane, rows, output):
            rows_lane.take_all()
            for step in range(1, mp_size):
                source = rows_lane.source(step)
                output[part(source, strip), :] = rows[source].astype(output.dtype)

        place(lane.out_rows, r.y_rows, r.layer_output)
        send_home(4, r.layer_output, r.home_output)
        lane.in_rows.take_all()
        send_home(5, r.grad_rows, r.home_rows)
        lane.squares.take_all()
        total = r.sq_recv[0]
        for index in range(1, chips * mp_size):
            total = total + r.sq_recv[index]
        r.sq_pair[...] = total
        lane.squares_pair.start_all()
        lane.squares_pair.take_all()
        r.square_sum[...] = (total + r.sq_far[...])[:1, :1]
        for entry in every_lane:
            entry.sent_all()
        for index in range(3):
            passing(index, False).wait_send()
        for entry in leaving:
            entry.wait()

    vmem = pl.BlockSpec(memory_space=pltpu.VMEM)
    any_space = pl.BlockSpec(memory_space=pl.ANY)
    sem_shapes = [pltpu.SemaphoreType.DMA((5,)), pltpu.SemaphoreType.DMA((6,))]
    for name, kind in LANES.items():
        count = 2 * HALVED.get(name, 1)
        slots = vars(groups)[kind].size - 1 if kind == PAIR or name in STEPWISE else 1
        sem_shapes += [pltpu.SemaphoreType.DMA((slots,))] * count
    sem_shapes += [pltpu.SemaphoreType.DMA((4,))] * 2 * (4 + pieces)
    sem_shapes += [pltpu.SemaphoreType.DMA((6,))] * 2 * (4 + pieces)
    sem_shapes += [pltpu.SemaphoreType.DMA((3,))] * 2
    results = pl.pallas_call(
        kernel,
        out_shape=list(outs.values()) + list(homes.values()),
        in_specs=[vmem] * 2 + [any_space] * 5 + [vmem],
        out_specs=[vmem] * len(outs) + [any_space] * len(homes),
        scratch_shapes=[pltpu.VMEM(*entry) for entry in scratch.values()] + sem_shapes,
        compiler_params=pltpu.CompilerParams(
            collective_id=30, has_side_effects=True, vmem_limit_bytes=VMEM_LIMIT
        ),
    )(x, segments, cotangent, joint_w, out_w, expand_w, contract_w, norms)
    return SimpleNamespace(**dict(zip(list(outs) + list(homes), results)))


VMEM_LIMIT = 60 * 2**20


CHUNKS = 4
TILE_ROWS = 16


def adam_kernel(shapes, *refs):
    squares, output, grad_rows = refs[:3]
    ins = [refs[3 + 4 * k : 7 + 4 * k] for k in range(4)]
    norm_ins = refs[19:23]
    norm_out, output_out, input_grad = refs[23:26]
    outs = [refs[26 + 5 * k : 31 + 5 * k] for k in range(5)]
    held = [refs[51 + 5 * k : 56 + 5 * k] for k in range(4)]
    output_held, rows_held, grad_held, in_sems, out_sems, row_sems = refs[71:]

    chunks = []
    for k in (2, 3, 0, 1):
        total = shapes[k][0]
        count = max(total // CHUNKS, 64)
        chunks += [(k, first, count) for first in range(0, total, count)]
    loads = [
        [
            pltpu.make_async_copy(
                ins[k][a].at[pl.ds(first, count), :],
                held[k][a].at[pl.ds(first, count), :],
                in_sems.at[4 * index + a],
            )
            for a in range(4)
        ]
        for index, (k, first, count) in enumerate(chunks)
    ]
    for group in loads:
        for load in group:
            load.start()
    row_loads = [
        pltpu.make_async_copy(output, output_held, row_sems.at[0]),
        pltpu.make_async_copy(grad_rows, rows_held, row_sems.at[1]),
    ]
    for load in row_loads:
        load.start()
    norm = jnp.sqrt(squares[...])
    norm_out[...] = norm
    clip = jnp.minimum(1.0, MAX_NORM / (norm + CLIP_EPSILON))

    stores = []
    for index, (k, first, count) in enumerate(chunks):
        for load in loads[index]:
            load.wait()
        low, weight, moment, square, whole = held[k]

        def tile(i, none, k=k, first=first, refs=held[k]):
            low, weight, moment, square, whole = refs
            here = pl.ds(pl.multiple_of(first + i * TILE_ROWS, TILE_ROWS), TILE_ROWS)
            grad = low[here, :].astype(F32)
            entries = adam_update(
                weight[here, :], grad, moment[here, :], square[here, :], LEARN_RATES[k], clip
            )
            whole[here, :] = grad
            moment[here, :], square[here, :], weight[here, :] = entries
            low[here, :] = entries[2].astype(BF16)
            return none

        lax.fori_loop(0, count // TILE_ROWS, tile, None)
        for a, source in enumerate((whole, moment, square, weight, low)):
            stores.append(
                pltpu.make_async_copy(
                    source.at[pl.ds(first, count), :],
                    outs[k][a].at[pl.ds(first, count), :],
                    out_sems.at[5 * index + a],
                )
            )
            stores[-1].start()
    for load in row_loads:
        load.wait()
    grad_held[...] = rows_held[...].astype(F32)
    stores.append(pltpu.make_async_copy(output_held, output_out, row_sems.at[2]))
    stores[-1].start()
    stores.append(pltpu.make_async_copy(grad_held, input_grad, row_sems.at[3]))
    stores[-1].start()
    own, weight, moment, square = (entry[...] for entry in norm_ins)
    entries = adam_update(weight, own, moment, square, LEARN_RATES[4], clip)
    for target, entry in zip(outs[4], (own, *entries, entries[2].astype(BF16))):
        target[...] = entry
    for store in stores:
        store.wait()


def optimizer(r, params, firsts, seconds):
    def rows(array):
        return array.reshape(-1, array.shape[-1])

    vmem, any_space = pl.BlockSpec(memory_space=pltpu.VMEM), pl.BlockSpec(memory_space=pl.ANY)
    sums = (r.sum_joint, r.sum_out, r.sum_expand, r.sum_contract)
    operands = [r.square_sum, r.home_output, rows(r.home_rows)]
    results = [shape((1, 1), F32), shape(operands[1].shape), shape(operands[2].shape, F32)]
    scratch, shapes = [], []
    for total, weight, first, second in zip(sums, params, firsts, seconds):
        arrays = [rows(a) for a in (total, weight, first, second)]
        operands += arrays
        shapes.append(arrays[0].shape)
        results += [shape(shapes[-1], F32)] * 4 + [shape(shapes[-1])]
        scratch += [pltpu.VMEM(a.shape, a.dtype) for a in arrays] + [pltpu.VMEM(shapes[-1], F32)]
    operands += [r.own_norms, params[4], firsts[4], seconds[4]]
    results += [shape(r.own_norms.shape, F32)] * 4 + [shape(r.own_norms.shape)]
    count = sum(entry[0] // max(entry[0] // CHUNKS, 64) for entry in shapes)
    out = pl.pallas_call(
        functools.partial(adam_kernel, shapes),
        in_specs=[vmem] + [any_space] * 18 + [vmem] * 4,
        out_specs=[vmem] + [any_space] * 22 + [vmem] * 5,
        out_shape=results,
        scratch_shapes=scratch
        + [pltpu.VMEM(entry.shape, entry.dtype) for entry in (operands[1], operands[2], results[2])]
        + [pltpu.SemaphoreType.DMA((4 * count,)), pltpu.SemaphoreType.DMA((5 * count,))]
        + [pltpu.SemaphoreType.DMA((4,))],
        compiler_params=pltpu.CompilerParams(vmem_limit_bytes=VMEM_LIMIT),
    )(*operands)
    sets = [
        [entry.reshape(params[k].shape) for entry in out[3 + 5 * k : 8 + 5 * k]] for k in range(5)
    ]
    return (out[1], out[2]), sets, out[0].reshape(())


def local(dp_size, mp_size, *arrays):
    params, firsts, seconds = arrays[3:8], arrays[8:13], arrays[13:18]
    r = layer(dp_size, mp_size, arrays[:8])
    rows, sets, gradient_norm = optimizer(r, params, firsts, seconds)
    return (*rows, *[sets[k][c] for c in range(5) for k in range(5)], gradient_norm)


def solution(mesh):
    rows = P("dp", None)
    sets = (
        P(None, "dp", "mp"),
        P(("mp", "dp"), None),
        P("dp", "mp"),
        P(("mp", "dp"), None),
        P(None, "dp"),
    )
    form = local if mesh.shape["dp"] == 8 else local_steps
    return jax.shard_map(
        functools.partial(form, mesh.shape["dp"], mesh.shape["mp"]),
        mesh=mesh,
        in_specs=(rows, rows, rows) + sets * 3,
        out_specs=(rows, rows) + sets * 5 + (P(),),
        check_vma=False,
    )
```
